32 devices in a mesh: strip: 8 (over z, y), chan: 4 (over x, core).
Axes of the slice: x: 2, y: 2, z: 4, core: 2. Of those that a mesh axis runs over, the one named last changes fastest.
Arguments:
- grid: bfloat16 [2, 64, 1024, 1024], P(None, 'chan', 'strip'), may hold values from -6 to 6
- model_image: float32 [64, 1024, 1024], P('chan', 'strip'), may hold values from -160 to 160
- step_size: float32 [64], P('chan'), may hold values from 0.5 to 1.5
- highpass: float32 [3, 4], replicated, may hold values from -1.4 to 1.4
- shrinkage: float32 [8], P('strip'), may hold values from 0.1 to 0.5
Outputs:
- updated: float32 [64, 1024, 1024], P('chan', 'strip')
The draws below stay inside these ranges and needn't reach their ends.
All inputs are finite; a program needn't handle non-finite values.
Results may differ from the reference program's by a relative error of at most 0.0019.
Values may be sent and summed in bfloat16 or wider, within the bound.
No kernel may reach another device: no remote copies, remote signals or barrier semaphores. Data moves between devices by JAX's collectives and lax.ppermute only.
A program may use at most 128 MiB of HBM per device.

```python
import math
import jax
import jax.numpy as jnp
from jax import lax

CH = 64
IMG = 1024
LEVELS = 3
FILT = 4
NS_ITERS = 5
FACET_ROWS = 128
FACETS = 8


def draw_model_image(key, part):
    subkeys = jax.random.split(jax.random.fold_in(key, 17), 6)
    log_low = math.log(0.3)
    log_high = math.log(3.0)
    row_scale = jnp.exp(jax.random.uniform(subkeys[0], (CH, IMG, 1), jnp.float32, log_low, log_high))
    col_scale = jnp.exp(jax.random.uniform(subkeys[1], (CH, 1, IMG), jnp.float32, log_low, log_high))
    region_side = IMG // 16
    region_scale = jnp.exp(jax.random.uniform(subkeys[2], (CH, 16, 16), jnp.float32, log_low, log_high))
    region_full = jnp.repeat(jnp.repeat(region_scale, region_side, axis=1), region_side, axis=2)
    row_index = jnp.arange(IMG, dtype=jnp.int32)
    row_ramp = 1.0 + (row_index % FACET_ROWS).astype(jnp.float32) / FACET_ROWS
    col_ramp = 1.0 + row_index.astype(jnp.float32) / IMG
    noise_field = jnp.clip(jax.random.normal(subkeys[3], (CH, IMG, IMG), jnp.float32), -4.0, 4.0)
    mixing = 0.6
    shared = jnp.clip(jax.random.normal(subkeys[4], (1, IMG, IMG), jnp.float32), -4.0, 4.0)
    loading = jnp.clip(jax.random.normal(subkeys[5], (CH, 16, 16), jnp.float32), -4.0, 4.0)
    loading_full = jnp.repeat(jnp.repeat(loading, region_side, axis=1), region_side, axis=2)
    values = 0.3 * region_full * row_scale * col_scale * row_ramp[None, :, None] * col_ramp[None, None, :] * noise_field
    return values + mixing * shared * loading_full


def block_levels(rng, extent, pieces, smallest, top_value):
    def one(dim, blocks):
        heights = jax.random.uniform(jax.random.fold_in(jax.random.fold_in(rng, 6), dim), (blocks,), jnp.float32, smallest / len(pieces), top_value / len(pieces))
        return jnp.repeat(jnp.exp(heights), extent[dim] // blocks).reshape((-1,) + (1,) * (len(extent) - dim - 1))

    factor_of = one(*pieces[0])
    for cut in pieces[1:]:
        factor_of = factor_of * one(*cut)
    return factor_of


def noise(stream_key, dims, deviation, reach, pieces=(), kind=jnp.bfloat16):
    array = deviation * jax.random.normal(stream_key, dims, jnp.float32)
    if pieces:
        array = array * block_levels(stream_key, dims, pieces, -0.22, 0.18)
    return jnp.clip(array, -reach, reach).astype(kind)


def setup_inputs(seed: int = 0) -> dict:
    splits = jax.random.split(jax.random.key(seed), 6)
    grid = noise(splits[0], (2, CH, IMG, IMG), 1.0, 6.0, ((1, 4), (2, 8)))
    model_image = draw_model_image(jax.random.fold_in(splits[5], 71), 0)
    step_size = jnp.clip(jnp.exp(math.log(1.5) - 1.0986123 * jax.random.uniform(splits[2], (CH,), jnp.float32) ** block_levels(splits[2], (CH,), ((0, 4),), -0.2, 0.2)), 0.5, 1.5)
    highpass = noise(splits[3], (LEVELS, FILT), 0.35, 1.4, (), jnp.float32)
    shrinkage = jnp.clip(jnp.exp(math.log(0.5) - 1.609438 * jax.random.uniform(splits[4], (FACETS,), jnp.float32) ** block_levels(splits[4], (FACETS,), ((0, 8),), -0.2, 0.2)), 0.1, 0.5)
    return dict(grid=grid, model_image=model_image, step_size=step_size, highpass=highpass, shrinkage=shrinkage)


def make_tables():
    indices = jnp.arange(IMG, dtype=jnp.int32)
    products = indices[:, None] * indices[None, :] % IMG
    phases = products.astype(jnp.float32) * (2.0 * 3.141592653589793 / IMG)
    unit_scale = float(IMG) ** (-0.5)
    cosine = (jnp.cos(phases) * unit_scale).astype(jnp.bfloat16)
    sine_table = (jnp.sin(phases) * unit_scale).astype(jnp.bfloat16)
    return (cosine, sine_table)

def dirty_channel(cosine, sine_table, plane):
    real_part = plane[0]
    imag_part = plane[1]
    half_real = jnp.dot(real_part, cosine, preferred_element_type=jnp.float32) - jnp.dot(imag_part, sine_table, preferred_element_type=jnp.float32)
    half_imag = jnp.dot(real_part, sine_table, preferred_element_type=jnp.float32) + jnp.dot(imag_part, cosine, preferred_element_type=jnp.float32)
    half_real = half_real.astype(jnp.bfloat16)
    half_imag = half_imag.astype(jnp.bfloat16)
    return jnp.dot(half_real.T, cosine, preferred_element_type=jnp.float32) - jnp.dot(half_imag.T, sine_table, preferred_element_type=jnp.float32)

def wavelet_gradient(image, highpass):
    running = jnp.zeros(image.shape, jnp.float32)
    half_taps = FILT // 2
    for level_idx in range(LEVELS):
        dilation = 2 ** level_idx
        reach_rows = half_taps * dilation
        padded = jnp.pad(image, ((0, 0), (reach_rows, reach_rows), (0, 0)))
        detail = jnp.zeros(image.shape, jnp.float32)
        for tap_index in range(FILT):
            offset = (tap_index - half_taps) * dilation
            detail = detail + highpass[level_idx, tap_index] * padded[:, reach_rows + offset:reach_rows + offset + IMG, :]
        padded = jnp.pad(detail, ((0, 0), (reach_rows, reach_rows), (0, 0)))
        for tap_index in range(FILT):
            offset = (tap_index - half_taps) * dilation
            running = running + highpass[level_idx, tap_index] * padded[:, reach_rows - offset:reach_rows - offset + IMG, :]
    return running

def newton_schulz(gram_sum):
    frob_norm = jnp.sqrt(jnp.sum(gram_sum * gram_sum))
    identity = jnp.eye(gram_sum.shape[0], dtype=jnp.float32)
    current = gram_sum / frob_norm
    inverse = identity
    for iteration in range(NS_ITERS):
        middle = 0.5 * (3.0 * identity - jnp.dot(inverse, current, precision=lax.Precision.HIGHEST))
        current = jnp.dot(current, middle, precision=lax.Precision.HIGHEST)
        inverse = jnp.dot(middle, inverse, precision=lax.Precision.HIGHEST)
    return (inverse, frob_norm)

def facet_prox(packed):
    pixels, shrink_one = packed
    gram_sum = jnp.dot(pixels, pixels.T, precision=lax.Precision.HIGHEST)
    inverse, frob_norm = newton_schulz(gram_sum)
    polar = jnp.sqrt(pixels.shape[1] / frob_norm) * jnp.dot(inverse.T, pixels, precision=lax.Precision.HIGHEST)
    return pixels - shrink_one * polar

def reference(grid, model_image, step_size, highpass, shrinkage):
    cosine, sine_table = make_tables()
    planes = jnp.moveaxis(grid, 1, 0)
    dirty_image = lax.map(lambda plane: dirty_channel(cosine, sine_table, plane), planes)
    wavelet_grad = wavelet_gradient(model_image, highpass)
    moved = model_image + step_size[:, None, None] * (dirty_image - wavelet_grad)
    blocks = moved.reshape(CH, FACETS, FACET_ROWS * IMG).transpose(1, 0, 2)
    results = lax.map(facet_prox, (blocks, shrinkage))
    return results.transpose(1, 0, 2).reshape(CH, IMG, IMG)
```

```python
import functools

import jax
import jax.numpy as jnp
import ml_dtypes
import numpy as np
from jax import lax
from jax.experimental import pallas as pl
from jax.experimental.pallas import tpu as pltpu
from jax.sharding import PartitionSpec as P

NS_ITERS = 5
CHUNK_ROWS = 16
HIGHEST = lax.Precision.HIGHEST
F32 = jnp.float32
BF16 = jnp.bfloat16
MIB = 1 << 20


def make_tables(side_len):
    indices = np.arange(side_len, dtype=np.int64)
    phases = (np.outer(indices, indices) % side_len).astype(np.float32) * np.float32(
        2.0 * 3.141592653589793 / side_len
    )
    unit_scale = np.float32(float(side_len) ** (-0.5))
    cosine = (np.cos(phases) * unit_scale).astype(ml_dtypes.bfloat16)
    sine_table = (np.sin(phases) * unit_scale).astype(ml_dtypes.bfloat16)
    return cosine, sine_table


def dot_nt(a, b, precision=None):
    return lax.dot_general(
        a, b, (((1,), (1,)), ((), ())), precision=precision, preferred_element_type=F32
    )


def dot_nn(a, b, precision=None):
    return lax.dot_general(
        a, b, (((1,), (0,)), ((), ())), precision=precision, preferred_element_type=F32
    )


def first_body(table_ref, grid_ref, out_ref):
    strips, _, chans, rows, width = out_ref.shape
    side_len = table_ref.shape[-1]
    table = table_ref[0]
    middle = strips * rows
    turned = jnp.concatenate([-table[middle:], table[:middle]], axis=0)
    total = dot_nt(table, grid_ref[0].reshape(chans * width, side_len))
    total = total + dot_nt(turned, grid_ref[1].reshape(chans * width, side_len))
    total = total.astype(BF16)
    for part in range(2):
        for strip in range(strips):
            first = (part * strips + strip) * rows
            for chan in range(chans):
                out_ref[strip, part, chan] = total[
                    first : first + rows, chan * width : (chan + 1) * width
                ]


def first_transform(tables, grid, chunk, strips):
    _, chans, width, side_len = grid.shape
    rows = tables.shape[1] // (2 * strips)
    shape = (strips, 2, chans, rows, width)
    if width % 128 or rows % 16:
        middle = strips * rows
        table = tables[chunk]
        turned = jnp.concatenate([-table[middle:], table[:middle]], axis=0)
        total = jnp.einsum("mv,cuv->mcu", table, grid[0], preferred_element_type=F32)
        total = total + jnp.einsum("mv,cuv->mcu", turned, grid[1], preferred_element_type=F32)
        total = total.astype(BF16).reshape(2, strips, rows, chans, width)
        return total.transpose(1, 0, 3, 2, 4)
    block = 4 if chans % 4 == 0 else 1
    return pl.pallas_call(
        first_body,
        grid=(chans // block,),
        in_specs=[
            pl.BlockSpec((1,) + tables.shape[1:], lambda i: (chunk, 0, 0)),
            pl.BlockSpec((2, block, width, side_len), lambda i: (0, i, 0, 0)),
        ],
        out_specs=pl.BlockSpec((strips, 2, block, rows, width), lambda i: (0, 0, i, 0, 0)),
        out_shape=jax.ShapeDtypeStruct(shape, BF16),
        compiler_params=pltpu.CompilerParams(vmem_limit_bytes=48 * MIB),
        cost_estimate=pl.CostEstimate(
            flops=4 * 2 * strips * rows * chans * width * side_len // 2,
            bytes_accessed=2 * grid.size,
            transcendentals=0,
        ),
        name="first_transform",
    )(tables, grid)


def band_matrix(highpass, own_rows, reach, first_row, image_rows):
    levels, taps = highpass.shape
    half_taps = taps // 2
    row = lax.broadcasted_iota(jnp.int32, (own_rows, own_rows + 2 * reach), 0)
    column = lax.broadcasted_iota(jnp.int32, (own_rows, own_rows + 2 * reach), 1) - reach
    total = jnp.zeros(row.shape, F32)
    for level in range(levels):
        dilation = 2**level
        for outer in range(taps):
            detail_row = row - (outer - half_taps) * dilation
            inside = (detail_row + first_row >= 0) & (detail_row + first_row < image_rows)
            for inner in range(taps):
                hit = inside & (column == detail_row + (inner - half_taps) * dilation)
                total = total + jnp.where(hit, highpass[level, outer] * highpass[level, inner], 0.0)
    return total


def base_body(step_ref, own_ref, side_ref, model_ref, edge_ref, out_ref):
    first = pl.program_id(0) * model_ref.shape[0]
    for chan in range(model_ref.shape[0]):
        model = model_ref[chan]
        gradient = dot_nn(own_ref[...], model, HIGHEST)
        gradient = gradient + dot_nn(side_ref[...], edge_ref[chan].astype(F32), HIGHEST)
        out_ref[chan] = model - step_ref[first + chan] * gradient


def base_step(step_size, own_band, side_band, model_image, edges):
    chans, rows, side_len = model_image.shape
    block = 2 if chans % 2 == 0 else 1
    return pl.pallas_call(
        base_body,
        grid=(chans // block,),
        in_specs=[
            pl.BlockSpec(memory_space=pltpu.SMEM),
            pl.BlockSpec(own_band.shape, lambda i: (0, 0)),
            pl.BlockSpec(side_band.shape, lambda i: (0, 0)),
            pl.BlockSpec((block, rows, side_len), lambda i: (i, 0, 0)),
            pl.BlockSpec((block, edges.shape[1], side_len), lambda i: (i, 0, 0)),
        ],
        out_specs=pl.BlockSpec((block, rows, side_len), lambda i: (i, 0, 0)),
        out_shape=jax.ShapeDtypeStruct(model_image.shape, F32),
        compiler_params=pltpu.CompilerParams(vmem_limit_bytes=32 * MIB),
        cost_estimate=pl.CostEstimate(
            flops=12 * rows * rows * chans * side_len, bytes_accessed=8 * model_image.size, transcendentals=0
        ),
        name="base_step",
    )(step_size, own_band, side_band, model_image, edges)


def second_body(step_ref, half_ref, cosine_ref, sine_ref, base_ref, moved_ref, pixels_ref):
    strips, _, chans, rows, width = half_ref.shape
    real = jnp.concatenate([half_ref[s, 0].reshape(chans * rows, width) for s in range(strips)], axis=1)
    imag = jnp.concatenate([half_ref[s, 1].reshape(chans * rows, width) for s in range(strips)], axis=1)
    dirty = dot_nn(real, cosine_ref[...]) - dot_nn(imag, sine_ref[...])
    pieces = []
    for chan in range(chans):
        moved = base_ref[chan] + step_ref[chan] * dirty[chan * rows : (chan + 1) * rows]
        moved_ref[chan] = moved
        pieces.append(moved)
    pixels_ref[...] = jnp.swapaxes(jnp.stack(pieces), 0, 1).astype(BF16)


def second_transform(step_size, half, cosine, sine_table, base, chunk):
    strips, _, chans, rows, width = half.shape
    side_len = cosine.shape[0]
    if width % 128 or rows % 16 or chans % 16:
        dirty = jnp.einsum("scmu,sul->cml", half[:, 0], cosine.reshape(strips, width, side_len), preferred_element_type=F32)
        dirty = dirty - jnp.einsum(
            "scmu,sul->cml", half[:, 1], sine_table.reshape(strips, width, side_len), preferred_element_type=F32
        )
        moved = base[:, chunk * rows : (chunk + 1) * rows] + step_size[:, None, None] * dirty
        pixels = moved.astype(BF16).transpose(1, 0, 2)
        return lax.dynamic_update_slice(base, moved, (0, chunk * rows, 0)), pixels
    block = min(256, side_len)
    return pl.pallas_call(
        second_body,
        grid=(side_len // block,),
        in_specs=[
            pl.BlockSpec(memory_space=pltpu.SMEM),
            pl.BlockSpec(half.shape, lambda i: (0, 0, 0, 0, 0)),
            pl.BlockSpec((side_len, block), lambda i: (0, i)),
            pl.BlockSpec((side_len, block), lambda i: (0, i)),
            pl.BlockSpec((chans, rows, block), lambda i: (0, chunk, i)),
        ],
        out_specs=[
            pl.BlockSpec((chans, rows, block), lambda i: (0, chunk, i)),
            pl.BlockSpec((rows, chans, block), lambda i: (0, 0, i)),
        ],
        out_shape=[
            jax.ShapeDtypeStruct(base.shape, F32),
            jax.ShapeDtypeStruct((rows, chans, side_len), BF16),
        ],
        input_output_aliases={4: 0},
        compiler_params=pltpu.CompilerParams(vmem_limit_bytes=32 * MIB),
        cost_estimate=pl.CostEstimate(
            flops=4 * chans * rows * side_len * side_len,
            bytes_accessed=4 * side_len * side_len + 10 * chans * rows * side_len,
            transcendentals=0,
        ),
        name="second_transform",
    )(step_size, half, cosine, sine_table, base)


GRAM_ROWS = 4
POLAR_ROWS = 8


def stacked(pixels_ref, first, count):
    groups = pixels_ref.shape[0]
    pieces = [pixels_ref[g, first + i] for i in range(count) for g in range(groups)]
    return jnp.concatenate(pieces, axis=0)


def gram_body(pixels_ref, before_ref, total_ref):
    @pl.when(pl.program_id(0) == 0)
    def _():
        total_ref[...] = before_ref[...]

    pixels = stacked(pixels_ref, 0, GRAM_ROWS)
    total_ref[...] += dot_nt(pixels, pixels)


def gram_step(pixels, before):
    groups, rows, chans, side_len = pixels.shape
    return pl.pallas_call(
        gram_body,
        grid=(rows // GRAM_ROWS,),
        in_specs=[
            pl.BlockSpec((groups, GRAM_ROWS, chans, side_len), lambda i: (0, i, 0, 0)),
            pl.BlockSpec(before.shape, lambda i: (0, 0)),
        ],
        out_specs=pl.BlockSpec(before.shape, lambda i: (0, 0)),
        out_shape=jax.ShapeDtypeStruct(before.shape, F32),
        compiler_params=pltpu.CompilerParams(vmem_limit_bytes=32 * MIB),
        cost_estimate=pl.CostEstimate(
            flops=2 * before.size * side_len * rows // GRAM_ROWS, bytes_accessed=2 * pixels.size, transcendentals=0
        ),
        name="gram_step",
    )(pixels, before)


def iota(shape, dim):
    return lax.broadcasted_iota(jnp.int32, shape, dim)


def newton_schulz(gram):
    size = gram.shape[0]
    frob_norm = jnp.sqrt(jnp.sum(gram * gram))
    identity = (iota((size, size), 0) == iota((size, size), 1)).astype(F32)
    current = gram / frob_norm
    inverse = identity
    for iteration in range(NS_ITERS):
        middle = 0.5 * (3.0 * identity - dot_nn(inverse, current, HIGHEST))
        if iteration + 1 < NS_ITERS:
            current = dot_nn(current, middle, HIGHEST)
        inverse = dot_nn(middle, inverse, HIGHEST)
    return inverse, frob_norm


def polar_body(chunks, shrink_ref, select_ref, gram_ref, moved_hbm, *refs):
    pixels_hbm = refs[:chunks]
    out_hbm, pixels, moved, in_sems, moved_sems, out_sems = refs[chunks:]
    own, all_rows, side_len = moved.shape
    rows = all_rows // chunks
    size = select_ref.shape[1]
    moved_copies = []
    pixel_copies = []
    for chunk in range(chunks):
        copy = pltpu.make_async_copy(pixels_hbm[chunk], pixels.at[chunk], in_sems.at[chunk])
        copy.start()
        pixel_copies.append(copy)
        part = pl.ds(chunk * rows, rows)
        copy = pltpu.make_async_copy(moved_hbm.at[:, part], moved.at[:, part], moved_sems.at[chunk])
        copy.start()
        moved_copies.append(copy)
    gram = jnp.zeros((size, size), F32)
    for i in range(GRAM_ROWS):
        gram = gram + gram_ref[i * size : (i + 1) * size, i * size : (i + 1) * size]
    inverse, frob_norm = newton_schulz(gram)
    factor = shrink_ref[0] * jnp.sqrt(all_rows * side_len / frob_norm)
    weights = dot_nt(select_ref[...], inverse, HIGHEST) * factor
    spread = POLAR_ROWS * own
    wide = POLAR_ROWS * size
    repeat = (iota((spread, own), 0) // POLAR_ROWS == iota((spread, own), 1)).astype(BF16)
    weights = dot_nn(repeat, weights.astype(BF16)).astype(BF16)
    repeat = (iota((size, wide), 1) % size == iota((size, wide), 0)).astype(BF16)
    weights = dot_nn(weights, repeat)
    keep = iota((spread, wide), 0) % POLAR_ROWS == iota((spread, wide), 1) // size
    weights = jnp.where(keep, weights, 0.0).astype(BF16)
    out_copies = []
    for chunk in range(chunks):
        pixel_copies[chunk].wait()
        moved_copies[chunk].wait()
        for group in range(rows // POLAR_ROWS):
            data = stacked(pixels.at[chunk], group * POLAR_ROWS, POLAR_ROWS)
            polar = dot_nn(weights, data).reshape(own, POLAR_ROWS, side_len)
            first = chunk * rows + group * POLAR_ROWS
            moved[:, first : first + POLAR_ROWS] -= polar
        part = pl.ds(chunk * rows, rows)
        copy = pltpu.make_async_copy(moved.at[:, part], out_hbm.at[:, part], out_sems.at[chunk])
        copy.start()
        out_copies.append(copy)
    for copy in out_copies:
        copy.wait()


def polar_step(shrinkage, select, gram, moved, pixels):
    chunks = len(pixels)
    hbm = pl.BlockSpec(memory_space=pl.ANY)
    return pl.pallas_call(
        functools.partial(polar_body, chunks),
        in_specs=[
            pl.BlockSpec(memory_space=pltpu.SMEM),
            pl.BlockSpec(memory_space=pltpu.VMEM),
            pl.BlockSpec(memory_space=pltpu.VMEM),
            hbm,
        ]
        + [hbm] * chunks,
        out_specs=hbm,
        out_shape=jax.ShapeDtypeStruct(moved.shape, F32),
        scratch_shapes=[
            pltpu.VMEM((chunks,) + pixels[0].shape, BF16),
            pltpu.VMEM(moved.shape, F32),
            pltpu.SemaphoreType.DMA((chunks,)),
            pltpu.SemaphoreType.DMA((chunks,)),
            pltpu.SemaphoreType.DMA((chunks,)),
        ],
        compiler_params=pltpu.CompilerParams(vmem_limit_bytes=48 * MIB),
        name="polar_step",
    )(shrinkage, select, gram, moved, *pixels)


def neighbour_rows(model_image, reach):
    count = lax.axis_size("strip")
    ends = count - 1
    head = model_image[:, :reach].astype(BF16)
    tail = model_image[:, model_image.shape[1] - reach :].astype(BF16)
    before = lax.ppermute(tail, "strip", [(i, i + 1) for i in range(ends)])
    after = lax.ppermute(head, "strip", [(i + 1, i) for i in range(ends)])
    return jnp.concatenate([before, after], axis=1)


def local(grid, model_image, step_size, highpass, shrinkage):
    chans, own_rows, side_len = model_image.shape
    strips = lax.axis_size("strip")
    chan_devices = lax.axis_size("chan")
    size = chans * chan_devices
    rows = CHUNK_ROWS
    chunks = own_rows // rows

    cosine, sine_table = make_tables(side_len)
    split = (strips, chunks, rows, side_len)
    tables = np.stack([cosine.reshape(split), sine_table.reshape(split)])
    tables = tables.transpose(2, 0, 1, 3, 4).reshape(chunks, 2 * strips * rows, side_len)

    levels, taps = highpass.shape
    reach = (taps - 1) * 2 ** (levels - 1)
    edges = neighbour_rows(model_image, reach)

    halves = []
    for chunk in range(chunks):
        sent = first_transform(tables, grid, chunk, strips)
        halves.append(lax.all_to_all(sent, "strip", split_axis=0, concat_axis=0, tiled=True))

    first_row = lax.axis_index("strip") * own_rows
    band = band_matrix(highpass, own_rows, reach, first_row, strips * own_rows)
    own_band = band[:, reach : reach + own_rows]
    side_band = jnp.concatenate([band[:, :reach], band[:, reach + own_rows :]], axis=1)
    moved = base_step(step_size, own_band, side_band, model_image, edges)

    gram = jnp.zeros((GRAM_ROWS * size, GRAM_ROWS * size), F32)
    gathered = []
    for chunk in range(chunks):
        moved, pixels = second_transform(step_size, halves[chunk], cosine, sine_table, moved, chunk)
        pixels = lax.all_gather(pixels, "chan", axis=0, tiled=False)
        if chans % 16:
            pixels = pixels.transpose(1, 0, 2, 3).reshape(1, rows, size, side_len)
        gram = gram_step(pixels, gram)
        gathered.append(pixels)

    own = lax.axis_index("chan") * chans + jnp.arange(chans, dtype=jnp.int32)
    select = (own[:, None] == jnp.arange(size, dtype=jnp.int32)[None, :]).astype(F32)
    return polar_step(shrinkage, select, gram, moved, gathered)


def solution(mesh):
    return jax.shard_map(
        local,
        mesh=mesh,
        in_specs=(
            P(None, "chan", "strip", None),
            P("chan", "strip", None),
            P("chan"),
            P(),
            P("strip"),
        ),
        out_specs=P("chan", "strip", None),
        check_vma=False,
    )
```

```python
import functools

import jax
import jax.numpy as jnp
import ml_dtypes
import numpy as np
from jax import lax
from jax.experimental import pallas as pl
from jax.experimental.pallas import tpu as pltpu
from jax.sharding import PartitionSpec as P

NS_ITERS = 5
SMALL_ROWS = 16
LARGE_ROWS = 32
GRAM_ROWS = 4
POLAR_ROWS = 8
HIGHEST = lax.Precision.HIGHEST
F32 = jnp.float32
BF16 = jnp.bfloat16
VMEM_LIMIT = 60 << 20
BYTES_PER_US = 3690000

ANY = pl.BlockSpec(memory_space=pl.ANY)
SMEM = pl.BlockSpec(memory_space=pltpu.SMEM)


def kernel_params():
    return pltpu.CompilerParams(vmem_limit_bytes=VMEM_LIMIT)


def cost(micros):
    return pl.CostEstimate(flops=0, bytes_accessed=int(micros * BYTES_PER_US), transcendentals=0)


def dot_nt(a, b, precision=None):
    return lax.dot_general(
        a, b, (((1,), (1,)), ((), ())), precision=precision, preferred_element_type=F32
    )


def dot_nn(a, b, precision=None):
    return lax.dot_general(
        a, b, (((1,), (0,)), ((), ())), precision=precision, preferred_element_type=F32
    )


def iota(shape, dim):
    return lax.broadcasted_iota(jnp.int32, shape, dim)


def make_tables(side_len):
    indices = np.arange(side_len, dtype=np.int64)
    phases = (np.outer(indices, indices) % side_len).astype(np.float32) * np.float32(
        2.0 * 3.141592653589793 / side_len
    )
    unit_scale = np.float32(float(side_len) ** (-0.5))
    cosine = (np.cos(phases) * unit_scale).astype(ml_dtypes.bfloat16)
    sine_table = (np.sin(phases) * unit_scale).astype(ml_dtypes.bfloat16)
    return cosine, sine_table


def chunk_rows(own_rows):
    large = [(first, LARGE_ROWS) for first in range(2 * SMALL_ROWS, own_rows - LARGE_ROWS + 1, LARGE_ROWS)]
    covered = 2 * SMALL_ROWS + LARGE_ROWS * len(large)
    rest = [(first, SMALL_ROWS) for first in range(covered, own_rows, SMALL_ROWS)]
    return [(0, SMALL_ROWS)] + large + rest + [(SMALL_ROWS, SMALL_ROWS)]


def first_body(strips, strip_ref, table_ref, grid_ref, after_ref, *out_refs):
    _, chans, rows, width = out_refs[0].shape
    side_len = table_ref.shape[-1]
    cosine = jnp.concatenate([table_ref[strip_ref[0] ^ k, 0] for k in range(strips)], axis=0)
    sine_table = jnp.concatenate([table_ref[strip_ref[0] ^ k, 1] for k in range(strips)], axis=0)
    total = dot_nt(jnp.concatenate([cosine, sine_table], axis=0), grid_ref[0].reshape(chans * width, side_len))
    total = total + dot_nt(
        jnp.concatenate([-sine_table, cosine], axis=0), grid_ref[1].reshape(chans * width, side_len)
    )
    total = total.astype(BF16)
    for part in range(2):
        for k in range(strips):
            first = (part * strips + k) * rows
            for chan in range(chans):
                out_refs[k][part, chan] = total[first : first + rows, chan * width : (chan + 1) * width]


def first_transform(strip, tables, grid, after):
    strips, _, rows, side_len = tables.shape
    _, chans, width, _ = grid.shape
    if width % 128 or rows % 16:
        order = strip[0] ^ jnp.arange(strips, dtype=jnp.int32)
        cosine = jnp.take(tables[:, 0], order, axis=0)
        sine_table = jnp.take(tables[:, 1], order, axis=0)

        def product(table, part):
            return jnp.einsum("kmv,cuv->kcmu", table, part, preferred_element_type=F32)

        real = product(cosine, grid[0]) - product(sine_table, grid[1])
        imag = product(sine_table, grid[0]) + product(cosine, grid[1])
        both = jnp.stack([real, imag], axis=1).astype(BF16)
        return [both[k] for k in range(strips)]
    block = 4 if chans % 4 == 0 else 1
    return pl.pallas_call(
        functools.partial(first_body, strips),
        grid=(chans // block,),
        in_specs=[
            SMEM,
            pl.BlockSpec(tables.shape, lambda i: (0, 0, 0, 0)),
            pl.BlockSpec((2, block, width, side_len), lambda i: (0, i, 0, 0)),
            ANY,
        ],
        out_specs=[pl.BlockSpec((2, block, rows, width), lambda i: (0, i, 0, 0))] * strips,
        out_shape=[jax.ShapeDtypeStruct((2, chans, rows, width), BF16)] * strips,
        compiler_params=kernel_params(),
        cost_estimate=cost(4 + rows // 6),
        name="first_transform",
    )(strip, tables, grid, after)


def band_matrix(taps_of, levels, taps, own_rows, reach, first_row, image_rows):
    half_taps = taps // 2
    shape = (own_rows, own_rows + 2 * reach)
    row = iota(shape, 0)
    column = iota(shape, 1)
    place = jnp.where(
        column < own_rows, column, jnp.where(column < own_rows + reach, column - own_rows - reach, column - reach)
    )
    total = jnp.zeros(shape, F32)
    for level in range(levels):
        dilation = 2**level
        for outer in range(taps):
            detail_row = row - (outer - half_taps) * dilation
            inside = (detail_row + first_row >= 0) & (detail_row + first_row < image_rows)
            for inner in range(taps):
                hit = inside & (place == detail_row + (inner - half_taps) * dilation)
                total = total + jnp.where(hit, taps_of(level, outer) * taps_of(level, inner), 0.0)
    return total


def base_body(levels, taps, reach, strips, strip_ref, step_ref, highpass_ref, model_ref, edge_ref, after_ref, out_ref, high, low):
    block, own_rows, side_len = model_ref.shape

    @pl.when(pl.program_id(0) == 0)
    def _():
        band = band_matrix(
            lambda level, tap: highpass_ref[level, tap],
            levels,
            taps,
            own_rows,
            reach,
            strip_ref[0] * own_rows,
            strips * own_rows,
        )
        top = band.astype(BF16)
        high[...] = top
        low[...] = (band - top.astype(F32)).astype(BF16)

    first = pl.program_id(0) * block
    for chan in range(block):
        model = model_ref[chan]
        top = model.astype(BF16)
        rest = (model - top.astype(F32)).astype(BF16)
        edge = edge_ref[chan].astype(F32)
        whole = jnp.concatenate([top.astype(F32), edge], axis=0).astype(BF16)
        gradient = dot_nn(high[...], whole)
        gradient = gradient + dot_nn(low[...], whole)
        gradient = gradient + dot_nn(high[:, :own_rows], rest)
        out_ref[chan] = model - step_ref[first + chan] * gradient


def base_step(strip, strips, step_size, highpass, model_image, edges, after):
    chans, rows, side_len = model_image.shape
    levels, taps = highpass.shape
    reach = edges.shape[1] // 2
    block = 2 if chans % 2 == 0 else 1
    wide = rows + 2 * reach
    return pl.pallas_call(
        functools.partial(base_body, levels, taps, reach, strips),
        grid=(chans // block,),
        in_specs=[
            SMEM,
            SMEM,
            SMEM,
            pl.BlockSpec((block, rows, side_len), lambda i: (i, 0, 0)),
            pl.BlockSpec((block, 2 * reach, side_len), lambda i: (i, 0, 0)),
            ANY,
        ],
        out_specs=pl.BlockSpec((block, rows, side_len), lambda i: (i, 0, 0)),
        out_shape=jax.ShapeDtypeStruct(model_image.shape, F32),
        scratch_shapes=[pltpu.VMEM((rows, wide), BF16), pltpu.VMEM((rows, wide), BF16)],
        compiler_params=kernel_params(),
        cost_estimate=cost(9),
        name="base_step",
    )(strip, step_size, highpass, model_image, edges, after)


def second_body(strips, strip_ref, step_ref, cosine_ref, sine_ref, base_ref, after_ref, *refs):
    halves = refs[:strips]
    moved_ref, pixels_ref = refs[strips:]
    _, chans, rows, width = halves[0].shape
    real = jnp.concatenate([half[0].reshape(chans * rows, width) for half in halves], axis=1)
    imag = jnp.concatenate([half[1].reshape(chans * rows, width) for half in halves], axis=1)

    def ordered(table_ref):
        parts = [table_ref[pl.ds(pl.multiple_of((strip_ref[0] ^ k) * width, width), width), :] for k in range(strips)]
        return jnp.concatenate(parts, axis=0)

    dirty = dot_nn(real, ordered(cosine_ref)) - dot_nn(imag, ordered(sine_ref))
    pieces = []
    for chan in range(chans):
        moved = base_ref[chan] + step_ref[chan] * dirty[chan * rows : (chan + 1) * rows]
        moved_ref[chan] = moved
        pieces.append(moved)
    pixels_ref[...] = jnp.swapaxes(jnp.stack(pieces), 0, 1).astype(BF16)


def second_transform(strip, step_size, halves, cosine, sine_table, base, first_row, after):
    strips = len(halves)
    _, chans, rows, width = halves[0].shape
    side_len = cosine.shape[0]
    if width % 128 or rows % 16 or chans % 16:
        order = strip[0] ^ jnp.arange(strips, dtype=jnp.int32)
        both = jnp.stack(halves)

        def product(part, table):
            parts = jnp.take(table.reshape(strips, width, side_len), order, axis=0)
            return jnp.einsum("kcmu,kul->cml", part, parts, preferred_element_type=F32)

        dirty = product(both[:, 0], jnp.asarray(cosine)) - product(both[:, 1], jnp.asarray(sine_table))
        moved = base[:, first_row : first_row + rows] + step_size[:, None, None] * dirty
        pixels = moved.astype(BF16).transpose(1, 0, 2)
        return lax.dynamic_update_slice(base, moved, (0, first_row, 0)), pixels
    block = min(256, side_len)
    place = first_row // rows
    halves_spec = pl.BlockSpec(halves[0].shape, lambda i: (0, 0, 0, 0))
    return pl.pallas_call(
        functools.partial(second_body, strips),
        grid=(side_len // block,),
        in_specs=[
            SMEM,
            SMEM,
            pl.BlockSpec((side_len, block), lambda i: (0, i)),
            pl.BlockSpec((side_len, block), lambda i: (0, i)),
            pl.BlockSpec((chans, rows, block), lambda i: (0, place, i)),
            ANY,
        ]
        + [halves_spec] * strips,
        out_specs=[
            pl.BlockSpec((chans, rows, block), lambda i: (0, place, i)),
            pl.BlockSpec((rows, chans, block), lambda i: (0, 0, i)),
        ],
        out_shape=[
            jax.ShapeDtypeStruct(base.shape, F32),
            jax.ShapeDtypeStruct((rows, chans, side_len), BF16),
        ],
        input_output_aliases={4: 0},
        compiler_params=kernel_params(),
        cost_estimate=cost(2 + rows // 10),
        name="second_transform",
    )(strip, step_size, cosine, sine_table, base, after, *halves)


def stacked(group_refs, first, count):
    return jnp.concatenate([ref[first + i] for i in range(count) for ref in group_refs], axis=0)


def gram_body(groups, before_ref, after_ref, *refs):
    total_ref = refs[groups]

    @pl.when(pl.program_id(0) == 0)
    def _():
        total_ref[...] = before_ref[...]

    pixels = stacked(refs[:groups], 0, GRAM_ROWS)
    total_ref[...] += dot_nt(pixels, pixels)


def gram_step(groups, before, after):
    rows, chans, side_len = groups[0].shape
    spec = pl.BlockSpec((GRAM_ROWS, chans, side_len), lambda i: (i, 0, 0))
    return pl.pallas_call(
        functools.partial(gram_body, len(groups)),
        grid=(rows // GRAM_ROWS,),
        in_specs=[pl.BlockSpec(before.shape, lambda i: (0, 0)), ANY] + [spec] * len(groups),
        out_specs=pl.BlockSpec(before.shape, lambda i: (0, 0)),
        out_shape=jax.ShapeDtypeStruct(before.shape, F32),
        compiler_params=kernel_params(),
        cost_estimate=cost(1 + rows // 16),
        name="gram_step",
    )(before, after, *groups)


def newton_schulz(gram):
    size = gram.shape[0]
    frob_norm = jnp.sqrt(jnp.sum(gram * gram))
    identity = (iota((size, size), 0) == iota((size, size), 1)).astype(F32)
    current = gram / frob_norm
    inverse = identity
    for iteration in range(NS_ITERS):
        middle = 0.5 * (3.0 * identity - dot_nn(inverse, current, HIGHEST))
        if iteration + 1 < NS_ITERS:
            current = dot_nn(current, middle, HIGHEST)
        inverse = dot_nn(middle, inverse, HIGHEST)
    return inverse, frob_norm


def polar_body(starts, sizes, groups, shrink_ref, gram_ref, moved_hbm, *refs):
    chunks = len(sizes)
    pixels_hbm = refs[: chunks * groups]
    out_hbm, moved, in_sems, moved_sems, out_sems = refs[chunks * groups : chunks * groups + 5]
    pixels = refs[chunks * groups + 5 :]
    own, all_rows, side_len = moved.shape
    size = pixels[0].shape[2] * groups
    moved_copies = []
    pixel_copies = []
    for chunk in range(chunks):
        copies = []
        for group in range(groups):
            place = chunk * groups + group
            copy = pltpu.make_async_copy(pixels_hbm[place], pixels[chunk].at[group], in_sems.at[place])
            copy.start()
            copies.append(copy)
        pixel_copies.append(copies)
        part = pl.ds(starts[chunk], sizes[chunk])
        copy = pltpu.make_async_copy(moved_hbm.at[:, part], moved.at[:, part], moved_sems.at[chunk])
        copy.start()
        moved_copies.append(copy)
    gram = jnp.zeros((size, size), F32)
    for i in range(GRAM_ROWS):
        gram = gram + gram_ref[i * size : (i + 1) * size, i * size : (i + 1) * size]
    inverse, frob_norm = newton_schulz(gram)
    factor = shrink_ref[0] * jnp.sqrt(all_rows * side_len / frob_norm)
    select = (iota((own, size), 0) == iota((own, size), 1)).astype(F32)
    weights = dot_nt(select, inverse, HIGHEST) * factor
    spread = POLAR_ROWS * own
    wide = POLAR_ROWS * size
    repeat = (iota((spread, own), 0) // POLAR_ROWS == iota((spread, own), 1)).astype(BF16)
    weights = dot_nn(repeat, weights.astype(BF16)).astype(BF16)
    repeat = (iota((size, wide), 1) % size == iota((size, wide), 0)).astype(BF16)
    weights = dot_nn(weights, repeat)
    keep = iota((spread, wide), 0) % POLAR_ROWS == iota((spread, wide), 1) // size
    weights = jnp.where(keep, weights, 0.0).astype(BF16)
    out_copies = []
    for chunk in range(chunks):
        for copy in pixel_copies[chunk]:
            copy.wait()
        moved_copies[chunk].wait()
        for step in range(sizes[chunk] // POLAR_ROWS):
            data = stacked([pixels[chunk].at[group] for group in range(groups)], step * POLAR_ROWS, POLAR_ROWS)
            polar = dot_nn(weights, data).reshape(own, POLAR_ROWS, side_len)
            first = starts[chunk] + step * POLAR_ROWS
            moved[:, first : first + POLAR_ROWS] -= polar
        part = pl.ds(starts[chunk], sizes[chunk])
        copy = pltpu.make_async_copy(moved.at[:, part], out_hbm.at[:, part], out_sems.at[chunk])
        copy.start()
        out_copies.append(copy)
    for copy in out_copies:
        copy.wait()


def polar_step(shrinkage, gram, moved, gathered, starts):
    chunks = len(gathered)
    groups = len(gathered[0])
    sizes = [pieces[0].shape[0] for pieces in gathered]
    flat = [piece for pieces in gathered for piece in pieces]
    return pl.pallas_call(
        functools.partial(polar_body, starts, sizes, groups),
        in_specs=[SMEM, pl.BlockSpec(memory_space=pltpu.VMEM), ANY] + [ANY] * len(flat),
        out_specs=ANY,
        out_shape=jax.ShapeDtypeStruct(moved.shape, F32),
        scratch_shapes=[
            pltpu.VMEM(moved.shape, F32),
            pltpu.SemaphoreType.DMA((chunks * groups,)),
            pltpu.SemaphoreType.DMA((chunks,)),
            pltpu.SemaphoreType.DMA((chunks,)),
        ]
        + [pltpu.VMEM((groups,) + pieces[0].shape, BF16) for pieces in gathered],
        compiler_params=kernel_params(),
        cost_estimate=cost(11),
        name="polar_step",
    )(shrinkage, gram, moved, *flat)


def swap(value, axis, bits):
    count = lax.axis_size(axis)
    return lax.ppermute(value, axis, [(i, i ^ bits) for i in range(count)])


def neighbour_rows(model_image, reach):
    ends = lax.axis_size("strip") - 1
    head = model_image[:, :reach].astype(BF16)
    tail = model_image[:, model_image.shape[1] - reach :].astype(BF16)
    before = lax.ppermute(tail, "strip", [(i, i + 1) for i in range(ends)])
    after = lax.ppermute(head, "strip", [(i + 1, i) for i in range(ends)])
    return jnp.concatenate([before, after], axis=1)


def exchange(pieces):
    order = sorted(range(1, len(pieces)), reverse=True)
    arrived = {k: swap(pieces[k], "strip", k) for k in order}
    return [pieces[0]] + [arrived[k] for k in range(1, len(pieces))]


def gather_channels(pixels):
    devices = lax.axis_size("chan")
    far = [swap(pixels, "chan", bits) for bits in range(2, devices, 2)]
    kept = [pixels] + far
    if devices == 1:
        return kept
    return kept + [swap(piece, "chan", 1) for piece in kept]


def local(grid, model_image, step_size, highpass, shrinkage):
    chans, own_rows, side_len = model_image.shape
    strips = lax.axis_size("strip")
    size = chans * lax.axis_size("chan")
    starts, sizes = zip(*chunk_rows(own_rows))
    chunks = len(sizes)
    strip = lax.axis_index("strip").astype(jnp.int32).reshape(1)

    cosine, sine_table = make_tables(side_len)
    split = np.stack([cosine.reshape(strips, own_rows, side_len), sine_table.reshape(strips, own_rows, side_len)], axis=1)
    tables = [np.ascontiguousarray(split[:, :, start : start + rows]) for start, rows in zip(starts, sizes)]

    levels, taps = highpass.shape
    reach = (taps - 1) * 2 ** (levels - 1)
    edges = neighbour_rows(model_image, reach)

    ahead = 2
    halves = {}
    moved = None
    gathered = []
    gram = jnp.zeros((GRAM_ROWS * size, GRAM_ROWS * size), F32)
    last = strip
    for chunk in range(chunks + ahead):
        if chunk < chunks:
            pieces = first_transform(strip, tables[chunk], grid, last)
            last = pieces[0]
            halves[chunk] = exchange(pieces)
        if chunk == ahead - 1:
            moved = base_step(strip, strips, step_size, highpass, model_image, edges, last)
            last = moved
        if chunk >= ahead:
            done = chunk - ahead
            moved, pixels = second_transform(
                strip, step_size, halves[done], cosine, sine_table, moved, starts[done], last
            )
            last = pixels
            groups = gather_channels(pixels)
            if chans % 16:
                groups = [jnp.concatenate(groups, axis=1)]
            gathered.append(groups)
            if done > 0:
                gram = gram_step(gathered[done - 1], gram, last)
                last = gram
    gram = gram_step(gathered[-1], gram, last)
    return polar_step(shrinkage, gram, moved, gathered, starts)


def solution(mesh):
    return jax.shard_map(
        local,
        mesh=mesh,
        in_specs=(
            P(None, "chan", "strip", None),
            P("chan", "strip", None),
            P("chan"),
            P(),
            P("strip"),
        ),
        out_specs=P("chan", "strip", None),
        check_vma=False,
    )
```

```python
import functools

import jax
import jax.numpy as jnp
import ml_dtypes
import numpy as np
from jax import lax
from jax.experimental import pallas as pl
from jax.experimental.pallas import tpu as pltpu
from jax.sharding import PartitionSpec as P

NS_ITERS = 5
SMALL_ROWS = 16
LARGE_ROWS = 32
GRAM_ROWS = 4
POLAR_ROWS = 8
HIGHEST = lax.Precision.HIGHEST
F32 = jnp.float32
BF16 = jnp.bfloat16
VMEM_LIMIT = 60 << 20
BYTES_PER_US = 3690000

ANY = pl.BlockSpec(memory_space=pl.ANY)
SMEM = pl.BlockSpec(memory_space=pltpu.SMEM)


def kernel_params():
    return pltpu.CompilerParams(vmem_limit_bytes=VMEM_LIMIT)


def cost(micros):
    return pl.CostEstimate(flops=0, bytes_accessed=int(micros * BYTES_PER_US), transcendentals=0)


def dot_nt(a, b, precision=None):
    return lax.dot_general(
        a, b, (((1,), (1,)), ((), ())), precision=precision, preferred_element_type=F32
    )


def dot_nn(a, b, precision=None):
    return lax.dot_general(
        a, b, (((1,), (0,)), ((), ())), precision=precision, preferred_element_type=F32
    )


def iota(shape, dim):
    return lax.broadcasted_iota(jnp.int32, shape, dim)


def make_tables(side_len):
    indices = np.arange(side_len, dtype=np.int64)
    phases = (np.outer(indices, indices) % side_len).astype(np.float32) * np.float32(
        2.0 * 3.141592653589793 / side_len
    )
    unit_scale = np.float32(float(side_len) ** (-0.5))
    cosine = (np.cos(phases) * unit_scale).astype(ml_dtypes.bfloat16)
    sine_table = (np.sin(phases) * unit_scale).astype(ml_dtypes.bfloat16)
    return cosine, sine_table


def chunk_rows(own_rows):
    large = [(first, LARGE_ROWS) for first in range(2 * SMALL_ROWS, own_rows - LARGE_ROWS + 1, LARGE_ROWS)]
    covered = 2 * SMALL_ROWS + LARGE_ROWS * len(large)
    rest = [(first, SMALL_ROWS) for first in range(covered, own_rows, SMALL_ROWS)]
    return [(0, SMALL_ROWS)] + large + rest + [(SMALL_ROWS, SMALL_ROWS)]


def first_body(table_ref, grid_ref, after_ref, out_ref):
    strips, _, chans, rows, width = out_ref.shape
    side_len = table_ref.shape[-1]
    table = table_ref[...]
    middle = strips * rows
    turned = jnp.concatenate([-table[middle:], table[:middle]], axis=0)
    total = dot_nt(table, grid_ref[0].reshape(chans * width, side_len))
    total = total + dot_nt(turned, grid_ref[1].reshape(chans * width, side_len))
    total = total.astype(BF16)
    for part in range(2):
        for strip in range(strips):
            first = (part * strips + strip) * rows
            for chan in range(chans):
                out_ref[strip, part, chan] = total[first : first + rows, chan * width : (chan + 1) * width]


def first_transform(table, grid, strips, after):
    _, chans, width, side_len = grid.shape
    rows = table.shape[0] // (2 * strips)
    shape = (strips, 2, chans, rows, width)
    if width % 128 or rows % 16:
        middle = strips * rows
        turned = jnp.concatenate([-table[middle:], table[:middle]], axis=0)
        total = jnp.einsum("mv,cuv->mcu", table, grid[0], preferred_element_type=F32)
        total = total + jnp.einsum("mv,cuv->mcu", turned, grid[1], preferred_element_type=F32)
        total = total.astype(BF16).reshape(2, strips, rows, chans, width)
        return total.transpose(1, 0, 3, 2, 4)
    block = 4 if chans % 4 == 0 else 1
    return pl.pallas_call(
        first_body,
        grid=(chans // block,),
        in_specs=[
            pl.BlockSpec(table.shape, lambda i: (0, 0)),
            pl.BlockSpec((2, block, width, side_len), lambda i: (0, i, 0, 0)),
            ANY,
        ],
        out_specs=pl.BlockSpec((strips, 2, block, rows, width), lambda i: (0, 0, i, 0, 0)),
        out_shape=jax.ShapeDtypeStruct(shape, BF16),
        compiler_params=kernel_params(),
        cost_estimate=cost(4 + rows // 6),
        name="first_transform",
    )(table, grid, after)


def band_matrix(taps_of, levels, taps, own_rows, reach, first_row, image_rows):
    half_taps = taps // 2
    shape = (own_rows, own_rows + 2 * reach)
    row = iota(shape, 0)
    column = iota(shape, 1)
    place = jnp.where(
        column < own_rows, column, jnp.where(column < own_rows + reach, column - own_rows - reach, column - reach)
    )
    total = jnp.zeros(shape, F32)
    for level in range(levels):
        dilation = 2**level
        for outer in range(taps):
            detail_row = row - (outer - half_taps) * dilation
            inside = (detail_row + first_row >= 0) & (detail_row + first_row < image_rows)
            for inner in range(taps):
                hit = inside & (place == detail_row + (inner - half_taps) * dilation)
                total = total + jnp.where(hit, taps_of(level, outer) * taps_of(level, inner), 0.0)
    return total


def base_body(levels, taps, reach, strips, strip_ref, step_ref, highpass_ref, model_ref, edge_ref, after_ref, out_ref, high, low):
    block, own_rows, side_len = model_ref.shape

    @pl.when(pl.program_id(0) == 0)
    def _():
        band = band_matrix(
            lambda level, tap: highpass_ref[level, tap],
            levels,
            taps,
            own_rows,
            reach,
            strip_ref[0] * own_rows,
            strips * own_rows,
        )
        top = band.astype(BF16)
        high[...] = top
        low[...] = (band - top.astype(F32)).astype(BF16)

    first = pl.program_id(0) * block
    for chan in range(block):
        model = model_ref[chan]
        top = model.astype(BF16)
        rest = (model - top.astype(F32)).astype(BF16)
        edge = edge_ref[chan].astype(F32)
        whole = jnp.concatenate([top.astype(F32), edge], axis=0).astype(BF16)
        gradient = dot_nn(high[...], whole)
        gradient = gradient + dot_nn(low[...], whole)
        gradient = gradient + dot_nn(high[:, :own_rows], rest)
        out_ref[chan] = model - step_ref[first + chan] * gradient


def base_step(strip, strips, step_size, highpass, model_image, edges, after):
    chans, rows, side_len = model_image.shape
    levels, taps = highpass.shape
    reach = edges.shape[1] // 2
    block = 2 if chans % 2 == 0 else 1
    wide = rows + 2 * reach
    return pl.pallas_call(
        functools.partial(base_body, levels, taps, reach, strips),
        grid=(chans // block,),
        in_specs=[
            SMEM,
            SMEM,
            SMEM,
            pl.BlockSpec((block, rows, side_len), lambda i: (i, 0, 0)),
            pl.BlockSpec((block, 2 * reach, side_len), lambda i: (i, 0, 0)),
            ANY,
        ],
        out_specs=pl.BlockSpec((block, rows, side_len), lambda i: (i, 0, 0)),
        out_shape=jax.ShapeDtypeStruct(model_image.shape, F32),
        scratch_shapes=[pltpu.VMEM((rows, wide), BF16), pltpu.VMEM((rows, wide), BF16)],
        compiler_params=kernel_params(),
        cost_estimate=cost(9),
        name="base_step",
    )(strip, step_size, highpass, model_image, edges, after)


def second_body(step_ref, half_ref, cosine_ref, sine_ref, base_ref, after_ref, moved_ref, pixels_ref):
    strips, _, chans, rows, width = half_ref.shape
    real = jnp.concatenate([half_ref[s, 0].reshape(chans * rows, width) for s in range(strips)], axis=1)
    imag = jnp.concatenate([half_ref[s, 1].reshape(chans * rows, width) for s in range(strips)], axis=1)
    dirty = dot_nn(real, cosine_ref[...]) - dot_nn(imag, sine_ref[...])
    pieces = []
    for chan in range(chans):
        moved = base_ref[chan] + step_ref[chan] * dirty[chan * rows : (chan + 1) * rows]
        moved_ref[chan] = moved
        pieces.append(moved)
    pixels_ref[...] = jnp.swapaxes(jnp.stack(pieces), 0, 1).astype(BF16)


def second_transform(step_size, half, cosine, sine_table, base, first_row, after):
    strips, _, chans, rows, width = half.shape
    side_len = cosine.shape[0]
    if width % 128 or rows % 16 or chans % 16:
        split = (strips, width, side_len)
        dirty = jnp.einsum("scmu,sul->cml", half[:, 0], cosine.reshape(split), preferred_element_type=F32)
        dirty = dirty - jnp.einsum("scmu,sul->cml", half[:, 1], sine_table.reshape(split), preferred_element_type=F32)
        moved = base[:, first_row : first_row + rows] + step_size[:, None, None] * dirty
        pixels = moved.astype(BF16).transpose(1, 0, 2)
        return lax.dynamic_update_slice(base, moved, (0, first_row, 0)), pixels
    block = min(256, side_len)
    place = first_row // rows
    return pl.pallas_call(
        second_body,
        grid=(side_len // block,),
        in_specs=[
            SMEM,
            pl.BlockSpec(half.shape, lambda i: (0, 0, 0, 0, 0)),
            pl.BlockSpec((side_len, block), lambda i: (0, i)),
            pl.BlockSpec((side_len, block), lambda i: (0, i)),
            pl.BlockSpec((chans, rows, block), lambda i: (0, place, i)),
            ANY,
        ],
        out_specs=[
            pl.BlockSpec((chans, rows, block), lambda i: (0, place, i)),
            pl.BlockSpec((rows, chans, block), lambda i: (0, 0, i)),
        ],
        out_shape=[
            jax.ShapeDtypeStruct(base.shape, F32),
            jax.ShapeDtypeStruct((rows, chans, side_len), BF16),
        ],
        input_output_aliases={4: 0},
        compiler_params=kernel_params(),
        cost_estimate=cost(2 + rows // 10),
        name="second_transform",
    )(step_size, half, cosine, sine_table, base, after)


def stacked(group_refs, first, count):
    return jnp.concatenate([ref[first + i] for i in range(count) for ref in group_refs], axis=0)


def gram_body(before_ref, after_ref, pixels_ref, total_ref):
    groups, rows, _, _ = pixels_ref.shape

    @pl.when(pl.program_id(0) == 0)
    def _():
        total_ref[...] = before_ref[...]

    total = total_ref[...]
    for first in range(0, rows, GRAM_ROWS):
        pixels = stacked([pixels_ref.at[group] for group in range(groups)], first, GRAM_ROWS)
        total = total + dot_nt(pixels, pixels)
    total_ref[...] = total


def gram_step(pixels, before, after):
    groups, rows, chans, side_len = pixels.shape
    block = 8
    return pl.pallas_call(
        gram_body,
        grid=(rows // block,),
        in_specs=[
            pl.BlockSpec(before.shape, lambda i: (0, 0)),
            ANY,
            pl.BlockSpec((groups, block, chans, side_len), lambda i: (0, i, 0, 0)),
        ],
        out_specs=pl.BlockSpec(before.shape, lambda i: (0, 0)),
        out_shape=jax.ShapeDtypeStruct(before.shape, F32),
        compiler_params=kernel_params(),
        cost_estimate=cost(1 + rows // 16),
        name="gram_step",
    )(before, after, pixels)


def newton_schulz(gram):
    size = gram.shape[0]
    frob_norm = jnp.sqrt(jnp.sum(gram * gram))
    identity = (iota((size, size), 0) == iota((size, size), 1)).astype(F32)
    current = gram / frob_norm
    inverse = identity
    for iteration in range(NS_ITERS):
        middle = 0.5 * (3.0 * identity - dot_nn(inverse, current, HIGHEST))
        if iteration + 1 < NS_ITERS:
            current = dot_nn(current, middle, HIGHEST)
        inverse = dot_nn(middle, inverse, HIGHEST)
    return inverse, frob_norm


def polar_body(starts, sizes, shrink_ref, select_ref, gram_ref, moved_hbm, *refs):
    chunks = len(sizes)
    pixels_hbm = refs[:chunks]
    out_hbm, moved, in_sems, moved_sems, out_sems = refs[chunks : chunks + 5]
    pixels = refs[chunks + 5 :]
    own, all_rows, side_len = moved.shape
    groups = pixels[0].shape[0]
    size = pixels[0].shape[2] * groups
    moved_copies = []
    pixel_copies = []
    for chunk in range(chunks):
        copy = pltpu.make_async_copy(pixels_hbm[chunk], pixels[chunk], in_sems.at[chunk])
        copy.start()
        pixel_copies.append(copy)
        part = pl.ds(starts[chunk], sizes[chunk])
        copy = pltpu.make_async_copy(moved_hbm.at[:, part], moved.at[:, part], moved_sems.at[chunk])
        copy.start()
        moved_copies.append(copy)
    gram = jnp.zeros((size, size), F32)
    for i in range(GRAM_ROWS):
        gram = gram + gram_ref[i * size : (i + 1) * size, i * size : (i + 1) * size]
    inverse, frob_norm = newton_schulz(gram)
    factor = shrink_ref[0] * jnp.sqrt(all_rows * side_len / frob_norm)
    weights = dot_nt(select_ref[...], inverse, HIGHEST) * factor
    spread = POLAR_ROWS * own
    wide = POLAR_ROWS * size
    repeat = (iota((spread, own), 0) // POLAR_ROWS == iota((spread, own), 1)).astype(BF16)
    weights = dot_nn(repeat, weights.astype(BF16)).astype(BF16)
    repeat = (iota((size, wide), 1) % size == iota((size, wide), 0)).astype(BF16)
    weights = dot_nn(weights, repeat)
    keep = iota((spread, wide), 0) % POLAR_ROWS == iota((spread, wide), 1) // size
    weights = jnp.where(keep, weights, 0.0).astype(BF16)
    out_copies = []
    for chunk in range(chunks):
        pixel_copies[chunk].wait()
        moved_copies[chunk].wait()
        for step in range(sizes[chunk] // POLAR_ROWS):
            data = stacked([pixels[chunk].at[group] for group in range(groups)], step * POLAR_ROWS, POLAR_ROWS)
            polar = dot_nn(weights, data).reshape(own, POLAR_ROWS, side_len)
            first = starts[chunk] + step * POLAR_ROWS
            moved[:, first : first + POLAR_ROWS] -= polar
        part = pl.ds(starts[chunk], sizes[chunk])
        copy = pltpu.make_async_copy(moved.at[:, part], out_hbm.at[:, part], out_sems.at[chunk])
        copy.start()
        out_copies.append(copy)
    for copy in out_copies:
        copy.wait()


def polar_step(shrinkage, select, gram, moved, gathered, starts):
    chunks = len(gathered)
    sizes = [pieces.shape[1] for pieces in gathered]
    return pl.pallas_call(
        functools.partial(polar_body, starts, sizes),
        in_specs=[SMEM, pl.BlockSpec(memory_space=pltpu.VMEM), pl.BlockSpec(memory_space=pltpu.VMEM), ANY] + [ANY] * chunks,
        out_specs=ANY,
        out_shape=jax.ShapeDtypeStruct(moved.shape, F32),
        scratch_shapes=[
            pltpu.VMEM(moved.shape, F32),
            pltpu.SemaphoreType.DMA((chunks,)),
            pltpu.SemaphoreType.DMA((chunks,)),
            pltpu.SemaphoreType.DMA((chunks,)),
        ]
        + [pltpu.VMEM(pieces.shape, BF16) for pieces in gathered],
        compiler_params=kernel_params(),
        cost_estimate=cost(11),
        name="polar_step",
    )(shrinkage, select, gram, moved, *gathered)


def neighbour_rows(model_image, reach):
    ends = lax.axis_size("strip") - 1
    head, tail = lax.optimization_barrier((model_image[:, :reach], model_image[:, model_image.shape[1] - reach :]))
    before = lax.ppermute(tail.astype(BF16), "strip", [(i, i + 1) for i in range(ends)])
    after = lax.ppermute(head.astype(BF16), "strip", [(i + 1, i) for i in range(ends)])
    return jnp.concatenate([before, after], axis=1)


def local(grid, model_image, step_size, highpass, shrinkage):
    chans, own_rows, side_len = model_image.shape
    strips = lax.axis_size("strip")
    size = chans * lax.axis_size("chan")
    starts, sizes = zip(*chunk_rows(own_rows))
    chunks = len(sizes)
    strip = lax.axis_index("strip").astype(jnp.int32).reshape(1)

    cosine, sine_table = make_tables(side_len)
    split = np.stack([cosine.reshape(strips, own_rows, side_len), sine_table.reshape(strips, own_rows, side_len)])
    tables = [
        np.ascontiguousarray(split[:, :, start : start + rows]).reshape(2 * strips * rows, side_len)
        for start, rows in zip(starts, sizes)
    ]

    levels, taps = highpass.shape
    reach = (taps - 1) * 2 ** (levels - 1)

    halves = {}
    gathered = []
    gram = jnp.zeros((GRAM_ROWS * size, GRAM_ROWS * size), F32)
    last = strip
    moved = None
    for chunk in range(chunks + 1):
        if chunk < chunks:
            sent = first_transform(tables[chunk], grid, strips, last)
            last = sent
            halves[chunk] = lax.all_to_all(sent, "strip", split_axis=0, concat_axis=0, tiled=True)
        if chunk == 0:
            edges = neighbour_rows(model_image, reach)
            moved = base_step(strip, strips, step_size, highpass, model_image, edges, last)
            last = moved
        else:
            done = chunk - 1
            moved, pixels = second_transform(step_size, halves[done], cosine, sine_table, moved, starts[done], last)
            last = pixels
            pixels = lax.all_gather(pixels, "chan", axis=0, tiled=False)
            if chans % 16:
                pixels = pixels.transpose(1, 0, 2, 3).reshape(1, sizes[done], size, side_len)
            gathered.append(pixels)
        if chunk > 1:
            gram = gram_step(gathered[chunk - 2], gram, last)
            last = gram
    gram = gram_step(gathered[-1], gram, last)

    own = lax.axis_index("chan") * chans + jnp.arange(chans, dtype=jnp.int32)
    select = (own[:, None] == jnp.arange(size, dtype=jnp.int32)[None, :]).astype(F32)
    return polar_step(shrinkage, select, gram, moved, gathered, starts)


def solution(mesh):
    return jax.shard_map(
        local,
        mesh=mesh,
        in_specs=(
            P(None, "chan", "strip", None),
            P("chan", "strip", None),
            P("chan"),
            P(),
            P("strip"),
        ),
        out_specs=P("chan", "strip", None),
        check_vma=False,
    )
```

```python
import functools

import jax
import jax.numpy as jnp
import ml_dtypes
import numpy as np
from jax import lax
from jax.experimental import pallas as pl
from jax.experimental.pallas import tpu as pltpu
from jax.sharding import PartitionSpec as P

NS_ITERS = 5
EDGE_ROWS = 16
GRAM_ROWS = 4
POLAR_ROWS = 8
HIGHEST = lax.Precision.HIGHEST
F32 = jnp.float32
BF16 = jnp.bfloat16
MIB = 1 << 20

ANY = pl.BlockSpec(memory_space=pl.ANY)
SMEM = pl.BlockSpec(memory_space=pltpu.SMEM)


def kernel_params(mebibytes):
    return pltpu.CompilerParams(vmem_limit_bytes=mebibytes * MIB)


COST = pl.CostEstimate(flops=0, bytes_accessed=1 << 16, transcendentals=0)


def dot_nt(a, b, precision=None):
    return lax.dot_general(
        a, b, (((1,), (1,)), ((), ())), precision=precision, preferred_element_type=F32
    )


def dot_nn(a, b, precision=None):
    return lax.dot_general(
        a, b, (((1,), (0,)), ((), ())), precision=precision, preferred_element_type=F32
    )


def iota(shape, dim):
    return lax.broadcasted_iota(jnp.int32, shape, dim)


def make_tables(side_len):
    indices = np.arange(side_len, dtype=np.int64)
    phases = (np.outer(indices, indices) % side_len).astype(np.float32) * np.float32(
        2.0 * 3.141592653589793 / side_len
    )
    unit_scale = np.float32(float(side_len) ** (-0.5))
    cosine = (np.cos(phases) * unit_scale).astype(ml_dtypes.bfloat16)
    sine_table = (np.sin(phases) * unit_scale).astype(ml_dtypes.bfloat16)
    return cosine, sine_table


def chunk_rows(own_rows):
    inner = own_rows - 2 * EDGE_ROWS
    pieces = 2 if inner >= 4 * EDGE_ROWS and inner % (2 * EDGE_ROWS) == 0 else 1
    sizes = [EDGE_ROWS] + [inner // pieces] * pieces + [EDGE_ROWS]
    return [sum(sizes[:place]) for place in range(len(sizes))], sizes


def first_body(table_ref, grid_ref, after_ref, out_ref):
    strips, _, chans, rows, width = out_ref.shape
    side_len = table_ref.shape[-1]
    table = table_ref[...]
    middle = strips * rows
    turned = jnp.concatenate([-table[middle:], table[:middle]], axis=0)
    total = dot_nt(table, grid_ref[0].reshape(chans * width, side_len))
    total = total + dot_nt(turned, grid_ref[1].reshape(chans * width, side_len))
    total = total.astype(BF16)
    for part in range(2):
        for strip in range(strips):
            first = (part * strips + strip) * rows
            for chan in range(chans):
                out_ref[strip, part, chan] = total[first : first + rows, chan * width : (chan + 1) * width]


def first_transform(table, grid, strips, after):
    _, chans, width, side_len = grid.shape
    rows = table.shape[0] // (2 * strips)
    shape = (strips, 2, chans, rows, width)
    if width % 128 or rows % 16:
        middle = strips * rows
        turned = jnp.concatenate([-table[middle:], table[:middle]], axis=0)
        total = jnp.einsum("mv,cuv->mcu", table, grid[0], preferred_element_type=F32)
        total = total + jnp.einsum("mv,cuv->mcu", turned, grid[1], preferred_element_type=F32)
        total = total.astype(BF16).reshape(2, strips, rows, chans, width)
        return total.transpose(1, 0, 3, 2, 4)
    block = 4 if chans % 4 == 0 else 1
    return pl.pallas_call(
        first_body,
        grid=(chans // block,),
        in_specs=[
            pl.BlockSpec(table.shape, lambda i: (0, 0)),
            pl.BlockSpec((2, block, width, side_len), lambda i: (0, i, 0, 0)),
            ANY,
        ],
        out_specs=pl.BlockSpec((strips, 2, block, rows, width), lambda i: (0, 0, i, 0, 0)),
        out_shape=jax.ShapeDtypeStruct(shape, BF16),
        compiler_params=kernel_params(28),
        cost_estimate=COST,
        name="first_transform",
    )(table, grid, after)


def band_matrix(taps_of, levels, taps, own_rows, reach, first_row, image_rows):
    half_taps = taps // 2
    shape = (own_rows, own_rows + 2 * reach)
    row = iota(shape, 0)
    column = iota(shape, 1)
    place = jnp.where(
        column < own_rows, column, jnp.where(column < own_rows + reach, column - own_rows - reach, column - reach)
    )
    total = jnp.zeros(shape, F32)
    for level in range(levels):
        dilation = 2**level
        for outer in range(taps):
            detail_row = row - (outer - half_taps) * dilation
            inside = (detail_row + first_row >= 0) & (detail_row + first_row < image_rows)
            for inner in range(taps):
                hit = inside & (place == detail_row + (inner - half_taps) * dilation)
                total = total + jnp.where(hit, taps_of(level, outer) * taps_of(level, inner), 0.0)
    return total


def base_body(levels, taps, starts, strips, strip_ref, step_ref, highpass_ref, model_ref, edge_ref, after_ref, *refs):
    high, low = refs[-2:]
    out_refs = refs[:-2]
    block, own_rows, side_len = model_ref.shape
    reach = edge_ref.shape[1] // 2

    @pl.when(pl.program_id(0) == 0)
    def _():
        band = band_matrix(
            lambda level, tap: highpass_ref[level, tap],
            levels,
            taps,
            own_rows,
            reach,
            strip_ref[0] * own_rows,
            strips * own_rows,
        )
        top = band.astype(BF16)
        high[...] = top
        low[...] = (band - top.astype(F32)).astype(BF16)

    first = pl.program_id(0) * block
    for chan in range(block):
        model = model_ref[chan]
        top = model.astype(BF16)
        rest = (model - top.astype(F32)).astype(BF16)
        edge = edge_ref[chan].astype(F32)
        whole = jnp.concatenate([top.astype(F32), edge], axis=0).astype(BF16)
        gradient = dot_nn(high[...], whole)
        gradient = gradient + dot_nn(low[...], whole)
        gradient = gradient + dot_nn(high[:, :own_rows], rest)
        base = model - step_ref[first + chan] * gradient
        for start, out_ref in zip(starts, out_refs):
            out_ref[chan] = base[start : start + out_ref.shape[1]]


def base_step(strip, strips, step_size, highpass, model_image, edges, starts, sizes, after):
    chans, rows, side_len = model_image.shape
    levels, taps = highpass.shape
    reach = edges.shape[1] // 2
    block = 2 if chans % 2 == 0 else 1
    wide = rows + 2 * reach
    return pl.pallas_call(
        functools.partial(base_body, levels, taps, starts, strips),
        grid=(chans // block,),
        in_specs=[
            SMEM,
            SMEM,
            SMEM,
            pl.BlockSpec((block, rows, side_len), lambda i: (i, 0, 0)),
            pl.BlockSpec((block, 2 * reach, side_len), lambda i: (i, 0, 0)),
            ANY,
        ],
        out_specs=[pl.BlockSpec((block, part, side_len), lambda i: (i, 0, 0)) for part in sizes],
        out_shape=[jax.ShapeDtypeStruct((chans, part, side_len), F32) for part in sizes],
        scratch_shapes=[pltpu.VMEM((rows, wide), BF16), pltpu.VMEM((rows, wide), BF16)],
        compiler_params=kernel_params(20),
        cost_estimate=COST,
        name="base_step",
    )(strip, step_size, highpass, model_image, edges, after)


def second_body(step_ref, half_ref, cosine_ref, sine_ref, base_ref, after_ref, moved_ref, pixels_ref):
    strips, _, chans, rows, width = half_ref.shape
    real = jnp.concatenate([half_ref[s, 0].reshape(chans * rows, width) for s in range(strips)], axis=1)
    imag = jnp.concatenate([half_ref[s, 1].reshape(chans * rows, width) for s in range(strips)], axis=1)
    dirty = dot_nn(real, cosine_ref[...]) - dot_nn(imag, sine_ref[...])
    pieces = []
    for chan in range(chans):
        moved = base_ref[chan] + step_ref[chan] * dirty[chan * rows : (chan + 1) * rows]
        moved_ref[chan] = moved
        pieces.append(moved)
    pixels_ref[...] = jnp.swapaxes(jnp.stack(pieces), 0, 1).astype(BF16)


def second_transform(step_size, half, cosine, sine_table, base, after):
    strips, _, chans, rows, width = half.shape
    side_len = cosine.shape[0]
    if width % 128 or rows % 16 or chans % 16:
        split = (strips, width, side_len)
        dirty = jnp.einsum("scmu,sul->cml", half[:, 0], cosine.reshape(split), preferred_element_type=F32)
        dirty = dirty - jnp.einsum("scmu,sul->cml", half[:, 1], sine_table.reshape(split), preferred_element_type=F32)
        moved = base + step_size[:, None, None] * dirty
        return moved, moved.astype(BF16).transpose(1, 0, 2)
    block = min(256, side_len)
    return pl.pallas_call(
        second_body,
        grid=(side_len // block,),
        in_specs=[
            SMEM,
            pl.BlockSpec(half.shape, lambda i: (0, 0, 0, 0, 0)),
            pl.BlockSpec((side_len, block), lambda i: (0, i)),
            pl.BlockSpec((side_len, block), lambda i: (0, i)),
            pl.BlockSpec((chans, rows, block), lambda i: (0, 0, i)),
            ANY,
        ],
        out_specs=[
            pl.BlockSpec((chans, rows, block), lambda i: (0, 0, i)),
            pl.BlockSpec((rows, chans, block), lambda i: (0, 0, i)),
        ],
        out_shape=[
            jax.ShapeDtypeStruct(base.shape, F32),
            jax.ShapeDtypeStruct((rows, chans, side_len), BF16),
        ],
        compiler_params=kernel_params(24),
        cost_estimate=COST,
        name="second_transform",
    )(step_size, half, cosine, sine_table, base, after)


def stacked(group_refs, first, count):
    return jnp.concatenate([ref[first + i] for i in range(count) for ref in group_refs], axis=0)


def gram_body(groups, before_ref, after_ref, *refs):
    total_ref = refs[groups]

    @pl.when(pl.program_id(0) == 0)
    def _():
        total_ref[...] = before_ref[...]

    total = total_ref[...]
    for first in range(0, refs[0].shape[0], GRAM_ROWS):
        pixels = stacked(refs[:groups], first, GRAM_ROWS)
        total = total + dot_nt(pixels, pixels)
    total_ref[...] = total


def gram_step(pieces, before, after):
    rows, chans, side_len = pieces[0].shape
    block = EDGE_ROWS // 2
    spec = pl.BlockSpec((block, chans, side_len), lambda i: (i, 0, 0))
    return pl.pallas_call(
        functools.partial(gram_body, len(pieces)),
        grid=(rows // block,),
        in_specs=[pl.BlockSpec(before.shape, lambda i: (0, 0)), ANY] + [spec] * len(pieces),
        out_specs=pl.BlockSpec(before.shape, lambda i: (0, 0)),
        out_shape=jax.ShapeDtypeStruct(before.shape, F32),
        compiler_params=kernel_params(16),
        cost_estimate=COST,
        name="gram_step",
    )(before, after, *pieces)


def newton_schulz(gram):
    size = gram.shape[0]
    frob_norm = jnp.sqrt(jnp.sum(gram * gram))
    identity = (iota((size, size), 0) == iota((size, size), 1)).astype(F32)
    current = gram / frob_norm
    inverse = identity
    for iteration in range(NS_ITERS):
        middle = 0.5 * (3.0 * identity - dot_nn(inverse, current, HIGHEST))
        if iteration + 1 < NS_ITERS:
            current = dot_nn(current, middle, HIGHEST)
        inverse = dot_nn(middle, inverse, HIGHEST)
    return inverse, frob_norm


def polar_body(starts, sizes, groups, shrink_ref, gram_ref, *refs):
    chunks = len(sizes)
    moved_hbm = refs[:chunks]
    pixels_hbm = refs[chunks : chunks * (groups + 1)]
    out_hbm, moved, pixel_sems, moved_sems, out_sems = refs[chunks * (groups + 1) : chunks * (groups + 1) + 5]
    pixels = refs[chunks * (groups + 1) + 5 :]
    own, all_rows, side_len = moved.shape
    size = pixels[0].shape[2] * groups
    moved_copies = []
    pixel_copies = []
    for chunk in range(chunks):
        part = pl.ds(starts[chunk], sizes[chunk])
        copies = []
        for group in range(groups):
            place = chunk * groups + group
            copies.append(pltpu.make_async_copy(pixels_hbm[place], pixels[chunk].at[group], pixel_sems.at[place]))
        pixel_copies.append(copies)
        moved_copies.append(pltpu.make_async_copy(moved_hbm[chunk], moved.at[:, part], moved_sems.at[chunk]))
        for copy in copies + moved_copies[-1:]:
            copy.start()
    gram = jnp.zeros((size, size), F32)
    for i in range(GRAM_ROWS):
        gram = gram + gram_ref[i * size : (i + 1) * size, i * size : (i + 1) * size]
    inverse, frob_norm = newton_schulz(gram)
    factor = shrink_ref[0] * jnp.sqrt(all_rows * side_len / frob_norm)
    select = (iota((own, size), 0) == iota((own, size), 1)).astype(F32)
    weights = dot_nt(select, inverse, HIGHEST) * factor
    spread = POLAR_ROWS * own
    wide = POLAR_ROWS * size
    repeat = (iota((spread, own), 0) // POLAR_ROWS == iota((spread, own), 1)).astype(BF16)
    weights = dot_nn(repeat, weights.astype(BF16)).astype(BF16)
    repeat = (iota((size, wide), 1) % size == iota((size, wide), 0)).astype(BF16)
    weights = dot_nn(weights, repeat)
    keep = iota((spread, wide), 0) % POLAR_ROWS == iota((spread, wide), 1) // size
    weights = jnp.where(keep, weights, 0.0).astype(BF16)
    out_copies = []
    for chunk in range(chunks):
        for copy in pixel_copies[chunk]:
            copy.wait()
        moved_copies[chunk].wait()
        for step in range(sizes[chunk] // POLAR_ROWS):
            data = stacked([pixels[chunk].at[group] for group in range(groups)], step * POLAR_ROWS, POLAR_ROWS)
            polar = dot_nn(weights, data).reshape(own, POLAR_ROWS, side_len)
            first = starts[chunk] + step * POLAR_ROWS
            moved[:, first : first + POLAR_ROWS] -= polar
        part = pl.ds(starts[chunk], sizes[chunk])
        copy = pltpu.make_async_copy(moved.at[:, part], out_hbm.at[:, part], out_sems.at[chunk])
        copy.start()
        out_copies.append(copy)
    for copy in out_copies:
        copy.wait()


def polar_step(shrinkage, gram, moved, gathered, starts, sizes):
    chunks = len(gathered)
    groups = len(gathered[0])
    chans, _, side_len = moved[0].shape
    shape = (chans, sum(sizes), side_len)
    flat = [piece for pieces in gathered for piece in pieces]
    return pl.pallas_call(
        functools.partial(polar_body, starts, sizes, groups),
        in_specs=[SMEM, pl.BlockSpec(memory_space=pltpu.VMEM)] + [ANY] * (chunks + len(flat)),
        out_specs=ANY,
        out_shape=jax.ShapeDtypeStruct(shape, F32),
        scratch_shapes=[
            pltpu.VMEM(shape, F32),
            pltpu.SemaphoreType.DMA((chunks * groups,)),
            pltpu.SemaphoreType.DMA((chunks,)),
            pltpu.SemaphoreType.DMA((chunks,)),
        ]
        + [pltpu.VMEM((groups,) + pieces[0].shape, BF16) for pieces in gathered],
        compiler_params=kernel_params(40),
        cost_estimate=COST,
        name="polar_step",
    )(shrinkage, gram, *moved, *flat)


def neighbour_rows(model_image, reach):
    ends = lax.axis_size("strip") - 1
    head, tail = lax.optimization_barrier((model_image[:, :reach], model_image[:, model_image.shape[1] - reach :]))
    before = lax.ppermute(tail.astype(BF16), "strip", [(i, i + 1) for i in range(ends)])
    after = lax.ppermute(head.astype(BF16), "strip", [(i + 1, i) for i in range(ends)])
    return jnp.concatenate([before, after], axis=1)


def swap(value, axis, bits):
    count = lax.axis_size(axis)
    return lax.ppermute(value, axis, [(i, i ^ bits) for i in range(count)])


def gather_channels(pixels):
    devices = lax.axis_size("chan")
    kept = [pixels] + [swap(pixels, "chan", bits) for bits in range(2, devices, 2)]
    if devices == 1:
        return kept
    return kept + [swap(piece, "chan", 1) for piece in kept]


def local(grid, model_image, step_size, highpass, shrinkage):
    chans, own_rows, side_len = model_image.shape
    strips = lax.axis_size("strip")
    size = chans * lax.axis_size("chan")
    starts, sizes = chunk_rows(own_rows)
    chunks = len(sizes)
    strip = lax.axis_index("strip").astype(jnp.int32).reshape(1)

    cosine, sine_table = make_tables(side_len)
    split = np.stack([cosine.reshape(strips, own_rows, side_len), sine_table.reshape(strips, own_rows, side_len)])
    tables = [
        np.ascontiguousarray(split[:, :, start : start + rows]).reshape(2 * strips * rows, side_len)
        for start, rows in zip(starts, sizes)
    ]

    levels, taps = highpass.shape
    reach = (taps - 1) * 2 ** (levels - 1)
    edges = neighbour_rows(model_image, reach)

    halves = []
    moved = []
    gathered = []
    gram = jnp.zeros((GRAM_ROWS * size, GRAM_ROWS * size), F32)
    last = strip
    for chunk in range(chunks + 1):
        if chunk < chunks:
            sent = first_transform(tables[chunk], grid, strips, last)
            last = sent
            halves.append(lax.all_to_all(sent, "strip", split_axis=0, concat_axis=0, tiled=True))
        if chunk == 1:
            bases = base_step(strip, strips, step_size, highpass, model_image, edges, starts, sizes, last)
            last = bases[0]
        if chunk >= 1:
            done = chunk - 1
            result, pixels = second_transform(step_size, halves[done], cosine, sine_table, bases[done], last)
            last = pixels
            moved.append(result)
            pieces = gather_channels(pixels)
            if chans % 16:
                pieces = [jnp.concatenate(pieces, axis=1)]
            gathered.append(pieces)
        if chunk >= 2:
            gram = gram_step(gathered[chunk - 2], gram, last)
            last = gram
    gram = gram_step(gathered[-1], gram, last)
    return polar_step(shrinkage, gram, moved, gathered, starts, sizes)


def solution(mesh):
    return jax.shard_map(
        local,
        mesh=mesh,
        in_specs=(
            P(None, "chan", "strip", None),
            P("chan", "strip", None),
            P("chan"),
            P(),
            P("strip"),
        ),
        out_specs=P("chan", "strip", None),
        check_vma=False,
    )
```

```python
import functools

import jax
import jax.numpy as jnp
import ml_dtypes
import numpy as np
from jax import lax
from jax.experimental import pallas as pl
from jax.experimental.pallas import tpu as pltpu
from jax.sharding import PartitionSpec as P

NS_ITERS = 5
EDGE_ROWS = 16
GRAM_ROWS = 4
POLAR_ROWS = 8
HIGHEST = lax.Precision.HIGHEST
F32 = jnp.float32
BF16 = jnp.bfloat16
MIB = 1 << 20

ANY = pl.BlockSpec(memory_space=pl.ANY)
SMEM = pl.BlockSpec(memory_space=pltpu.SMEM)


def kernel_params(mebibytes):
    return pltpu.CompilerParams(vmem_limit_bytes=mebibytes * MIB)


COST = pl.CostEstimate(flops=0, bytes_accessed=1 << 16, transcendentals=0)


def dot_nt(a, b, precision=None):
    return lax.dot_general(
        a, b, (((1,), (1,)), ((), ())), precision=precision, preferred_element_type=F32
    )


def dot_nn(a, b, precision=None):
    return lax.dot_general(
        a, b, (((1,), (0,)), ((), ())), precision=precision, preferred_element_type=F32
    )


def iota(shape, dim):
    return lax.broadcasted_iota(jnp.int32, shape, dim)


def make_tables(side_len):
    indices = np.arange(side_len, dtype=np.int64)
    phases = (np.outer(indices, indices) % side_len).astype(np.float32) * np.float32(
        2.0 * 3.141592653589793 / side_len
    )
    unit_scale = np.float32(float(side_len) ** (-0.5))
    cosine = (np.cos(phases) * unit_scale).astype(ml_dtypes.bfloat16)
    sine_table = (np.sin(phases) * unit_scale).astype(ml_dtypes.bfloat16)
    return cosine, sine_table


def chunk_rows(own_rows):
    sizes = [EDGE_ROWS, own_rows // 2, own_rows // 2 - 2 * EDGE_ROWS, EDGE_ROWS]
    sizes = [size for size in sizes if size > 0]
    return [sum(sizes[:place]) for place in range(len(sizes))], sizes


def gate_body(value_ref, after_ref, out_ref):
    pass


def gate(value, after):
    return pl.pallas_call(
        gate_body,
        in_specs=[ANY, ANY],
        out_specs=ANY,
        out_shape=jax.ShapeDtypeStruct(value.shape, value.dtype),
        input_output_aliases={0: 0},
        cost_estimate=COST,
        name="gate",
    )(value, after)


def first_body(table_ref, grid_ref, after_ref, out_ref):
    strips, _, chans, rows, width = out_ref.shape
    side_len = table_ref.shape[-1]
    table = table_ref[...]
    middle = strips * rows
    turned = jnp.concatenate([-table[middle:], table[:middle]], axis=0)
    total = dot_nt(table, grid_ref[0].reshape(chans * width, side_len))
    total = total + dot_nt(turned, grid_ref[1].reshape(chans * width, side_len))
    total = total.astype(BF16)
    for part in range(2):
        for strip in range(strips):
            first = (part * strips + strip) * rows
            for chan in range(chans):
                out_ref[strip, part, chan] = total[first : first + rows, chan * width : (chan + 1) * width]


def first_transform(table, grid, strips, after):
    _, chans, width, side_len = grid.shape
    rows = table.shape[0] // (2 * strips)
    shape = (strips, 2, chans, rows, width)
    if width % 128 or rows % 16:
        middle = strips * rows
        turned = jnp.concatenate([-table[middle:], table[:middle]], axis=0)
        total = jnp.einsum("mv,cuv->mcu", table, grid[0], preferred_element_type=F32)
        total = total + jnp.einsum("mv,cuv->mcu", turned, grid[1], preferred_element_type=F32)
        total = total.astype(BF16).reshape(2, strips, rows, chans, width)
        return total.transpose(1, 0, 3, 2, 4)
    block = 4 if chans % 4 == 0 else 1
    return pl.pallas_call(
        first_body,
        grid=(chans // block,),
        in_specs=[
            pl.BlockSpec(table.shape, lambda i: (0, 0)),
            pl.BlockSpec((2, block, width, side_len), lambda i: (0, i, 0, 0)),
            ANY,
        ],
        out_specs=pl.BlockSpec((strips, 2, block, rows, width), lambda i: (0, 0, i, 0, 0)),
        out_shape=jax.ShapeDtypeStruct(shape, BF16),
        compiler_params=kernel_params(60),
        cost_estimate=COST,
        name="first_transform",
    )(table, grid, after)


def band_matrix(taps_of, levels, taps, own_rows, reach, first_row, image_rows):
    half_taps = taps // 2
    shape = (own_rows, own_rows + 2 * reach)
    row = iota(shape, 0)
    column = iota(shape, 1)
    place = jnp.where(
        column < own_rows, column, jnp.where(column < own_rows + reach, column - own_rows - reach, column - reach)
    )
    total = jnp.zeros(shape, F32)
    for level in range(levels):
        dilation = 2**level
        for outer in range(taps):
            detail_row = row - (outer - half_taps) * dilation
            inside = (detail_row + first_row >= 0) & (detail_row + first_row < image_rows)
            for inner in range(taps):
                hit = inside & (place == detail_row + (inner - half_taps) * dilation)
                total = total + jnp.where(hit, taps_of(level, outer) * taps_of(level, inner), 0.0)
    return total


def base_body(levels, taps, starts, strips, strip_ref, step_ref, highpass_ref, model_ref, edge_ref, after_ref, *refs):
    high, low = refs[-2:]
    out_refs = refs[:-2]
    block, own_rows, side_len = model_ref.shape
    reach = edge_ref.shape[1] // 2

    @pl.when(pl.program_id(0) == 0)
    def _():
        band = band_matrix(
            lambda level, tap: highpass_ref[level, tap],
            levels,
            taps,
            own_rows,
            reach,
            strip_ref[0] * own_rows,
            strips * own_rows,
        )
        top = band.astype(BF16)
        high[...] = top
        low[...] = (band - top.astype(F32)).astype(BF16)

    first = pl.program_id(0) * block
    for chan in range(block):
        model = model_ref[chan]
        top = model.astype(BF16)
        rest = (model - top.astype(F32)).astype(BF16)
        edge = edge_ref[chan].astype(F32)
        whole = jnp.concatenate([top.astype(F32), edge], axis=0).astype(BF16)
        gradient = dot_nn(high[...], whole)
        gradient = gradient + dot_nn(low[...], whole)
        gradient = gradient + dot_nn(high[:, :own_rows], rest)
        base = model - step_ref[first + chan] * gradient
        for start, out_ref in zip(starts, out_refs):
            out_ref[chan] = base[start : start + out_ref.shape[1]]


def base_step(strip, strips, step_size, highpass, model_image, edges, starts, sizes, after):
    chans, rows, side_len = model_image.shape
    levels, taps = highpass.shape
    reach = edges.shape[1] // 2
    block = 2 if chans % 2 == 0 else 1
    wide = rows + 2 * reach
    return pl.pallas_call(
        functools.partial(base_body, levels, taps, starts, strips),
        grid=(chans // block,),
        in_specs=[
            SMEM,
            SMEM,
            SMEM,
            pl.BlockSpec((block, rows, side_len), lambda i: (i, 0, 0)),
            pl.BlockSpec((block, 2 * reach, side_len), lambda i: (i, 0, 0)),
            ANY,
        ],
        out_specs=[pl.BlockSpec((block, part, side_len), lambda i: (i, 0, 0)) for part in sizes],
        out_shape=[jax.ShapeDtypeStruct((chans, part, side_len), F32) for part in sizes],
        scratch_shapes=[pltpu.VMEM((rows, wide), BF16), pltpu.VMEM((rows, wide), BF16)],
        compiler_params=kernel_params(60),
        cost_estimate=COST,
        name="base_step",
    )(strip, step_size, highpass, model_image, edges, after)


def second_body(step_ref, half_ref, cosine_ref, sine_ref, base_ref, after_ref, moved_ref, pixels_ref):
    strips, _, chans, rows, width = half_ref.shape
    real = jnp.concatenate([half_ref[s, 0].reshape(chans * rows, width) for s in range(strips)], axis=1)
    imag = jnp.concatenate([half_ref[s, 1].reshape(chans * rows, width) for s in range(strips)], axis=1)
    dirty = dot_nn(real, cosine_ref[...]) - dot_nn(imag, sine_ref[...])
    pieces = []
    for chan in range(chans):
        moved = base_ref[chan] + step_ref[chan] * dirty[chan * rows : (chan + 1) * rows]
        moved_ref[chan] = moved
        pieces.append(moved)
    pixels_ref[...] = jnp.swapaxes(jnp.stack(pieces), 0, 1).astype(BF16)


def second_transform(step_size, half, cosine, sine_table, base, after):
    strips, _, chans, rows, width = half.shape
    side_len = cosine.shape[0]
    if width % 128 or rows % 16 or chans % 16:
        split = (strips, width, side_len)
        dirty = jnp.einsum("scmu,sul->cml", half[:, 0], cosine.reshape(split), preferred_element_type=F32)
        dirty = dirty - jnp.einsum("scmu,sul->cml", half[:, 1], sine_table.reshape(split), preferred_element_type=F32)
        moved = base + step_size[:, None, None] * dirty
        return moved, moved.astype(BF16).transpose(1, 0, 2)
    block = min(256, side_len)
    return pl.pallas_call(
        second_body,
        grid=(side_len // block,),
        in_specs=[
            SMEM,
            pl.BlockSpec(half.shape, lambda i: (0, 0, 0, 0, 0)),
            pl.BlockSpec((side_len, block), lambda i: (0, i)),
            pl.BlockSpec((side_len, block), lambda i: (0, i)),
            pl.BlockSpec((chans, rows, block), lambda i: (0, 0, i)),
            ANY,
        ],
        out_specs=[
            pl.BlockSpec((chans, rows, block), lambda i: (0, 0, i)),
            pl.BlockSpec((rows, chans, block), lambda i: (0, 0, i)),
        ],
        out_shape=[
            jax.ShapeDtypeStruct(base.shape, F32),
            jax.ShapeDtypeStruct((rows, chans, side_len), BF16),
        ],
        compiler_params=kernel_params(60),
        cost_estimate=COST,
        name="second_transform",
    )(step_size, half, cosine, sine_table, base, after)


def stacked(group_refs, first, count):
    return jnp.concatenate([ref[first + i] for i in range(count) for ref in group_refs], axis=0)


def gram_body(groups, before_ref, after_ref, *refs):
    total_ref = refs[groups]

    @pl.when(pl.program_id(0) == 0)
    def _():
        total_ref[...] = before_ref[...]

    total = total_ref[...]
    for first in range(0, refs[0].shape[0], GRAM_ROWS):
        pixels = stacked(refs[:groups], first, GRAM_ROWS)
        total = total + dot_nt(pixels, pixels)
    total_ref[...] = total


def gram_step(pieces, before, after):
    rows, chans, side_len = pieces[0].shape
    block = EDGE_ROWS // 2
    spec = pl.BlockSpec((block, chans, side_len), lambda i: (i, 0, 0))
    return pl.pallas_call(
        functools.partial(gram_body, len(pieces)),
        grid=(rows // block,),
        in_specs=[pl.BlockSpec(before.shape, lambda i: (0, 0)), ANY] + [spec] * len(pieces),
        out_specs=pl.BlockSpec(before.shape, lambda i: (0, 0)),
        out_shape=jax.ShapeDtypeStruct(before.shape, F32),
        compiler_params=kernel_params(16),
        cost_estimate=COST,
        name="gram_step",
    )(before, after, *pieces)


def newton_schulz(gram):
    size = gram.shape[0]
    frob_norm = jnp.sqrt(jnp.sum(gram * gram))
    identity = (iota((size, size), 0) == iota((size, size), 1)).astype(F32)
    current = gram / frob_norm
    middle = 0.5 * (3.0 * identity - current)
    inverse = middle
    for iteration in range(1, NS_ITERS):
        current = dot_nn(current, middle, HIGHEST)
        middle = 0.5 * (3.0 * identity - dot_nn(inverse, current, HIGHEST))
        inverse = dot_nn(middle, inverse, HIGHEST)
    return inverse, frob_norm


def polar_body(starts, sizes, groups, shrink_ref, gram_ref, *refs):
    chunks = len(sizes)
    moved_hbm = refs[:chunks]
    pixels_hbm = refs[chunks : chunks * (groups + 1)]
    out_hbm, moved, pixel_sems, moved_sems, out_sems = refs[chunks * (groups + 1) : chunks * (groups + 1) + 5]
    pixels = refs[chunks * (groups + 1) + 5 :]
    own, all_rows, side_len = moved.shape
    size = pixels[0].shape[2] * groups
    moved_copies = []
    pixel_copies = []
    for chunk in range(chunks):
        part = pl.ds(starts[chunk], sizes[chunk])
        copies = []
        for group in range(groups):
            place = chunk * groups + group
            copies.append(pltpu.make_async_copy(pixels_hbm[place], pixels[chunk].at[group], pixel_sems.at[place]))
        pixel_copies.append(copies)
        moved_copies.append(pltpu.make_async_copy(moved_hbm[chunk], moved.at[:, part], moved_sems.at[chunk]))
        for copy in copies + moved_copies[-1:]:
            copy.start()
    gram = jnp.zeros((size, size), F32)
    for i in range(GRAM_ROWS):
        gram = gram + gram_ref[i * size : (i + 1) * size, i * size : (i + 1) * size]
    inverse, frob_norm = newton_schulz(gram)
    factor = shrink_ref[0] * jnp.sqrt(all_rows * side_len / frob_norm)
    select = (iota((own, size), 0) == iota((own, size), 1)).astype(F32)
    weights = dot_nt(select, inverse, HIGHEST) * factor
    spread = POLAR_ROWS * own
    wide = POLAR_ROWS * size
    repeat = (iota((spread, own), 0) // POLAR_ROWS == iota((spread, own), 1)).astype(BF16)
    weights = dot_nn(repeat, weights.astype(BF16)).astype(BF16)
    repeat = (iota((size, wide), 1) % size == iota((size, wide), 0)).astype(BF16)
    weights = dot_nn(weights, repeat)
    keep = iota((spread, wide), 0) % POLAR_ROWS == iota((spread, wide), 1) // size
    weights = jnp.where(keep, weights, 0.0).astype(BF16)
    out_copies = []
    for chunk in range(chunks):
        for copy in pixel_copies[chunk]:
            copy.wait()
        moved_copies[chunk].wait()
        for step in range(sizes[chunk] // POLAR_ROWS):
            data = stacked([pixels[chunk].at[group] for group in range(groups)], step * POLAR_ROWS, POLAR_ROWS)
            polar = dot_nn(weights, data).reshape(own, POLAR_ROWS, side_len)
            first = starts[chunk] + step * POLAR_ROWS
            moved[:, first : first + POLAR_ROWS] -= polar
        part = pl.ds(starts[chunk], sizes[chunk])
        copy = pltpu.make_async_copy(moved.at[:, part], out_hbm.at[:, part], out_sems.at[chunk])
        copy.start()
        out_copies.append(copy)
    for copy in out_copies:
        copy.wait()


def polar_step(shrinkage, gram, moved, gathered, starts, sizes):
    chunks = len(gathered)
    groups = len(gathered[0])
    chans, _, side_len = moved[0].shape
    shape = (chans, sum(sizes), side_len)
    flat = [piece for pieces in gathered for piece in pieces]
    return pl.pallas_call(
        functools.partial(polar_body, starts, sizes, groups),
        in_specs=[SMEM, pl.BlockSpec(memory_space=pltpu.VMEM)] + [ANY] * (chunks + len(flat)),
        out_specs=ANY,
        out_shape=jax.ShapeDtypeStruct(shape, F32),
        scratch_shapes=[
            pltpu.VMEM(shape, F32),
            pltpu.SemaphoreType.DMA((chunks * groups,)),
            pltpu.SemaphoreType.DMA((chunks,)),
            pltpu.SemaphoreType.DMA((chunks,)),
        ]
        + [pltpu.VMEM((groups,) + pieces[0].shape, BF16) for pieces in gathered],
        compiler_params=kernel_params(40),
        cost_estimate=COST,
        name="polar_step",
    )(shrinkage, gram, *moved, *flat)


def neighbour_rows(model_image, reach):
    ends = lax.axis_size("strip") - 1
    head, tail = lax.optimization_barrier((model_image[:, :reach], model_image[:, model_image.shape[1] - reach :]))
    before = lax.ppermute(tail.astype(BF16), "strip", [(i, i + 1) for i in range(ends)])
    after = lax.ppermute(head.astype(BF16), "strip", [(i + 1, i) for i in range(ends)])
    return jnp.concatenate([before, after], axis=1)


def swap(value, axis, bits):
    count = lax.axis_size(axis)
    return lax.ppermute(value, axis, [(i, i ^ bits) for i in range(count)])


def gather_channels(pixels, after=None):
    devices = lax.axis_size("chan")
    kept = [pixels] + [swap(pixels, "chan", bits) for bits in range(2, devices, 2)]
    if after is not None:
        kept = [pixels] + [gate(piece, after) for piece in kept[1:]]
    if devices == 1:
        return kept
    return kept + [swap(piece, "chan", 1) for piece in kept]


def local(grid, model_image, step_size, highpass, shrinkage):
    chans, own_rows, side_len = model_image.shape
    strips = lax.axis_size("strip")
    size = chans * lax.axis_size("chan")
    starts, sizes = chunk_rows(own_rows)
    chunks = len(sizes)
    strip = lax.axis_index("strip").astype(jnp.int32).reshape(1)

    cosine, sine_table = make_tables(side_len)
    split = np.stack([cosine.reshape(strips, own_rows, side_len), sine_table.reshape(strips, own_rows, side_len)])
    tables = [
        np.ascontiguousarray(split[:, :, start : start + rows]).reshape(2 * strips * rows, side_len)
        for start, rows in zip(starts, sizes)
    ]

    levels, taps = highpass.shape
    reach = (taps - 1) * 2 ** (levels - 1)
    edges = neighbour_rows(model_image, reach)

    halves = []
    moved = []
    gathered = []
    gram = jnp.zeros((GRAM_ROWS * size, GRAM_ROWS * size), F32)
    last = strip
    for chunk in range(chunks + 1):
        if chunk < chunks:
            sent = first_transform(tables[chunk], grid, strips, last)
            if chunk == 1:
                sent = gate(sent, edges)
            last = sent
            halves.append(lax.all_to_all(sent, "strip", split_axis=0, concat_axis=0, tiled=True))
        if chunk == 1:
            bases = base_step(strip, strips, step_size, highpass, model_image, edges, starts, sizes, last)
            last = bases[0]
        if chunk >= 1:
            done = chunk - 1
            result, pixels = second_transform(step_size, halves[done], cosine, sine_table, bases[done], last)
            last = pixels
            moved.append(result)
            if done >= 1:
                gram = gram_step(gathered[done - 1], gram, last)
                last = gram
            pieces = gather_channels(pixels, gram if chunk == chunks else None)
            if chans % 16:
                pieces = [jnp.concatenate(pieces, axis=1)]
            gathered.append(pieces)
    gram = gram_step(gathered[-1], gram, last)
    return polar_step(shrinkage, gram, moved, gathered, starts, sizes)


def solution(mesh):
    return jax.shard_map(
        local,
        mesh=mesh,
        in_specs=(
            P(None, "chan", "strip", None),
            P("chan", "strip", None),
            P("chan"),
            P(),
            P("strip"),
        ),
        out_specs=P("chan", "strip", None),
        check_vma=False,
    )
```

```python
import functools

import jax
import jax.numpy as jnp
import ml_dtypes
import numpy as np
from jax import lax
from jax.experimental import pallas as pl
from jax.experimental.pallas import tpu as pltpu
from jax.sharding import PartitionSpec as P

NS_ITERS = 5
EDGE_ROWS = 16
GRAM_ROWS = 4
POLAR_ROWS = 8
HIGHEST = lax.Precision.HIGHEST
F32 = jnp.float32
BF16 = jnp.bfloat16
MIB = 1 << 20

ANY = pl.BlockSpec(memory_space=pl.ANY)
SMEM = pl.BlockSpec(memory_space=pltpu.SMEM)


def kernel_params(mebibytes):
    return pltpu.CompilerParams(vmem_limit_bytes=mebibytes * MIB)


COST = pl.CostEstimate(flops=0, bytes_accessed=1 << 16, transcendentals=0)


def dot_nt(a, b, precision=None):
    return lax.dot_general(
        a, b, (((1,), (1,)), ((), ())), precision=precision, preferred_element_type=F32
    )


def dot_nn(a, b, precision=None):
    return lax.dot_general(
        a, b, (((1,), (0,)), ((), ())), precision=precision, preferred_element_type=F32
    )


def iota(shape, dim):
    return lax.broadcasted_iota(jnp.int32, shape, dim)


def make_tables(side_len):
    indices = np.arange(side_len, dtype=np.int64)
    phases = (np.outer(indices, indices) % side_len).astype(np.float32) * np.float32(
        2.0 * 3.141592653589793 / side_len
    )
    unit_scale = np.float32(float(side_len) ** (-0.5))
    cosine = (np.cos(phases) * unit_scale).astype(ml_dtypes.bfloat16)
    sine_table = (np.sin(phases) * unit_scale).astype(ml_dtypes.bfloat16)
    return cosine, sine_table


def chunk_rows(own_rows):
    sizes = [EDGE_ROWS, own_rows // 2, own_rows // 2 - 2 * EDGE_ROWS, EDGE_ROWS]
    sizes = [size for size in sizes if size > 0]
    return [sum(sizes[:place]) for place in range(len(sizes))], sizes


def gate_body(value_ref, after_ref, out_ref):
    pass


def gate(value, after):
    return pl.pallas_call(
        gate_body,
        in_specs=[ANY, ANY],
        out_specs=ANY,
        out_shape=jax.ShapeDtypeStruct(value.shape, value.dtype),
        input_output_aliases={0: 0},
        cost_estimate=COST,
        name="gate",
    )(value, after)


def first_body(table_ref, grid_ref, after_ref, out_ref):
    strips, _, chans, rows, width = out_ref.shape
    side_len = table_ref.shape[-1]
    table = table_ref[...]
    middle = strips * rows
    turned = jnp.concatenate([-table[middle:], table[:middle]], axis=0)
    total = dot_nt(table, grid_ref[0].reshape(chans * width, side_len))
    total = total + dot_nt(turned, grid_ref[1].reshape(chans * width, side_len))
    total = total.astype(BF16)
    for part in range(2):
        for strip in range(strips):
            first = (part * strips + strip) * rows
            for chan in range(chans):
                out_ref[strip, part, chan] = total[first : first + rows, chan * width : (chan + 1) * width]


def first_transform(table, grid, strips, after):
    _, chans, width, side_len = grid.shape
    rows = table.shape[0] // (2 * strips)
    shape = (strips, 2, chans, rows, width)
    if width % 128 or rows % 16:
        middle = strips * rows
        turned = jnp.concatenate([-table[middle:], table[:middle]], axis=0)
        total = jnp.einsum("mv,cuv->mcu", table, grid[0], preferred_element_type=F32)
        total = total + jnp.einsum("mv,cuv->mcu", turned, grid[1], preferred_element_type=F32)
        total = total.astype(BF16).reshape(2, strips, rows, chans, width)
        return total.transpose(1, 0, 3, 2, 4)
    block = 4 if chans % 4 == 0 else 1
    return pl.pallas_call(
        first_body,
        grid=(chans // block,),
        in_specs=[
            pl.BlockSpec(table.shape, lambda i: (0, 0)),
            pl.BlockSpec((2, block, width, side_len), lambda i: (0, i, 0, 0)),
            ANY,
        ],
        out_specs=pl.BlockSpec((strips, 2, block, rows, width), lambda i: (0, 0, i, 0, 0)),
        out_shape=jax.ShapeDtypeStruct(shape, BF16),
        compiler_params=kernel_params(60),
        cost_estimate=COST,
        name="first_transform",
    )(table, grid, after)


def band_matrix(taps_of, levels, taps, own_rows, reach, first_row, image_rows):
    half_taps = taps // 2
    shape = (own_rows, own_rows + 2 * reach)
    row = iota(shape, 0)
    column = iota(shape, 1)
    place = jnp.where(
        column < own_rows, column, jnp.where(column < own_rows + reach, column - own_rows - reach, column - reach)
    )
    total = jnp.zeros(shape, F32)
    for level in range(levels):
        dilation = 2**level
        for outer in range(taps):
            detail_row = row - (outer - half_taps) * dilation
            inside = (detail_row + first_row >= 0) & (detail_row + first_row < image_rows)
            for inner in range(taps):
                hit = inside & (place == detail_row + (inner - half_taps) * dilation)
                total = total + jnp.where(hit, taps_of(level, outer) * taps_of(level, inner), 0.0)
    return total


def base_body(levels, taps, starts, strips, strip_ref, step_ref, highpass_ref, model_ref, edge_ref, after_ref, *refs):
    high, low = refs[-2:]
    out_refs = refs[:-2]
    block, own_rows, side_len = model_ref.shape
    reach = edge_ref.shape[1] // 2

    @pl.when(pl.program_id(0) == 0)
    def _():
        band = band_matrix(
            lambda level, tap: highpass_ref[level, tap],
            levels,
            taps,
            own_rows,
            reach,
            strip_ref[0] * own_rows,
            strips * own_rows,
        )
        top = band.astype(BF16)
        high[...] = top
        low[...] = (band - top.astype(F32)).astype(BF16)

    first = pl.program_id(0) * block
    for chan in range(block):
        model = model_ref[chan]
        top = model.astype(BF16)
        rest = (model - top.astype(F32)).astype(BF16)
        edge = edge_ref[chan].astype(F32)
        whole = jnp.concatenate([top.astype(F32), edge], axis=0).astype(BF16)
        gradient = dot_nn(high[...], whole)
        gradient = gradient + dot_nn(low[...], whole)
        gradient = gradient + dot_nn(high[:, :own_rows], rest)
        base = model - step_ref[first + chan] * gradient
        for start, out_ref in zip(starts, out_refs):
            out_ref[chan] = base[start : start + out_ref.shape[1]]


def base_step(strip, strips, step_size, highpass, model_image, edges, starts, sizes, after):
    chans, rows, side_len = model_image.shape
    levels, taps = highpass.shape
    reach = edges.shape[1] // 2
    block = 2 if chans % 2 == 0 else 1
    wide = rows + 2 * reach
    return pl.pallas_call(
        functools.partial(base_body, levels, taps, starts, strips),
        grid=(chans // block,),
        in_specs=[
            SMEM,
            SMEM,
            SMEM,
            pl.BlockSpec((block, rows, side_len), lambda i: (i, 0, 0)),
            pl.BlockSpec((block, 2 * reach, side_len), lambda i: (i, 0, 0)),
            ANY,
        ],
        out_specs=[pl.BlockSpec((block, part, side_len), lambda i: (i, 0, 0)) for part in sizes],
        out_shape=[jax.ShapeDtypeStruct((chans, part, side_len), F32) for part in sizes],
        scratch_shapes=[pltpu.VMEM((rows, wide), BF16), pltpu.VMEM((rows, wide), BF16)],
        compiler_params=kernel_params(60),
        cost_estimate=COST,
        name="base_step",
    )(strip, step_size, highpass, model_image, edges, after)


def second_body(step_ref, half_ref, cosine_ref, sine_ref, base_ref, after_ref, moved_ref, pixels_ref):
    strips, _, chans, rows, width = half_ref.shape
    real = jnp.concatenate([half_ref[s, 0].reshape(chans * rows, width) for s in range(strips)], axis=1)
    imag = jnp.concatenate([half_ref[s, 1].reshape(chans * rows, width) for s in range(strips)], axis=1)
    dirty = dot_nn(real, cosine_ref[...]) - dot_nn(imag, sine_ref[...])
    pieces = []
    for chan in range(chans):
        moved = base_ref[chan] + step_ref[chan] * dirty[chan * rows : (chan + 1) * rows]
        moved_ref[chan] = moved
        pieces.append(moved)
    pixels_ref[...] = jnp.swapaxes(jnp.stack(pieces), 0, 1).astype(BF16)


def second_transform(step_size, half, cosine, sine_table, base, after):
    strips, _, chans, rows, width = half.shape
    side_len = cosine.shape[0]
    if width % 128 or rows % 16 or chans % 16:
        split = (strips, width, side_len)
        dirty = jnp.einsum("scmu,sul->cml", half[:, 0], cosine.reshape(split), preferred_element_type=F32)
        dirty = dirty - jnp.einsum("scmu,sul->cml", half[:, 1], sine_table.reshape(split), preferred_element_type=F32)
        moved = base + step_size[:, None, None] * dirty
        return moved, moved.astype(BF16).transpose(1, 0, 2)
    block = min(256, side_len)
    return pl.pallas_call(
        second_body,
        grid=(side_len // block,),
        in_specs=[
            SMEM,
            pl.BlockSpec(half.shape, lambda i: (0, 0, 0, 0, 0)),
            pl.BlockSpec((side_len, block), lambda i: (0, i)),
            pl.BlockSpec((side_len, block), lambda i: (0, i)),
            pl.BlockSpec((chans, rows, block), lambda i: (0, 0, i)),
            ANY,
        ],
        out_specs=[
            pl.BlockSpec((chans, rows, block), lambda i: (0, 0, i)),
            pl.BlockSpec((rows, chans, block), lambda i: (0, 0, i)),
        ],
        out_shape=[
            jax.ShapeDtypeStruct(base.shape, F32),
            jax.ShapeDtypeStruct((rows, chans, side_len), BF16),
        ],
        compiler_params=kernel_params(60),
        cost_estimate=COST,
        name="second_transform",
    )(step_size, half, cosine, sine_table, base, after)


def stacked(group_refs, first, count):
    return jnp.concatenate([ref[first + i] for i in range(count) for ref in group_refs], axis=0)


def gram_body(groups, before_ref, after_ref, *refs):
    total_ref = refs[groups]

    @pl.when(pl.program_id(0) == 0)
    def _():
        total_ref[...] = before_ref[...]

    total = total_ref[...]
    for first in range(0, refs[0].shape[0], GRAM_ROWS):
        pixels = stacked(refs[:groups], first, GRAM_ROWS)
        total = total + dot_nt(pixels, pixels)
    total_ref[...] = total


def gram_step(pieces, before, after):
    rows, chans, side_len = pieces[0].shape
    block = EDGE_ROWS // 2
    spec = pl.BlockSpec((block, chans, side_len), lambda i: (i, 0, 0))
    return pl.pallas_call(
        functools.partial(gram_body, len(pieces)),
        grid=(rows // block,),
        in_specs=[pl.BlockSpec(before.shape, lambda i: (0, 0)), ANY] + [spec] * len(pieces),
        out_specs=pl.BlockSpec(before.shape, lambda i: (0, 0)),
        out_shape=jax.ShapeDtypeStruct(before.shape, F32),
        compiler_params=kernel_params(16),
        cost_estimate=COST,
        name="gram_step",
    )(before, after, *pieces)


def newton_schulz(gram):
    size = gram.shape[0]
    frob_norm = jnp.sqrt(jnp.sum(gram * gram))
    identity = (iota((size, size), 0) == iota((size, size), 1)).astype(F32)
    current = gram / frob_norm
    middle = 0.5 * (3.0 * identity - current)
    inverse = middle
    for iteration in range(1, NS_ITERS):
        current = dot_nn(current, middle, HIGHEST)
        middle = 0.5 * (3.0 * identity - dot_nn(inverse, current, HIGHEST))
        inverse = dot_nn(middle, inverse, HIGHEST)
    return inverse, frob_norm


def polar_body(starts, sizes, groups, shrink_ref, gram_ref, *refs):
    chunks = len(sizes)
    moved_hbm = refs[:chunks]
    pixels_hbm = refs[chunks : chunks * (groups + 1)]
    out_hbm, moved, pixel_sems, moved_sems, out_sems = refs[chunks * (groups + 1) : chunks * (groups + 1) + 5]
    pixels = refs[chunks * (groups + 1) + 5 :]
    own, all_rows, side_len = moved.shape
    size = pixels[0].shape[2] * groups
    moved_copies = []
    pixel_copies = []
    for chunk in range(chunks):
        part = pl.ds(starts[chunk], sizes[chunk])
        copies = []
        for group in range(groups):
            place = chunk * groups + group
            copies.append(pltpu.make_async_copy(pixels_hbm[place], pixels[chunk].at[group], pixel_sems.at[place]))
        pixel_copies.append(copies)
        moved_copies.append(pltpu.make_async_copy(moved_hbm[chunk], moved.at[:, part], moved_sems.at[chunk]))
        for copy in copies + moved_copies[-1:]:
            copy.start()
    gram = jnp.zeros((size, size), F32)
    for i in range(GRAM_ROWS):
        gram = gram + gram_ref[i * size : (i + 1) * size, i * size : (i + 1) * size]
    inverse, frob_norm = newton_schulz(gram)
    factor = shrink_ref[0] * jnp.sqrt(all_rows * side_len / frob_norm)
    select = (iota((own, size), 0) == iota((own, size), 1)).astype(F32)
    weights = dot_nt(select, inverse, HIGHEST) * factor
    spread = POLAR_ROWS * own
    wide = POLAR_ROWS * size
    repeat = (iota((spread, own), 0) // POLAR_ROWS == iota((spread, own), 1)).astype(BF16)
    weights = dot_nn(repeat, weights.astype(BF16)).astype(BF16)
    repeat = (iota((size, wide), 1) % size == iota((size, wide), 0)).astype(BF16)
    weights = dot_nn(weights, repeat)
    keep = iota((spread, wide), 0) % POLAR_ROWS == iota((spread, wide), 1) // size
    weights = jnp.where(keep, weights, 0.0).astype(BF16)
    out_copies = []
    for chunk in range(chunks):
        for copy in pixel_copies[chunk]:
            copy.wait()
        moved_copies[chunk].wait()
        for step in range(sizes[chunk] // POLAR_ROWS):
            data = stacked([pixels[chunk].at[group] for group in range(groups)], step * POLAR_ROWS, POLAR_ROWS)
            polar = dot_nn(weights, data).reshape(own, POLAR_ROWS, side_len)
            first = starts[chunk] + step * POLAR_ROWS
            moved[:, first : first + POLAR_ROWS] -= polar
        part = pl.ds(starts[chunk], sizes[chunk])
        copy = pltpu.make_async_copy(moved.at[:, part], out_hbm.at[:, part], out_sems.at[chunk])
        copy.start()
        out_copies.append(copy)
    for copy in out_copies:
        copy.wait()


def polar_step(shrinkage, gram, moved, gathered, starts, sizes):
    chunks = len(gathered)
    groups = len(gathered[0])
    chans, _, side_len = moved[0].shape
    shape = (chans, sum(sizes), side_len)
    flat = [piece for pieces in gathered for piece in pieces]
    return pl.pallas_call(
        functools.partial(polar_body, starts, sizes, groups),
        in_specs=[SMEM, pl.BlockSpec(memory_space=pltpu.VMEM)] + [ANY] * (chunks + len(flat)),
        out_specs=ANY,
        out_shape=jax.ShapeDtypeStruct(shape, F32),
        scratch_shapes=[
            pltpu.VMEM(shape, F32),
            pltpu.SemaphoreType.DMA((chunks * groups,)),
            pltpu.SemaphoreType.DMA((chunks,)),
            pltpu.SemaphoreType.DMA((chunks,)),
        ]
        + [pltpu.VMEM((groups,) + pieces[0].shape, BF16) for pieces in gathered],
        compiler_params=kernel_params(40),
        cost_estimate=COST,
        name="polar_step",
    )(shrinkage, gram, *moved, *flat)


def neighbour_rows(model_image, reach):
    ends = lax.axis_size("strip") - 1
    head, tail = lax.optimization_barrier((model_image[:, :reach], model_image[:, model_image.shape[1] - reach :]))
    before = lax.ppermute(tail.astype(BF16), "strip", [(i, i + 1) for i in range(ends)])
    after = lax.ppermute(head.astype(BF16), "strip", [(i + 1, i) for i in range(ends)])
    return jnp.concatenate([before, after], axis=1)


def swap(value, axis, bits):
    count = lax.axis_size(axis)
    return lax.ppermute(value, axis, [(i, i ^ bits) for i in range(count)])


def gather_channels(pixels, after=None):
    devices = lax.axis_size("chan")
    kept = [pixels] + [swap(pixels, "chan", bits) for bits in range(2, devices, 2)]
    if after is not None:
        kept = [pixels] + [gate(piece, after) for piece in kept[1:]]
    if devices == 1:
        return kept
    return kept + [swap(piece, "chan", 1) for piece in kept]


def local(grid, model_image, step_size, highpass, shrinkage):
    chans, own_rows, side_len = model_image.shape
    strips = lax.axis_size("strip")
    size = chans * lax.axis_size("chan")
    starts, sizes = chunk_rows(own_rows)
    chunks = len(sizes)
    strip = lax.axis_index("strip").astype(jnp.int32).reshape(1)

    cosine, sine_table = make_tables(side_len)
    split = np.stack([cosine.reshape(strips, own_rows, side_len), sine_table.reshape(strips, own_rows, side_len)])
    tables = [
        np.ascontiguousarray(split[:, :, start : start + rows]).reshape(2 * strips * rows, side_len)
        for start, rows in zip(starts, sizes)
    ]

    levels, taps = highpass.shape
    reach = (taps - 1) * 2 ** (levels - 1)
    edges = neighbour_rows(model_image, reach)

    halves = {}
    moved = {}
    gathered = {}
    state = dict(last=strip, gram=jnp.zeros((GRAM_ROWS * size, GRAM_ROWS * size), F32), bases=None)

    def first(chunk):
        sent = first_transform(tables[chunk], grid, strips, state["last"])
        if chunk == 1:
            sent = gate(sent, edges)
        state["last"] = sent
        halves[chunk] = lax.all_to_all(sent, "strip", split_axis=0, concat_axis=0, tiled=True)

    def base():
        state["bases"] = base_step(
            strip, strips, step_size, highpass, model_image, edges, starts, sizes, state["last"]
        )
        state["last"] = state["bases"][0]

    def second(chunk):
        moved[chunk], pixels = second_transform(
            step_size, halves[chunk], cosine, sine_table, state["bases"][chunk], state["last"]
        )
        state["last"] = pixels
        return pixels

    def gather(chunk, pixels, after=None):
        pieces = gather_channels(pixels, after)
        if chans % 16:
            pieces = [jnp.concatenate(pieces, axis=1)]
        gathered[chunk] = pieces

    def gram(chunk):
        state["gram"] = gram_step(gathered[chunk], state["gram"], state["last"])
        state["last"] = state["gram"]

    first(0)
    if chunks > 1:
        first(1)
    base()
    for chunk in range(chunks):
        pixels = second(chunk)
        if chunk + 2 < chunks:
            first(chunk + 2)
        if chunk > 1 or (chunk == 1 and chunks < 4):
            gram(chunk - 1)
        gather(chunk, pixels, state["gram"] if chunk + 1 == chunks else None)
        if chunk == 0 and chunks >= 4:
            gram(0)
    gram(chunks - 1)
    order = range(chunks)
    return polar_step(
        shrinkage, state["gram"], [moved[k] for k in order], [gathered[k] for k in order], starts, sizes
    )


def solution(mesh):
    return jax.shard_map(
        local,
        mesh=mesh,
        in_specs=(
            P(None, "chan", "strip", None),
            P("chan", "strip", None),
            P("chan"),
            P(),
            P("strip"),
        ),
        out_specs=P("chan", "strip", None),
        check_vma=False,
    )
```

```python
import functools

import jax
import jax.numpy as jnp
import ml_dtypes
import numpy as np
from jax import lax
from jax.experimental import pallas as pl
from jax.experimental.pallas import tpu as pltpu
from jax.sharding import PartitionSpec as P

NS_ITERS = 5
EDGE_ROWS = 16
GRAM_ROWS = 4
POLAR_ROWS = 8
HIGHEST = lax.Precision.HIGHEST
F32 = jnp.float32
BF16 = jnp.bfloat16
MIB = 1 << 20

ANY = pl.BlockSpec(memory_space=pl.ANY)
SMEM = pl.BlockSpec(memory_space=pltpu.SMEM)


def kernel_params(mebibytes):
    return pltpu.CompilerParams(vmem_limit_bytes=mebibytes * MIB)


COST = pl.CostEstimate(flops=0, bytes_accessed=1 << 16, transcendentals=0)


def dot_nt(a, b, precision=None):
    return lax.dot_general(
        a, b, (((1,), (1,)), ((), ())), precision=precision, preferred_element_type=F32
    )


def dot_nn(a, b, precision=None):
    return lax.dot_general(
        a, b, (((1,), (0,)), ((), ())), precision=precision, preferred_element_type=F32
    )


def iota(shape, dim):
    return lax.broadcasted_iota(jnp.int32, shape, dim)


def make_tables(side_len):
    indices = np.arange(side_len, dtype=np.int64)
    phases = (np.outer(indices, indices) % side_len).astype(np.float32) * np.float32(
        2.0 * 3.141592653589793 / side_len
    )
    unit_scale = np.float32(float(side_len) ** (-0.5))
    cosine = (np.cos(phases) * unit_scale).astype(ml_dtypes.bfloat16)
    sine_table = (np.sin(phases) * unit_scale).astype(ml_dtypes.bfloat16)
    return cosine, sine_table


def chunk_rows(own_rows):
    sizes = [EDGE_ROWS, own_rows // 2, own_rows // 2 - 2 * EDGE_ROWS, EDGE_ROWS]
    sizes = [size for size in sizes if size > 0]
    return [sum(sizes[:place]) for place in range(len(sizes))], sizes


def gate_body(value_ref, after_ref, out_ref):
    pass


def gate(value, after):
    return pl.pallas_call(
        gate_body,
        in_specs=[ANY, ANY],
        out_specs=ANY,
        out_shape=jax.ShapeDtypeStruct(value.shape, value.dtype),
        input_output_aliases={0: 0},
        cost_estimate=COST,
        name="gate",
    )(value, after)


def first_body(table_ref, grid_ref, after_ref, out_ref, token_ref):
    token_ref[...] = jnp.zeros(token_ref.shape, F32)
    strips, _, chans, rows, width = out_ref.shape
    side_len = table_ref.shape[-1]
    table = table_ref[...]
    middle = strips * rows
    turned = jnp.concatenate([-table[middle:], table[:middle]], axis=0)
    total = dot_nt(table, grid_ref[0].reshape(chans * width, side_len))
    total = total + dot_nt(turned, grid_ref[1].reshape(chans * width, side_len))
    total = total.astype(BF16)
    for part in range(2):
        for strip in range(strips):
            first = (part * strips + strip) * rows
            for chan in range(chans):
                out_ref[strip, part, chan] = total[first : first + rows, chan * width : (chan + 1) * width]


def first_transform(table, grid, strips, after):
    _, chans, width, side_len = grid.shape
    rows = table.shape[0] // (2 * strips)
    shape = (strips, 2, chans, rows, width)
    if width % 128 or rows % 16:
        middle = strips * rows
        turned = jnp.concatenate([-table[middle:], table[:middle]], axis=0)
        total = jnp.einsum("mv,cuv->mcu", table, grid[0], preferred_element_type=F32)
        total = total + jnp.einsum("mv,cuv->mcu", turned, grid[1], preferred_element_type=F32)
        total = total.astype(BF16).reshape(2, strips, rows, chans, width)
        return total.transpose(1, 0, 3, 2, 4), jnp.zeros((8, 128), F32)
    block = 4 if chans % 4 == 0 else 1
    return pl.pallas_call(
        first_body,
        grid=(chans // block,),
        in_specs=[
            pl.BlockSpec(table.shape, lambda i: (0, 0)),
            pl.BlockSpec((2, block, width, side_len), lambda i: (0, i, 0, 0)),
            ANY,
        ],
        out_specs=[
            pl.BlockSpec((strips, 2, block, rows, width), lambda i: (0, 0, i, 0, 0)),
            pl.BlockSpec((8, 128), lambda i: (0, 0)),
        ],
        out_shape=[jax.ShapeDtypeStruct(shape, BF16), jax.ShapeDtypeStruct((8, 128), F32)],
        compiler_params=kernel_params(60),
        cost_estimate=COST,
        name="first_transform",
    )(table, grid, after)


def band_matrix(taps_of, levels, taps, own_rows, reach, first_row, image_rows):
    half_taps = taps // 2
    shape = (own_rows, own_rows + 2 * reach)
    row = iota(shape, 0)
    column = iota(shape, 1)
    place = jnp.where(
        column < own_rows, column, jnp.where(column < own_rows + reach, column - own_rows - reach, column - reach)
    )
    total = jnp.zeros(shape, F32)
    for level in range(levels):
        dilation = 2**level
        for outer in range(taps):
            detail_row = row - (outer - half_taps) * dilation
            inside = (detail_row + first_row >= 0) & (detail_row + first_row < image_rows)
            for inner in range(taps):
                hit = inside & (place == detail_row + (inner - half_taps) * dilation)
                total = total + jnp.where(hit, taps_of(level, outer) * taps_of(level, inner), 0.0)
    return total


def base_body(levels, taps, starts, strips, strip_ref, step_ref, highpass_ref, model_ref, edge_ref, after_ref, *refs):
    high, low = refs[-2:]
    out_refs = refs[:-2]
    block, own_rows, side_len = model_ref.shape
    reach = edge_ref.shape[1] // 2

    @pl.when(pl.program_id(0) == 0)
    def _():
        band = band_matrix(
            lambda level, tap: highpass_ref[level, tap],
            levels,
            taps,
            own_rows,
            reach,
            strip_ref[0] * own_rows,
            strips * own_rows,
        )
        top = band.astype(BF16)
        high[...] = top
        low[...] = (band - top.astype(F32)).astype(BF16)

    first = pl.program_id(0) * block
    for chan in range(block):
        model = model_ref[chan]
        top = model.astype(BF16)
        rest = (model - top.astype(F32)).astype(BF16)
        edge = edge_ref[chan].astype(F32)
        whole = jnp.concatenate([top.astype(F32), edge], axis=0).astype(BF16)
        gradient = dot_nn(high[...], whole)
        gradient = gradient + dot_nn(low[...], whole)
        gradient = gradient + dot_nn(high[:, :own_rows], rest)
        base = model - step_ref[first + chan] * gradient
        for start, out_ref in zip(starts, out_refs):
            out_ref[chan] = base[start : start + out_ref.shape[1]]


def base_step(strip, strips, step_size, highpass, model_image, edges, starts, sizes, after):
    chans, rows, side_len = model_image.shape
    levels, taps = highpass.shape
    reach = edges.shape[1] // 2
    block = 2 if chans % 2 == 0 else 1
    wide = rows + 2 * reach
    return pl.pallas_call(
        functools.partial(base_body, levels, taps, starts, strips),
        grid=(chans // block,),
        in_specs=[
            SMEM,
            SMEM,
            SMEM,
            pl.BlockSpec((block, rows, side_len), lambda i: (i, 0, 0)),
            pl.BlockSpec((block, 2 * reach, side_len), lambda i: (i, 0, 0)),
            ANY,
        ],
        out_specs=[pl.BlockSpec((block, part, side_len), lambda i: (i, 0, 0)) for part in sizes],
        out_shape=[jax.ShapeDtypeStruct((chans, part, side_len), F32) for part in sizes],
        scratch_shapes=[pltpu.VMEM((rows, wide), BF16), pltpu.VMEM((rows, wide), BF16)],
        compiler_params=kernel_params(60),
        cost_estimate=COST,
        name="base_step",
    )(strip, step_size, highpass, model_image, edges, after)


def second_body(step_ref, half_ref, cosine_ref, sine_ref, base_ref, after_ref, moved_ref, pixels_ref):
    strips, _, chans, rows, width = half_ref.shape
    real = jnp.concatenate([half_ref[s, 0].reshape(chans * rows, width) for s in range(strips)], axis=1)
    imag = jnp.concatenate([half_ref[s, 1].reshape(chans * rows, width) for s in range(strips)], axis=1)
    dirty = dot_nn(real, cosine_ref[...]) - dot_nn(imag, sine_ref[...])
    pieces = []
    for chan in range(chans):
        moved = base_ref[chan] + step_ref[chan] * dirty[chan * rows : (chan + 1) * rows]
        moved_ref[chan] = moved
        pieces.append(moved)
    pixels_ref[...] = jnp.swapaxes(jnp.stack(pieces), 0, 1).astype(BF16)


def second_transform(step_size, half, cosine, sine_table, base, after):
    strips, _, chans, rows, width = half.shape
    side_len = cosine.shape[0]
    if width % 128 or rows % 16 or chans % 16:
        split = (strips, width, side_len)
        dirty = jnp.einsum("scmu,sul->cml", half[:, 0], cosine.reshape(split), preferred_element_type=F32)
        dirty = dirty - jnp.einsum("scmu,sul->cml", half[:, 1], sine_table.reshape(split), preferred_element_type=F32)
        moved = base + step_size[:, None, None] * dirty
        return moved, moved.astype(BF16).transpose(1, 0, 2)
    block = min(256, side_len)
    return pl.pallas_call(
        second_body,
        grid=(side_len // block,),
        in_specs=[
            SMEM,
            pl.BlockSpec(half.shape, lambda i: (0, 0, 0, 0, 0)),
            pl.BlockSpec((side_len, block), lambda i: (0, i)),
            pl.BlockSpec((side_len, block), lambda i: (0, i)),
            pl.BlockSpec((chans, rows, block), lambda i: (0, 0, i)),
            ANY,
        ],
        out_specs=[
            pl.BlockSpec((chans, rows, block), lambda i: (0, 0, i)),
            pl.BlockSpec((rows, chans, block), lambda i: (0, 0, i)),
        ],
        out_shape=[
            jax.ShapeDtypeStruct(base.shape, F32),
            jax.ShapeDtypeStruct((rows, chans, side_len), BF16),
        ],
        compiler_params=kernel_params(60),
        cost_estimate=COST,
        name="second_transform",
    )(step_size, half, cosine, sine_table, base, after)


def stacked(group_refs, first, count):
    return jnp.concatenate([ref[first + i] for i in range(count) for ref in group_refs], axis=0)


def gram_body(groups, before_ref, after_ref, *refs):
    total_ref = refs[groups]

    @pl.when(pl.program_id(0) == 0)
    def _():
        total_ref[...] = before_ref[...]

    total = total_ref[...]
    for first in range(0, refs[0].shape[0], GRAM_ROWS):
        pixels = stacked(refs[:groups], first, GRAM_ROWS)
        total = total + dot_nt(pixels, pixels)
    total_ref[...] = total


def gram_step(pieces, before, after):
    rows, chans, side_len = pieces[0].shape
    block = EDGE_ROWS // 2
    spec = pl.BlockSpec((block, chans, side_len), lambda i: (i, 0, 0))
    return pl.pallas_call(
        functools.partial(gram_body, len(pieces)),
        grid=(rows // block,),
        in_specs=[pl.BlockSpec(before.shape, lambda i: (0, 0)), ANY] + [spec] * len(pieces),
        out_specs=pl.BlockSpec(before.shape, lambda i: (0, 0)),
        out_shape=jax.ShapeDtypeStruct(before.shape, F32),
        compiler_params=kernel_params(16),
        cost_estimate=COST,
        name="gram_step",
    )(before, after, *pieces)


def newton_schulz(gram):
    size = gram.shape[0]
    frob_norm = jnp.sqrt(jnp.sum(gram * gram))
    identity = (iota((size, size), 0) == iota((size, size), 1)).astype(F32)
    current = gram / frob_norm
    middle = 0.5 * (3.0 * identity - current)
    inverse = middle
    for iteration in range(1, NS_ITERS):
        current = dot_nn(current, middle, HIGHEST)
        middle = 0.5 * (3.0 * identity - dot_nn(inverse, current, HIGHEST))
        inverse = dot_nn(middle, inverse, HIGHEST)
    return inverse, frob_norm


def polar_body(starts, sizes, groups, shrink_ref, gram_ref, *refs):
    chunks = len(sizes)
    moved_hbm = refs[:chunks]
    pixels_hbm = refs[chunks : chunks * (groups + 1)]
    out_hbm, moved, pixel_sems, moved_sems, out_sems = refs[chunks * (groups + 1) : chunks * (groups + 1) + 5]
    pixels = refs[chunks * (groups + 1) + 5 :]
    own, all_rows, side_len = moved.shape
    size = pixels[0].shape[2] * groups
    moved_copies = []
    pixel_copies = []
    for chunk in range(chunks):
        part = pl.ds(starts[chunk], sizes[chunk])
        copies = []
        for group in range(groups):
            place = chunk * groups + group
            copies.append(pltpu.make_async_copy(pixels_hbm[place], pixels[chunk].at[group], pixel_sems.at[place]))
        pixel_copies.append(copies)
        moved_copies.append(pltpu.make_async_copy(moved_hbm[chunk], moved.at[:, part], moved_sems.at[chunk]))
        for copy in copies + moved_copies[-1:]:
            copy.start()
    gram = jnp.zeros((size, size), F32)
    for i in range(GRAM_ROWS):
        gram = gram + gram_ref[i * size : (i + 1) * size, i * size : (i + 1) * size]
    inverse, frob_norm = newton_schulz(gram)
    factor = shrink_ref[0] * jnp.sqrt(all_rows * side_len / frob_norm)
    select = (iota((own, size), 0) == iota((own, size), 1)).astype(F32)
    weights = dot_nt(select, inverse, HIGHEST) * factor
    spread = POLAR_ROWS * own
    wide = POLAR_ROWS * size
    repeat = (iota((spread, own), 0) // POLAR_ROWS == iota((spread, own), 1)).astype(BF16)
    weights = dot_nn(repeat, weights.astype(BF16)).astype(BF16)
    repeat = (iota((size, wide), 1) % size == iota((size, wide), 0)).astype(BF16)
    weights = dot_nn(weights, repeat)
    keep = iota((spread, wide), 0) % POLAR_ROWS == iota((spread, wide), 1) // size
    weights = jnp.where(keep, weights, 0.0).astype(BF16)
    out_copies = []
    for chunk in range(chunks):
        for copy in pixel_copies[chunk]:
            copy.wait()
        moved_copies[chunk].wait()
        for step in range(sizes[chunk] // POLAR_ROWS):
            data = stacked([pixels[chunk].at[group] for group in range(groups)], step * POLAR_ROWS, POLAR_ROWS)
            polar = dot_nn(weights, data).reshape(own, POLAR_ROWS, side_len)
            first = starts[chunk] + step * POLAR_ROWS
            moved[:, first : first + POLAR_ROWS] -= polar
        part = pl.ds(starts[chunk], sizes[chunk])
        copy = pltpu.make_async_copy(moved.at[:, part], out_hbm.at[:, part], out_sems.at[chunk])
        copy.start()
        out_copies.append(copy)
    for copy in out_copies:
        copy.wait()


def polar_step(shrinkage, gram, moved, gathered, starts, sizes):
    chunks = len(gathered)
    groups = len(gathered[0])
    chans, _, side_len = moved[0].shape
    shape = (chans, sum(sizes), side_len)
    flat = [piece for pieces in gathered for piece in pieces]
    return pl.pallas_call(
        functools.partial(polar_body, starts, sizes, groups),
        in_specs=[SMEM, pl.BlockSpec(memory_space=pltpu.VMEM)] + [ANY] * (chunks + len(flat)),
        out_specs=ANY,
        out_shape=jax.ShapeDtypeStruct(shape, F32),
        scratch_shapes=[
            pltpu.VMEM(shape, F32),
            pltpu.SemaphoreType.DMA((chunks * groups,)),
            pltpu.SemaphoreType.DMA((chunks,)),
            pltpu.SemaphoreType.DMA((chunks,)),
        ]
        + [pltpu.VMEM((groups,) + pieces[0].shape, BF16) for pieces in gathered],
        compiler_params=kernel_params(40),
        cost_estimate=COST,
        name="polar_step",
    )(shrinkage, gram, *moved, *flat)


def neighbour_rows(model_image, reach):
    ends = lax.axis_size("strip") - 1
    head, tail = lax.optimization_barrier((model_image[:, :reach], model_image[:, model_image.shape[1] - reach :]))
    before = lax.ppermute(tail.astype(BF16), "strip", [(i, i + 1) for i in range(ends)])
    after = lax.ppermute(head.astype(BF16), "strip", [(i + 1, i) for i in range(ends)])
    return jnp.concatenate([before, after], axis=1)


def swap(value, axis, bits):
    count = lax.axis_size(axis)
    return lax.ppermute(value, axis, [(i, i ^ bits) for i in range(count)])


def gather_channels(pixels, after=None):
    devices = lax.axis_size("chan")
    kept = [pixels] + [swap(pixels, "chan", bits) for bits in range(2, devices, 2)]
    if after is not None:
        kept = [pixels] + [gate(piece, after) for piece in kept[1:]]
    if devices == 1:
        return kept
    return kept + [swap(piece, "chan", 1) for piece in kept]


def local(grid, model_image, step_size, highpass, shrinkage):
    chans, own_rows, side_len = model_image.shape
    strips = lax.axis_size("strip")
    size = chans * lax.axis_size("chan")
    starts, sizes = chunk_rows(own_rows)
    chunks = len(sizes)
    strip = lax.axis_index("strip").astype(jnp.int32).reshape(1)

    cosine, sine_table = make_tables(side_len)
    split = np.stack([cosine.reshape(strips, own_rows, side_len), sine_table.reshape(strips, own_rows, side_len)])
    tables = [
        np.ascontiguousarray(split[:, :, start : start + rows]).reshape(2 * strips * rows, side_len)
        for start, rows in zip(starts, sizes)
    ]

    levels, taps = highpass.shape
    reach = (taps - 1) * 2 ** (levels - 1)
    edges = neighbour_rows(model_image, reach)

    halves = {}
    moved = {}
    gathered = {}
    pixels = {}
    state = dict(last=strip, gram=jnp.zeros((GRAM_ROWS * size, GRAM_ROWS * size), F32), bases=None)

    def first(chunk):
        sent, state["last"] = first_transform(tables[chunk], grid, strips, state["last"])
        if chunk == 1:
            sent = gate(sent, edges)
        if chunk == 2:
            gather(0, gram_after=True)
            sent = gate(sent, state["gram"])
        halves[chunk] = lax.all_to_all(sent, "strip", split_axis=0, concat_axis=0, tiled=True)

    def base():
        state["bases"] = base_step(
            strip, strips, step_size, highpass, model_image, edges, starts, sizes, state["last"]
        )
        state["last"] = state["bases"][0]

    def second(chunk):
        moved[chunk], pixels[chunk] = second_transform(
            step_size, halves[chunk], cosine, sine_table, state["bases"][chunk], state["last"]
        )
        state["last"] = pixels[chunk]

    def gather(chunk, gram_after):
        pieces = gather_channels(pixels[chunk], state["last"])
        if chans % 16:
            pieces = [jnp.concatenate(pieces, axis=1)]
        gathered[chunk] = pieces
        if gram_after:
            state["gram"] = gram_step(pieces, state["gram"], state["last"])
            state["last"] = state["gram"]

    first(0)
    if chunks > 1:
        first(1)
    base()
    for chunk in range(chunks):
        second(chunk)
        if chunk + 2 < chunks:
            first(chunk + 2)
        if chunk >= 1 and chunk - 1 not in gathered:
            gather(chunk - 1, gram_after=True)
    gather(chunks - 1, gram_after=True)
    order = range(chunks)
    return polar_step(
        shrinkage, state["gram"], [moved[k] for k in order], [gathered[k] for k in order], starts, sizes
    )


def solution(mesh):
    return jax.shard_map(
        local,
        mesh=mesh,
        in_specs=(
            P(None, "chan", "strip", None),
            P("chan", "strip", None),
            P("chan"),
            P(),
            P("strip"),
        ),
        out_specs=P("chan", "strip", None),
        check_vma=False,
    )
```

```python
import functools

import jax
import jax.numpy as jnp
import ml_dtypes
import numpy as np
from jax import lax
from jax.experimental import pallas as pl
from jax.experimental.pallas import tpu as pltpu
from jax.sharding import PartitionSpec as P

NS_ITERS = 5
EDGE_ROWS = 16
GRAM_ROWS = 4
POLAR_ROWS = 8
HIGHEST = lax.Precision.HIGHEST
F32 = jnp.float32
BF16 = jnp.bfloat16
MIB = 1 << 20

ANY = pl.BlockSpec(memory_space=pl.ANY)
SMEM = pl.BlockSpec(memory_space=pltpu.SMEM)


def kernel_params(mebibytes):
    return pltpu.CompilerParams(vmem_limit_bytes=mebibytes * MIB)


COST = pl.CostEstimate(flops=0, bytes_accessed=1 << 16, transcendentals=0)


def dot_nt(a, b, precision=None):
    return lax.dot_general(
        a, b, (((1,), (1,)), ((), ())), precision=precision, preferred_element_type=F32
    )


def dot_nn(a, b, precision=None):
    return lax.dot_general(
        a, b, (((1,), (0,)), ((), ())), precision=precision, preferred_element_type=F32
    )


def iota(shape, dim):
    return lax.broadcasted_iota(jnp.int32, shape, dim)


def make_tables(side_len):
    indices = np.arange(side_len, dtype=np.int64)
    phases = (np.outer(indices, indices) % side_len).astype(np.float32) * np.float32(
        2.0 * 3.141592653589793 / side_len
    )
    unit_scale = np.float32(float(side_len) ** (-0.5))
    cosine = (np.cos(phases) * unit_scale).astype(ml_dtypes.bfloat16)
    sine_table = (np.sin(phases) * unit_scale).astype(ml_dtypes.bfloat16)
    return cosine, sine_table


def chunk_rows(own_rows):
    quarter = own_rows // 4
    sizes = [quarter, own_rows - 2 * quarter - EDGE_ROWS, quarter, EDGE_ROWS]
    sizes = [size for size in sizes if size > 0]
    return [sum(sizes[:place]) for place in range(len(sizes))], sizes


def gate_body(value_ref, after_ref, out_ref):
    pass


def gate(value, after):
    return pl.pallas_call(
        gate_body,
        in_specs=[ANY, ANY],
        out_specs=ANY,
        out_shape=jax.ShapeDtypeStruct(value.shape, value.dtype),
        input_output_aliases={0: 0},
        cost_estimate=COST,
        name="gate",
    )(value, after)


def first_body(table_ref, grid_ref, after_ref, out_ref, token_ref):
    token_ref[...] = jnp.zeros(token_ref.shape, F32)
    strips, _, chans, rows, width = out_ref.shape
    side_len = table_ref.shape[-1]
    table = table_ref[...]
    middle = strips * rows
    turned = jnp.concatenate([-table[middle:], table[:middle]], axis=0)
    total = dot_nt(table, grid_ref[0].reshape(chans * width, side_len))
    total = total + dot_nt(turned, grid_ref[1].reshape(chans * width, side_len))
    total = total.astype(BF16)
    for part in range(2):
        for strip in range(strips):
            first = (part * strips + strip) * rows
            for chan in range(chans):
                out_ref[strip, part, chan] = total[first : first + rows, chan * width : (chan + 1) * width]


def first_transform(table, grid, strips, after):
    _, chans, width, side_len = grid.shape
    rows = table.shape[0] // (2 * strips)
    shape = (strips, 2, chans, rows, width)
    if width % 128 or rows % 16:
        middle = strips * rows
        turned = jnp.concatenate([-table[middle:], table[:middle]], axis=0)
        total = jnp.einsum("mv,cuv->mcu", table, grid[0], preferred_element_type=F32)
        total = total + jnp.einsum("mv,cuv->mcu", turned, grid[1], preferred_element_type=F32)
        total = total.astype(BF16).reshape(2, strips, rows, chans, width)
        return total.transpose(1, 0, 3, 2, 4), jnp.zeros((8, 128), F32)
    block = 4 if chans % 4 == 0 else 1
    return pl.pallas_call(
        first_body,
        grid=(chans // block,),
        in_specs=[
            pl.BlockSpec(table.shape, lambda i: (0, 0)),
            pl.BlockSpec((2, block, width, side_len), lambda i: (0, i, 0, 0)),
            ANY,
        ],
        out_specs=[
            pl.BlockSpec((strips, 2, block, rows, width), lambda i: (0, 0, i, 0, 0)),
            pl.BlockSpec((8, 128), lambda i: (0, 0)),
        ],
        out_shape=[jax.ShapeDtypeStruct(shape, BF16), jax.ShapeDtypeStruct((8, 128), F32)],
        compiler_params=kernel_params(60),
        cost_estimate=COST,
        name="first_transform",
    )(table, grid, after)


def band_matrix(taps_of, levels, taps, own_rows, reach, first_row, image_rows):
    half_taps = taps // 2
    shape = (own_rows, own_rows + 2 * reach)
    row = iota(shape, 0)
    column = iota(shape, 1)
    place = jnp.where(
        column < own_rows, column, jnp.where(column < own_rows + reach, column - own_rows - reach, column - reach)
    )
    total = jnp.zeros(shape, F32)
    for level in range(levels):
        dilation = 2**level
        for outer in range(taps):
            detail_row = row - (outer - half_taps) * dilation
            inside = (detail_row + first_row >= 0) & (detail_row + first_row < image_rows)
            for inner in range(taps):
                hit = inside & (place == detail_row + (inner - half_taps) * dilation)
                total = total + jnp.where(hit, taps_of(level, outer) * taps_of(level, inner), 0.0)
    return total


def base_body(levels, taps, starts, strips, strip_ref, step_ref, highpass_ref, model_ref, edge_ref, after_ref, *refs):
    high, low = refs[-2:]
    out_refs = refs[:-2]
    block, own_rows, side_len = model_ref.shape
    reach = edge_ref.shape[1] // 2

    @pl.when(pl.program_id(0) == 0)
    def _():
        band = band_matrix(
            lambda level, tap: highpass_ref[level, tap],
            levels,
            taps,
            own_rows,
            reach,
            strip_ref[0] * own_rows,
            strips * own_rows,
        )
        top = band.astype(BF16)
        high[...] = top
        low[...] = (band - top.astype(F32)).astype(BF16)

    first = pl.program_id(0) * block
    for chan in range(block):
        model = model_ref[chan]
        top = model.astype(BF16)
        rest = (model - top.astype(F32)).astype(BF16)
        edge = edge_ref[chan].astype(F32)
        whole = jnp.concatenate([top.astype(F32), edge], axis=0).astype(BF16)
        gradient = dot_nn(high[...], whole)
        gradient = gradient + dot_nn(low[...], whole)
        gradient = gradient + dot_nn(high[:, :own_rows], rest)
        base = model - step_ref[first + chan] * gradient
        for start, out_ref in zip(starts, out_refs):
            out_ref[chan] = base[start : start + out_ref.shape[1]]


def base_step(strip, strips, step_size, highpass, model_image, edges, starts, sizes, after):
    chans, rows, side_len = model_image.shape
    levels, taps = highpass.shape
    reach = edges.shape[1] // 2
    block = 2 if chans % 2 == 0 else 1
    wide = rows + 2 * reach
    return pl.pallas_call(
        functools.partial(base_body, levels, taps, starts, strips),
        grid=(chans // block,),
        in_specs=[
            SMEM,
            SMEM,
            SMEM,
            pl.BlockSpec((block, rows, side_len), lambda i: (i, 0, 0)),
            pl.BlockSpec((block, 2 * reach, side_len), lambda i: (i, 0, 0)),
            ANY,
        ],
        out_specs=[pl.BlockSpec((block, part, side_len), lambda i: (i, 0, 0)) for part in sizes],
        out_shape=[jax.ShapeDtypeStruct((chans, part, side_len), F32) for part in sizes],
        scratch_shapes=[pltpu.VMEM((rows, wide), BF16), pltpu.VMEM((rows, wide), BF16)],
        compiler_params=kernel_params(60),
        cost_estimate=COST,
        name="base_step",
    )(strip, step_size, highpass, model_image, edges, after)


def second_body(step_ref, half_ref, cosine_ref, sine_ref, base_ref, after_ref, moved_ref, pixels_ref):
    strips, _, chans, rows, width = half_ref.shape
    real = jnp.concatenate([half_ref[s, 0].reshape(chans * rows, width) for s in range(strips)], axis=1)
    imag = jnp.concatenate([half_ref[s, 1].reshape(chans * rows, width) for s in range(strips)], axis=1)
    dirty = dot_nn(real, cosine_ref[...]) - dot_nn(imag, sine_ref[...])
    pieces = []
    for chan in range(chans):
        moved = base_ref[chan] + step_ref[chan] * dirty[chan * rows : (chan + 1) * rows]
        moved_ref[chan] = moved
        pieces.append(moved)
    pixels_ref[...] = jnp.swapaxes(jnp.stack(pieces), 0, 1).astype(BF16)


def second_transform(step_size, half, cosine, sine_table, base, after):
    strips, _, chans, rows, width = half.shape
    side_len = cosine.shape[0]
    if width % 128 or rows % 16 or chans % 16:
        split = (strips, width, side_len)
        dirty = jnp.einsum("scmu,sul->cml", half[:, 0], cosine.reshape(split), preferred_element_type=F32)
        dirty = dirty - jnp.einsum("scmu,sul->cml", half[:, 1], sine_table.reshape(split), preferred_element_type=F32)
        moved = base + step_size[:, None, None] * dirty
        return moved, moved.astype(BF16).transpose(1, 0, 2)
    block = min(256, side_len)
    return pl.pallas_call(
        second_body,
        grid=(side_len // block,),
        in_specs=[
            SMEM,
            pl.BlockSpec(half.shape, lambda i: (0, 0, 0, 0, 0)),
            pl.BlockSpec((side_len, block), lambda i: (0, i)),
            pl.BlockSpec((side_len, block), lambda i: (0, i)),
            pl.BlockSpec((chans, rows, block), lambda i: (0, 0, i)),
            ANY,
        ],
        out_specs=[
            pl.BlockSpec((chans, rows, block), lambda i: (0, 0, i)),
            pl.BlockSpec((rows, chans, block), lambda i: (0, 0, i)),
        ],
        out_shape=[
            jax.ShapeDtypeStruct(base.shape, F32),
            jax.ShapeDtypeStruct((rows, chans, side_len), BF16),
        ],
        compiler_params=kernel_params(60),
        cost_estimate=COST,
        name="second_transform",
    )(step_size, half, cosine, sine_table, base, after)


def stacked(group_refs, first, count):
    return jnp.concatenate([ref[first + i] for i in range(count) for ref in group_refs], axis=0)


def gram_body(groups, before_ref, after_ref, *refs):
    total_ref = refs[groups]

    @pl.when(pl.program_id(0) == 0)
    def _():
        total_ref[...] = before_ref[...]

    total = total_ref[...]
    for first in range(0, refs[0].shape[0], GRAM_ROWS):
        pixels = stacked(refs[:groups], first, GRAM_ROWS)
        total = total + dot_nt(pixels, pixels)
    total_ref[...] = total


def gram_step(pieces, before, after):
    rows, chans, side_len = pieces[0].shape
    block = EDGE_ROWS // 2
    spec = pl.BlockSpec((block, chans, side_len), lambda i: (i, 0, 0))
    return pl.pallas_call(
        functools.partial(gram_body, len(pieces)),
        grid=(rows // block,),
        in_specs=[pl.BlockSpec(before.shape, lambda i: (0, 0)), ANY] + [spec] * len(pieces),
        out_specs=pl.BlockSpec(before.shape, lambda i: (0, 0)),
        out_shape=jax.ShapeDtypeStruct(before.shape, F32),
        compiler_params=kernel_params(60),
        cost_estimate=COST,
        name="gram_step",
    )(before, after, *pieces)


def newton_schulz(gram):
    size = gram.shape[0]
    frob_norm = jnp.sqrt(jnp.sum(gram * gram))
    identity = (iota((size, size), 0) == iota((size, size), 1)).astype(F32)
    current = gram / frob_norm
    middle = 0.5 * (3.0 * identity - current)
    inverse = middle
    for iteration in range(1, NS_ITERS):
        current = dot_nn(current, middle, HIGHEST)
        middle = 0.5 * (3.0 * identity - dot_nn(inverse, current, HIGHEST))
        inverse = dot_nn(middle, inverse, HIGHEST)
    return inverse, frob_norm


def polar_body(starts, sizes, groups, shrink_ref, gram_ref, *refs):
    chunks = len(sizes)
    moved_hbm = refs[:chunks]
    pixels_hbm = refs[chunks : chunks * (groups + 1)]
    out_hbm, moved, pixel_sems, moved_sems, out_sems = refs[chunks * (groups + 1) : chunks * (groups + 1) + 5]
    pixels = refs[chunks * (groups + 1) + 5 :]
    own, all_rows, side_len = moved.shape
    size = pixels[0].shape[2] * groups

    blocks = [
        (chunk, row) for chunk in [chunks - 1] + list(range(chunks - 1)) for row in range(0, sizes[chunk], EDGE_ROWS)
    ]
    pixel_copies = []
    moved_copies = []
    for place, (chunk, row) in enumerate(blocks):
        part = pl.ds(row, EDGE_ROWS)
        into = pl.ds(starts[chunk] + row, EDGE_ROWS)
        copies = [
            pltpu.make_async_copy(
                pixels_hbm[chunk * groups + group].at[part], pixels[chunk].at[group, part], pixel_sems.at[place, group]
            )
            for group in range(groups)
        ]
        pixel_copies.append(copies)
        moved_copies.append(
            pltpu.make_async_copy(moved_hbm[chunk].at[:, part], moved.at[:, into], moved_sems.at[place])
        )
        for copy in copies + moved_copies[-1:]:
            copy.start()

    last_blocks = sizes[-1] // EDGE_ROWS
    for copies in pixel_copies[:last_blocks]:
        for copy in copies:
            copy.wait()
    total = gram_ref[...]
    for first in range(0, sizes[-1], GRAM_ROWS):
        data = stacked([pixels[-1].at[group] for group in range(groups)], first, GRAM_ROWS)
        total = total + dot_nt(data, data)
    gram = jnp.zeros((size, size), F32)
    for i in range(GRAM_ROWS):
        gram = gram + total[i * size : (i + 1) * size, i * size : (i + 1) * size]
    inverse, frob_norm = newton_schulz(gram)
    factor = shrink_ref[0] * jnp.sqrt(all_rows * side_len / frob_norm)
    select = (iota((own, size), 0) == iota((own, size), 1)).astype(F32)
    weights = dot_nt(select, inverse, HIGHEST) * factor
    spread = POLAR_ROWS * own
    wide = POLAR_ROWS * size
    repeat = (iota((spread, own), 0) // POLAR_ROWS == iota((spread, own), 1)).astype(BF16)
    weights = dot_nn(repeat, weights.astype(BF16)).astype(BF16)
    repeat = (iota((size, wide), 1) % size == iota((size, wide), 0)).astype(BF16)
    weights = dot_nn(weights, repeat)
    keep = iota((spread, wide), 0) % POLAR_ROWS == iota((spread, wide), 1) // size
    weights = jnp.where(keep, weights, 0.0).astype(BF16)

    out_copies = []
    for place, (chunk, row) in enumerate(blocks):
        if place >= last_blocks:
            for copy in pixel_copies[place]:
                copy.wait()
        moved_copies[place].wait()
        for first in range(row, row + EDGE_ROWS, POLAR_ROWS):
            data = stacked([pixels[chunk].at[group] for group in range(groups)], first, POLAR_ROWS)
            polar = dot_nn(weights, data).reshape(own, POLAR_ROWS, side_len)
            into = starts[chunk] + first
            moved[:, into : into + POLAR_ROWS] -= polar
        part = pl.ds(starts[chunk] + row, EDGE_ROWS)
        copy = pltpu.make_async_copy(moved.at[:, part], out_hbm.at[:, part], out_sems.at[place])
        copy.start()
        out_copies.append(copy)
    for copy in out_copies:
        copy.wait()


def polar_step(shrinkage, gram, moved, gathered, starts, sizes):
    chunks = len(gathered)
    groups = len(gathered[0])
    chans, _, side_len = moved[0].shape
    shape = (chans, sum(sizes), side_len)
    blocks = sum(sizes) // EDGE_ROWS
    flat = [piece for pieces in gathered for piece in pieces]
    return pl.pallas_call(
        functools.partial(polar_body, starts, sizes, groups),
        in_specs=[SMEM, pl.BlockSpec(memory_space=pltpu.VMEM)] + [ANY] * (chunks + len(flat)),
        out_specs=ANY,
        out_shape=jax.ShapeDtypeStruct(shape, F32),
        scratch_shapes=[
            pltpu.VMEM(shape, F32),
            pltpu.SemaphoreType.DMA((blocks, groups)),
            pltpu.SemaphoreType.DMA((blocks,)),
            pltpu.SemaphoreType.DMA((blocks,)),
        ]
        + [pltpu.VMEM((groups,) + pieces[0].shape, BF16) for pieces in gathered],
        compiler_params=kernel_params(60),
        cost_estimate=COST,
        name="polar_step",
    )(shrinkage, gram, *moved, *flat)


def neighbour_rows(model_image, reach):
    ends = lax.axis_size("strip") - 1
    head, tail = lax.optimization_barrier((model_image[:, :reach], model_image[:, model_image.shape[1] - reach :]))
    before = lax.ppermute(tail.astype(BF16), "strip", [(i, i + 1) for i in range(ends)])
    after = lax.ppermute(head.astype(BF16), "strip", [(i + 1, i) for i in range(ends)])
    return jnp.concatenate([before, after], axis=1)


def swap(value, axis, bits):
    count = lax.axis_size(axis)
    return lax.ppermute(value, axis, [(i, i ^ bits) for i in range(count)])


def gather_channels(pixels, after=None):
    devices = lax.axis_size("chan")
    kept = [pixels] + [swap(pixels, "chan", bits) for bits in range(2, devices, 2)]
    if after is not None:
        kept = [pixels] + [gate(piece, after) for piece in kept[1:]]
    if devices == 1:
        return kept
    return kept + [swap(piece, "chan", 1) for piece in kept]


def local(grid, model_image, step_size, highpass, shrinkage):
    chans, own_rows, side_len = model_image.shape
    strips = lax.axis_size("strip")
    size = chans * lax.axis_size("chan")
    starts, sizes = chunk_rows(own_rows)
    chunks = len(sizes)
    strip = lax.axis_index("strip").astype(jnp.int32).reshape(1)

    cosine, sine_table = make_tables(side_len)
    split = np.stack([cosine.reshape(strips, own_rows, side_len), sine_table.reshape(strips, own_rows, side_len)])
    tables = [
        np.ascontiguousarray(split[:, :, start : start + rows]).reshape(2 * strips * rows, side_len)
        for start, rows in zip(starts, sizes)
    ]

    levels, taps = highpass.shape
    reach = (taps - 1) * 2 ** (levels - 1)
    edges = neighbour_rows(model_image, reach)

    halves = {}
    moved = {}
    gathered = {}
    pixels = {}
    done = set()
    state = dict(last=strip, gram=jnp.zeros((GRAM_ROWS * size, GRAM_ROWS * size), F32), bases=None)

    def first(chunk):
        sent, state["last"] = first_transform(tables[chunk], grid, strips, state["last"])
        if chunk == 1:
            sent = gate(sent, edges)
        if chunk == 2:
            gather(0)
            gram(0)
            done.add(0)
            sent = gate(sent, state["gram"])
        halves[chunk] = lax.all_to_all(sent, "strip", split_axis=0, concat_axis=0, tiled=True)

    def base():
        state["bases"] = base_step(
            strip, strips, step_size, highpass, model_image, edges, starts, sizes, state["last"]
        )
        state["last"] = state["bases"][0]

    def second(chunk):
        moved[chunk], pixels[chunk] = second_transform(
            step_size, halves[chunk], cosine, sine_table, state["bases"][chunk], state["last"]
        )
        state["last"] = pixels[chunk]

    def gather(chunk):
        pieces = gather_channels(pixels[chunk], state["last"])
        if chans % 16:
            pieces = [jnp.concatenate(pieces, axis=1)]
        gathered[chunk] = pieces

    def gram(chunk):
        state["gram"] = gram_step(gathered[chunk], state["gram"], state["last"])
        state["last"] = state["gram"]

    first(0)
    if chunks > 1:
        first(1)
    base()
    for chunk in range(chunks):
        second(chunk)
        if chunk + 2 < chunks:
            first(chunk + 2)
        if chunk == 1:
            gather(1)
        if chunk >= 1 and chunk - 1 not in done:
            if chunk - 1 not in gathered:
                gather(chunk - 1)
            gram(chunk - 1)
    if chunks - 1 not in gathered:
        gather(chunks - 1)
    order = range(chunks)
    return polar_step(
        shrinkage, state["gram"], [moved[k] for k in order], [gathered[k] for k in order], starts, sizes
    )


def solution(mesh):
    return jax.shard_map(
        local,
        mesh=mesh,
        in_specs=(
            P(None, "chan", "strip", None),
            P("chan", "strip", None),
            P("chan"),
            P(),
            P("strip"),
        ),
        out_specs=P("chan", "strip", None),
        check_vma=False,
    )
```

```python
import functools

import jax
import jax.numpy as jnp
import ml_dtypes
import numpy as np
from jax import lax
from jax.experimental import pallas as pl
from jax.experimental.pallas import tpu as pltpu
from jax.sharding import PartitionSpec as P

NS_ITERS = 5
EDGE_ROWS = 16
GRAM_ROWS = 4
POLAR_ROWS = 8
HIGHEST = lax.Precision.HIGHEST
F32 = jnp.float32
BF16 = jnp.bfloat16
MIB = 1 << 20

ANY = pl.BlockSpec(memory_space=pl.ANY)
SMEM = pl.BlockSpec(memory_space=pltpu.SMEM)


def kernel_params(mebibytes):
    return pltpu.CompilerParams(vmem_limit_bytes=mebibytes * MIB)


COST = pl.CostEstimate(flops=0, bytes_accessed=1 << 16, transcendentals=0)


def dot_nt(a, b, precision=None):
    return lax.dot_general(
        a, b, (((1,), (1,)), ((), ())), precision=precision, preferred_element_type=F32
    )


def dot_nn(a, b, precision=None):
    return lax.dot_general(
        a, b, (((1,), (0,)), ((), ())), precision=precision, preferred_element_type=F32
    )


def iota(shape, dim):
    return lax.broadcasted_iota(jnp.int32, shape, dim)


def make_tables(side_len):
    indices = np.arange(side_len, dtype=np.int64)
    phases = (np.outer(indices, indices) % side_len).astype(np.float32) * np.float32(
        2.0 * 3.141592653589793 / side_len
    )
    unit_scale = np.float32(float(side_len) ** (-0.5))
    cosine = (np.cos(phases) * unit_scale).astype(ml_dtypes.bfloat16)
    sine_table = (np.sin(phases) * unit_scale).astype(ml_dtypes.bfloat16)
    return cosine, sine_table


def chunk_rows(own_rows):
    sizes = [EDGE_ROWS, own_rows // 2, own_rows // 2 - 2 * EDGE_ROWS, EDGE_ROWS]
    sizes = [size for size in sizes if size > 0]
    return [sum(sizes[:place]) for place in range(len(sizes))], sizes


def gate_body(value_ref, after_ref, out_ref):
    pass


def gate(value, after):
    return pl.pallas_call(
        gate_body,
        in_specs=[ANY, ANY],
        out_specs=ANY,
        out_shape=jax.ShapeDtypeStruct(value.shape, value.dtype),
        input_output_aliases={0: 0},
        cost_estimate=COST,
        name="gate",
    )(value, after)


def first_body(table_ref, grid_ref, after_ref, out_ref, token_ref):
    token_ref[...] = jnp.zeros(token_ref.shape, F32)
    strips, _, chans, rows, width = out_ref.shape
    side_len = table_ref.shape[-1]
    table = table_ref[...]
    middle = strips * rows
    turned = jnp.concatenate([-table[middle:], table[:middle]], axis=0)
    total = dot_nt(table, grid_ref[0].reshape(chans * width, side_len))
    total = total + dot_nt(turned, grid_ref[1].reshape(chans * width, side_len))
    total = total.astype(BF16)
    for part in range(2):
        for strip in range(strips):
            first = (part * strips + strip) * rows
            for chan in range(chans):
                out_ref[strip, part, chan] = total[first : first + rows, chan * width : (chan + 1) * width]


def first_transform(table, grid, strips, after):
    _, chans, width, side_len = grid.shape
    rows = table.shape[0] // (2 * strips)
    shape = (strips, 2, chans, rows, width)
    if width % 128 or rows % 16:
        middle = strips * rows
        turned = jnp.concatenate([-table[middle:], table[:middle]], axis=0)
        total = jnp.einsum("mv,cuv->mcu", table, grid[0], preferred_element_type=F32)
        total = total + jnp.einsum("mv,cuv->mcu", turned, grid[1], preferred_element_type=F32)
        total = total.astype(BF16).reshape(2, strips, rows, chans, width)
        return total.transpose(1, 0, 3, 2, 4), jnp.zeros((8, 128), F32)
    block = 4 if chans % 4 == 0 else 1
    return pl.pallas_call(
        first_body,
        grid=(chans // block,),
        in_specs=[
            pl.BlockSpec(table.shape, lambda i: (0, 0)),
            pl.BlockSpec((2, block, width, side_len), lambda i: (0, i, 0, 0)),
            ANY,
        ],
        out_specs=[
            pl.BlockSpec((strips, 2, block, rows, width), lambda i: (0, 0, i, 0, 0)),
            pl.BlockSpec((8, 128), lambda i: (0, 0)),
        ],
        out_shape=[jax.ShapeDtypeStruct(shape, BF16), jax.ShapeDtypeStruct((8, 128), F32)],
        compiler_params=kernel_params(60),
        cost_estimate=COST,
        name="first_transform",
    )(table, grid, after)


def pieces_body(strips, strip_ref, table_ref, grid_ref, after_ref, *refs):
    out_refs = refs[:strips]
    refs[strips][...] = jnp.zeros(refs[strips].shape, F32)
    _, chans, rows, width = out_refs[0].shape
    side_len = table_ref.shape[-1]
    cosine = jnp.concatenate([table_ref[0, strip_ref[0] ^ k] for k in range(strips)], axis=0)
    sine_table = jnp.concatenate([table_ref[1, strip_ref[0] ^ k] for k in range(strips)], axis=0)
    total = dot_nt(jnp.concatenate([cosine, sine_table], axis=0), grid_ref[0].reshape(chans * width, side_len))
    total = total + dot_nt(
        jnp.concatenate([-sine_table, cosine], axis=0), grid_ref[1].reshape(chans * width, side_len)
    )
    total = total.astype(BF16)
    for part in range(2):
        for k in range(strips):
            first = (part * strips + k) * rows
            for chan in range(chans):
                out_refs[k][part, chan] = total[first : first + rows, chan * width : (chan + 1) * width]


def first_pieces(strip, table, grid, strips, after):
    _, chans, width, side_len = grid.shape
    rows = table.shape[0] // (2 * strips)
    table = table.reshape(2, strips, rows, side_len)
    if width % 128 or rows % 16:
        order = strip[0] ^ jnp.arange(strips, dtype=jnp.int32)
        cosine, sine_table = (jnp.take(table[part], order, axis=0) for part in range(2))

        def product(table, part):
            return jnp.einsum("kmv,cuv->kcmu", table, part, preferred_element_type=F32)

        real = product(cosine, grid[0]) - product(sine_table, grid[1])
        imag = product(sine_table, grid[0]) + product(cosine, grid[1])
        both = jnp.stack([real, imag], axis=1).astype(BF16)
        return [both[k] for k in range(strips)], jnp.zeros((8, 128), F32)
    block = 4 if chans % 4 == 0 else 1
    results = pl.pallas_call(
        functools.partial(pieces_body, strips),
        grid=(chans // block,),
        in_specs=[
            SMEM,
            pl.BlockSpec(table.shape, lambda i: (0, 0, 0, 0)),
            pl.BlockSpec((2, block, width, side_len), lambda i: (0, i, 0, 0)),
            ANY,
        ],
        out_specs=[pl.BlockSpec((2, block, rows, width), lambda i: (0, i, 0, 0))] * strips
        + [pl.BlockSpec((8, 128), lambda i: (0, 0))],
        out_shape=[jax.ShapeDtypeStruct((2, chans, rows, width), BF16)] * strips
        + [jax.ShapeDtypeStruct((8, 128), F32)],
        compiler_params=kernel_params(60),
        cost_estimate=COST,
        name="first_pieces",
    )(strip, table, grid, after)
    return results[:strips], results[strips]


def band_matrix(taps_of, levels, taps, own_rows, reach, first_row, image_rows):
    half_taps = taps // 2
    shape = (own_rows, own_rows + 2 * reach)
    row = iota(shape, 0)
    column = iota(shape, 1)
    place = jnp.where(
        column < own_rows, column, jnp.where(column < own_rows + reach, column - own_rows - reach, column - reach)
    )
    total = jnp.zeros(shape, F32)
    for level in range(levels):
        dilation = 2**level
        for outer in range(taps):
            detail_row = row - (outer - half_taps) * dilation
            inside = (detail_row + first_row >= 0) & (detail_row + first_row < image_rows)
            for inner in range(taps):
                hit = inside & (place == detail_row + (inner - half_taps) * dilation)
                total = total + jnp.where(hit, taps_of(level, outer) * taps_of(level, inner), 0.0)
    return total


def base_body(levels, taps, starts, strips, strip_ref, step_ref, highpass_ref, model_ref, edge_ref, after_ref, *refs):
    high, low = refs[-2:]
    out_refs = refs[:-2]
    block, own_rows, side_len = model_ref.shape
    reach = edge_ref.shape[1] // 2

    @pl.when(pl.program_id(0) == 0)
    def _():
        band = band_matrix(
            lambda level, tap: highpass_ref[level, tap],
            levels,
            taps,
            own_rows,
            reach,
            strip_ref[0] * own_rows,
            strips * own_rows,
        )
        top = band.astype(BF16)
        high[...] = top
        low[...] = (band - top.astype(F32)).astype(BF16)

    first = pl.program_id(0) * block
    for chan in range(block):
        model = model_ref[chan]
        top = model.astype(BF16)
        rest = (model - top.astype(F32)).astype(BF16)
        edge = edge_ref[chan].astype(F32)
        whole = jnp.concatenate([top.astype(F32), edge], axis=0).astype(BF16)
        gradient = dot_nn(high[...], whole)
        gradient = gradient + dot_nn(low[...], whole)
        gradient = gradient + dot_nn(high[:, :own_rows], rest)
        base = model - step_ref[first + chan] * gradient
        for start, out_ref in zip(starts, out_refs):
            out_ref[chan] = base[start : start + out_ref.shape[1]]


def base_step(strip, strips, step_size, highpass, model_image, edges, starts, sizes, after):
    chans, rows, side_len = model_image.shape
    levels, taps = highpass.shape
    reach = edges.shape[1] // 2
    block = 2 if chans % 2 == 0 else 1
    wide = rows + 2 * reach
    return pl.pallas_call(
        functools.partial(base_body, levels, taps, starts, strips),
        grid=(chans // block,),
        in_specs=[
            SMEM,
            SMEM,
            SMEM,
            pl.BlockSpec((block, rows, side_len), lambda i: (i, 0, 0)),
            pl.BlockSpec((block, 2 * reach, side_len), lambda i: (i, 0, 0)),
            ANY,
        ],
        out_specs=[pl.BlockSpec((block, part, side_len), lambda i: (i, 0, 0)) for part in sizes],
        out_shape=[jax.ShapeDtypeStruct((chans, part, side_len), F32) for part in sizes],
        scratch_shapes=[pltpu.VMEM((rows, wide), BF16), pltpu.VMEM((rows, wide), BF16)],
        compiler_params=kernel_params(60),
        cost_estimate=COST,
        name="base_step",
    )(strip, step_size, highpass, model_image, edges, after)


def second_body(step_ref, half_ref, cosine_ref, sine_ref, base_ref, after_ref, moved_ref, pixels_ref):
    strips, _, chans, rows, width = half_ref.shape
    real = jnp.concatenate([half_ref[s, 0].reshape(chans * rows, width) for s in range(strips)], axis=1)
    imag = jnp.concatenate([half_ref[s, 1].reshape(chans * rows, width) for s in range(strips)], axis=1)
    dirty = dot_nn(real, cosine_ref[...]) - dot_nn(imag, sine_ref[...])
    pieces = []
    for chan in range(chans):
        moved = base_ref[chan] + step_ref[chan] * dirty[chan * rows : (chan + 1) * rows]
        moved_ref[chan] = moved
        pieces.append(moved)
    pixels_ref[...] = jnp.swapaxes(jnp.stack(pieces), 0, 1).astype(BF16)


def second_transform(step_size, half, cosine, sine_table, base, after):
    strips, _, chans, rows, width = half.shape
    side_len = cosine.shape[0]
    if width % 128 or rows % 16 or chans % 16:
        split = (strips, width, side_len)
        dirty = jnp.einsum("scmu,sul->cml", half[:, 0], cosine.reshape(split), preferred_element_type=F32)
        dirty = dirty - jnp.einsum("scmu,sul->cml", half[:, 1], sine_table.reshape(split), preferred_element_type=F32)
        moved = base + step_size[:, None, None] * dirty
        return moved, moved.astype(BF16).transpose(1, 0, 2)
    block = min(256, side_len)
    return pl.pallas_call(
        second_body,
        grid=(side_len // block,),
        in_specs=[
            SMEM,
            pl.BlockSpec(half.shape, lambda i: (0, 0, 0, 0, 0)),
            pl.BlockSpec((side_len, block), lambda i: (0, i)),
            pl.BlockSpec((side_len, block), lambda i: (0, i)),
            pl.BlockSpec((chans, rows, block), lambda i: (0, 0, i)),
            ANY,
        ],
        out_specs=[
            pl.BlockSpec((chans, rows, block), lambda i: (0, 0, i)),
            pl.BlockSpec((rows, chans, block), lambda i: (0, 0, i)),
        ],
        out_shape=[
            jax.ShapeDtypeStruct(base.shape, F32),
            jax.ShapeDtypeStruct((rows, chans, side_len), BF16),
        ],
        compiler_params=kernel_params(60),
        cost_estimate=COST,
        name="second_transform",
    )(step_size, half, cosine, sine_table, base, after)


def second_pieces_body(strips, strip_ref, step_ref, cosine_ref, sine_ref, base_ref, after_ref, *refs):
    halves = refs[:strips]
    moved_ref, pixels_ref = refs[strips:]
    _, chans, rows, width = halves[0].shape
    real = jnp.concatenate([half[0].reshape(chans * rows, width) for half in halves], axis=1)
    imag = jnp.concatenate([half[1].reshape(chans * rows, width) for half in halves], axis=1)

    def ordered(table_ref):
        parts = [table_ref[pl.ds(pl.multiple_of((strip_ref[0] ^ k) * width, width), width), :] for k in range(strips)]
        return jnp.concatenate(parts, axis=0)

    dirty = dot_nn(real, ordered(cosine_ref)) - dot_nn(imag, ordered(sine_ref))
    pieces = []
    for chan in range(chans):
        moved = base_ref[chan] + step_ref[chan] * dirty[chan * rows : (chan + 1) * rows]
        moved_ref[chan] = moved
        pieces.append(moved)
    pixels_ref[...] = jnp.swapaxes(jnp.stack(pieces), 0, 1).astype(BF16)


def second_pieces(strip, step_size, halves, cosine, sine_table, base, after):
    strips = len(halves)
    _, chans, rows, width = halves[0].shape
    side_len = cosine.shape[0]
    if width % 128 or rows % 16 or chans % 16:
        order = strip[0] ^ jnp.arange(strips, dtype=jnp.int32)
        both = jnp.stack(halves)

        def product(part, table):
            parts = jnp.take(jnp.asarray(table).reshape(strips, width, side_len), order, axis=0)
            return jnp.einsum("kcmu,kul->cml", part, parts, preferred_element_type=F32)

        moved = base + step_size[:, None, None] * (product(both[:, 0], cosine) - product(both[:, 1], sine_table))
        return moved, moved.astype(BF16).transpose(1, 0, 2)
    block = min(256, side_len)
    half_spec = pl.BlockSpec(halves[0].shape, lambda i: (0, 0, 0, 0))
    return pl.pallas_call(
        functools.partial(second_pieces_body, strips),
        grid=(side_len // block,),
        in_specs=[
            SMEM,
            SMEM,
            pl.BlockSpec((side_len, block), lambda i: (0, i)),
            pl.BlockSpec((side_len, block), lambda i: (0, i)),
            pl.BlockSpec((chans, rows, block), lambda i: (0, 0, i)),
            ANY,
        ]
        + [half_spec] * strips,
        out_specs=[
            pl.BlockSpec((chans, rows, block), lambda i: (0, 0, i)),
            pl.BlockSpec((rows, chans, block), lambda i: (0, 0, i)),
        ],
        out_shape=[
            jax.ShapeDtypeStruct(base.shape, F32),
            jax.ShapeDtypeStruct((rows, chans, side_len), BF16),
        ],
        compiler_params=kernel_params(60),
        cost_estimate=COST,
        name="second_pieces",
    )(strip, step_size, cosine, sine_table, base, after, *halves)


def stacked(group_refs, first, count):
    return jnp.concatenate([ref[first + i] for i in range(count) for ref in group_refs], axis=0)


def gram_body(groups, before_ref, after_ref, *refs):
    total_ref = refs[groups]

    @pl.when(pl.program_id(0) == 0)
    def _():
        total_ref[...] = before_ref[...]

    total = total_ref[...]
    for first in range(0, refs[0].shape[0], GRAM_ROWS):
        pixels = stacked(refs[:groups], first, GRAM_ROWS)
        total = total + dot_nt(pixels, pixels)
    total_ref[...] = total


def gram_step(pieces, before, after):
    rows, chans, side_len = pieces[0].shape
    block = EDGE_ROWS // 2
    spec = pl.BlockSpec((block, chans, side_len), lambda i: (i, 0, 0))
    return pl.pallas_call(
        functools.partial(gram_body, len(pieces)),
        grid=(rows // block,),
        in_specs=[pl.BlockSpec(before.shape, lambda i: (0, 0)), ANY] + [spec] * len(pieces),
        out_specs=pl.BlockSpec(before.shape, lambda i: (0, 0)),
        out_shape=jax.ShapeDtypeStruct(before.shape, F32),
        compiler_params=kernel_params(60),
        cost_estimate=COST,
        name="gram_step",
    )(before, after, *pieces)


def newton_schulz(gram):
    size = gram.shape[0]
    frob_norm = jnp.sqrt(jnp.sum(gram * gram))
    identity = (iota((size, size), 0) == iota((size, size), 1)).astype(F32)
    current = gram / frob_norm
    middle = 0.5 * (3.0 * identity - current)
    inverse = middle
    for iteration in range(1, NS_ITERS):
        current = dot_nn(current, middle, HIGHEST)
        middle = 0.5 * (3.0 * identity - dot_nn(inverse, current, HIGHEST))
        inverse = dot_nn(middle, inverse, HIGHEST)
    return inverse, frob_norm


def polar_body(starts, sizes, groups, shrink_ref, gram_ref, *refs):
    chunks = len(sizes)
    moved_hbm = refs[:chunks]
    pixels_hbm = refs[chunks : chunks * (groups + 1)]
    out_hbm, moved, pixel_sems, moved_sems, out_sems = refs[chunks * (groups + 1) : chunks * (groups + 1) + 5]
    pixels = refs[chunks * (groups + 1) + 5 :]
    own, all_rows, side_len = moved.shape
    size = pixels[0].shape[2] * groups

    blocks = [
        (chunk, row) for chunk in [chunks - 1] + list(range(chunks - 1)) for row in range(0, sizes[chunk], EDGE_ROWS)
    ]
    pixel_copies = []
    moved_copies = []
    for place, (chunk, row) in enumerate(blocks):
        part = pl.ds(row, EDGE_ROWS)
        into = pl.ds(starts[chunk] + row, EDGE_ROWS)
        copies = [
            pltpu.make_async_copy(
                pixels_hbm[chunk * groups + group].at[part], pixels[chunk].at[group, part], pixel_sems.at[place, group]
            )
            for group in range(groups)
        ]
        pixel_copies.append(copies)
        moved_copies.append(
            pltpu.make_async_copy(moved_hbm[chunk].at[:, part], moved.at[:, into], moved_sems.at[place])
        )
        for copy in copies + moved_copies[-1:]:
            copy.start()

    last_blocks = sizes[-1] // EDGE_ROWS
    for copies in pixel_copies[:last_blocks]:
        for copy in copies:
            copy.wait()
    total = gram_ref[...]
    for first in range(0, sizes[-1], GRAM_ROWS):
        data = stacked([pixels[-1].at[group] for group in range(groups)], first, GRAM_ROWS)
        total = total + dot_nt(data, data)
    gram = jnp.zeros((size, size), F32)
    for i in range(GRAM_ROWS):
        gram = gram + total[i * size : (i + 1) * size, i * size : (i + 1) * size]
    inverse, frob_norm = newton_schulz(gram)
    factor = shrink_ref[0] * jnp.sqrt(all_rows * side_len / frob_norm)
    select = (iota((own, size), 0) == iota((own, size), 1)).astype(F32)
    weights = dot_nt(select, inverse, HIGHEST) * factor
    spread = POLAR_ROWS * own
    wide = POLAR_ROWS * size
    repeat = (iota((spread, own), 0) // POLAR_ROWS == iota((spread, own), 1)).astype(BF16)
    weights = dot_nn(repeat, weights.astype(BF16)).astype(BF16)
    repeat = (iota((size, wide), 1) % size == iota((size, wide), 0)).astype(BF16)
    weights = dot_nn(weights, repeat)
    keep = iota((spread, wide), 0) % POLAR_ROWS == iota((spread, wide), 1) // size
    weights = jnp.where(keep, weights, 0.0).astype(BF16)

    out_copies = []
    for place, (chunk, row) in enumerate(blocks):
        if place >= last_blocks:
            for copy in pixel_copies[place]:
                copy.wait()
        moved_copies[place].wait()
        for first in range(row, row + EDGE_ROWS, POLAR_ROWS):
            data = stacked([pixels[chunk].at[group] for group in range(groups)], first, POLAR_ROWS)
            polar = dot_nn(weights, data).reshape(own, POLAR_ROWS, side_len)
            into = starts[chunk] + first
            moved[:, into : into + POLAR_ROWS] -= polar
        part = pl.ds(starts[chunk] + row, EDGE_ROWS)
        copy = pltpu.make_async_copy(moved.at[:, part], out_hbm.at[:, part], out_sems.at[place])
        copy.start()
        out_copies.append(copy)
    for copy in out_copies:
        copy.wait()


def polar_step(shrinkage, gram, moved, gathered, starts, sizes):
    chunks = len(gathered)
    groups = len(gathered[0])
    chans, _, side_len = moved[0].shape
    shape = (chans, sum(sizes), side_len)
    blocks = sum(sizes) // EDGE_ROWS
    flat = [piece for pieces in gathered for piece in pieces]
    return pl.pallas_call(
        functools.partial(polar_body, starts, sizes, groups),
        in_specs=[SMEM, pl.BlockSpec(memory_space=pltpu.VMEM)] + [ANY] * (chunks + len(flat)),
        out_specs=ANY,
        out_shape=jax.ShapeDtypeStruct(shape, F32),
        scratch_shapes=[
            pltpu.VMEM(shape, F32),
            pltpu.SemaphoreType.DMA((blocks, groups)),
            pltpu.SemaphoreType.DMA((blocks,)),
            pltpu.SemaphoreType.DMA((blocks,)),
        ]
        + [pltpu.VMEM((groups,) + pieces[0].shape, BF16) for pieces in gathered],
        compiler_params=kernel_params(60),
        cost_estimate=COST,
        name="polar_step",
    )(shrinkage, gram, *moved, *flat)


def neighbour_rows(model_image, reach):
    ends = lax.axis_size("strip") - 1
    head, tail = lax.optimization_barrier((model_image[:, :reach], model_image[:, model_image.shape[1] - reach :]))
    before = lax.ppermute(tail.astype(BF16), "strip", [(i, i + 1) for i in range(ends)])
    after = lax.ppermute(head.astype(BF16), "strip", [(i + 1, i) for i in range(ends)])
    return jnp.concatenate([before, after], axis=1)


def swap(value, axis, bits):
    count = lax.axis_size(axis)
    return lax.ppermute(value, axis, [(i, i ^ bits) for i in range(count)])


def gather_channels(pixels, after):
    devices = lax.axis_size("chan")
    kept = [pixels] + [gate(swap(pixels, "chan", bits), after) for bits in range(2, devices, 2)]
    if devices == 1:
        return kept
    return kept + [swap(piece, "chan", 1) for piece in kept]


def exchange(pieces):
    order = [k for k in (1, 2) if k < len(pieces)] + list(range(4, len(pieces))) + [3][: max(0, len(pieces) - 3)]
    arrived = {k: swap(pieces[k], "strip", k) for k in order}
    return [pieces[0]] + [arrived[k] for k in range(1, len(pieces))]


def local(grid, model_image, step_size, highpass, shrinkage):
    chans, own_rows, side_len = model_image.shape
    strips = lax.axis_size("strip")
    size = chans * lax.axis_size("chan")
    starts, sizes = chunk_rows(own_rows)
    chunks = len(sizes)
    strip = lax.axis_index("strip").astype(jnp.int32).reshape(1)

    cosine, sine_table = make_tables(side_len)
    split = np.stack([cosine.reshape(strips, own_rows, side_len), sine_table.reshape(strips, own_rows, side_len)])
    tables = [
        np.ascontiguousarray(split[:, :, start : start + rows]).reshape(2 * strips * rows, side_len)
        for start, rows in zip(starts, sizes)
    ]

    levels, taps = highpass.shape
    reach = (taps - 1) * 2 ** (levels - 1)
    edges = neighbour_rows(model_image, reach)

    halves = {}
    moved = {}
    gathered = {}
    pixels = {}
    done = set()
    state = dict(last=strip, gram=jnp.zeros((GRAM_ROWS * size, GRAM_ROWS * size), F32), bases=None)

    def first(chunk):
        if chunk == 0:
            sent, state["last"] = first_pieces(strip, tables[chunk], grid, strips, state["last"])
            halves[chunk] = exchange(sent)
            return
        sent, state["last"] = first_transform(tables[chunk], grid, strips, state["last"])
        if chunk == 1:
            sent = gate(sent, edges)
        if chunk == 2:
            gather(0)
            gram(0)
            done.add(0)
            sent = gate(sent, state["gram"])
        halves[chunk] = lax.all_to_all(sent, "strip", split_axis=0, concat_axis=0, tiled=True)

    def base():
        state["bases"] = base_step(
            strip, strips, step_size, highpass, model_image, edges, starts, sizes, state["last"]
        )
        state["last"] = state["bases"][0]

    def second(chunk):
        inputs = (step_size, halves[chunk], cosine, sine_table, state["bases"][chunk], state["last"])
        if chunk == 0:
            moved[chunk], pixels[chunk] = second_pieces(strip, *inputs)
        else:
            moved[chunk], pixels[chunk] = second_transform(*inputs)
        state["last"] = pixels[chunk]

    def gather(chunk):
        pieces = gather_channels(pixels[chunk], state["last"])
        if chans % 16:
            pieces = [jnp.concatenate(pieces, axis=1)]
        gathered[chunk] = pieces

    def gram(chunk):
        state["gram"] = gram_step(gathered[chunk], state["gram"], state["last"])
        state["last"] = state["gram"]

    first(0)
    if chunks > 1:
        first(1)
    base()
    for chunk in range(chunks):
        second(chunk)
        if chunk + 2 < chunks:
            first(chunk + 2)
        if chunk == 1:
            gather(1)
        if chunk >= 1 and chunk - 1 not in done:
            if chunk - 1 not in gathered:
                gather(chunk - 1)
            gram(chunk - 1)
    if chunks - 1 not in gathered:
        gather(chunks - 1)
    order = range(chunks)
    return polar_step(
        shrinkage, state["gram"], [moved[k] for k in order], [gathered[k] for k in order], starts, sizes
    )


def solution(mesh):
    return jax.shard_map(
        local,
        mesh=mesh,
        in_specs=(
            P(None, "chan", "strip", None),
            P("chan", "strip", None),
            P("chan"),
            P(),
            P("strip"),
        ),
        out_specs=P("chan", "strip", None),
        check_vma=False,
    )
```

```python
import functools

import jax
import jax.numpy as jnp
import ml_dtypes
import numpy as np
from jax import lax
from jax.experimental import pallas as pl
from jax.experimental.pallas import tpu as pltpu
from jax.sharding import PartitionSpec as P

NS_ITERS = 5
EDGE_ROWS = 16
GRAM_ROWS = 4
POLAR_ROWS = 8
HIGHEST = lax.Precision.HIGHEST
F32 = jnp.float32
BF16 = jnp.bfloat16
MIB = 1 << 20

ANY = pl.BlockSpec(memory_space=pl.ANY)
SMEM = pl.BlockSpec(memory_space=pltpu.SMEM)


def kernel_params(mebibytes):
    return pltpu.CompilerParams(vmem_limit_bytes=mebibytes * MIB)


COST = pl.CostEstimate(flops=0, bytes_accessed=1 << 16, transcendentals=0)


def dot_nt(a, b, precision=None):
    return lax.dot_general(
        a, b, (((1,), (1,)), ((), ())), precision=precision, preferred_element_type=F32
    )


def dot_nn(a, b, precision=None):
    return lax.dot_general(
        a, b, (((1,), (0,)), ((), ())), precision=precision, preferred_element_type=F32
    )


def iota(shape, dim):
    return lax.broadcasted_iota(jnp.int32, shape, dim)


def make_tables(side_len):
    indices = np.arange(side_len, dtype=np.int64)
    phases = (np.outer(indices, indices) % side_len).astype(np.float32) * np.float32(
        2.0 * 3.141592653589793 / side_len
    )
    unit_scale = np.float32(float(side_len) ** (-0.5))
    cosine = (np.cos(phases) * unit_scale).astype(ml_dtypes.bfloat16)
    sine_table = (np.sin(phases) * unit_scale).astype(ml_dtypes.bfloat16)
    return cosine, sine_table


def chunk_rows(own_rows):
    quarter = own_rows // 4
    sizes = [own_rows - 2 * quarter - EDGE_ROWS, quarter, quarter, EDGE_ROWS]
    return [sum(sizes[:place]) for place in range(len(sizes))], sizes


def gate_body(value_ref, after_ref, out_ref):
    pass


def gate(value, after):
    return pl.pallas_call(
        gate_body,
        in_specs=[ANY, ANY],
        out_specs=ANY,
        out_shape=jax.ShapeDtypeStruct(value.shape, value.dtype),
        input_output_aliases={0: 0},
        cost_estimate=COST,
        name="gate",
    )(value, after)


def first_body(table_ref, grid_ref, after_ref, out_ref, token_ref):
    token_ref[...] = jnp.zeros(token_ref.shape, F32)
    strips, _, chans, rows, width = out_ref.shape
    side_len = table_ref.shape[-1]
    table = table_ref[...]
    middle = strips * rows
    turned = jnp.concatenate([-table[middle:], table[:middle]], axis=0)
    total = dot_nt(table, grid_ref[0].reshape(chans * width, side_len))
    total = total + dot_nt(turned, grid_ref[1].reshape(chans * width, side_len))
    total = total.astype(BF16)
    for part in range(2):
        for strip in range(strips):
            first = (part * strips + strip) * rows
            for chan in range(chans):
                out_ref[strip, part, chan] = total[first : first + rows, chan * width : (chan + 1) * width]


def first_transform(table, grid, strips, after):
    _, chans, width, side_len = grid.shape
    rows = table.shape[0] // (2 * strips)
    shape = (strips, 2, chans, rows, width)
    if width % 128 or rows % 16:
        middle = strips * rows
        turned = jnp.concatenate([-table[middle:], table[:middle]], axis=0)
        total = jnp.einsum("mv,cuv->mcu", table, grid[0], preferred_element_type=F32)
        total = total + jnp.einsum("mv,cuv->mcu", turned, grid[1], preferred_element_type=F32)
        total = total.astype(BF16).reshape(2, strips, rows, chans, width)
        return total.transpose(1, 0, 3, 2, 4), jnp.zeros((8, 128), F32)
    block = 4 if chans % 4 == 0 else 1
    return pl.pallas_call(
        first_body,
        grid=(chans // block,),
        in_specs=[
            pl.BlockSpec(table.shape, lambda i: (0, 0)),
            pl.BlockSpec((2, block, width, side_len), lambda i: (0, i, 0, 0)),
            ANY,
        ],
        out_specs=[
            pl.BlockSpec((strips, 2, block, rows, width), lambda i: (0, 0, i, 0, 0)),
            pl.BlockSpec((8, 128), lambda i: (0, 0)),
        ],
        out_shape=[jax.ShapeDtypeStruct(shape, BF16), jax.ShapeDtypeStruct((8, 128), F32)],
        compiler_params=kernel_params(60),
        cost_estimate=COST,
        name="first_transform",
    )(table, grid, after)


def pieces_body(strips, strip_ref, table_ref, grid_ref, after_ref, *refs):
    out_refs = refs[:strips]
    refs[strips][...] = jnp.zeros(refs[strips].shape, F32)
    _, chans, rows, width = out_refs[0].shape
    side_len = table_ref.shape[-1]
    cosine = jnp.concatenate([table_ref[0, strip_ref[0] ^ k] for k in range(strips)], axis=0)
    sine_table = jnp.concatenate([table_ref[1, strip_ref[0] ^ k] for k in range(strips)], axis=0)
    total = dot_nt(jnp.concatenate([cosine, sine_table], axis=0), grid_ref[0].reshape(chans * width, side_len))
    total = total + dot_nt(
        jnp.concatenate([-sine_table, cosine], axis=0), grid_ref[1].reshape(chans * width, side_len)
    )
    total = total.astype(BF16)
    for part in range(2):
        for k in range(strips):
            first = (part * strips + k) * rows
            for chan in range(chans):
                out_refs[k][part, chan] = total[first : first + rows, chan * width : (chan + 1) * width]


def first_pieces(strip, table, grid, strips, after):
    _, chans, width, side_len = grid.shape
    rows = table.shape[0] // (2 * strips)
    table = table.reshape(2, strips, rows, side_len)
    if width % 128 or rows % 16:
        order = strip[0] ^ jnp.arange(strips, dtype=jnp.int32)
        cosine, sine_table = (jnp.take(table[part], order, axis=0) for part in range(2))

        def product(table, part):
            return jnp.einsum("kmv,cuv->kcmu", table, part, preferred_element_type=F32)

        real = product(cosine, grid[0]) - product(sine_table, grid[1])
        imag = product(sine_table, grid[0]) + product(cosine, grid[1])
        both = jnp.stack([real, imag], axis=1).astype(BF16)
        return [both[k] for k in range(strips)], jnp.zeros((8, 128), F32)
    block = 4 if chans % 4 == 0 else 1
    results = pl.pallas_call(
        functools.partial(pieces_body, strips),
        grid=(chans // block,),
        in_specs=[
            SMEM,
            pl.BlockSpec(table.shape, lambda i: (0, 0, 0, 0)),
            pl.BlockSpec((2, block, width, side_len), lambda i: (0, i, 0, 0)),
            ANY,
        ],
        out_specs=[pl.BlockSpec((2, block, rows, width), lambda i: (0, i, 0, 0))] * strips
        + [pl.BlockSpec((8, 128), lambda i: (0, 0))],
        out_shape=[jax.ShapeDtypeStruct((2, chans, rows, width), BF16)] * strips
        + [jax.ShapeDtypeStruct((8, 128), F32)],
        compiler_params=kernel_params(60),
        cost_estimate=COST,
        name="first_pieces",
    )(strip, table, grid, after)
    return results[:strips], results[strips]


def band_matrix(taps_of, levels, taps, own_rows, reach, first_row, image_rows):
    half_taps = taps // 2
    shape = (own_rows, own_rows + 2 * reach)
    row = iota(shape, 0)
    column = iota(shape, 1)
    place = jnp.where(
        column < own_rows, column, jnp.where(column < own_rows + reach, column - own_rows - reach, column - reach)
    )
    total = jnp.zeros(shape, F32)
    for level in range(levels):
        dilation = 2**level
        for outer in range(taps):
            detail_row = row - (outer - half_taps) * dilation
            inside = (detail_row + first_row >= 0) & (detail_row + first_row < image_rows)
            for inner in range(taps):
                hit = inside & (place == detail_row + (inner - half_taps) * dilation)
                total = total + jnp.where(hit, taps_of(level, outer) * taps_of(level, inner), 0.0)
    return total


def base_body(levels, taps, starts, strips, strip_ref, step_ref, highpass_ref, model_ref, edge_ref, after_ref, *refs):
    high, low = refs[-2:]
    out_refs = refs[:-2]
    block, own_rows, side_len = model_ref.shape
    reach = edge_ref.shape[1] // 2

    @pl.when(pl.program_id(0) == 0)
    def _():
        band = band_matrix(
            lambda level, tap: highpass_ref[level, tap],
            levels,
            taps,
            own_rows,
            reach,
            strip_ref[0] * own_rows,
            strips * own_rows,
        )
        top = band.astype(BF16)
        high[...] = top
        low[...] = (band - top.astype(F32)).astype(BF16)

    first = pl.program_id(0) * block
    for chan in range(block):
        model = model_ref[chan]
        top = model.astype(BF16)
        rest = (model - top.astype(F32)).astype(BF16)
        edge = edge_ref[chan].astype(F32)
        whole = jnp.concatenate([top.astype(F32), edge], axis=0).astype(BF16)
        gradient = dot_nn(high[...], whole)
        gradient = gradient + dot_nn(low[...], whole)
        gradient = gradient + dot_nn(high[:, :own_rows], rest)
        base = model - step_ref[first + chan] * gradient
        for start, out_ref in zip(starts, out_refs):
            out_ref[chan] = base[start : start + out_ref.shape[1]]


def base_step(strip, strips, step_size, highpass, model_image, edges, starts, sizes, after):
    chans, rows, side_len = model_image.shape
    levels, taps = highpass.shape
    reach = edges.shape[1] // 2
    block = 2 if chans % 2 == 0 else 1
    wide = rows + 2 * reach
    return pl.pallas_call(
        functools.partial(base_body, levels, taps, starts, strips),
        grid=(chans // block,),
        in_specs=[
            SMEM,
            SMEM,
            SMEM,
            pl.BlockSpec((block, rows, side_len), lambda i: (i, 0, 0)),
            pl.BlockSpec((block, 2 * reach, side_len), lambda i: (i, 0, 0)),
            ANY,
        ],
        out_specs=[pl.BlockSpec((block, part, side_len), lambda i: (i, 0, 0)) for part in sizes],
        out_shape=[jax.ShapeDtypeStruct((chans, part, side_len), F32) for part in sizes],
        scratch_shapes=[pltpu.VMEM((rows, wide), BF16), pltpu.VMEM((rows, wide), BF16)],
        compiler_params=kernel_params(60),
        cost_estimate=COST,
        name="base_step",
    )(strip, step_size, highpass, model_image, edges, after)


def second_body(step_ref, half_ref, cosine_ref, sine_ref, base_ref, after_ref, moved_ref, pixels_ref):
    strips, _, chans, rows, width = half_ref.shape
    real = jnp.concatenate([half_ref[s, 0].reshape(chans * rows, width) for s in range(strips)], axis=1)
    imag = jnp.concatenate([half_ref[s, 1].reshape(chans * rows, width) for s in range(strips)], axis=1)
    dirty = dot_nn(real, cosine_ref[...]) - dot_nn(imag, sine_ref[...])
    pieces = []
    for chan in range(chans):
        moved = base_ref[chan] + step_ref[chan] * dirty[chan * rows : (chan + 1) * rows]
        moved_ref[chan] = moved
        pieces.append(moved)
    pixels_ref[...] = jnp.swapaxes(jnp.stack(pieces), 0, 1).astype(BF16)


def second_transform(step_size, half, cosine, sine_table, base, after):
    strips, _, chans, rows, width = half.shape
    side_len = cosine.shape[0]
    if width % 128 or rows % 16 or chans % 16:
        split = (strips, width, side_len)
        dirty = jnp.einsum("scmu,sul->cml", half[:, 0], cosine.reshape(split), preferred_element_type=F32)
        dirty = dirty - jnp.einsum("scmu,sul->cml", half[:, 1], sine_table.reshape(split), preferred_element_type=F32)
        moved = base + step_size[:, None, None] * dirty
        return moved, moved.astype(BF16).transpose(1, 0, 2)
    block = min(256, side_len)
    return pl.pallas_call(
        second_body,
        grid=(side_len // block,),
        in_specs=[
            SMEM,
            pl.BlockSpec(half.shape, lambda i: (0, 0, 0, 0, 0)),
            pl.BlockSpec((side_len, block), lambda i: (0, i)),
            pl.BlockSpec((side_len, block), lambda i: (0, i)),
            pl.BlockSpec((chans, rows, block), lambda i: (0, 0, i)),
            ANY,
        ],
        out_specs=[
            pl.BlockSpec((chans, rows, block), lambda i: (0, 0, i)),
            pl.BlockSpec((rows, chans, block), lambda i: (0, 0, i)),
        ],
        out_shape=[
            jax.ShapeDtypeStruct(base.shape, F32),
            jax.ShapeDtypeStruct((rows, chans, side_len), BF16),
        ],
        compiler_params=kernel_params(60),
        cost_estimate=COST,
        name="second_transform",
    )(step_size, half, cosine, sine_table, base, after)


def second_pieces_body(strips, strip_ref, step_ref, cosine_ref, sine_ref, base_ref, after_ref, *refs):
    halves = refs[:strips]
    moved_ref, pixels_ref = refs[strips:]
    _, chans, rows, width = halves[0].shape
    real = jnp.concatenate([half[0].reshape(chans * rows, width) for half in halves], axis=1)
    imag = jnp.concatenate([half[1].reshape(chans * rows, width) for half in halves], axis=1)

    def ordered(table_ref):
        parts = [table_ref[pl.ds(pl.multiple_of((strip_ref[0] ^ k) * width, width), width), :] for k in range(strips)]
        return jnp.concatenate(parts, axis=0)

    dirty = dot_nn(real, ordered(cosine_ref)) - dot_nn(imag, ordered(sine_ref))
    pieces = []
    for chan in range(chans):
        moved = base_ref[chan] + step_ref[chan] * dirty[chan * rows : (chan + 1) * rows]
        moved_ref[chan] = moved
        pieces.append(moved)
    pixels_ref[...] = jnp.swapaxes(jnp.stack(pieces), 0, 1).astype(BF16)


def second_pieces(strip, step_size, halves, cosine, sine_table, base, after):
    strips = len(halves)
    _, chans, rows, width = halves[0].shape
    side_len = cosine.shape[0]
    if width % 128 or rows % 16 or chans % 16:
        order = strip[0] ^ jnp.arange(strips, dtype=jnp.int32)
        both = jnp.stack(halves)

        def product(part, table):
            parts = jnp.take(jnp.asarray(table).reshape(strips, width, side_len), order, axis=0)
            return jnp.einsum("kcmu,kul->cml", part, parts, preferred_element_type=F32)

        moved = base + step_size[:, None, None] * (product(both[:, 0], cosine) - product(both[:, 1], sine_table))
        return moved, moved.astype(BF16).transpose(1, 0, 2)
    block = min(256, side_len)
    half_spec = pl.BlockSpec(halves[0].shape, lambda i: (0, 0, 0, 0))
    return pl.pallas_call(
        functools.partial(second_pieces_body, strips),
        grid=(side_len // block,),
        in_specs=[
            SMEM,
            SMEM,
            pl.BlockSpec((side_len, block), lambda i: (0, i)),
            pl.BlockSpec((side_len, block), lambda i: (0, i)),
            pl.BlockSpec((chans, rows, block), lambda i: (0, 0, i)),
            ANY,
        ]
        + [half_spec] * strips,
        out_specs=[
            pl.BlockSpec((chans, rows, block), lambda i: (0, 0, i)),
            pl.BlockSpec((rows, chans, block), lambda i: (0, 0, i)),
        ],
        out_shape=[
            jax.ShapeDtypeStruct(base.shape, F32),
            jax.ShapeDtypeStruct((rows, chans, side_len), BF16),
        ],
        compiler_params=kernel_params(60),
        cost_estimate=COST,
        name="second_pieces",
    )(strip, step_size, cosine, sine_table, base, after, *halves)


def stacked(group_refs, first, count):
    return jnp.concatenate([ref[first + i] for i in range(count) for ref in group_refs], axis=0)


def gram_body(groups, before_ref, after_ref, *refs):
    total_ref = refs[groups]

    @pl.when(pl.program_id(0) == 0)
    def _():
        total_ref[...] = before_ref[...]

    total = total_ref[...]
    for first in range(0, refs[0].shape[0], GRAM_ROWS):
        pixels = stacked(refs[:groups], first, GRAM_ROWS)
        total = total + dot_nt(pixels, pixels)
    total_ref[...] = total


def gram_step(pieces, before, after):
    rows, chans, side_len = pieces[0].shape
    block = EDGE_ROWS // 2
    spec = pl.BlockSpec((block, chans, side_len), lambda i: (i, 0, 0))
    return pl.pallas_call(
        functools.partial(gram_body, len(pieces)),
        grid=(rows // block,),
        in_specs=[pl.BlockSpec(before.shape, lambda i: (0, 0)), ANY] + [spec] * len(pieces),
        out_specs=pl.BlockSpec(before.shape, lambda i: (0, 0)),
        out_shape=jax.ShapeDtypeStruct(before.shape, F32),
        compiler_params=kernel_params(60),
        cost_estimate=COST,
        name="gram_step",
    )(before, after, *pieces)


def newton_schulz(gram):
    size = gram.shape[0]
    frob_norm = jnp.sqrt(jnp.sum(gram * gram))
    identity = (iota((size, size), 0) == iota((size, size), 1)).astype(F32)
    current = gram / frob_norm
    middle = 0.5 * (3.0 * identity - current)
    inverse = middle
    for iteration in range(1, NS_ITERS):
        current = dot_nn(current, middle, HIGHEST)
        middle = 0.5 * (3.0 * identity - dot_nn(inverse, current, HIGHEST))
        inverse = dot_nn(middle, inverse, HIGHEST)
    return inverse, frob_norm


def polar_body(starts, sizes, groups, shrink_ref, gram_ref, *refs):
    chunks = len(sizes)
    moved_hbm = refs[:chunks]
    pixels_hbm = refs[chunks : chunks * (groups + 1)]
    out_hbm, moved, pixel_sems, moved_sems, out_sems = refs[chunks * (groups + 1) : chunks * (groups + 1) + 5]
    pixels = refs[chunks * (groups + 1) + 5 :]
    own, all_rows, side_len = moved.shape
    size = pixels[0].shape[2] * groups

    blocks = [
        (chunk, row) for chunk in [chunks - 1] + list(range(chunks - 1)) for row in range(0, sizes[chunk], EDGE_ROWS)
    ]
    pixel_copies = []
    moved_copies = []
    for place, (chunk, row) in enumerate(blocks):
        part = pl.ds(row, EDGE_ROWS)
        into = pl.ds(starts[chunk] + row, EDGE_ROWS)
        copies = [
            pltpu.make_async_copy(
                pixels_hbm[chunk * groups + group].at[part], pixels[chunk].at[group, part], pixel_sems.at[place, group]
            )
            for group in range(groups)
        ]
        pixel_copies.append(copies)
        moved_copies.append(
            pltpu.make_async_copy(moved_hbm[chunk].at[:, part], moved.at[:, into], moved_sems.at[place])
        )
        for copy in copies + moved_copies[-1:]:
            copy.start()

    last_blocks = sizes[-1] // EDGE_ROWS
    for copies in pixel_copies[:last_blocks]:
        for copy in copies:
            copy.wait()
    total = gram_ref[...]
    for first in range(0, sizes[-1], GRAM_ROWS):
        data = stacked([pixels[-1].at[group] for group in range(groups)], first, GRAM_ROWS)
        total = total + dot_nt(data, data)
    gram = jnp.zeros((size, size), F32)
    for i in range(GRAM_ROWS):
        gram = gram + total[i * size : (i + 1) * size, i * size : (i + 1) * size]
    inverse, frob_norm = newton_schulz(gram)
    factor = shrink_ref[0] * jnp.sqrt(all_rows * side_len / frob_norm)
    select = (iota((own, size), 0) == iota((own, size), 1)).astype(F32)
    weights = dot_nt(select, inverse, HIGHEST) * factor
    spread = POLAR_ROWS * own
    wide = POLAR_ROWS * size
    repeat = (iota((spread, own), 0) // POLAR_ROWS == iota((spread, own), 1)).astype(BF16)
    weights = dot_nn(repeat, weights.astype(BF16)).astype(BF16)
    repeat = (iota((size, wide), 1) % size == iota((size, wide), 0)).astype(BF16)
    weights = dot_nn(weights, repeat)
    keep = iota((spread, wide), 0) % POLAR_ROWS == iota((spread, wide), 1) // size
    weights = jnp.where(keep, weights, 0.0).astype(BF16)

    out_copies = []
    for place, (chunk, row) in enumerate(blocks):
        if place >= last_blocks:
            for copy in pixel_copies[place]:
                copy.wait()
        moved_copies[place].wait()
        for first in range(row, row + EDGE_ROWS, POLAR_ROWS):
            data = stacked([pixels[chunk].at[group] for group in range(groups)], first, POLAR_ROWS)
            polar = dot_nn(weights, data).reshape(own, POLAR_ROWS, side_len)
            into = starts[chunk] + first
            moved[:, into : into + POLAR_ROWS] -= polar
        part = pl.ds(starts[chunk] + row, EDGE_ROWS)
        copy = pltpu.make_async_copy(moved.at[:, part], out_hbm.at[:, part], out_sems.at[place])
        copy.start()
        out_copies.append(copy)
    for copy in out_copies:
        copy.wait()


def polar_step(shrinkage, gram, moved, gathered, starts, sizes):
    chunks = len(gathered)
    groups = len(gathered[0])
    chans, _, side_len = moved[0].shape
    shape = (chans, sum(sizes), side_len)
    blocks = sum(sizes) // EDGE_ROWS
    flat = [piece for pieces in gathered for piece in pieces]
    return pl.pallas_call(
        functools.partial(polar_body, starts, sizes, groups),
        in_specs=[SMEM, pl.BlockSpec(memory_space=pltpu.VMEM)] + [ANY] * (chunks + len(flat)),
        out_specs=ANY,
        out_shape=jax.ShapeDtypeStruct(shape, F32),
        scratch_shapes=[
            pltpu.VMEM(shape, F32),
            pltpu.SemaphoreType.DMA((blocks, groups)),
            pltpu.SemaphoreType.DMA((blocks,)),
            pltpu.SemaphoreType.DMA((blocks,)),
        ]
        + [pltpu.VMEM((groups,) + pieces[0].shape, BF16) for pieces in gathered],
        compiler_params=kernel_params(60),
        cost_estimate=COST,
        name="polar_step",
    )(shrinkage, gram, *moved, *flat)


def neighbour_rows(model_image, reach):
    ends = lax.axis_size("strip") - 1
    head, tail = lax.optimization_barrier((model_image[:, :reach], model_image[:, model_image.shape[1] - reach :]))
    before = lax.ppermute(tail.astype(BF16), "strip", [(i, i + 1) for i in range(ends)])
    after = lax.ppermute(head.astype(BF16), "strip", [(i + 1, i) for i in range(ends)])
    return jnp.concatenate([before, after], axis=1)


def swap(value, axis, bits):
    count = lax.axis_size(axis)
    return lax.ppermute(value, axis, [(i, i ^ bits) for i in range(count)])


def gather_channels(pixels, after):
    devices = lax.axis_size("chan")
    kept = [pixels] + [gate(swap(pixels, "chan", bits), after) for bits in range(2, devices, 2)]
    if devices == 1:
        return kept
    return kept + [swap(piece, "chan", 1) for piece in kept]


def exchange(pieces):
    half = len(pieces) // 2
    order = list(range(half, len(pieces))) + list(range(1, half))
    arrived = {k: swap(pieces[k], "strip", k) for k in order}
    return [pieces[0]] + [arrived[k] for k in range(1, len(pieces))]


def local(grid, model_image, step_size, highpass, shrinkage):
    chans, own_rows, side_len = model_image.shape
    strips = lax.axis_size("strip")
    size = chans * lax.axis_size("chan")
    starts, sizes = chunk_rows(own_rows)
    chunks = len(sizes)
    strip = lax.axis_index("strip").astype(jnp.int32).reshape(1)

    cosine, sine_table = make_tables(side_len)
    split = np.stack([cosine.reshape(strips, own_rows, side_len), sine_table.reshape(strips, own_rows, side_len)])
    tables = [
        np.ascontiguousarray(split[:, :, start : start + rows]).reshape(2 * strips * rows, side_len)
        for start, rows in zip(starts, sizes)
    ]

    levels, taps = highpass.shape
    reach = (taps - 1) * 2 ** (levels - 1)
    edges = neighbour_rows(model_image, reach)

    halves = {}
    moved = {}
    gathered = {}
    pixels = {}
    state = dict(last=strip, gram=jnp.zeros((GRAM_ROWS * size, GRAM_ROWS * size), F32), bases=None)

    def first(chunk):
        if chunk == 1:
            sent, state["last"] = first_pieces(strip, tables[chunk], grid, strips, state["last"])
            halves[chunk] = exchange(sent)
        else:
            sent, state["last"] = first_transform(tables[chunk], grid, strips, state["last"])
            halves[chunk] = lax.all_to_all(sent, "strip", split_axis=0, concat_axis=0, tiled=True)

    def base():
        state["bases"] = base_step(
            strip, strips, step_size, highpass, model_image, edges, starts, sizes, state["last"]
        )
        state["last"] = state["bases"][0]

    def second(chunk):
        inputs = (step_size, halves[chunk], cosine, sine_table, state["bases"][chunk], state["last"])
        if chunk == 1:
            moved[chunk], pixels[chunk] = second_pieces(strip, *inputs)
        else:
            moved[chunk], pixels[chunk] = second_transform(*inputs)
        state["last"] = pixels[chunk]

    def gather(chunk):
        pieces = gather_channels(pixels[chunk], state["last"])
        if chans % 16:
            pieces = [jnp.concatenate(pieces, axis=1)]
        gathered[chunk] = pieces

    def gram(chunk):
        state["gram"] = gram_step(gathered[chunk], state["gram"], state["last"])
        state["last"] = state["gram"]

    first(0)
    first(1)
    state["last"] = gate(state["last"], edges)
    first(2)
    base()
    second(1)
    second(0)
    gather(1)
    first(3)
    gather(0)
    gram(1)
    second(2)
    gram(0)
    second(3)
    gather(2)
    gram(2)
    gather(3)
    order = range(chunks)
    return polar_step(
        shrinkage, state["gram"], [moved[k] for k in order], [gathered[k] for k in order], starts, sizes
    )


def solution(mesh):
    return jax.shard_map(
        local,
        mesh=mesh,
        in_specs=(
            P(None, "chan", "strip", None),
            P("chan", "strip", None),
            P("chan"),
            P(),
            P("strip"),
        ),
        out_specs=P("chan", "strip", None),
        check_vma=False,
    )
```

```python
import functools

import jax
import jax.numpy as jnp
import ml_dtypes
import numpy as np
from jax import lax
from jax.experimental import pallas as pl
from jax.experimental.pallas import tpu as pltpu
from jax.sharding import PartitionSpec as P

NS_ITERS = 5
EDGE_ROWS = 16
GRAM_ROWS = 4
POLAR_ROWS = 8
HIGHEST = lax.Precision.HIGHEST
F32 = jnp.float32
BF16 = jnp.bfloat16
MIB = 1 << 20

ANY = pl.BlockSpec(memory_space=pl.ANY)
SMEM = pl.BlockSpec(memory_space=pltpu.SMEM)


def kernel_params(mebibytes):
    return pltpu.CompilerParams(vmem_limit_bytes=mebibytes * MIB)


COST = pl.CostEstimate(flops=0, bytes_accessed=1 << 16, transcendentals=0)


def dot_nt(a, b, precision=None):
    return lax.dot_general(
        a, b, (((1,), (1,)), ((), ())), precision=precision, preferred_element_type=F32
    )


def dot_nn(a, b, precision=None):
    return lax.dot_general(
        a, b, (((1,), (0,)), ((), ())), precision=precision, preferred_element_type=F32
    )


def iota(shape, dim):
    return lax.broadcasted_iota(jnp.int32, shape, dim)


def make_tables(side_len):
    indices = np.arange(side_len, dtype=np.int64)
    phases = (np.outer(indices, indices) % side_len).astype(np.float32) * np.float32(
        2.0 * 3.141592653589793 / side_len
    )
    unit_scale = np.float32(float(side_len) ** (-0.5))
    cosine = (np.cos(phases) * unit_scale).astype(ml_dtypes.bfloat16)
    sine_table = (np.sin(phases) * unit_scale).astype(ml_dtypes.bfloat16)
    return cosine, sine_table


def chunk_rows(own_rows):
    quarter = own_rows // 4
    sizes = [own_rows - 2 * quarter - EDGE_ROWS, quarter, quarter, EDGE_ROWS]
    return [sum(sizes[:place]) for place in range(len(sizes))], sizes


def gate_body(value_ref, after_ref, out_ref):
    pass


def gate(value, after):
    return pl.pallas_call(
        gate_body,
        in_specs=[ANY, ANY],
        out_specs=ANY,
        out_shape=jax.ShapeDtypeStruct(value.shape, value.dtype),
        input_output_aliases={0: 0},
        cost_estimate=COST,
        name="gate",
    )(value, after)


def first_body(table_ref, grid_ref, after_ref, out_ref, token_ref):
    token_ref[...] = jnp.zeros(token_ref.shape, F32)
    strips, _, chans, rows, width = out_ref.shape
    side_len = table_ref.shape[-1]
    table = table_ref[...]
    middle = strips * rows
    turned = jnp.concatenate([-table[middle:], table[:middle]], axis=0)
    total = dot_nt(table, grid_ref[0].reshape(chans * width, side_len))
    total = total + dot_nt(turned, grid_ref[1].reshape(chans * width, side_len))
    total = total.astype(BF16)
    for part in range(2):
        for strip in range(strips):
            first = (part * strips + strip) * rows
            for chan in range(chans):
                out_ref[strip, part, chan] = total[first : first + rows, chan * width : (chan + 1) * width]


def first_transform(table, grid, strips, after):
    _, chans, width, side_len = grid.shape
    rows = table.shape[0] // (2 * strips)
    shape = (strips, 2, chans, rows, width)
    if width % 128 or rows % 16:
        middle = strips * rows
        turned = jnp.concatenate([-table[middle:], table[:middle]], axis=0)
        total = jnp.einsum("mv,cuv->mcu", table, grid[0], preferred_element_type=F32)
        total = total + jnp.einsum("mv,cuv->mcu", turned, grid[1], preferred_element_type=F32)
        total = total.astype(BF16).reshape(2, strips, rows, chans, width)
        return total.transpose(1, 0, 3, 2, 4), jnp.zeros((8, 128), F32)
    block = 4 if chans % 4 == 0 else 1
    return pl.pallas_call(
        first_body,
        grid=(chans // block,),
        in_specs=[
            pl.BlockSpec(table.shape, lambda i: (0, 0)),
            pl.BlockSpec((2, block, width, side_len), lambda i: (0, i, 0, 0)),
            ANY,
        ],
        out_specs=[
            pl.BlockSpec((strips, 2, block, rows, width), lambda i: (0, 0, i, 0, 0)),
            pl.BlockSpec((8, 128), lambda i: (0, 0)),
        ],
        out_shape=[jax.ShapeDtypeStruct(shape, BF16), jax.ShapeDtypeStruct((8, 128), F32)],
        compiler_params=kernel_params(60),
        cost_estimate=COST,
        name="first_transform",
    )(table, grid, after)


def pieces_body(strips, strip_ref, table_ref, grid_ref, after_ref, *refs):
    out_refs = refs[:strips]
    refs[strips][...] = jnp.zeros(refs[strips].shape, F32)
    _, chans, rows, width = out_refs[0].shape
    side_len = table_ref.shape[-1]
    cosine = jnp.concatenate([table_ref[0, strip_ref[0] ^ k] for k in range(strips)], axis=0)
    sine_table = jnp.concatenate([table_ref[1, strip_ref[0] ^ k] for k in range(strips)], axis=0)
    total = dot_nt(jnp.concatenate([cosine, sine_table], axis=0), grid_ref[0].reshape(chans * width, side_len))
    total = total + dot_nt(
        jnp.concatenate([-sine_table, cosine], axis=0), grid_ref[1].reshape(chans * width, side_len)
    )
    total = total.astype(BF16)
    for part in range(2):
        for k in range(strips):
            first = (part * strips + k) * rows
            for chan in range(chans):
                out_refs[k][part, chan] = total[first : first + rows, chan * width : (chan + 1) * width]


def first_pieces(strip, table, grid, strips, after):
    _, chans, width, side_len = grid.shape
    rows = table.shape[0] // (2 * strips)
    table = table.reshape(2, strips, rows, side_len)
    if width % 128 or rows % 16:
        order = strip[0] ^ jnp.arange(strips, dtype=jnp.int32)
        cosine, sine_table = (jnp.take(table[part], order, axis=0) for part in range(2))

        def product(table, part):
            return jnp.einsum("kmv,cuv->kcmu", table, part, preferred_element_type=F32)

        real = product(cosine, grid[0]) - product(sine_table, grid[1])
        imag = product(sine_table, grid[0]) + product(cosine, grid[1])
        both = jnp.stack([real, imag], axis=1).astype(BF16)
        return [both[k] for k in range(strips)], jnp.zeros((8, 128), F32)
    block = 4 if chans % 4 == 0 else 1
    results = pl.pallas_call(
        functools.partial(pieces_body, strips),
        grid=(chans // block,),
        in_specs=[
            SMEM,
            pl.BlockSpec(table.shape, lambda i: (0, 0, 0, 0)),
            pl.BlockSpec((2, block, width, side_len), lambda i: (0, i, 0, 0)),
            ANY,
        ],
        out_specs=[pl.BlockSpec((2, block, rows, width), lambda i: (0, i, 0, 0))] * strips
        + [pl.BlockSpec((8, 128), lambda i: (0, 0))],
        out_shape=[jax.ShapeDtypeStruct((2, chans, rows, width), BF16)] * strips
        + [jax.ShapeDtypeStruct((8, 128), F32)],
        compiler_params=kernel_params(60),
        cost_estimate=COST,
        name="first_pieces",
    )(strip, table, grid, after)
    return results[:strips], results[strips]


def band_matrix(taps_of, levels, taps, own_rows, reach, first_row, image_rows):
    half_taps = taps // 2
    shape = (own_rows, own_rows + 2 * reach)
    row = iota(shape, 0)
    column = iota(shape, 1)
    place = jnp.where(
        column < own_rows, column, jnp.where(column < own_rows + reach, column - own_rows - reach, column - reach)
    )
    total = jnp.zeros(shape, F32)
    for level in range(levels):
        dilation = 2**level
        for outer in range(taps):
            detail_row = row - (outer - half_taps) * dilation
            inside = (detail_row + first_row >= 0) & (detail_row + first_row < image_rows)
            for inner in range(taps):
                hit = inside & (place == detail_row + (inner - half_taps) * dilation)
                total = total + jnp.where(hit, taps_of(level, outer) * taps_of(level, inner), 0.0)
    return total


def base_body(levels, taps, starts, strips, strip_ref, step_ref, highpass_ref, model_ref, edge_ref, after_ref, *refs):
    high, low = refs[-2:]
    out_refs = refs[:-2]
    block, own_rows, side_len = model_ref.shape
    reach = edge_ref.shape[1] // 2

    @pl.when(pl.program_id(0) == 0)
    def _():
        band = band_matrix(
            lambda level, tap: highpass_ref[level, tap],
            levels,
            taps,
            own_rows,
            reach,
            strip_ref[0] * own_rows,
            strips * own_rows,
        )
        top = band.astype(BF16)
        high[...] = top
        low[...] = (band - top.astype(F32)).astype(BF16)

    first = pl.program_id(0) * block
    for chan in range(block):
        model = model_ref[chan]
        top = model.astype(BF16)
        rest = (model - top.astype(F32)).astype(BF16)
        edge = edge_ref[chan].astype(F32)
        whole = jnp.concatenate([top.astype(F32), edge], axis=0).astype(BF16)
        gradient = dot_nn(high[...], whole)
        gradient = gradient + dot_nn(low[...], whole)
        gradient = gradient + dot_nn(high[:, :own_rows], rest)
        base = model - step_ref[first + chan] * gradient
        for start, out_ref in zip(starts, out_refs):
            out_ref[chan] = base[start : start + out_ref.shape[1]]


def base_step(strip, strips, step_size, highpass, model_image, edges, starts, sizes, after):
    chans, rows, side_len = model_image.shape
    levels, taps = highpass.shape
    reach = edges.shape[1] // 2
    block = 2 if chans % 2 == 0 else 1
    wide = rows + 2 * reach
    return pl.pallas_call(
        functools.partial(base_body, levels, taps, starts, strips),
        grid=(chans // block,),
        in_specs=[
            SMEM,
            SMEM,
            SMEM,
            pl.BlockSpec((block, rows, side_len), lambda i: (i, 0, 0)),
            pl.BlockSpec((block, 2 * reach, side_len), lambda i: (i, 0, 0)),
            ANY,
        ],
        out_specs=[pl.BlockSpec((block, part, side_len), lambda i: (i, 0, 0)) for part in sizes],
        out_shape=[jax.ShapeDtypeStruct((chans, part, side_len), F32) for part in sizes],
        scratch_shapes=[pltpu.VMEM((rows, wide), BF16), pltpu.VMEM((rows, wide), BF16)],
        compiler_params=kernel_params(60),
        cost_estimate=COST,
        name="base_step",
    )(strip, step_size, highpass, model_image, edges, after)


def second_body(step_ref, half_ref, cosine_ref, sine_ref, base_ref, after_ref, moved_ref, pixels_ref):
    strips, _, chans, rows, width = half_ref.shape
    real = jnp.concatenate([half_ref[s, 0].reshape(chans * rows, width) for s in range(strips)], axis=1)
    imag = jnp.concatenate([half_ref[s, 1].reshape(chans * rows, width) for s in range(strips)], axis=1)
    dirty = dot_nn(real, cosine_ref[...]) - dot_nn(imag, sine_ref[...])
    pieces = []
    for chan in range(chans):
        moved = base_ref[chan] + step_ref[chan] * dirty[chan * rows : (chan + 1) * rows]
        moved_ref[chan] = moved
        pieces.append(moved)
    pixels_ref[...] = jnp.swapaxes(jnp.stack(pieces), 0, 1).astype(BF16)


def second_transform(step_size, half, cosine, sine_table, base, after):
    strips, _, chans, rows, width = half.shape
    side_len = cosine.shape[0]
    if width % 128 or rows % 16 or chans % 16:
        split = (strips, width, side_len)
        dirty = jnp.einsum("scmu,sul->cml", half[:, 0], cosine.reshape(split), preferred_element_type=F32)
        dirty = dirty - jnp.einsum("scmu,sul->cml", half[:, 1], sine_table.reshape(split), preferred_element_type=F32)
        moved = base + step_size[:, None, None] * dirty
        return moved, moved.astype(BF16).transpose(1, 0, 2)
    block = min(256, side_len)
    return pl.pallas_call(
        second_body,
        grid=(side_len // block,),
        in_specs=[
            SMEM,
            pl.BlockSpec(half.shape, lambda i: (0, 0, 0, 0, 0)),
            pl.BlockSpec((side_len, block), lambda i: (0, i)),
            pl.BlockSpec((side_len, block), lambda i: (0, i)),
            pl.BlockSpec((chans, rows, block), lambda i: (0, 0, i)),
            ANY,
        ],
        out_specs=[
            pl.BlockSpec((chans, rows, block), lambda i: (0, 0, i)),
            pl.BlockSpec((rows, chans, block), lambda i: (0, 0, i)),
        ],
        out_shape=[
            jax.ShapeDtypeStruct(base.shape, F32),
            jax.ShapeDtypeStruct((rows, chans, side_len), BF16),
        ],
        compiler_params=kernel_params(60),
        cost_estimate=COST,
        name="second_transform",
    )(step_size, half, cosine, sine_table, base, after)


def second_pieces_body(strips, strip_ref, step_ref, cosine_ref, sine_ref, base_ref, after_ref, *refs):
    halves = refs[:strips]
    moved_ref, pixels_ref = refs[strips:]
    _, chans, rows, width = halves[0].shape
    real = jnp.concatenate([half[0].reshape(chans * rows, width) for half in halves], axis=1)
    imag = jnp.concatenate([half[1].reshape(chans * rows, width) for half in halves], axis=1)

    def ordered(table_ref):
        parts = [table_ref[pl.ds(pl.multiple_of((strip_ref[0] ^ k) * width, width), width), :] for k in range(strips)]
        return jnp.concatenate(parts, axis=0)

    dirty = dot_nn(real, ordered(cosine_ref)) - dot_nn(imag, ordered(sine_ref))
    pieces = []
    for chan in range(chans):
        moved = base_ref[chan] + step_ref[chan] * dirty[chan * rows : (chan + 1) * rows]
        moved_ref[chan] = moved
        pieces.append(moved)
    pixels_ref[...] = jnp.swapaxes(jnp.stack(pieces), 0, 1).astype(BF16)


def second_pieces(strip, step_size, halves, cosine, sine_table, base, after):
    strips = len(halves)
    _, chans, rows, width = halves[0].shape
    side_len = cosine.shape[0]
    if width % 128 or rows % 16 or chans % 16:
        order = strip[0] ^ jnp.arange(strips, dtype=jnp.int32)
        both = jnp.stack(halves)

        def product(part, table):
            parts = jnp.take(jnp.asarray(table).reshape(strips, width, side_len), order, axis=0)
            return jnp.einsum("kcmu,kul->cml", part, parts, preferred_element_type=F32)

        moved = base + step_size[:, None, None] * (product(both[:, 0], cosine) - product(both[:, 1], sine_table))
        return moved, moved.astype(BF16).transpose(1, 0, 2)
    block = min(256, side_len)
    half_spec = pl.BlockSpec(halves[0].shape, lambda i: (0, 0, 0, 0))
    return pl.pallas_call(
        functools.partial(second_pieces_body, strips),
        grid=(side_len // block,),
        in_specs=[
            SMEM,
            SMEM,
            pl.BlockSpec((side_len, block), lambda i: (0, i)),
            pl.BlockSpec((side_len, block), lambda i: (0, i)),
            pl.BlockSpec((chans, rows, block), lambda i: (0, 0, i)),
            ANY,
        ]
        + [half_spec] * strips,
        out_specs=[
            pl.BlockSpec((chans, rows, block), lambda i: (0, 0, i)),
            pl.BlockSpec((rows, chans, block), lambda i: (0, 0, i)),
        ],
        out_shape=[
            jax.ShapeDtypeStruct(base.shape, F32),
            jax.ShapeDtypeStruct((rows, chans, side_len), BF16),
        ],
        compiler_params=kernel_params(60),
        cost_estimate=COST,
        name="second_pieces",
    )(strip, step_size, cosine, sine_table, base, after, *halves)


def stacked(group_refs, first, count):
    return jnp.concatenate([ref[first + i] for i in range(count) for ref in group_refs], axis=0)


def gram_body(groups, before_ref, after_ref, *refs):
    total_ref = refs[groups]

    @pl.when(pl.program_id(0) == 0)
    def _():
        total_ref[...] = before_ref[...]

    total = total_ref[...]
    for first in range(0, refs[0].shape[0], GRAM_ROWS):
        pixels = stacked(refs[:groups], first, GRAM_ROWS)
        total = total + dot_nt(pixels, pixels)
    total_ref[...] = total


def gram_step(pieces, before, after):
    rows, chans, side_len = pieces[0].shape
    block = EDGE_ROWS // 2
    spec = pl.BlockSpec((block, chans, side_len), lambda i: (i, 0, 0))
    return pl.pallas_call(
        functools.partial(gram_body, len(pieces)),
        grid=(rows // block,),
        in_specs=[pl.BlockSpec(before.shape, lambda i: (0, 0)), ANY] + [spec] * len(pieces),
        out_specs=pl.BlockSpec(before.shape, lambda i: (0, 0)),
        out_shape=jax.ShapeDtypeStruct(before.shape, F32),
        compiler_params=kernel_params(60),
        cost_estimate=COST,
        name="gram_step",
    )(before, after, *pieces)


def newton_schulz(gram):
    size = gram.shape[0]
    frob_norm = jnp.sqrt(jnp.sum(gram * gram))
    identity = (iota((size, size), 0) == iota((size, size), 1)).astype(F32)
    current = gram / frob_norm
    middle = 0.5 * (3.0 * identity - current)
    inverse = middle
    for iteration in range(1, NS_ITERS):
        current = dot_nn(current, middle, HIGHEST)
        middle = 0.5 * (3.0 * identity - dot_nn(inverse, current, HIGHEST))
        inverse = dot_nn(middle, inverse, HIGHEST)
    return inverse, frob_norm


def polar_body(starts, sizes, groups, shrink_ref, gram_ref, *refs):
    chunks = len(sizes)
    moved_hbm = refs[:chunks]
    pixels_hbm = refs[chunks : chunks * (groups + 1)]
    out_hbm, moved, pixel_sems, moved_sems, out_sems = refs[chunks * (groups + 1) : chunks * (groups + 1) + 5]
    pixels = refs[chunks * (groups + 1) + 5 :]
    own, all_rows, side_len = moved.shape
    size = pixels[0].shape[2] * groups

    blocks = [
        (chunk, row) for chunk in [chunks - 1] + list(range(chunks - 1)) for row in range(0, sizes[chunk], EDGE_ROWS)
    ]
    pixel_copies = []
    moved_copies = []
    for place, (chunk, row) in enumerate(blocks):
        part = pl.ds(row, EDGE_ROWS)
        into = pl.ds(starts[chunk] + row, EDGE_ROWS)
        copies = [
            pltpu.make_async_copy(
                pixels_hbm[chunk * groups + group].at[part], pixels[chunk].at[group, part], pixel_sems.at[place, group]
            )
            for group in range(groups)
        ]
        pixel_copies.append(copies)
        moved_copies.append(
            pltpu.make_async_copy(moved_hbm[chunk].at[:, part], moved.at[:, into], moved_sems.at[place])
        )
        for copy in copies + moved_copies[-1:]:
            copy.start()

    last_blocks = sizes[-1] // EDGE_ROWS
    for copies in pixel_copies[:last_blocks]:
        for copy in copies:
            copy.wait()
    total = gram_ref[...]
    for first in range(0, sizes[-1], GRAM_ROWS):
        data = stacked([pixels[-1].at[group] for group in range(groups)], first, GRAM_ROWS)
        total = total + dot_nt(data, data)
    gram = jnp.zeros((size, size), F32)
    for i in range(GRAM_ROWS):
        gram = gram + total[i * size : (i + 1) * size, i * size : (i + 1) * size]
    inverse, frob_norm = newton_schulz(gram)
    factor = shrink_ref[0] * jnp.sqrt(all_rows * side_len / frob_norm)
    select = (iota((own, size), 0) == iota((own, size), 1)).astype(F32)
    weights = dot_nt(select, inverse, HIGHEST) * factor
    spread = POLAR_ROWS * own
    wide = POLAR_ROWS * size
    repeat = (iota((spread, own), 0) // POLAR_ROWS == iota((spread, own), 1)).astype(BF16)
    weights = dot_nn(repeat, weights.astype(BF16)).astype(BF16)
    repeat = (iota((size, wide), 1) % size == iota((size, wide), 0)).astype(BF16)
    weights = dot_nn(weights, repeat)
    keep = iota((spread, wide), 0) % POLAR_ROWS == iota((spread, wide), 1) // size
    weights = jnp.where(keep, weights, 0.0).astype(BF16)

    out_copies = []
    for place, (chunk, row) in enumerate(blocks):
        if place >= last_blocks:
            for copy in pixel_copies[place]:
                copy.wait()
        moved_copies[place].wait()
        for first in range(row, row + EDGE_ROWS, POLAR_ROWS):
            data = stacked([pixels[chunk].at[group] for group in range(groups)], first, POLAR_ROWS)
            polar = dot_nn(weights, data).reshape(own, POLAR_ROWS, side_len)
            into = starts[chunk] + first
            moved[:, into : into + POLAR_ROWS] -= polar
        part = pl.ds(starts[chunk] + row, EDGE_ROWS)
        copy = pltpu.make_async_copy(moved.at[:, part], out_hbm.at[:, part], out_sems.at[place])
        copy.start()
        out_copies.append(copy)
    for copy in out_copies:
        copy.wait()


def polar_step(shrinkage, gram, moved, gathered, starts, sizes):
    chunks = len(gathered)
    groups = len(gathered[0])
    chans, _, side_len = moved[0].shape
    shape = (chans, sum(sizes), side_len)
    blocks = sum(sizes) // EDGE_ROWS
    flat = [piece for pieces in gathered for piece in pieces]
    return pl.pallas_call(
        functools.partial(polar_body, starts, sizes, groups),
        in_specs=[SMEM, pl.BlockSpec(memory_space=pltpu.VMEM)] + [ANY] * (chunks + len(flat)),
        out_specs=ANY,
        out_shape=jax.ShapeDtypeStruct(shape, F32),
        scratch_shapes=[
            pltpu.VMEM(shape, F32),
            pltpu.SemaphoreType.DMA((blocks, groups)),
            pltpu.SemaphoreType.DMA((blocks,)),
            pltpu.SemaphoreType.DMA((blocks,)),
        ]
        + [pltpu.VMEM((groups,) + pieces[0].shape, BF16) for pieces in gathered],
        compiler_params=kernel_params(60),
        cost_estimate=COST,
        name="polar_step",
    )(shrinkage, gram, *moved, *flat)


def neighbour_rows(model_image, reach):
    ends = lax.axis_size("strip") - 1
    head, tail = lax.optimization_barrier((model_image[:, :reach], model_image[:, model_image.shape[1] - reach :]))
    before = lax.ppermute(tail.astype(BF16), "strip", [(i, i + 1) for i in range(ends)])
    after = lax.ppermute(head.astype(BF16), "strip", [(i + 1, i) for i in range(ends)])
    return jnp.concatenate([before, after], axis=1)


def swap(value, axis, bits):
    count = lax.axis_size(axis)
    return lax.ppermute(value, axis, [(i, i ^ bits) for i in range(count)])


def gather_channels(pixels, after):
    devices = lax.axis_size("chan")
    kept = [pixels] + [gate(swap(pixels, "chan", bits), after) for bits in range(2, devices, 2)]
    if devices == 1:
        return kept
    return kept + [swap(piece, "chan", 1) for piece in kept]


def exchange(pieces):
    half = len(pieces) // 2
    order = list(range(half, len(pieces))) + list(range(1, half))
    arrived = {k: swap(pieces[k], "strip", k) for k in order}
    return [pieces[0]] + [arrived[k] for k in range(1, len(pieces))]


def local(grid, model_image, step_size, highpass, shrinkage):
    chans, own_rows, side_len = model_image.shape
    strips = lax.axis_size("strip")
    size = chans * lax.axis_size("chan")
    starts, sizes = chunk_rows(own_rows)
    chunks = len(sizes)
    strip = lax.axis_index("strip").astype(jnp.int32).reshape(1)

    cosine, sine_table = make_tables(side_len)
    split = np.stack([cosine.reshape(strips, own_rows, side_len), sine_table.reshape(strips, own_rows, side_len)])
    tables = [
        np.ascontiguousarray(split[:, :, start : start + rows]).reshape(2 * strips * rows, side_len)
        for start, rows in zip(starts, sizes)
    ]

    levels, taps = highpass.shape
    reach = (taps - 1) * 2 ** (levels - 1)
    edges = neighbour_rows(model_image, reach)

    halves = {}
    moved = {}
    gathered = {}
    pixels = {}
    state = dict(last=strip, gram=jnp.zeros((GRAM_ROWS * size, GRAM_ROWS * size), F32), bases=None)

    def first(chunk):
        if chunk == 2:
            sent, state["last"] = first_pieces(strip, tables[chunk], grid, strips, state["last"])
            halves[chunk] = exchange(sent)
        else:
            sent, state["last"] = first_transform(tables[chunk], grid, strips, state["last"])
            halves[chunk] = lax.all_to_all(sent, "strip", split_axis=0, concat_axis=0, tiled=True)

    def base():
        state["bases"] = base_step(
            strip, strips, step_size, highpass, model_image, edges, starts, sizes, state["last"]
        )
        state["last"] = state["bases"][0]

    def second(chunk):
        inputs = (step_size, halves[chunk], cosine, sine_table, state["bases"][chunk], state["last"])
        if chunk == 2:
            moved[chunk], pixels[chunk] = second_pieces(strip, *inputs)
        else:
            moved[chunk], pixels[chunk] = second_transform(*inputs)
        state["last"] = pixels[chunk]

    def gather(chunk):
        pieces = gather_channels(pixels[chunk], state["last"])
        if chans % 16:
            pieces = [jnp.concatenate(pieces, axis=1)]
        gathered[chunk] = pieces

    def gram(chunk):
        state["gram"] = gram_step(gathered[chunk], state["gram"], state["last"])
        state["last"] = state["gram"]

    first(0)
    first(1)
    first(2)
    base()
    second(0)
    first(3)
    gather(0)
    second(2)
    gram(0)
    gather(2)
    second(1)
    gram(2)
    second(3)
    gather(1)
    gram(1)
    gather(3)
    order = range(chunks)
    return polar_step(
        shrinkage, state["gram"], [moved[k] for k in order], [gathered[k] for k in order], starts, sizes
    )


def solution(mesh):
    return jax.shard_map(
        local,
        mesh=mesh,
        in_specs=(
            P(None, "chan", "strip", None),
            P("chan", "strip", None),
            P("chan"),
            P(),
            P("strip"),
        ),
        out_specs=P("chan", "strip", None),
        check_vma=False,
    )
```

```python
import functools

import jax
import jax.numpy as jnp
import ml_dtypes
import numpy as np
from jax import lax
from jax.experimental import pallas as pl
from jax.experimental.pallas import tpu as pltpu
from jax.sharding import PartitionSpec as P

NS_ITERS = 5
EDGE_ROWS = 16
GRAM_ROWS = 4
POLAR_ROWS = 8
HIGHEST = lax.Precision.HIGHEST
F32 = jnp.float32
BF16 = jnp.bfloat16
MIB = 1 << 20

ANY = pl.BlockSpec(memory_space=pl.ANY)
SMEM = pl.BlockSpec(memory_space=pltpu.SMEM)


def kernel_params(mebibytes):
    return pltpu.CompilerParams(vmem_limit_bytes=mebibytes * MIB)


COST = pl.CostEstimate(flops=0, bytes_accessed=1 << 16, transcendentals=0)


def dot_nt(a, b, precision=None):
    return lax.dot_general(
        a, b, (((1,), (1,)), ((), ())), precision=precision, preferred_element_type=F32
    )


def dot_nn(a, b, precision=None):
    return lax.dot_general(
        a, b, (((1,), (0,)), ((), ())), precision=precision, preferred_element_type=F32
    )


def iota(shape, dim):
    return lax.broadcasted_iota(jnp.int32, shape, dim)


def make_tables(side_len):
    indices = np.arange(side_len, dtype=np.int64)
    phases = (np.outer(indices, indices) % side_len).astype(np.float32) * np.float32(
        2.0 * 3.141592653589793 / side_len
    )
    unit_scale = np.float32(float(side_len) ** (-0.5))
    cosine = (np.cos(phases) * unit_scale).astype(ml_dtypes.bfloat16)
    sine_table = (np.sin(phases) * unit_scale).astype(ml_dtypes.bfloat16)
    return cosine, sine_table


def chunk_rows(own_rows):
    quarter = own_rows // 4
    sizes = [own_rows - 2 * quarter - EDGE_ROWS, quarter, quarter, EDGE_ROWS]
    return [sum(sizes[:place]) for place in range(len(sizes))], sizes


def gate_body(value_ref, after_ref, out_ref):
    pass


def gate(value, after):
    return pl.pallas_call(
        gate_body,
        in_specs=[ANY, ANY],
        out_specs=ANY,
        out_shape=jax.ShapeDtypeStruct(value.shape, value.dtype),
        input_output_aliases={0: 0},
        cost_estimate=COST,
        name="gate",
    )(value, after)


def first_body(table_ref, grid_ref, after_ref, out_ref, token_ref):
    token_ref[...] = jnp.zeros(token_ref.shape, F32)
    strips, _, chans, rows, width = out_ref.shape
    side_len = table_ref.shape[-1]
    table = table_ref[...]
    middle = strips * rows
    turned = jnp.concatenate([-table[middle:], table[:middle]], axis=0)
    total = dot_nt(table, grid_ref[0].reshape(chans * width, side_len))
    total = total + dot_nt(turned, grid_ref[1].reshape(chans * width, side_len))
    total = total.astype(BF16)
    for part in range(2):
        for strip in range(strips):
            first = (part * strips + strip) * rows
            for chan in range(chans):
                out_ref[strip, part, chan] = total[first : first + rows, chan * width : (chan + 1) * width]


def first_transform(table, grid, strips, after):
    _, chans, width, side_len = grid.shape
    rows = table.shape[0] // (2 * strips)
    shape = (strips, 2, chans, rows, width)
    if width % 128 or rows % 16:
        middle = strips * rows
        turned = jnp.concatenate([-table[middle:], table[:middle]], axis=0)
        total = jnp.einsum("mv,cuv->mcu", table, grid[0], preferred_element_type=F32)
        total = total + jnp.einsum("mv,cuv->mcu", turned, grid[1], preferred_element_type=F32)
        total = total.astype(BF16).reshape(2, strips, rows, chans, width)
        return total.transpose(1, 0, 3, 2, 4), jnp.zeros((8, 128), F32)
    block = 4 if chans % 4 == 0 else 1
    return pl.pallas_call(
        first_body,
        grid=(chans // block,),
        in_specs=[
            pl.BlockSpec(table.shape, lambda i: (0, 0)),
            pl.BlockSpec((2, block, width, side_len), lambda i: (0, i, 0, 0)),
            ANY,
        ],
        out_specs=[
            pl.BlockSpec((strips, 2, block, rows, width), lambda i: (0, 0, i, 0, 0)),
            pl.BlockSpec((8, 128), lambda i: (0, 0)),
        ],
        out_shape=[jax.ShapeDtypeStruct(shape, BF16), jax.ShapeDtypeStruct((8, 128), F32)],
        compiler_params=kernel_params(60),
        cost_estimate=COST,
        name="first_transform",
    )(table, grid, after)


def pieces_body(strips, strip_ref, table_ref, grid_ref, after_ref, *refs):
    out_refs = refs[:strips]
    refs[strips][...] = jnp.zeros(refs[strips].shape, F32)
    _, chans, rows, width = out_refs[0].shape
    side_len = table_ref.shape[-1]
    cosine = jnp.concatenate([table_ref[0, strip_ref[0] ^ k] for k in range(strips)], axis=0)
    sine_table = jnp.concatenate([table_ref[1, strip_ref[0] ^ k] for k in range(strips)], axis=0)
    total = dot_nt(jnp.concatenate([cosine, sine_table], axis=0), grid_ref[0].reshape(chans * width, side_len))
    total = total + dot_nt(
        jnp.concatenate([-sine_table, cosine], axis=0), grid_ref[1].reshape(chans * width, side_len)
    )
    total = total.astype(BF16)
    for part in range(2):
        for k in range(strips):
            first = (part * strips + k) * rows
            for chan in range(chans):
                out_refs[k][part, chan] = total[first : first + rows, chan * width : (chan + 1) * width]


def first_pieces(strip, table, grid, strips, after):
    _, chans, width, side_len = grid.shape
    rows = table.shape[0] // (2 * strips)
    table = table.reshape(2, strips, rows, side_len)
    if width % 128 or rows % 16:
        order = strip[0] ^ jnp.arange(strips, dtype=jnp.int32)
        cosine, sine_table = (jnp.take(table[part], order, axis=0) for part in range(2))

        def product(table, part):
            return jnp.einsum("kmv,cuv->kcmu", table, part, preferred_element_type=F32)

        real = product(cosine, grid[0]) - product(sine_table, grid[1])
        imag = product(sine_table, grid[0]) + product(cosine, grid[1])
        both = jnp.stack([real, imag], axis=1).astype(BF16)
        return [both[k] for k in range(strips)], jnp.zeros((8, 128), F32)
    block = 4 if chans % 4 == 0 else 1
    results = pl.pallas_call(
        functools.partial(pieces_body, strips),
        grid=(chans // block,),
        in_specs=[
            SMEM,
            pl.BlockSpec(table.shape, lambda i: (0, 0, 0, 0)),
            pl.BlockSpec((2, block, width, side_len), lambda i: (0, i, 0, 0)),
            ANY,
        ],
        out_specs=[pl.BlockSpec((2, block, rows, width), lambda i: (0, i, 0, 0))] * strips
        + [pl.BlockSpec((8, 128), lambda i: (0, 0))],
        out_shape=[jax.ShapeDtypeStruct((2, chans, rows, width), BF16)] * strips
        + [jax.ShapeDtypeStruct((8, 128), F32)],
        compiler_params=kernel_params(60),
        cost_estimate=COST,
        name="first_pieces",
    )(strip, table, grid, after)
    return results[:strips], results[strips]


def band_matrix(taps_of, levels, taps, own_rows, reach, first_row, image_rows):
    half_taps = taps // 2
    shape = (own_rows, own_rows + 2 * reach)
    row = iota(shape, 0)
    column = iota(shape, 1)
    place = jnp.where(
        column < own_rows, column, jnp.where(column < own_rows + reach, column - own_rows - reach, column - reach)
    )
    total = jnp.zeros(shape, F32)
    for level in range(levels):
        dilation = 2**level
        for outer in range(taps):
            detail_row = row - (outer - half_taps) * dilation
            inside = (detail_row + first_row >= 0) & (detail_row + first_row < image_rows)
            for inner in range(taps):
                hit = inside & (place == detail_row + (inner - half_taps) * dilation)
                total = total + jnp.where(hit, taps_of(level, outer) * taps_of(level, inner), 0.0)
    return total


def base_body(levels, taps, starts, strips, strip_ref, step_ref, highpass_ref, model_ref, edge_ref, after_ref, *refs):
    high, low = refs[-2:]
    out_refs = refs[:-2]
    block, own_rows, side_len = model_ref.shape
    reach = edge_ref.shape[1] // 2

    @pl.when(pl.program_id(0) == 0)
    def _():
        band = band_matrix(
            lambda level, tap: highpass_ref[level, tap],
            levels,
            taps,
            own_rows,
            reach,
            strip_ref[0] * own_rows,
            strips * own_rows,
        )
        top = band.astype(BF16)
        high[...] = top
        low[...] = (band - top.astype(F32)).astype(BF16)

    first = pl.program_id(0) * block
    for chan in range(block):
        model = model_ref[chan]
        top = model.astype(BF16)
        rest = (model - top.astype(F32)).astype(BF16)
        edge = edge_ref[chan].astype(F32)
        whole = jnp.concatenate([top.astype(F32), edge], axis=0).astype(BF16)
        gradient = dot_nn(high[...], whole)
        gradient = gradient + dot_nn(low[...], whole)
        gradient = gradient + dot_nn(high[:, :own_rows], rest)
        base = model - step_ref[first + chan] * gradient
        for start, out_ref in zip(starts, out_refs):
            out_ref[chan] = base[start : start + out_ref.shape[1]]


def base_step(strip, strips, step_size, highpass, model_image, edges, starts, sizes, after):
    chans, rows, side_len = model_image.shape
    levels, taps = highpass.shape
    reach = edges.shape[1] // 2
    block = 2 if chans % 2 == 0 else 1
    wide = rows + 2 * reach
    return pl.pallas_call(
        functools.partial(base_body, levels, taps, starts, strips),
        grid=(chans // block,),
        in_specs=[
            SMEM,
            SMEM,
            SMEM,
            pl.BlockSpec((block, rows, side_len), lambda i: (i, 0, 0)),
            pl.BlockSpec((block, 2 * reach, side_len), lambda i: (i, 0, 0)),
            ANY,
        ],
        out_specs=[pl.BlockSpec((block, part, side_len), lambda i: (i, 0, 0)) for part in sizes],
        out_shape=[jax.ShapeDtypeStruct((chans, part, side_len), F32) for part in sizes],
        scratch_shapes=[pltpu.VMEM((rows, wide), BF16), pltpu.VMEM((rows, wide), BF16)],
        compiler_params=kernel_params(60),
        cost_estimate=COST,
        name="base_step",
    )(strip, step_size, highpass, model_image, edges, after)


def second_body(step_ref, half_ref, cosine_ref, sine_ref, base_ref, after_ref, moved_ref, pixels_ref):
    strips, _, chans, rows, width = half_ref.shape
    real = jnp.concatenate([half_ref[s, 0].reshape(chans * rows, width) for s in range(strips)], axis=1)
    imag = jnp.concatenate([half_ref[s, 1].reshape(chans * rows, width) for s in range(strips)], axis=1)
    dirty = dot_nn(real, cosine_ref[...]) - dot_nn(imag, sine_ref[...])
    pieces = []
    for chan in range(chans):
        moved = base_ref[chan] + step_ref[chan] * dirty[chan * rows : (chan + 1) * rows]
        moved_ref[chan] = moved
        pieces.append(moved)
    pixels_ref[...] = jnp.swapaxes(jnp.stack(pieces), 0, 1).astype(BF16)


def second_transform(step_size, half, cosine, sine_table, base, after):
    strips, _, chans, rows, width = half.shape
    side_len = cosine.shape[0]
    if width % 128 or rows % 16 or chans % 16:
        split = (strips, width, side_len)
        dirty = jnp.einsum("scmu,sul->cml", half[:, 0], cosine.reshape(split), preferred_element_type=F32)
        dirty = dirty - jnp.einsum("scmu,sul->cml", half[:, 1], sine_table.reshape(split), preferred_element_type=F32)
        moved = base + step_size[:, None, None] * dirty
        return moved, moved.astype(BF16).transpose(1, 0, 2)
    block = min(256, side_len)
    return pl.pallas_call(
        second_body,
        grid=(side_len // block,),
        in_specs=[
            SMEM,
            pl.BlockSpec(half.shape, lambda i: (0, 0, 0, 0, 0)),
            pl.BlockSpec((side_len, block), lambda i: (0, i)),
            pl.BlockSpec((side_len, block), lambda i: (0, i)),
            pl.BlockSpec((chans, rows, block), lambda i: (0, 0, i)),
            ANY,
        ],
        out_specs=[
            pl.BlockSpec((chans, rows, block), lambda i: (0, 0, i)),
            pl.BlockSpec((rows, chans, block), lambda i: (0, 0, i)),
        ],
        out_shape=[
            jax.ShapeDtypeStruct(base.shape, F32),
            jax.ShapeDtypeStruct((rows, chans, side_len), BF16),
        ],
        compiler_params=kernel_params(60),
        cost_estimate=COST,
        name="second_transform",
    )(step_size, half, cosine, sine_table, base, after)


def second_pieces_body(strips, strip_ref, step_ref, cosine_ref, sine_ref, base_ref, after_ref, *refs):
    halves = refs[:strips]
    moved_ref, pixels_ref = refs[strips:]
    _, chans, rows, width = halves[0].shape
    real = jnp.concatenate([half[0].reshape(chans * rows, width) for half in halves], axis=1)
    imag = jnp.concatenate([half[1].reshape(chans * rows, width) for half in halves], axis=1)

    def ordered(table_ref):
        parts = [table_ref[pl.ds(pl.multiple_of((strip_ref[0] ^ k) * width, width), width), :] for k in range(strips)]
        return jnp.concatenate(parts, axis=0)

    dirty = dot_nn(real, ordered(cosine_ref)) - dot_nn(imag, ordered(sine_ref))
    pieces = []
    for chan in range(chans):
        moved = base_ref[chan] + step_ref[chan] * dirty[chan * rows : (chan + 1) * rows]
        moved_ref[chan] = moved
        pieces.append(moved)
    pixels_ref[...] = jnp.swapaxes(jnp.stack(pieces), 0, 1).astype(BF16)


def second_pieces(strip, step_size, halves, cosine, sine_table, base, after):
    strips = len(halves)
    _, chans, rows, width = halves[0].shape
    side_len = cosine.shape[0]
    if width % 128 or rows % 16 or chans % 16:
        order = strip[0] ^ jnp.arange(strips, dtype=jnp.int32)
        both = jnp.stack(halves)

        def product(part, table):
            parts = jnp.take(jnp.asarray(table).reshape(strips, width, side_len), order, axis=0)
            return jnp.einsum("kcmu,kul->cml", part, parts, preferred_element_type=F32)

        moved = base + step_size[:, None, None] * (product(both[:, 0], cosine) - product(both[:, 1], sine_table))
        return moved, moved.astype(BF16).transpose(1, 0, 2)
    block = min(256, side_len)
    half_spec = pl.BlockSpec(halves[0].shape, lambda i: (0, 0, 0, 0))
    return pl.pallas_call(
        functools.partial(second_pieces_body, strips),
        grid=(side_len // block,),
        in_specs=[
            SMEM,
            SMEM,
            pl.BlockSpec((side_len, block), lambda i: (0, i)),
            pl.BlockSpec((side_len, block), lambda i: (0, i)),
            pl.BlockSpec((chans, rows, block), lambda i: (0, 0, i)),
            ANY,
        ]
        + [half_spec] * strips,
        out_specs=[
            pl.BlockSpec((chans, rows, block), lambda i: (0, 0, i)),
            pl.BlockSpec((rows, chans, block), lambda i: (0, 0, i)),
        ],
        out_shape=[
            jax.ShapeDtypeStruct(base.shape, F32),
            jax.ShapeDtypeStruct((rows, chans, side_len), BF16),
        ],
        compiler_params=kernel_params(60),
        cost_estimate=COST,
        name="second_pieces",
    )(strip, step_size, cosine, sine_table, base, after, *halves)


def stacked(group_refs, first, count):
    return jnp.concatenate([ref[first + i] for i in range(count) for ref in group_refs], axis=0)


def gram_body(groups, before_ref, after_ref, *refs):
    total_ref = refs[groups]

    @pl.when(pl.program_id(0) == 0)
    def _():
        total_ref[...] = before_ref[...]

    total = total_ref[...]
    for first in range(0, refs[0].shape[0], GRAM_ROWS):
        pixels = stacked(refs[:groups], first, GRAM_ROWS)
        total = total + dot_nt(pixels, pixels)
    total_ref[...] = total


def gram_step(pieces, before, after):
    rows, chans, side_len = pieces[0].shape
    block = EDGE_ROWS // 2
    spec = pl.BlockSpec((block, chans, side_len), lambda i: (i, 0, 0))
    return pl.pallas_call(
        functools.partial(gram_body, len(pieces)),
        grid=(rows // block,),
        in_specs=[pl.BlockSpec(before.shape, lambda i: (0, 0)), ANY] + [spec] * len(pieces),
        out_specs=pl.BlockSpec(before.shape, lambda i: (0, 0)),
        out_shape=jax.ShapeDtypeStruct(before.shape, F32),
        compiler_params=kernel_params(60),
        cost_estimate=COST,
        name="gram_step",
    )(before, after, *pieces)


def newton_schulz(gram):
    size = gram.shape[0]
    frob_norm = jnp.sqrt(jnp.sum(gram * gram))
    identity = (iota((size, size), 0) == iota((size, size), 1)).astype(F32)
    current = gram / frob_norm
    middle = 0.5 * (3.0 * identity - current)
    inverse = middle
    for iteration in range(1, NS_ITERS):
        current = dot_nn(current, middle, HIGHEST)
        middle = 0.5 * (3.0 * identity - dot_nn(inverse, current, HIGHEST))
        inverse = dot_nn(middle, inverse, HIGHEST)
    return inverse, frob_norm


def polar_body(starts, sizes, groups, shrink_ref, gram_ref, *refs):
    chunks = len(sizes)
    moved_hbm = refs[:chunks]
    pixels_hbm = refs[chunks : chunks * (groups + 1)]
    out_hbm, moved, pixel_sems, moved_sems, out_sems = refs[chunks * (groups + 1) : chunks * (groups + 1) + 5]
    pixels = refs[chunks * (groups + 1) + 5 :]
    own, all_rows, side_len = moved.shape
    size = pixels[0].shape[2] * groups

    blocks = [
        (chunk, row) for chunk in [chunks - 1] + list(range(chunks - 1)) for row in range(0, sizes[chunk], EDGE_ROWS)
    ]
    pixel_copies = []
    moved_copies = []
    for place, (chunk, row) in enumerate(blocks):
        part = pl.ds(row, EDGE_ROWS)
        into = pl.ds(starts[chunk] + row, EDGE_ROWS)
        copies = [
            pltpu.make_async_copy(
                pixels_hbm[chunk * groups + group].at[part], pixels[chunk].at[group, part], pixel_sems.at[place, group]
            )
            for group in range(groups)
        ]
        pixel_copies.append(copies)
        moved_copies.append(
            pltpu.make_async_copy(moved_hbm[chunk].at[:, part], moved.at[:, into], moved_sems.at[place])
        )
        for copy in copies + moved_copies[-1:]:
            copy.start()

    last_blocks = sizes[-1] // EDGE_ROWS
    for copies in pixel_copies[:last_blocks]:
        for copy in copies:
            copy.wait()
    total = gram_ref[...]
    for first in range(0, sizes[-1], GRAM_ROWS):
        data = stacked([pixels[-1].at[group] for group in range(groups)], first, GRAM_ROWS)
        total = total + dot_nt(data, data)
    gram = jnp.zeros((size, size), F32)
    for i in range(GRAM_ROWS):
        gram = gram + total[i * size : (i + 1) * size, i * size : (i + 1) * size]
    inverse, frob_norm = newton_schulz(gram)
    factor = shrink_ref[0] * jnp.sqrt(all_rows * side_len / frob_norm)
    select = (iota((own, size), 0) == iota((own, size), 1)).astype(F32)
    weights = dot_nt(select, inverse, HIGHEST) * factor
    spread = POLAR_ROWS * own
    wide = POLAR_ROWS * size
    repeat = (iota((spread, own), 0) // POLAR_ROWS == iota((spread, own), 1)).astype(BF16)
    weights = dot_nn(repeat, weights.astype(BF16)).astype(BF16)
    repeat = (iota((size, wide), 1) % size == iota((size, wide), 0)).astype(BF16)
    weights = dot_nn(weights, repeat)
    keep = iota((spread, wide), 0) % POLAR_ROWS == iota((spread, wide), 1) // size
    weights = jnp.where(keep, weights, 0.0).astype(BF16)

    out_copies = []
    for place, (chunk, row) in enumerate(blocks):
        if place >= last_blocks:
            for copy in pixel_copies[place]:
                copy.wait()
        moved_copies[place].wait()
        for first in range(row, row + EDGE_ROWS, POLAR_ROWS):
            data = stacked([pixels[chunk].at[group] for group in range(groups)], first, POLAR_ROWS)
            polar = dot_nn(weights, data).reshape(own, POLAR_ROWS, side_len)
            into = starts[chunk] + first
            moved[:, into : into + POLAR_ROWS] -= polar
        part = pl.ds(starts[chunk] + row, EDGE_ROWS)
        copy = pltpu.make_async_copy(moved.at[:, part], out_hbm.at[:, part], out_sems.at[place])
        copy.start()
        out_copies.append(copy)
    for copy in out_copies:
        copy.wait()


def polar_step(shrinkage, gram, moved, gathered, starts, sizes):
    chunks = len(gathered)
    groups = len(gathered[0])
    chans, _, side_len = moved[0].shape
    shape = (chans, sum(sizes), side_len)
    blocks = sum(sizes) // EDGE_ROWS
    flat = [piece for pieces in gathered for piece in pieces]
    return pl.pallas_call(
        functools.partial(polar_body, starts, sizes, groups),
        in_specs=[SMEM, pl.BlockSpec(memory_space=pltpu.VMEM)] + [ANY] * (chunks + len(flat)),
        out_specs=ANY,
        out_shape=jax.ShapeDtypeStruct(shape, F32),
        scratch_shapes=[
            pltpu.VMEM(shape, F32),
            pltpu.SemaphoreType.DMA((blocks, groups)),
            pltpu.SemaphoreType.DMA((blocks,)),
            pltpu.SemaphoreType.DMA((blocks,)),
        ]
        + [pltpu.VMEM((groups,) + pieces[0].shape, BF16) for pieces in gathered],
        compiler_params=kernel_params(60),
        cost_estimate=COST,
        name="polar_step",
    )(shrinkage, gram, *moved, *flat)


def neighbour_rows(model_image, reach):
    ends = lax.axis_size("strip") - 1
    head, tail = lax.optimization_barrier((model_image[:, :reach], model_image[:, model_image.shape[1] - reach :]))
    before = lax.ppermute(tail.astype(BF16), "strip", [(i, i + 1) for i in range(ends)])
    after = lax.ppermute(head.astype(BF16), "strip", [(i + 1, i) for i in range(ends)])
    return jnp.concatenate([before, after], axis=1)


def swap(value, axis, bits):
    count = lax.axis_size(axis)
    return lax.ppermute(value, axis, [(i, i ^ bits) for i in range(count)])


def gather_channels(pixels, after):
    devices = lax.axis_size("chan")
    kept = [pixels] + [gate(swap(pixels, "chan", bits), after) for bits in range(2, devices, 2)]
    if devices == 1:
        return kept
    return kept + [swap(piece, "chan", 1) for piece in kept]


def exchange(pieces):
    half = len(pieces) // 2
    order = list(range(half, len(pieces))) + list(range(1, half))
    arrived = {k: swap(pieces[k], "strip", k) for k in order}
    return [pieces[0]] + [arrived[k] for k in range(1, len(pieces))]


def local(grid, model_image, step_size, highpass, shrinkage):
    chans, own_rows, side_len = model_image.shape
    strips = lax.axis_size("strip")
    size = chans * lax.axis_size("chan")
    starts, sizes = chunk_rows(own_rows)
    chunks = len(sizes)
    strip = lax.axis_index("strip").astype(jnp.int32).reshape(1)

    cosine, sine_table = make_tables(side_len)
    split = np.stack([cosine.reshape(strips, own_rows, side_len), sine_table.reshape(strips, own_rows, side_len)])
    tables = [
        np.ascontiguousarray(split[:, :, start : start + rows]).reshape(2 * strips * rows, side_len)
        for start, rows in zip(starts, sizes)
    ]

    levels, taps = highpass.shape
    reach = (taps - 1) * 2 ** (levels - 1)
    edges = neighbour_rows(model_image, reach)

    halves = {}
    moved = {}
    gathered = {}
    pixels = {}
    state = dict(last=strip, gram=jnp.zeros((GRAM_ROWS * size, GRAM_ROWS * size), F32), bases=None)

    def first(chunk):
        if chunk == 1:
            sent, state["last"] = first_pieces(strip, tables[chunk], grid, strips, state["last"])
            halves[chunk] = exchange(sent)
        else:
            sent, state["last"] = first_transform(tables[chunk], grid, strips, state["last"])
            if chunk == 2:
                for piece in [edges] + halves[1][1:]:
                    sent = gate(sent, piece)
            halves[chunk] = lax.all_to_all(sent, "strip", split_axis=0, concat_axis=0, tiled=True)

    def base():
        state["bases"] = base_step(
            strip, strips, step_size, highpass, model_image, edges, starts, sizes, state["last"]
        )
        state["last"] = state["bases"][0]

    def second(chunk):
        inputs = (step_size, halves[chunk], cosine, sine_table, state["bases"][chunk], state["last"])
        if chunk == 1:
            moved[chunk], pixels[chunk] = second_pieces(strip, *inputs)
        else:
            moved[chunk], pixels[chunk] = second_transform(*inputs)
        state["last"] = pixels[chunk]

    def gather(chunk):
        pieces = gather_channels(pixels[chunk], state["last"])
        if chans % 16:
            pieces = [jnp.concatenate(pieces, axis=1)]
        gathered[chunk] = pieces

    def gram(chunk):
        state["gram"] = gram_step(gathered[chunk], state["gram"], state["last"])
        state["last"] = state["gram"]

    first(0)
    first(1)
    first(2)
    base()
    second(1)
    second(0)
    gather(1)
    first(3)
    gather(0)
    gram(1)
    second(2)
    gram(0)
    second(3)
    gather(2)
    gram(2)
    gather(3)
    order = range(chunks)
    return polar_step(
        shrinkage, state["gram"], [moved[k] for k in order], [gathered[k] for k in order], starts, sizes
    )


def solution(mesh):
    return jax.shard_map(
        local,
        mesh=mesh,
        in_specs=(
            P(None, "chan", "strip", None),
            P("chan", "strip", None),
            P("chan"),
            P(),
            P("strip"),
        ),
        out_specs=P("chan", "strip", None),
        check_vma=False,
    )
```

```python
import functools

import jax
import jax.numpy as jnp
import ml_dtypes
import numpy as np
from jax import lax
from jax.experimental import pallas as pl
from jax.experimental.pallas import tpu as pltpu
from jax.sharding import PartitionSpec as P

NS_ITERS = 5
EDGE_ROWS = 16
GRAM_ROWS = 4
POLAR_ROWS = 8
HIGHEST = lax.Precision.HIGHEST
F32 = jnp.float32
BF16 = jnp.bfloat16
MIB = 1 << 20

ANY = pl.BlockSpec(memory_space=pl.ANY)
SMEM = pl.BlockSpec(memory_space=pltpu.SMEM)


def kernel_params(mebibytes):
    return pltpu.CompilerParams(vmem_limit_bytes=mebibytes * MIB)


COST = pl.CostEstimate(flops=0, bytes_accessed=1 << 16, transcendentals=0)


def dot_nt(a, b, precision=None):
    return lax.dot_general(
        a, b, (((1,), (1,)), ((), ())), precision=precision, preferred_element_type=F32
    )


def dot_nn(a, b, precision=None):
    return lax.dot_general(
        a, b, (((1,), (0,)), ((), ())), precision=precision, preferred_element_type=F32
    )


def iota(shape, dim):
    return lax.broadcasted_iota(jnp.int32, shape, dim)


def make_tables(side_len):
    indices = np.arange(side_len, dtype=np.int64)
    phases = (np.outer(indices, indices) % side_len).astype(np.float32) * np.float32(
        2.0 * 3.141592653589793 / side_len
    )
    unit_scale = np.float32(float(side_len) ** (-0.5))
    cosine = (np.cos(phases) * unit_scale).astype(ml_dtypes.bfloat16)
    sine_table = (np.sin(phases) * unit_scale).astype(ml_dtypes.bfloat16)
    return cosine, sine_table


def chunk_rows(own_rows):
    quarter = own_rows // 4
    sizes = [quarter, own_rows - 2 * quarter - EDGE_ROWS, quarter, EDGE_ROWS]
    sizes = [size for size in sizes if size > 0]
    return [sum(sizes[:place]) for place in range(len(sizes))], sizes


def gate_body(value_ref, after_ref, out_ref):
    pass


def gate(value, after):
    return pl.pallas_call(
        gate_body,
        in_specs=[ANY, ANY],
        out_specs=ANY,
        out_shape=jax.ShapeDtypeStruct(value.shape, value.dtype),
        input_output_aliases={0: 0},
        compiler_params=kernel_params(63),
        cost_estimate=COST,
        name="gate",
    )(value, after)


def first_body(table_ref, grid_ref, after_ref, out_ref, token_ref):
    token_ref[...] = jnp.zeros(token_ref.shape, F32)
    strips, _, chans, rows, width = out_ref.shape
    side_len = table_ref.shape[-1]
    table = table_ref[...]
    middle = strips * rows
    turned = jnp.concatenate([-table[middle:], table[:middle]], axis=0)
    total = dot_nt(table, grid_ref[0].reshape(chans * width, side_len))
    total = total + dot_nt(turned, grid_ref[1].reshape(chans * width, side_len))
    total = total.astype(BF16)
    for part in range(2):
        for strip in range(strips):
            first = (part * strips + strip) * rows
            for chan in range(chans):
                out_ref[strip, part, chan] = total[first : first + rows, chan * width : (chan + 1) * width]


def first_transform(table, grid, strips, after):
    _, chans, width, side_len = grid.shape
    rows = table.shape[0] // (2 * strips)
    shape = (strips, 2, chans, rows, width)
    if width % 128 or rows % 16:
        middle = strips * rows
        turned = jnp.concatenate([-table[middle:], table[:middle]], axis=0)
        total = jnp.einsum("mv,cuv->mcu", table, grid[0], preferred_element_type=F32)
        total = total + jnp.einsum("mv,cuv->mcu", turned, grid[1], preferred_element_type=F32)
        total = total.astype(BF16).reshape(2, strips, rows, chans, width)
        return total.transpose(1, 0, 3, 2, 4), jnp.zeros((8, 128), F32)
    block = 2 if chans % 2 == 0 else 1
    return pl.pallas_call(
        first_body,
        grid=(chans // block,),
        in_specs=[
            pl.BlockSpec(table.shape, lambda i: (0, 0)),
            pl.BlockSpec((2, block, width, side_len), lambda i: (0, i, 0, 0)),
            ANY,
        ],
        out_specs=[
            pl.BlockSpec((strips, 2, block, rows, width), lambda i: (0, 0, i, 0, 0)),
            pl.BlockSpec((8, 128), lambda i: (0, 0)),
        ],
        out_shape=[jax.ShapeDtypeStruct(shape, BF16), jax.ShapeDtypeStruct((8, 128), F32)],
        compiler_params=kernel_params(63),
        cost_estimate=COST,
        name="first_transform",
    )(table, grid, after)


def band_matrix(taps_of, levels, taps, own_rows, reach, first_row, image_rows):
    half_taps = taps // 2
    shape = (own_rows, own_rows + 2 * reach)
    row = iota(shape, 0)
    column = iota(shape, 1)
    place = jnp.where(
        column < own_rows, column, jnp.where(column < own_rows + reach, column - own_rows - reach, column - reach)
    )
    total = jnp.zeros(shape, F32)
    for level in range(levels):
        dilation = 2**level
        for outer in range(taps):
            detail_row = row - (outer - half_taps) * dilation
            inside = (detail_row + first_row >= 0) & (detail_row + first_row < image_rows)
            for inner in range(taps):
                hit = inside & (place == detail_row + (inner - half_taps) * dilation)
                total = total + jnp.where(hit, taps_of(level, outer) * taps_of(level, inner), 0.0)
    return total


def base_body(levels, taps, starts, strips, strip_ref, step_ref, highpass_ref, model_ref, edge_ref, after_ref, *refs):
    high, low = refs[-2:]
    out_refs = refs[:-2]
    block, own_rows, side_len = model_ref.shape
    reach = edge_ref.shape[1] // 2

    @pl.when(pl.program_id(0) == 0)
    def _():
        band = band_matrix(
            lambda level, tap: highpass_ref[level, tap],
            levels,
            taps,
            own_rows,
            reach,
            strip_ref[0] * own_rows,
            strips * own_rows,
        )
        top = band.astype(BF16)
        high[...] = top
        low[...] = (band - top.astype(F32)).astype(BF16)

    first = pl.program_id(0) * block
    for chan in range(block):
        model = model_ref[chan]
        top = model.astype(BF16)
        rest = (model - top.astype(F32)).astype(BF16)
        edge = edge_ref[chan].astype(F32)
        whole = jnp.concatenate([top.astype(F32), edge], axis=0).astype(BF16)
        gradient = dot_nn(high[...], whole)
        gradient = gradient + dot_nn(low[...], whole)
        gradient = gradient + dot_nn(high[:, :own_rows], rest)
        base = model - step_ref[first + chan] * gradient
        for start, out_ref in zip(starts, out_refs):
            out_ref[chan] = base[start : start + out_ref.shape[1]]


def base_step(strip, strips, step_size, highpass, model_image, edges, starts, sizes, after):
    chans, rows, side_len = model_image.shape
    levels, taps = highpass.shape
    reach = edges.shape[1] // 2
    block = 2 if chans % 2 == 0 else 1
    wide = rows + 2 * reach
    return pl.pallas_call(
        functools.partial(base_body, levels, taps, starts, strips),
        grid=(chans // block,),
        in_specs=[
            SMEM,
            SMEM,
            SMEM,
            pl.BlockSpec((block, rows, side_len), lambda i: (i, 0, 0)),
            pl.BlockSpec((block, 2 * reach, side_len), lambda i: (i, 0, 0)),
            ANY,
        ],
        out_specs=[pl.BlockSpec((block, part, side_len), lambda i: (i, 0, 0)) for part in sizes],
        out_shape=[jax.ShapeDtypeStruct((chans, part, side_len), F32) for part in sizes],
        scratch_shapes=[pltpu.VMEM((rows, wide), BF16), pltpu.VMEM((rows, wide), BF16)],
        compiler_params=kernel_params(63),
        cost_estimate=COST,
        name="base_step",
    )(strip, step_size, highpass, model_image, edges, after)


def second_body(step_ref, half_ref, cosine_ref, sine_ref, base_ref, after_ref, moved_ref, pixels_ref):
    strips, _, chans, rows, width = half_ref.shape
    real = jnp.concatenate([half_ref[s, 0].reshape(chans * rows, width) for s in range(strips)], axis=1)
    imag = jnp.concatenate([half_ref[s, 1].reshape(chans * rows, width) for s in range(strips)], axis=1)
    dirty = dot_nn(real, cosine_ref[...]) - dot_nn(imag, sine_ref[...])
    pieces = []
    for chan in range(chans):
        moved = base_ref[chan] + step_ref[chan] * dirty[chan * rows : (chan + 1) * rows]
        moved_ref[chan] = moved
        pieces.append(moved)
    pixels_ref[...] = jnp.swapaxes(jnp.stack(pieces), 0, 1).astype(BF16)


def second_transform(step_size, half, cosine, sine_table, base, after):
    strips, _, chans, rows, width = half.shape
    side_len = cosine.shape[0]
    if width % 128 or rows % 16 or chans % 16:
        split = (strips, width, side_len)
        dirty = jnp.einsum("scmu,sul->cml", half[:, 0], cosine.reshape(split), preferred_element_type=F32)
        dirty = dirty - jnp.einsum("scmu,sul->cml", half[:, 1], sine_table.reshape(split), preferred_element_type=F32)
        moved = base + step_size[:, None, None] * dirty
        return moved, moved.astype(BF16).transpose(1, 0, 2)
    block = min(256, side_len)
    return pl.pallas_call(
        second_body,
        grid=(side_len // block,),
        in_specs=[
            SMEM,
            pl.BlockSpec(half.shape, lambda i: (0, 0, 0, 0, 0)),
            pl.BlockSpec((side_len, block), lambda i: (0, i)),
            pl.BlockSpec((side_len, block), lambda i: (0, i)),
            pl.BlockSpec((chans, rows, block), lambda i: (0, 0, i)),
            ANY,
        ],
        out_specs=[
            pl.BlockSpec((chans, rows, block), lambda i: (0, 0, i)),
            pl.BlockSpec((rows, chans, block), lambda i: (0, 0, i)),
        ],
        out_shape=[
            jax.ShapeDtypeStruct(base.shape, F32),
            jax.ShapeDtypeStruct((rows, chans, side_len), BF16),
        ],
        compiler_params=kernel_params(63),
        cost_estimate=COST,
        name="second_transform",
    )(step_size, half, cosine, sine_table, base, after)


def stacked(group_refs, first, count):
    return jnp.concatenate([ref[first + i] for i in range(count) for ref in group_refs], axis=0)


def gram_body(groups, before_ref, after_ref, *refs):
    total_ref = refs[groups]

    @pl.when(pl.program_id(0) == 0)
    def _():
        total_ref[...] = before_ref[...]

    total = total_ref[...]
    for first in range(0, refs[0].shape[0], GRAM_ROWS):
        pixels = stacked(refs[:groups], first, GRAM_ROWS)
        total = total + dot_nt(pixels, pixels)
    total_ref[...] = total


def gram_step(pieces, before, after):
    rows, chans, side_len = pieces[0].shape
    block = EDGE_ROWS // 2
    spec = pl.BlockSpec((block, chans, side_len), lambda i: (i, 0, 0))
    return pl.pallas_call(
        functools.partial(gram_body, len(pieces)),
        grid=(rows // block,),
        in_specs=[pl.BlockSpec(before.shape, lambda i: (0, 0)), ANY] + [spec] * len(pieces),
        out_specs=pl.BlockSpec(before.shape, lambda i: (0, 0)),
        out_shape=jax.ShapeDtypeStruct(before.shape, F32),
        compiler_params=kernel_params(63),
        cost_estimate=COST,
        name="gram_step",
    )(before, after, *pieces)


def newton_schulz(gram):
    size = gram.shape[0]
    frob_norm = jnp.sqrt(jnp.sum(gram * gram))
    identity = (iota((size, size), 0) == iota((size, size), 1)).astype(F32)
    current = gram / frob_norm
    middle = 0.5 * (3.0 * identity - current)
    inverse = middle
    for iteration in range(1, NS_ITERS):
        current = dot_nn(current, middle, HIGHEST)
        middle = 0.5 * (3.0 * identity - dot_nn(inverse, current, HIGHEST))
        inverse = dot_nn(middle, inverse, HIGHEST)
    return inverse, frob_norm


def polar_body(starts, sizes, groups, shrink_ref, gram_ref, *refs):
    chunks = len(sizes)
    moved_hbm = refs[:chunks]
    pixels_hbm = refs[chunks : chunks * (groups + 1)]
    out_hbm, moved, pixel_sems, moved_sems, out_sems = refs[chunks * (groups + 1) : chunks * (groups + 1) + 5]
    pixels = refs[chunks * (groups + 1) + 5 :]
    own, all_rows, side_len = moved.shape
    size = pixels[0].shape[2] * groups

    blocks = [
        (chunk, row) for chunk in [chunks - 1] + list(range(chunks - 1)) for row in range(0, sizes[chunk], EDGE_ROWS)
    ]
    far = 1 if groups > 1 else 0
    pixel_copies = []
    moved_copies = []
    for place, (chunk, row) in enumerate(blocks):
        part = pl.ds(row, EDGE_ROWS)
        into = pl.ds(starts[chunk] + row, EDGE_ROWS)
        copies = [
            pltpu.make_async_copy(
                pixels_hbm[chunk * groups + group].at[part], pixels[chunk].at[group, part], pixel_sems.at[place, group]
            )
            for group in range(0 if chunk == chunks - 1 else far, groups)
        ]
        pixel_copies.append(copies)
        moved_copies.append(
            pltpu.make_async_copy(moved_hbm[chunk].at[:, part], moved.at[:, into], moved_sems.at[place])
        )
        for copy in copies + moved_copies[-1:]:
            copy.start()

    last_blocks = sizes[-1] // EDGE_ROWS
    for copies in pixel_copies[:last_blocks]:
        for copy in copies:
            copy.wait()
    total = gram_ref[...]
    for first in range(0, sizes[-1], GRAM_ROWS):
        data = stacked([pixels[-1].at[group] for group in range(groups)], first, GRAM_ROWS)
        total = total + dot_nt(data, data)
    gram = jnp.zeros((size, size), F32)
    for i in range(GRAM_ROWS):
        gram = gram + total[i * size : (i + 1) * size, i * size : (i + 1) * size]
    inverse, frob_norm = newton_schulz(gram)
    factor = shrink_ref[0] * jnp.sqrt(all_rows * side_len / frob_norm)
    select = (iota((own, size), 0) == iota((own, size), 1)).astype(F32)
    weights = (dot_nt(select, inverse, HIGHEST) * factor).astype(BF16)
    spread = POLAR_ROWS * own
    repeat = (iota((spread, own), 0) // POLAR_ROWS == iota((spread, own), 1)).astype(BF16)
    weights = dot_nn(repeat, weights).astype(BF16)

    def widened(count, first, channel_of, pixel_row_of):
        columns = iota((size, count), 1)
        chosen = dot_nn(weights, (iota((size, count), 0) == first + channel_of(columns)).astype(BF16))
        columns = iota((spread, count), 1)
        keep = iota((spread, count), 0) % POLAR_ROWS == pixel_row_of(columns)
        return jnp.where(keep, chosen, 0.0).astype(BF16)

    others = size - far * own
    far_weights = widened(POLAR_ROWS * others, far * own, lambda c: c % others, lambda c: c // others)
    if far:
        own_weights = widened(spread, 0, lambda c: c // POLAR_ROWS, lambda c: c % POLAR_ROWS)
        far_weights = jnp.concatenate([own_weights, far_weights], axis=1)

    out_copies = []
    for place, (chunk, row) in enumerate(blocks):
        if place >= last_blocks:
            for copy in pixel_copies[place]:
                copy.wait()
        moved_copies[place].wait()
        for first in range(row, row + EDGE_ROWS, POLAR_ROWS):
            into = starts[chunk] + first
            rows = moved[:, into : into + POLAR_ROWS]
            data = stacked([pixels[chunk].at[group] for group in range(far, groups)], first, POLAR_ROWS)
            if far:
                data = jnp.concatenate([rows.reshape(spread, side_len).astype(BF16), data], axis=0)
            polar = dot_nn(far_weights, data).reshape(own, POLAR_ROWS, side_len)
            moved[:, into : into + POLAR_ROWS] = rows - polar
        part = pl.ds(starts[chunk] + row, EDGE_ROWS)
        copy = pltpu.make_async_copy(moved.at[:, part], out_hbm.at[:, part], out_sems.at[place])
        copy.start()
        out_copies.append(copy)
    for copy in out_copies:
        copy.wait()


def polar_step(shrinkage, gram, moved, gathered, starts, sizes):
    chunks = len(gathered)
    groups = len(gathered[0])
    chans, _, side_len = moved[0].shape
    shape = (chans, sum(sizes), side_len)
    blocks = sum(sizes) // EDGE_ROWS
    flat = [piece for pieces in gathered for piece in pieces]
    return pl.pallas_call(
        functools.partial(polar_body, starts, sizes, groups),
        in_specs=[SMEM, pl.BlockSpec(memory_space=pltpu.VMEM)] + [ANY] * (chunks + len(flat)),
        out_specs=ANY,
        out_shape=jax.ShapeDtypeStruct(shape, F32),
        scratch_shapes=[
            pltpu.VMEM(shape, F32),
            pltpu.SemaphoreType.DMA((blocks, groups)),
            pltpu.SemaphoreType.DMA((blocks,)),
            pltpu.SemaphoreType.DMA((blocks,)),
        ]
        + [pltpu.VMEM((groups,) + pieces[0].shape, BF16) for pieces in gathered],
        compiler_params=kernel_params(63),
        cost_estimate=COST,
        name="polar_step",
    )(shrinkage, gram, *moved, *flat)


def neighbour_rows(model_image, reach):
    ends = lax.axis_size("strip") - 1
    head, tail = lax.optimization_barrier((model_image[:, :reach], model_image[:, model_image.shape[1] - reach :]))
    before = lax.ppermute(tail.astype(BF16), "strip", [(i, i + 1) for i in range(ends)])
    after = lax.ppermute(head.astype(BF16), "strip", [(i + 1, i) for i in range(ends)])
    return before, after


def swap(value, axis, bits):
    count = lax.axis_size(axis)
    return lax.ppermute(value, axis, [(i, i ^ bits) for i in range(count)])


def gather_channels(pixels, after=None):
    devices = lax.axis_size("chan")
    kept = [pixels] + [swap(pixels, "chan", bits) for bits in range(2, devices, 2)]
    if after is not None:
        kept = [pixels] + [gate(piece, after) for piece in kept[1:]]
    if devices == 1:
        return kept
    return kept + [swap(piece, "chan", 1) for piece in kept]


def local(grid, model_image, step_size, highpass, shrinkage):
    chans, own_rows, side_len = model_image.shape
    strips = lax.axis_size("strip")
    size = chans * lax.axis_size("chan")
    starts, sizes = chunk_rows(own_rows)
    chunks = len(sizes)
    strip = lax.axis_index("strip").astype(jnp.int32).reshape(1)

    cosine, sine_table = make_tables(side_len)
    split = np.stack([cosine.reshape(strips, own_rows, side_len), sine_table.reshape(strips, own_rows, side_len)])
    tables = [
        np.ascontiguousarray(split[:, :, start : start + rows]).reshape(2 * strips * rows, side_len)
        for start, rows in zip(starts, sizes)
    ]

    levels, taps = highpass.shape
    reach = (taps - 1) * 2 ** (levels - 1)
    sides = neighbour_rows(model_image, reach)
    edges = jnp.concatenate(sides, axis=1)

    halves = {}
    moved = {}
    gathered = {}
    pixels = {}
    done = set()
    state = dict(last=strip, gram=jnp.zeros((GRAM_ROWS * size, GRAM_ROWS * size), F32), bases=None)

    def first(chunk):
        sent, state["last"] = first_transform(tables[chunk], grid, strips, state["last"])
        if chunk == 0:
            for side in sides:
                sent = gate(sent, side)
                state["last"] = gate(state["last"], side)
        if chunk == 2:
            gather(0)
            gram(0)
            done.add(0)
            sent = gate(sent, state["gram"])
        halves[chunk] = lax.all_to_all(sent, "strip", split_axis=0, concat_axis=0, tiled=True)

    def base():
        state["bases"] = base_step(
            strip, strips, step_size, highpass, model_image, edges, starts, sizes, state["last"]
        )
        state["last"] = state["bases"][0]

    def second(chunk):
        moved[chunk], pixels[chunk] = second_transform(
            step_size, halves[chunk], cosine, sine_table, state["bases"][chunk], state["last"]
        )
        state["last"] = pixels[chunk]

    def gather(chunk):
        pieces = gather_channels(pixels[chunk], state["last"])
        if chans % 16:
            pieces = [jnp.concatenate(pieces, axis=1)]
        gathered[chunk] = pieces

    def gram(chunk):
        state["gram"] = gram_step(gathered[chunk], state["gram"], state["last"])
        state["last"] = state["gram"]

    first(0)
    if chunks > 1:
        first(1)
    base()
    for chunk in range(chunks):
        second(chunk)
        if chunk + 2 < chunks:
            first(chunk + 2)
        if chunk == 1:
            gather(1)
        if chunk >= 1 and chunk - 1 not in done:
            if chunk - 1 not in gathered:
                gather(chunk - 1)
            gram(chunk - 1)
    if chunks - 1 not in gathered:
        gather(chunks - 1)
    order = range(chunks)
    return polar_step(
        shrinkage, state["gram"], [moved[k] for k in order], [gathered[k] for k in order], starts, sizes
    )


def solution(mesh):
    return jax.shard_map(
        local,
        mesh=mesh,
        in_specs=(
            P(None, "chan", "strip", None),
            P("chan", "strip", None),
            P("chan"),
            P(),
            P("strip"),
        ),
        out_specs=P("chan", "strip", None),
        check_vma=False,
    )
```

```python
import functools

import jax
import jax.numpy as jnp
import ml_dtypes
import numpy as np
from jax import lax
from jax.experimental import pallas as pl
from jax.experimental.pallas import tpu as pltpu
from jax.sharding import PartitionSpec as P

NS_ITERS = 5
EDGE_ROWS = 16
GRAM_ROWS = 4
POLAR_ROWS = 8
HIGHEST = lax.Precision.HIGHEST
F32 = jnp.float32
BF16 = jnp.bfloat16
MIB = 1 << 20

ANY = pl.BlockSpec(memory_space=pl.ANY)
SMEM = pl.BlockSpec(memory_space=pltpu.SMEM)


def kernel_params(mebibytes):
    return pltpu.CompilerParams(vmem_limit_bytes=mebibytes * MIB)


COST = pl.CostEstimate(flops=0, bytes_accessed=1 << 16, transcendentals=0)


def dot_nt(a, b, precision=None):
    return lax.dot_general(
        a, b, (((1,), (1,)), ((), ())), precision=precision, preferred_element_type=F32
    )


def dot_nn(a, b, precision=None):
    return lax.dot_general(
        a, b, (((1,), (0,)), ((), ())), precision=precision, preferred_element_type=F32
    )


def iota(shape, dim):
    return lax.broadcasted_iota(jnp.int32, shape, dim)


def make_tables(side_len):
    indices = np.arange(side_len, dtype=np.int64)
    phases = (np.outer(indices, indices) % side_len).astype(np.float32) * np.float32(
        2.0 * 3.141592653589793 / side_len
    )
    unit_scale = np.float32(float(side_len) ** (-0.5))
    cosine = (np.cos(phases) * unit_scale).astype(ml_dtypes.bfloat16)
    sine_table = (np.sin(phases) * unit_scale).astype(ml_dtypes.bfloat16)
    return cosine, sine_table


def chunk_rows(own_rows):
    quarter = own_rows // 4
    sizes = [quarter, own_rows - 2 * quarter - EDGE_ROWS, quarter, EDGE_ROWS]
    sizes = [size for size in sizes if size > 0]
    return [sum(sizes[:place]) for place in range(len(sizes))], sizes


def gate_body(value_ref, after_ref, out_ref):
    pass


def gate(value, after):
    return pl.pallas_call(
        gate_body,
        in_specs=[ANY, ANY],
        out_specs=ANY,
        out_shape=jax.ShapeDtypeStruct(value.shape, value.dtype),
        input_output_aliases={0: 0},
        compiler_params=kernel_params(63),
        cost_estimate=COST,
        name="gate",
    )(value, after)


def first_body(table_ref, grid_ref, after_ref, out_ref, token_ref):
    token_ref[...] = jnp.zeros(token_ref.shape, F32)
    strips, _, chans, rows, width = out_ref.shape
    side_len = table_ref.shape[-1]
    table = table_ref[...]
    middle = strips * rows
    turned = jnp.concatenate([-table[middle:], table[:middle]], axis=0)
    total = dot_nt(table, grid_ref[0].reshape(chans * width, side_len))
    total = total + dot_nt(turned, grid_ref[1].reshape(chans * width, side_len))
    total = total.astype(BF16)
    for part in range(2):
        for strip in range(strips):
            first = (part * strips + strip) * rows
            for chan in range(chans):
                out_ref[strip, part, chan] = total[first : first + rows, chan * width : (chan + 1) * width]


def first_transform(table, grid, strips, after):
    _, chans, width, side_len = grid.shape
    rows = table.shape[0] // (2 * strips)
    shape = (strips, 2, chans, rows, width)
    if width % 128 or rows % 16:
        middle = strips * rows
        turned = jnp.concatenate([-table[middle:], table[:middle]], axis=0)
        total = jnp.einsum("mv,cuv->mcu", table, grid[0], preferred_element_type=F32)
        total = total + jnp.einsum("mv,cuv->mcu", turned, grid[1], preferred_element_type=F32)
        total = total.astype(BF16).reshape(2, strips, rows, chans, width)
        return total.transpose(1, 0, 3, 2, 4), jnp.zeros((8, 128), F32)
    block = 4 if chans % 4 == 0 else 1
    return pl.pallas_call(
        first_body,
        grid=(chans // block,),
        in_specs=[
            pl.BlockSpec(table.shape, lambda i: (0, 0)),
            pl.BlockSpec((2, block, width, side_len), lambda i: (0, i, 0, 0)),
            ANY,
        ],
        out_specs=[
            pl.BlockSpec((strips, 2, block, rows, width), lambda i: (0, 0, i, 0, 0)),
            pl.BlockSpec((8, 128), lambda i: (0, 0)),
        ],
        out_shape=[jax.ShapeDtypeStruct(shape, BF16), jax.ShapeDtypeStruct((8, 128), F32)],
        compiler_params=kernel_params(63),
        cost_estimate=COST,
        name="first_transform",
    )(table, grid, after)


def band_matrix(taps_of, levels, taps, own_rows, reach, first_row, image_rows):
    half_taps = taps // 2
    shape = (own_rows, own_rows + 2 * reach)
    row = iota(shape, 0)
    column = iota(shape, 1)
    place = jnp.where(
        column < own_rows, column, jnp.where(column < own_rows + reach, column - own_rows - reach, column - reach)
    )
    total = jnp.zeros(shape, F32)
    for level in range(levels):
        dilation = 2**level
        for outer in range(taps):
            detail_row = row - (outer - half_taps) * dilation
            inside = (detail_row + first_row >= 0) & (detail_row + first_row < image_rows)
            for inner in range(taps):
                hit = inside & (place == detail_row + (inner - half_taps) * dilation)
                total = total + jnp.where(hit, taps_of(level, outer) * taps_of(level, inner), 0.0)
    return total


def base_body(levels, taps, starts, strips, strip_ref, step_ref, highpass_ref, model_ref, edge_ref, after_ref, *refs):
    high, low = refs[-2:]
    out_refs = refs[:-2]
    block, own_rows, side_len = model_ref.shape
    reach = edge_ref.shape[1] // 2

    @pl.when(pl.program_id(0) == 0)
    def _():
        band = band_matrix(
            lambda level, tap: highpass_ref[level, tap],
            levels,
            taps,
            own_rows,
            reach,
            strip_ref[0] * own_rows,
            strips * own_rows,
        )
        top = band.astype(BF16)
        high[...] = top
        low[...] = (band - top.astype(F32)).astype(BF16)

    first = pl.program_id(0) * block
    for chan in range(block):
        model = model_ref[chan]
        top = model.astype(BF16)
        rest = (model - top.astype(F32)).astype(BF16)
        edge = edge_ref[chan].astype(F32)
        whole = jnp.concatenate([top.astype(F32), edge], axis=0).astype(BF16)
        gradient = dot_nn(high[...], whole)
        gradient = gradient + dot_nn(low[...], whole)
        gradient = gradient + dot_nn(high[:, :own_rows], rest)
        base = model - step_ref[first + chan] * gradient
        for start, out_ref in zip(starts, out_refs):
            out_ref[chan] = base[start : start + out_ref.shape[1]]


def base_step(strip, strips, step_size, highpass, model_image, edges, starts, sizes, after):
    chans, rows, side_len = model_image.shape
    levels, taps = highpass.shape
    reach = edges.shape[1] // 2
    block = 2 if chans % 2 == 0 else 1
    wide = rows + 2 * reach
    return pl.pallas_call(
        functools.partial(base_body, levels, taps, starts, strips),
        grid=(chans // block,),
        in_specs=[
            SMEM,
            SMEM,
            SMEM,
            pl.BlockSpec((block, rows, side_len), lambda i: (i, 0, 0)),
            pl.BlockSpec((block, 2 * reach, side_len), lambda i: (i, 0, 0)),
            ANY,
        ],
        out_specs=[pl.BlockSpec((block, part, side_len), lambda i: (i, 0, 0)) for part in sizes],
        out_shape=[jax.ShapeDtypeStruct((chans, part, side_len), F32) for part in sizes],
        scratch_shapes=[pltpu.VMEM((rows, wide), BF16), pltpu.VMEM((rows, wide), BF16)],
        compiler_params=kernel_params(63),
        cost_estimate=COST,
        name="base_step",
    )(strip, step_size, highpass, model_image, edges, after)


def second_body(step_ref, half_ref, cosine_ref, sine_ref, base_ref, after_ref, moved_ref, pixels_ref):
    strips, _, chans, rows, width = half_ref.shape
    real = jnp.concatenate([half_ref[s, 0].reshape(chans * rows, width) for s in range(strips)], axis=1)
    imag = jnp.concatenate([half_ref[s, 1].reshape(chans * rows, width) for s in range(strips)], axis=1)
    dirty = dot_nn(real, cosine_ref[...]) - dot_nn(imag, sine_ref[...])
    pieces = []
    for chan in range(chans):
        moved = base_ref[chan] + step_ref[chan] * dirty[chan * rows : (chan + 1) * rows]
        moved_ref[chan] = moved
        pieces.append(moved)
    pixels_ref[...] = jnp.swapaxes(jnp.stack(pieces), 0, 1).astype(BF16)


def second_transform(step_size, half, cosine, sine_table, base, after):
    strips, _, chans, rows, width = half.shape
    side_len = cosine.shape[0]
    if width % 128 or rows % 16 or chans % 16:
        split = (strips, width, side_len)
        dirty = jnp.einsum("scmu,sul->cml", half[:, 0], cosine.reshape(split), preferred_element_type=F32)
        dirty = dirty - jnp.einsum("scmu,sul->cml", half[:, 1], sine_table.reshape(split), preferred_element_type=F32)
        moved = base + step_size[:, None, None] * dirty
        return moved, moved.astype(BF16).transpose(1, 0, 2)
    block = min(256, side_len)
    return pl.pallas_call(
        second_body,
        grid=(side_len // block,),
        in_specs=[
            SMEM,
            pl.BlockSpec(half.shape, lambda i: (0, 0, 0, 0, 0)),
            pl.BlockSpec((side_len, block), lambda i: (0, i)),
            pl.BlockSpec((side_len, block), lambda i: (0, i)),
            pl.BlockSpec((chans, rows, block), lambda i: (0, 0, i)),
            ANY,
        ],
        out_specs=[
            pl.BlockSpec((chans, rows, block), lambda i: (0, 0, i)),
            pl.BlockSpec((rows, chans, block), lambda i: (0, 0, i)),
        ],
        out_shape=[
            jax.ShapeDtypeStruct(base.shape, F32),
            jax.ShapeDtypeStruct((rows, chans, side_len), BF16),
        ],
        compiler_params=kernel_params(63),
        cost_estimate=COST,
        name="second_transform",
    )(step_size, half, cosine, sine_table, base, after)


def stacked(group_refs, first, count):
    return jnp.concatenate([ref[first + i] for i in range(count) for ref in group_refs], axis=0)


def gram_body(groups, before_ref, after_ref, *refs):
    total_ref = refs[groups]

    @pl.when(pl.program_id(0) == 0)
    def _():
        total_ref[...] = before_ref[...]

    total = total_ref[...]
    for first in range(0, refs[0].shape[0], GRAM_ROWS):
        pixels = stacked(refs[:groups], first, GRAM_ROWS)
        total = total + dot_nt(pixels, pixels)
    total_ref[...] = total


def gram_step(pieces, before, after):
    rows, chans, side_len = pieces[0].shape
    block = EDGE_ROWS // 2
    spec = pl.BlockSpec((block, chans, side_len), lambda i: (i, 0, 0))
    return pl.pallas_call(
        functools.partial(gram_body, len(pieces)),
        grid=(rows // block,),
        in_specs=[pl.BlockSpec(before.shape, lambda i: (0, 0)), ANY] + [spec] * len(pieces),
        out_specs=pl.BlockSpec(before.shape, lambda i: (0, 0)),
        out_shape=jax.ShapeDtypeStruct(before.shape, F32),
        compiler_params=kernel_params(63),
        cost_estimate=COST,
        name="gram_step",
    )(before, after, *pieces)


def newton_schulz(gram):
    size = gram.shape[0]
    frob_norm = jnp.sqrt(jnp.sum(gram * gram))
    identity = (iota((size, size), 0) == iota((size, size), 1)).astype(F32)
    current = gram / frob_norm
    middle = 0.5 * (3.0 * identity - current)
    inverse = middle
    for iteration in range(1, NS_ITERS):
        current = dot_nn(current, middle, HIGHEST)
        middle = 0.5 * (3.0 * identity - dot_nn(inverse, current, HIGHEST))
        inverse = dot_nn(middle, inverse, HIGHEST)
    return inverse, frob_norm


def polar_body(starts, sizes, groups, shrink_ref, gram_ref, *refs):
    chunks = len(sizes)
    moved_hbm = refs[:chunks]
    pixels_hbm = refs[chunks : chunks * (groups + 1)]
    out_hbm, moved, pixel_sems, moved_sems, out_sems = refs[chunks * (groups + 1) : chunks * (groups + 1) + 5]
    pixels = refs[chunks * (groups + 1) + 5 :]
    own, all_rows, side_len = moved.shape
    size = pixels[0].shape[2] * groups

    blocks = [
        (chunk, row) for chunk in [chunks - 1] + list(range(chunks - 1)) for row in range(0, sizes[chunk], EDGE_ROWS)
    ]
    far = 1 if groups > 1 else 0
    pixel_copies = []
    moved_copies = []
    for place, (chunk, row) in enumerate(blocks):
        part = pl.ds(row, EDGE_ROWS)
        into = pl.ds(starts[chunk] + row, EDGE_ROWS)
        copies = [
            pltpu.make_async_copy(
                pixels_hbm[chunk * groups + group].at[part], pixels[chunk].at[group, part], pixel_sems.at[place, group]
            )
            for group in range(0 if chunk == chunks - 1 else far, groups)
        ]
        pixel_copies.append(copies)
        moved_copies.append(
            pltpu.make_async_copy(moved_hbm[chunk].at[:, part], moved.at[:, into], moved_sems.at[place])
        )
        for copy in copies + moved_copies[-1:]:
            copy.start()

    last_blocks = sizes[-1] // EDGE_ROWS
    for copies in pixel_copies[:last_blocks]:
        for copy in copies:
            copy.wait()
    total = gram_ref[...]
    for first in range(0, sizes[-1], GRAM_ROWS):
        data = stacked([pixels[-1].at[group] for group in range(groups)], first, GRAM_ROWS)
        total = total + dot_nt(data, data)
    gram = jnp.zeros((size, size), F32)
    for i in range(GRAM_ROWS):
        gram = gram + total[i * size : (i + 1) * size, i * size : (i + 1) * size]
    inverse, frob_norm = newton_schulz(gram)
    factor = shrink_ref[0] * jnp.sqrt(all_rows * side_len / frob_norm)
    select = (iota((own, size), 0) == iota((own, size), 1)).astype(F32)
    weights = (dot_nt(select, inverse, HIGHEST) * factor).astype(BF16)
    spread = POLAR_ROWS * own
    repeat = (iota((spread, own), 0) // POLAR_ROWS == iota((spread, own), 1)).astype(BF16)
    weights = dot_nn(repeat, weights).astype(BF16)

    def widened(count, first, channel_of, pixel_row_of):
        columns = iota((size, count), 1)
        chosen = dot_nn(weights, (iota((size, count), 0) == first + channel_of(columns)).astype(BF16))
        columns = iota((spread, count), 1)
        keep = iota((spread, count), 0) % POLAR_ROWS == pixel_row_of(columns)
        return jnp.where(keep, chosen, 0.0).astype(BF16)

    others = size - far * own
    far_weights = widened(POLAR_ROWS * others, far * own, lambda c: c % others, lambda c: c // others)
    if far:
        own_weights = widened(spread, 0, lambda c: c // POLAR_ROWS, lambda c: c % POLAR_ROWS)
        far_weights = jnp.concatenate([own_weights, far_weights], axis=1)

    out_copies = []
    for place, (chunk, row) in enumerate(blocks):
        if place >= last_blocks:
            for copy in pixel_copies[place]:
                copy.wait()
        moved_copies[place].wait()
        for first in range(row, row + EDGE_ROWS, POLAR_ROWS):
            into = starts[chunk] + first
            rows = moved[:, into : into + POLAR_ROWS]
            data = stacked([pixels[chunk].at[group] for group in range(far, groups)], first, POLAR_ROWS)
            if far:
                data = jnp.concatenate([rows.reshape(spread, side_len).astype(BF16), data], axis=0)
            polar = dot_nn(far_weights, data).reshape(own, POLAR_ROWS, side_len)
            moved[:, into : into + POLAR_ROWS] = rows - polar
        part = pl.ds(starts[chunk] + row, EDGE_ROWS)
        copy = pltpu.make_async_copy(moved.at[:, part], out_hbm.at[:, part], out_sems.at[place])
        copy.start()
        out_copies.append(copy)
    for copy in out_copies:
        copy.wait()


def polar_step(shrinkage, gram, moved, gathered, starts, sizes):
    chunks = len(gathered)
    groups = len(gathered[0])
    chans, _, side_len = moved[0].shape
    shape = (chans, sum(sizes), side_len)
    blocks = sum(sizes) // EDGE_ROWS
    flat = [piece for pieces in gathered for piece in pieces]
    return pl.pallas_call(
        functools.partial(polar_body, starts, sizes, groups),
        in_specs=[SMEM, pl.BlockSpec(memory_space=pltpu.VMEM)] + [ANY] * (chunks + len(flat)),
        out_specs=ANY,
        out_shape=jax.ShapeDtypeStruct(shape, F32),
        scratch_shapes=[
            pltpu.VMEM(shape, F32),
            pltpu.SemaphoreType.DMA((blocks, groups)),
            pltpu.SemaphoreType.DMA((blocks,)),
            pltpu.SemaphoreType.DMA((blocks,)),
        ]
        + [pltpu.VMEM((groups,) + pieces[0].shape, BF16) for pieces in gathered],
        compiler_params=kernel_params(63),
        cost_estimate=COST,
        name="polar_step",
    )(shrinkage, gram, *moved, *flat)


def neighbour_rows(model_image, reach):
    ends = lax.axis_size("strip") - 1
    head, tail = lax.optimization_barrier((model_image[:, :reach], model_image[:, model_image.shape[1] - reach :]))
    before = lax.ppermute(tail.astype(BF16), "strip", [(i, i + 1) for i in range(ends)])
    after = lax.ppermute(head.astype(BF16), "strip", [(i + 1, i) for i in range(ends)])
    return before, after


def swap(value, axis, bits):
    count = lax.axis_size(axis)
    return lax.ppermute(value, axis, [(i, i ^ bits) for i in range(count)])


def gather_channels(pixels, after=None):
    devices = lax.axis_size("chan")
    kept = [pixels] + [swap(pixels, "chan", bits) for bits in range(2, devices, 2)]
    if after is not None:
        kept = [pixels] + [gate(piece, after) for piece in kept[1:]]
    if devices == 1:
        return kept
    return kept + [swap(piece, "chan", 1) for piece in kept]


def local(grid, model_image, step_size, highpass, shrinkage):
    chans, own_rows, side_len = model_image.shape
    strips = lax.axis_size("strip")
    size = chans * lax.axis_size("chan")
    starts, sizes = chunk_rows(own_rows)
    chunks = len(sizes)
    strip = lax.axis_index("strip").astype(jnp.int32).reshape(1)

    cosine, sine_table = make_tables(side_len)
    split = np.stack([cosine.reshape(strips, own_rows, side_len), sine_table.reshape(strips, own_rows, side_len)])
    tables = [
        np.ascontiguousarray(split[:, :, start : start + rows]).reshape(2 * strips * rows, side_len)
        for start, rows in zip(starts, sizes)
    ]

    levels, taps = highpass.shape
    reach = (taps - 1) * 2 ** (levels - 1)
    sides = neighbour_rows(model_image, reach)
    edges = jnp.concatenate(sides, axis=1)

    halves = {}
    moved = {}
    gathered = {}
    pixels = {}
    done = set()
    state = dict(last=strip, gram=jnp.zeros((GRAM_ROWS * size, GRAM_ROWS * size), F32), bases=None)

    def first(chunk):
        sent, state["last"] = first_transform(tables[chunk], grid, strips, state["last"])
        if chunk == 1:
            for side in sides:
                sent = gate(sent, side)
        if chunk == 2:
            gather(0)
            gram(0)
            done.add(0)
            sent = gate(sent, state["gram"])
        halves[chunk] = lax.all_to_all(sent, "strip", split_axis=0, concat_axis=0, tiled=True)

    def base():
        state["bases"] = base_step(
            strip, strips, step_size, highpass, model_image, edges, starts, sizes, state["last"]
        )
        state["last"] = state["bases"][0]

    def second(chunk):
        moved[chunk], pixels[chunk] = second_transform(
            step_size, halves[chunk], cosine, sine_table, state["bases"][chunk], state["last"]
        )
        state["last"] = pixels[chunk]

    def gather(chunk):
        pieces = gather_channels(pixels[chunk], state["last"])
        if chans % 16:
            pieces = [jnp.concatenate(pieces, axis=1)]
        gathered[chunk] = pieces

    def gram(chunk):
        state["gram"] = gram_step(gathered[chunk], state["gram"], state["last"])
        state["last"] = state["gram"]

    first(0)
    if chunks > 1:
        first(1)
    base()
    for chunk in range(chunks):
        second(chunk)
        if chunk + 2 < chunks:
            first(chunk + 2)
        if chunk == 1:
            gather(1)
        if chunk >= 1 and chunk - 1 not in done:
            if chunk - 1 not in gathered:
                gather(chunk - 1)
            gram(chunk - 1)
    if chunks - 1 not in gathered:
        gather(chunks - 1)
    order = range(chunks)
    return polar_step(
        shrinkage, state["gram"], [moved[k] for k in order], [gathered[k] for k in order], starts, sizes
    )


def solution(mesh):
    return jax.shard_map(
        local,
        mesh=mesh,
        in_specs=(
            P(None, "chan", "strip", None),
            P("chan", "strip", None),
            P("chan"),
            P(),
            P("strip"),
        ),
        out_specs=P("chan", "strip", None),
        check_vma=False,
    )
```

```python
import functools

import jax
import jax.numpy as jnp
import ml_dtypes
import numpy as np
from jax import lax
from jax.experimental import pallas as pl
from jax.experimental.pallas import tpu as pltpu
from jax.sharding import PartitionSpec as P

NS_ITERS = 5
EDGE_ROWS = 16
GRAM_ROWS = 4
POLAR_ROWS = 8
HIGHEST = lax.Precision.HIGHEST
F32 = jnp.float32
BF16 = jnp.bfloat16
MIB = 1 << 20

ANY = pl.BlockSpec(memory_space=pl.ANY)
SMEM = pl.BlockSpec(memory_space=pltpu.SMEM)


def kernel_params(mebibytes):
    return pltpu.CompilerParams(vmem_limit_bytes=mebibytes * MIB)


COST = pl.CostEstimate(flops=0, bytes_accessed=1 << 16, transcendentals=0)


def dot_nt(a, b, precision=None):
    return lax.dot_general(
        a, b, (((1,), (1,)), ((), ())), precision=precision, preferred_element_type=F32
    )


def dot_nn(a, b, precision=None):
    return lax.dot_general(
        a, b, (((1,), (0,)), ((), ())), precision=precision, preferred_element_type=F32
    )


def iota(shape, dim):
    return lax.broadcasted_iota(jnp.int32, shape, dim)


def make_tables(side_len):
    indices = np.arange(side_len, dtype=np.int64)
    phases = (np.outer(indices, indices) % side_len).astype(np.float32) * np.float32(
        2.0 * 3.141592653589793 / side_len
    )
    unit_scale = np.float32(float(side_len) ** (-0.5))
    cosine = (np.cos(phases) * unit_scale).astype(ml_dtypes.bfloat16)
    sine_table = (np.sin(phases) * unit_scale).astype(ml_dtypes.bfloat16)
    return cosine, sine_table


def chunk_blocks(own_rows, reach):
    blocks = list(range(0, own_rows, EDGE_ROWS))
    near = [row for row in blocks if row < reach or row + EDGE_ROWS > own_rows - reach]
    inner = [row for row in blocks if row not in near]
    quarter = len(blocks) // 4
    sizes = [quarter, len(blocks) - 2 * quarter - 1, quarter, 1]
    ahead = sizes[0] + sizes[1]
    order = inner[:ahead] + near + inner[ahead:]
    chunks = [order[sum(sizes[:place]) : sum(sizes[: place + 1])] for place in range(len(sizes))]
    return chunks, [any(row in near for row in chunk) for chunk in chunks]


def gate_body(value_ref, after_ref, out_ref):
    pass


def gate(value, after):
    return pl.pallas_call(
        gate_body,
        in_specs=[ANY, ANY],
        out_specs=ANY,
        out_shape=jax.ShapeDtypeStruct(value.shape, value.dtype),
        input_output_aliases={0: 0},
        compiler_params=kernel_params(63),
        cost_estimate=COST,
        name="gate",
    )(value, after)


def first_body(table_ref, grid_ref, after_ref, out_ref, token_ref):
    token_ref[...] = jnp.zeros(token_ref.shape, F32)
    strips, _, chans, rows, width = out_ref.shape
    side_len = table_ref.shape[-1]
    table = table_ref[...]
    middle = strips * rows
    turned = jnp.concatenate([-table[middle:], table[:middle]], axis=0)
    total = dot_nt(table, grid_ref[0].reshape(chans * width, side_len))
    total = total + dot_nt(turned, grid_ref[1].reshape(chans * width, side_len))
    total = total.astype(BF16)
    for part in range(2):
        for strip in range(strips):
            first = (part * strips + strip) * rows
            for chan in range(chans):
                out_ref[strip, part, chan] = total[first : first + rows, chan * width : (chan + 1) * width]


def first_transform(table, grid, strips, after):
    _, chans, width, side_len = grid.shape
    rows = table.shape[0] // (2 * strips)
    shape = (strips, 2, chans, rows, width)
    if width % 128 or rows % 16:
        middle = strips * rows
        turned = jnp.concatenate([-table[middle:], table[:middle]], axis=0)
        total = jnp.einsum("mv,cuv->mcu", table, grid[0], preferred_element_type=F32)
        total = total + jnp.einsum("mv,cuv->mcu", turned, grid[1], preferred_element_type=F32)
        total = total.astype(BF16).reshape(2, strips, rows, chans, width)
        return total.transpose(1, 0, 3, 2, 4), jnp.zeros((8, 128), F32)
    block = 4 if chans % 4 == 0 else 1
    return pl.pallas_call(
        first_body,
        grid=(chans // block,),
        in_specs=[
            pl.BlockSpec(table.shape, lambda i: (0, 0)),
            pl.BlockSpec((2, block, width, side_len), lambda i: (0, i, 0, 0)),
            ANY,
        ],
        out_specs=[
            pl.BlockSpec((strips, 2, block, rows, width), lambda i: (0, 0, i, 0, 0)),
            pl.BlockSpec((8, 128), lambda i: (0, 0)),
        ],
        out_shape=[jax.ShapeDtypeStruct(shape, BF16), jax.ShapeDtypeStruct((8, 128), F32)],
        compiler_params=kernel_params(63),
        cost_estimate=COST,
        name="first_transform",
    )(table, grid, after)


def band_matrix(taps_of, levels, taps, own_rows, reach, first_row, image_rows):
    half_taps = taps // 2
    shape = (own_rows, own_rows + 2 * reach)
    row = iota(shape, 0)
    column = iota(shape, 1)
    place = jnp.where(
        column < own_rows, column, jnp.where(column < own_rows + reach, column - own_rows - reach, column - reach)
    )
    total = jnp.zeros(shape, F32)
    for level in range(levels):
        dilation = 2**level
        for outer in range(taps):
            detail_row = row - (outer - half_taps) * dilation
            inside = (detail_row + first_row >= 0) & (detail_row + first_row < image_rows)
            for inner in range(taps):
                hit = inside & (place == detail_row + (inner - half_taps) * dilation)
                total = total + jnp.where(hit, taps_of(level, outer) * taps_of(level, inner), 0.0)
    return total


def base_body(levels, taps, blocks, strips, reach, with_edges, strip_ref, step_ref, highpass_ref, model_ref, *refs):
    high, low = refs[-2:]
    out_refs = refs[2:-2] if with_edges else refs[1:-2]
    count, own_rows, side_len = model_ref.shape

    @pl.when(pl.program_id(0) == 0)
    def _():
        band = band_matrix(
            lambda level, tap: highpass_ref[level, tap],
            levels,
            taps,
            own_rows,
            reach,
            strip_ref[0] * own_rows,
            strips * own_rows,
        )
        top = band.astype(BF16)
        high[...] = top
        low[...] = (band - top.astype(F32)).astype(BF16)

    wide = own_rows + 2 * reach if with_edges else own_rows
    first = pl.program_id(0) * count
    for chan in range(count):
        model = model_ref[chan]
        top = model.astype(BF16)
        rest = (model - top.astype(F32)).astype(BF16)
        whole = top
        if with_edges:
            whole = jnp.concatenate([top.astype(F32), refs[0][chan].astype(F32)], axis=0).astype(BF16)
        gradient = dot_nn(high[:, :wide], whole)
        gradient = gradient + dot_nn(low[:, :wide], whole)
        gradient = gradient + dot_nn(high[:, :own_rows], rest)
        base = model - step_ref[first + chan] * gradient
        for rows, out_ref in zip(blocks, out_refs):
            for place, row in enumerate(rows):
                out_ref[chan, place * EDGE_ROWS : (place + 1) * EDGE_ROWS] = base[row : row + EDGE_ROWS]


def base_step(strip, strips, step_size, highpass, model_image, edges, reach, blocks, after):
    chans, rows, side_len = model_image.shape
    levels, taps = highpass.shape
    count = 2 if chans % 2 == 0 else 1
    wide = rows + 2 * reach
    sizes = [len(chunk) * EDGE_ROWS for chunk in blocks]
    with_edges = edges is not None
    edge_specs = [pl.BlockSpec((count, 2 * reach, side_len), lambda i: (i, 0, 0))] if with_edges else []
    return pl.pallas_call(
        functools.partial(base_body, levels, taps, blocks, strips, reach, with_edges),
        grid=(chans // count,),
        in_specs=[SMEM, SMEM, SMEM, pl.BlockSpec((count, rows, side_len), lambda i: (i, 0, 0))] + edge_specs + [ANY],
        out_specs=[pl.BlockSpec((count, part, side_len), lambda i: (i, 0, 0)) for part in sizes],
        out_shape=[jax.ShapeDtypeStruct((chans, part, side_len), F32) for part in sizes],
        scratch_shapes=[pltpu.VMEM((rows, wide), BF16), pltpu.VMEM((rows, wide), BF16)],
        compiler_params=kernel_params(63),
        cost_estimate=COST,
        name="base_step",
    )(strip, step_size, highpass, model_image, *([edges] if with_edges else []), after)


def second_body(step_ref, half_ref, cosine_ref, sine_ref, base_ref, after_ref, moved_ref, pixels_ref):
    strips, _, chans, rows, width = half_ref.shape
    real = jnp.concatenate([half_ref[s, 0].reshape(chans * rows, width) for s in range(strips)], axis=1)
    imag = jnp.concatenate([half_ref[s, 1].reshape(chans * rows, width) for s in range(strips)], axis=1)
    dirty = dot_nn(real, cosine_ref[...]) - dot_nn(imag, sine_ref[...])
    pieces = []
    for chan in range(chans):
        moved = base_ref[chan] + step_ref[chan] * dirty[chan * rows : (chan + 1) * rows]
        moved_ref[chan] = moved
        pieces.append(moved)
    pixels_ref[...] = jnp.swapaxes(jnp.stack(pieces), 0, 1).astype(BF16)


def second_transform(step_size, half, cosine, sine_table, base, after):
    strips, _, chans, rows, width = half.shape
    side_len = cosine.shape[0]
    if width % 128 or rows % 16 or chans % 16:
        split = (strips, width, side_len)
        dirty = jnp.einsum("scmu,sul->cml", half[:, 0], cosine.reshape(split), preferred_element_type=F32)
        dirty = dirty - jnp.einsum("scmu,sul->cml", half[:, 1], sine_table.reshape(split), preferred_element_type=F32)
        moved = base + step_size[:, None, None] * dirty
        return moved, moved.astype(BF16).transpose(1, 0, 2)
    block = min(256, side_len)
    return pl.pallas_call(
        second_body,
        grid=(side_len // block,),
        in_specs=[
            SMEM,
            pl.BlockSpec(half.shape, lambda i: (0, 0, 0, 0, 0)),
            pl.BlockSpec((side_len, block), lambda i: (0, i)),
            pl.BlockSpec((side_len, block), lambda i: (0, i)),
            pl.BlockSpec((chans, rows, block), lambda i: (0, 0, i)),
            ANY,
        ],
        out_specs=[
            pl.BlockSpec((chans, rows, block), lambda i: (0, 0, i)),
            pl.BlockSpec((rows, chans, block), lambda i: (0, 0, i)),
        ],
        out_shape=[
            jax.ShapeDtypeStruct(base.shape, F32),
            jax.ShapeDtypeStruct((rows, chans, side_len), BF16),
        ],
        compiler_params=kernel_params(63),
        cost_estimate=COST,
        name="second_transform",
    )(step_size, half, cosine, sine_table, base, after)


def stacked(group_refs, first, count):
    return jnp.concatenate([ref[first + i] for i in range(count) for ref in group_refs], axis=0)


def gram_body(groups, before_ref, after_ref, *refs):
    total_ref = refs[groups]

    @pl.when(pl.program_id(0) == 0)
    def _():
        total_ref[...] = before_ref[...]

    total = total_ref[...]
    for first in range(0, refs[0].shape[0], GRAM_ROWS):
        pixels = stacked(refs[:groups], first, GRAM_ROWS)
        total = total + dot_nt(pixels, pixels)
    total_ref[...] = total


def gram_step(pieces, before, after):
    rows, chans, side_len = pieces[0].shape
    block = EDGE_ROWS // 2
    spec = pl.BlockSpec((block, chans, side_len), lambda i: (i, 0, 0))
    return pl.pallas_call(
        functools.partial(gram_body, len(pieces)),
        grid=(rows // block,),
        in_specs=[pl.BlockSpec(before.shape, lambda i: (0, 0)), ANY] + [spec] * len(pieces),
        out_specs=pl.BlockSpec(before.shape, lambda i: (0, 0)),
        out_shape=jax.ShapeDtypeStruct(before.shape, F32),
        compiler_params=kernel_params(63),
        cost_estimate=COST,
        name="gram_step",
    )(before, after, *pieces)


def newton_schulz(gram):
    size = gram.shape[0]
    frob_norm = jnp.sqrt(jnp.sum(gram * gram))
    identity = (iota((size, size), 0) == iota((size, size), 1)).astype(F32)
    current = gram / frob_norm
    middle = 0.5 * (3.0 * identity - current)
    inverse = middle
    for iteration in range(1, NS_ITERS):
        current = dot_nn(current, middle, HIGHEST)
        middle = 0.5 * (3.0 * identity - dot_nn(inverse, current, HIGHEST))
        inverse = dot_nn(middle, inverse, HIGHEST)
    return inverse, frob_norm


def polar_body(block_rows, groups, shrink_ref, gram_ref, *refs):
    chunks = len(block_rows)
    sizes = [len(rows) * EDGE_ROWS for rows in block_rows]
    moved_hbm = refs[:chunks]
    pixels_hbm = refs[chunks : chunks * (groups + 1)]
    out_hbm, moved, pixel_sems, moved_sems, out_sems = refs[chunks * (groups + 1) : chunks * (groups + 1) + 5]
    pixels = refs[chunks * (groups + 1) + 5 :]
    own, all_rows, side_len = moved.shape
    size = pixels[0].shape[2] * groups

    blocks = [
        (chunk, row) for chunk in [chunks - 1] + list(range(chunks - 1)) for row in range(0, sizes[chunk], EDGE_ROWS)
    ]
    far = 1 if groups > 1 else 0
    pixel_copies = []
    moved_copies = []
    for place, (chunk, row) in enumerate(blocks):
        part = pl.ds(row, EDGE_ROWS)
        into = pl.ds(block_rows[chunk][row // EDGE_ROWS], EDGE_ROWS)
        copies = [
            pltpu.make_async_copy(
                pixels_hbm[chunk * groups + group].at[part], pixels[chunk].at[group, part], pixel_sems.at[place, group]
            )
            for group in range(0 if chunk == chunks - 1 else far, groups)
        ]
        pixel_copies.append(copies)
        moved_copies.append(
            pltpu.make_async_copy(moved_hbm[chunk].at[:, part], moved.at[:, into], moved_sems.at[place])
        )
        for copy in copies + moved_copies[-1:]:
            copy.start()

    last_blocks = sizes[-1] // EDGE_ROWS
    for copies in pixel_copies[:last_blocks]:
        for copy in copies:
            copy.wait()
    total = gram_ref[...]
    for first in range(0, sizes[-1], GRAM_ROWS):
        data = stacked([pixels[-1].at[group] for group in range(groups)], first, GRAM_ROWS)
        total = total + dot_nt(data, data)
    gram = jnp.zeros((size, size), F32)
    for i in range(GRAM_ROWS):
        gram = gram + total[i * size : (i + 1) * size, i * size : (i + 1) * size]
    inverse, frob_norm = newton_schulz(gram)
    factor = shrink_ref[0] * jnp.sqrt(all_rows * side_len / frob_norm)
    select = (iota((own, size), 0) == iota((own, size), 1)).astype(F32)
    weights = (dot_nt(select, inverse, HIGHEST) * factor).astype(BF16)
    spread = POLAR_ROWS * own
    repeat = (iota((spread, own), 0) // POLAR_ROWS == iota((spread, own), 1)).astype(BF16)
    weights = dot_nn(repeat, weights).astype(BF16)

    def widened(count, first, channel_of, pixel_row_of):
        columns = iota((size, count), 1)
        chosen = dot_nn(weights, (iota((size, count), 0) == first + channel_of(columns)).astype(BF16))
        columns = iota((spread, count), 1)
        keep = iota((spread, count), 0) % POLAR_ROWS == pixel_row_of(columns)
        return jnp.where(keep, chosen, 0.0).astype(BF16)

    others = size - far * own
    far_weights = widened(POLAR_ROWS * others, far * own, lambda c: c % others, lambda c: c // others)
    if far:
        own_weights = widened(spread, 0, lambda c: c // POLAR_ROWS, lambda c: c % POLAR_ROWS)
        far_weights = jnp.concatenate([own_weights, far_weights], axis=1)

    out_copies = []
    for place, (chunk, row) in enumerate(blocks):
        if place >= last_blocks:
            for copy in pixel_copies[place]:
                copy.wait()
        moved_copies[place].wait()
        for first in range(row, row + EDGE_ROWS, POLAR_ROWS):
            into = block_rows[chunk][row // EDGE_ROWS] + first - row
            rows = moved[:, into : into + POLAR_ROWS]
            data = stacked([pixels[chunk].at[group] for group in range(far, groups)], first, POLAR_ROWS)
            if far:
                data = jnp.concatenate([rows.reshape(spread, side_len).astype(BF16), data], axis=0)
            polar = dot_nn(far_weights, data).reshape(own, POLAR_ROWS, side_len)
            moved[:, into : into + POLAR_ROWS] = rows - polar
        part = pl.ds(block_rows[chunk][row // EDGE_ROWS], EDGE_ROWS)
        copy = pltpu.make_async_copy(moved.at[:, part], out_hbm.at[:, part], out_sems.at[place])
        copy.start()
        out_copies.append(copy)
    for copy in out_copies:
        copy.wait()


def polar_step(shrinkage, gram, moved, gathered, block_rows):
    chunks = len(gathered)
    groups = len(gathered[0])
    chans, _, side_len = moved[0].shape
    blocks = sum(len(rows) for rows in block_rows)
    shape = (chans, blocks * EDGE_ROWS, side_len)
    flat = [piece for pieces in gathered for piece in pieces]
    return pl.pallas_call(
        functools.partial(polar_body, block_rows, groups),
        in_specs=[SMEM, pl.BlockSpec(memory_space=pltpu.VMEM)] + [ANY] * (chunks + len(flat)),
        out_specs=ANY,
        out_shape=jax.ShapeDtypeStruct(shape, F32),
        scratch_shapes=[
            pltpu.VMEM(shape, F32),
            pltpu.SemaphoreType.DMA((blocks, groups)),
            pltpu.SemaphoreType.DMA((blocks,)),
            pltpu.SemaphoreType.DMA((blocks,)),
        ]
        + [pltpu.VMEM((groups,) + pieces[0].shape, BF16) for pieces in gathered],
        compiler_params=kernel_params(63),
        cost_estimate=COST,
        name="polar_step",
    )(shrinkage, gram, *moved, *flat)


def neighbour_rows(model_image, reach):
    ends = lax.axis_size("strip") - 1
    head, tail = lax.optimization_barrier((model_image[:, :reach], model_image[:, model_image.shape[1] - reach :]))
    before = lax.ppermute(tail.astype(BF16), "strip", [(i, i + 1) for i in range(ends)])
    after = lax.ppermute(head.astype(BF16), "strip", [(i + 1, i) for i in range(ends)])
    return before, after


def swap(value, axis, bits):
    count = lax.axis_size(axis)
    return lax.ppermute(value, axis, [(i, i ^ bits) for i in range(count)])


def gather_channels(pixels, after=None):
    devices = lax.axis_size("chan")
    kept = [pixels] + [swap(pixels, "chan", bits) for bits in range(2, devices, 2)]
    if after is not None:
        kept = [pixels] + [gate(piece, after) for piece in kept[1:]]
    if devices == 1:
        return kept
    return kept + [swap(piece, "chan", 1) for piece in kept]


def local(grid, model_image, step_size, highpass, shrinkage):
    chans, own_rows, side_len = model_image.shape
    strips = lax.axis_size("strip")
    size = chans * lax.axis_size("chan")
    levels, taps = highpass.shape
    reach = (taps - 1) * 2 ** (levels - 1)
    blocks, near = chunk_blocks(own_rows, reach)
    chunks = len(blocks)
    strip = lax.axis_index("strip").astype(jnp.int32).reshape(1)

    cosine, sine_table = make_tables(side_len)
    split = np.stack([cosine.reshape(strips, own_rows, side_len), sine_table.reshape(strips, own_rows, side_len)])
    tables = [
        np.concatenate([split[:, :, row : row + EDGE_ROWS] for row in rows], axis=2).reshape(-1, side_len)
        for rows in blocks
    ]

    sides = neighbour_rows(model_image, reach)
    edges = jnp.concatenate(sides, axis=1)

    halves = {}
    moved = {}
    gathered = {}
    pixels = {}
    done = set()
    state = dict(last=strip, gram=jnp.zeros((GRAM_ROWS * size, GRAM_ROWS * size), F32), bases={})

    def first(chunk):
        sent, state["last"] = first_transform(tables[chunk], grid, strips, state["last"])
        if chunk == 2:
            gather(0)
            gram(0)
            done.add(0)
            for value in [state["gram"]] + list(sides):
                sent = gate(sent, value)
        halves[chunk] = lax.all_to_all(sent, "strip", split_axis=0, concat_axis=0, tiled=True)

    def base(with_edges):
        wanted = [chunk for chunk in range(chunks) if near[chunk] == with_edges]
        results = base_step(
            strip,
            strips,
            step_size,
            highpass,
            model_image,
            edges if with_edges else None,
            reach,
            [blocks[chunk] for chunk in wanted],
            state["last"],
        )
        state["bases"].update(zip(wanted, results))
        state["last"] = results[0]

    def second(chunk):
        moved[chunk], pixels[chunk] = second_transform(
            step_size, halves[chunk], cosine, sine_table, state["bases"][chunk], state["last"]
        )
        state["last"] = pixels[chunk]

    def gather(chunk):
        pieces = gather_channels(pixels[chunk], state["last"])
        if chans % 16:
            pieces = [jnp.concatenate(pieces, axis=1)]
        gathered[chunk] = pieces

    def gram(chunk):
        state["gram"] = gram_step(gathered[chunk], state["gram"], state["last"])
        state["last"] = state["gram"]

    first(0)
    if chunks > 1:
        first(1)
    base(False)
    for chunk in range(chunks):
        second(chunk)
        if chunk + 2 < chunks:
            first(chunk + 2)
        if chunk == 1:
            base(True)
            gather(1)
        if chunk >= 1 and chunk - 1 not in done:
            if chunk - 1 not in gathered:
                gather(chunk - 1)
            gram(chunk - 1)
    if chunks - 1 not in gathered:
        gather(chunks - 1)
    order = range(chunks)
    return polar_step(
        shrinkage, state["gram"], [moved[k] for k in order], [gathered[k] for k in order], blocks
    )


def solution(mesh):
    return jax.shard_map(
        local,
        mesh=mesh,
        in_specs=(
            P(None, "chan", "strip", None),
            P("chan", "strip", None),
            P("chan"),
            P(),
            P("strip"),
        ),
        out_specs=P("chan", "strip", None),
        check_vma=False,
    )
```

```python
import functools

import jax
import jax.numpy as jnp
import ml_dtypes
import numpy as np
from jax import lax
from jax.experimental import pallas as pl
from jax.experimental.pallas import tpu as pltpu
from jax.sharding import PartitionSpec as P

NS_ITERS = 5
EDGE_ROWS = 16
GRAM_ROWS = 4
POLAR_ROWS = 8
HIGHEST = lax.Precision.HIGHEST
F32 = jnp.float32
BF16 = jnp.bfloat16
MIB = 1 << 20

ANY = pl.BlockSpec(memory_space=pl.ANY)
SMEM = pl.BlockSpec(memory_space=pltpu.SMEM)


def kernel_params(mebibytes):
    return pltpu.CompilerParams(vmem_limit_bytes=mebibytes * MIB)


COST = pl.CostEstimate(flops=0, bytes_accessed=1 << 16, transcendentals=0)


def dot_nt(a, b, precision=None):
    return lax.dot_general(
        a, b, (((1,), (1,)), ((), ())), precision=precision, preferred_element_type=F32
    )


def dot_nn(a, b, precision=None):
    return lax.dot_general(
        a, b, (((1,), (0,)), ((), ())), precision=precision, preferred_element_type=F32
    )


def iota(shape, dim):
    return lax.broadcasted_iota(jnp.int32, shape, dim)


def make_tables(side_len):
    indices = np.arange(side_len, dtype=np.int64)
    phases = (np.outer(indices, indices) % side_len).astype(np.float32) * np.float32(
        2.0 * 3.141592653589793 / side_len
    )
    unit_scale = np.float32(float(side_len) ** (-0.5))
    cosine = (np.cos(phases) * unit_scale).astype(ml_dtypes.bfloat16)
    sine_table = (np.sin(phases) * unit_scale).astype(ml_dtypes.bfloat16)
    return cosine, sine_table


def chunk_blocks(own_rows, reach):
    blocks = list(range(0, own_rows, EDGE_ROWS))
    near = [row for row in blocks if row < reach or row + EDGE_ROWS > own_rows - reach]
    inner = [row for row in blocks if row not in near]
    quarter = len(blocks) // 4
    sizes = [quarter, len(blocks) - 2 * quarter - 1, quarter, 1]
    ahead = sizes[0] + sizes[1]
    order = inner[:ahead] + near + inner[ahead:]
    chunks = [order[sum(sizes[:place]) : sum(sizes[: place + 1])] for place in range(len(sizes))]
    return chunks, [any(row in near for row in chunk) for chunk in chunks]


def gate_body(value_ref, after_ref, out_ref):
    pass


def gate(value, after):
    return pl.pallas_call(
        gate_body,
        in_specs=[ANY, ANY],
        out_specs=ANY,
        out_shape=jax.ShapeDtypeStruct(value.shape, value.dtype),
        input_output_aliases={0: 0},
        compiler_params=kernel_params(63),
        cost_estimate=COST,
        name="gate",
    )(value, after)


def first_body(table_ref, grid_ref, after_ref, out_ref, token_ref):
    token_ref[...] = jnp.zeros(token_ref.shape, F32)
    strips, _, chans, rows, width = out_ref.shape
    side_len = table_ref.shape[-1]
    table = table_ref[...]
    middle = strips * rows
    turned = jnp.concatenate([-table[middle:], table[:middle]], axis=0)
    total = dot_nt(table, grid_ref[0].reshape(chans * width, side_len))
    total = total + dot_nt(turned, grid_ref[1].reshape(chans * width, side_len))
    total = total.astype(BF16)
    for part in range(2):
        for strip in range(strips):
            first = (part * strips + strip) * rows
            for chan in range(chans):
                out_ref[strip, part, chan] = total[first : first + rows, chan * width : (chan + 1) * width]


def first_transform(table, grid, strips, after):
    _, chans, width, side_len = grid.shape
    rows = table.shape[0] // (2 * strips)
    shape = (strips, 2, chans, rows, width)
    if width % 128 or rows % 16:
        middle = strips * rows
        turned = jnp.concatenate([-table[middle:], table[:middle]], axis=0)
        total = jnp.einsum("mv,cuv->mcu", table, grid[0], preferred_element_type=F32)
        total = total + jnp.einsum("mv,cuv->mcu", turned, grid[1], preferred_element_type=F32)
        total = total.astype(BF16).reshape(2, strips, rows, chans, width)
        return total.transpose(1, 0, 3, 2, 4), jnp.zeros((8, 128), F32)
    block = 4 if chans % 4 == 0 else 1
    return pl.pallas_call(
        first_body,
        grid=(chans // block,),
        in_specs=[
            pl.BlockSpec(table.shape, lambda i: (0, 0)),
            pl.BlockSpec((2, block, width, side_len), lambda i: (0, i, 0, 0)),
            ANY,
        ],
        out_specs=[
            pl.BlockSpec((strips, 2, block, rows, width), lambda i: (0, 0, i, 0, 0)),
            pl.BlockSpec((8, 128), lambda i: (0, 0)),
        ],
        out_shape=[jax.ShapeDtypeStruct(shape, BF16), jax.ShapeDtypeStruct((8, 128), F32)],
        compiler_params=kernel_params(63),
        cost_estimate=COST,
        name="first_transform",
    )(table, grid, after)


def band_matrix(taps_of, levels, taps, own_rows, reach, first_row, image_rows):
    half_taps = taps // 2
    shape = (own_rows, own_rows + 2 * reach)
    row = iota(shape, 0)
    column = iota(shape, 1)
    place = jnp.where(
        column < own_rows, column, jnp.where(column < own_rows + reach, column - own_rows - reach, column - reach)
    )
    total = jnp.zeros(shape, F32)
    for level in range(levels):
        dilation = 2**level
        for outer in range(taps):
            detail_row = row - (outer - half_taps) * dilation
            inside = (detail_row + first_row >= 0) & (detail_row + first_row < image_rows)
            for inner in range(taps):
                hit = inside & (place == detail_row + (inner - half_taps) * dilation)
                total = total + jnp.where(hit, taps_of(level, outer) * taps_of(level, inner), 0.0)
    return total


def base_body(levels, taps, blocks, strips, reach, with_edges, strip_ref, step_ref, highpass_ref, model_ref, *refs):
    high, low = refs[-2:]
    out_refs = refs[2:-2] if with_edges else refs[1:-2]
    count, own_rows, side_len = model_ref.shape

    @pl.when(pl.program_id(0) == 0)
    def _():
        band = band_matrix(
            lambda level, tap: highpass_ref[level, tap],
            levels,
            taps,
            own_rows,
            reach,
            strip_ref[0] * own_rows,
            strips * own_rows,
        )
        top = band.astype(BF16)
        high[...] = top
        low[...] = (band - top.astype(F32)).astype(BF16)

    wide = own_rows + 2 * reach if with_edges else own_rows
    first = pl.program_id(0) * count
    for chan in range(count):
        model = model_ref[chan]
        top = model.astype(BF16)
        rest = (model - top.astype(F32)).astype(BF16)
        whole = top
        if with_edges:
            whole = jnp.concatenate([top.astype(F32), refs[0][chan].astype(F32)], axis=0).astype(BF16)
        gradient = dot_nn(high[:, :wide], whole)
        gradient = gradient + dot_nn(low[:, :wide], whole)
        gradient = gradient + dot_nn(high[:, :own_rows], rest)
        base = model - step_ref[first + chan] * gradient
        for rows, out_ref in zip(blocks, out_refs):
            for place, row in enumerate(rows):
                out_ref[chan, place * EDGE_ROWS : (place + 1) * EDGE_ROWS] = base[row : row + EDGE_ROWS]


def base_step(strip, strips, step_size, highpass, model_image, edges, reach, blocks, after):
    chans, rows, side_len = model_image.shape
    levels, taps = highpass.shape
    count = 2 if chans % 2 == 0 else 1
    wide = rows + 2 * reach
    sizes = [len(chunk) * EDGE_ROWS for chunk in blocks]
    with_edges = edges is not None
    edge_specs = [pl.BlockSpec((count, 2 * reach, side_len), lambda i: (i, 0, 0))] if with_edges else []
    return pl.pallas_call(
        functools.partial(base_body, levels, taps, blocks, strips, reach, with_edges),
        grid=(chans // count,),
        in_specs=[SMEM, SMEM, SMEM, pl.BlockSpec((count, rows, side_len), lambda i: (i, 0, 0))] + edge_specs + [ANY],
        out_specs=[pl.BlockSpec((count, part, side_len), lambda i: (i, 0, 0)) for part in sizes],
        out_shape=[jax.ShapeDtypeStruct((chans, part, side_len), F32) for part in sizes],
        scratch_shapes=[pltpu.VMEM((rows, wide), BF16), pltpu.VMEM((rows, wide), BF16)],
        compiler_params=kernel_params(63),
        cost_estimate=COST,
        name="base_step",
    )(strip, step_size, highpass, model_image, *([edges] if with_edges else []), after)


def second_body(step_ref, half_ref, cosine_ref, sine_ref, base_ref, after_ref, moved_ref, pixels_ref):
    strips, _, chans, rows, width = half_ref.shape
    real = jnp.concatenate([half_ref[s, 0].reshape(chans * rows, width) for s in range(strips)], axis=1)
    imag = jnp.concatenate([half_ref[s, 1].reshape(chans * rows, width) for s in range(strips)], axis=1)
    dirty = dot_nn(real, cosine_ref[...]) - dot_nn(imag, sine_ref[...])
    pieces = []
    for chan in range(chans):
        moved = base_ref[chan] + step_ref[chan] * dirty[chan * rows : (chan + 1) * rows]
        moved_ref[chan] = moved
        pieces.append(moved)
    pixels_ref[...] = jnp.swapaxes(jnp.stack(pieces), 0, 1).astype(BF16)


def second_transform(step_size, half, cosine, sine_table, base, after):
    strips, _, chans, rows, width = half.shape
    side_len = cosine.shape[0]
    if width % 128 or rows % 16 or chans % 16:
        split = (strips, width, side_len)
        dirty = jnp.einsum("scmu,sul->cml", half[:, 0], cosine.reshape(split), preferred_element_type=F32)
        dirty = dirty - jnp.einsum("scmu,sul->cml", half[:, 1], sine_table.reshape(split), preferred_element_type=F32)
        moved = base + step_size[:, None, None] * dirty
        return moved, moved.astype(BF16).transpose(1, 0, 2)
    block = min(256, side_len)
    return pl.pallas_call(
        second_body,
        grid=(side_len // block,),
        in_specs=[
            SMEM,
            pl.BlockSpec(half.shape, lambda i: (0, 0, 0, 0, 0)),
            pl.BlockSpec((side_len, block), lambda i: (0, i)),
            pl.BlockSpec((side_len, block), lambda i: (0, i)),
            pl.BlockSpec((chans, rows, block), lambda i: (0, 0, i)),
            ANY,
        ],
        out_specs=[
            pl.BlockSpec((chans, rows, block), lambda i: (0, 0, i)),
            pl.BlockSpec((rows, chans, block), lambda i: (0, 0, i)),
        ],
        out_shape=[
            jax.ShapeDtypeStruct(base.shape, F32),
            jax.ShapeDtypeStruct((rows, chans, side_len), BF16),
        ],
        compiler_params=kernel_params(63),
        cost_estimate=COST,
        name="second_transform",
    )(step_size, half, cosine, sine_table, base, after)


def stacked(group_refs, first, count):
    return jnp.concatenate([ref[first + i] for i in range(count) for ref in group_refs], axis=0)


def gram_body(groups, before_ref, after_ref, *refs):
    total_ref = refs[groups]

    @pl.when(pl.program_id(0) == 0)
    def _():
        total_ref[...] = before_ref[...]

    total = total_ref[...]
    for first in range(0, refs[0].shape[0], GRAM_ROWS):
        pixels = stacked(refs[:groups], first, GRAM_ROWS)
        total = total + dot_nt(pixels, pixels)
    total_ref[...] = total


def gram_step(pieces, before, after):
    rows, chans, side_len = pieces[0].shape
    block = EDGE_ROWS // 2
    spec = pl.BlockSpec((block, chans, side_len), lambda i: (i, 0, 0))
    return pl.pallas_call(
        functools.partial(gram_body, len(pieces)),
        grid=(rows // block,),
        in_specs=[pl.BlockSpec(before.shape, lambda i: (0, 0)), ANY] + [spec] * len(pieces),
        out_specs=pl.BlockSpec(before.shape, lambda i: (0, 0)),
        out_shape=jax.ShapeDtypeStruct(before.shape, F32),
        compiler_params=kernel_params(63),
        cost_estimate=COST,
        name="gram_step",
    )(before, after, *pieces)


def newton_schulz(gram):
    size = gram.shape[0]
    frob_norm = jnp.sqrt(jnp.sum(gram * gram))
    identity = (iota((size, size), 0) == iota((size, size), 1)).astype(F32)
    current = gram / frob_norm
    middle = 0.5 * (3.0 * identity - current)
    inverse = middle
    for iteration in range(1, NS_ITERS):
        current = dot_nn(current, middle, HIGHEST)
        middle = 0.5 * (3.0 * identity - dot_nn(inverse, current, HIGHEST))
        inverse = dot_nn(middle, inverse, HIGHEST)
    return inverse, frob_norm


def polar_body(block_rows, groups, shrink_ref, gram_ref, *refs):
    chunks = len(block_rows)
    sizes = [len(rows) * EDGE_ROWS for rows in block_rows]
    moved_hbm = refs[:chunks]
    pixels_hbm = refs[chunks : chunks * (groups + 1)]
    out_hbm, moved, pixel_sems, moved_sems, out_sems = refs[chunks * (groups + 1) : chunks * (groups + 1) + 5]
    pixels = refs[chunks * (groups + 1) + 5 :]
    own, all_rows, side_len = moved.shape
    size = pixels[0].shape[2] * groups

    blocks = [
        (chunk, row) for chunk in [chunks - 1] + list(range(chunks - 1)) for row in range(0, sizes[chunk], EDGE_ROWS)
    ]
    far = 1 if groups > 1 else 0
    pixel_copies = []
    moved_copies = []
    for place, (chunk, row) in enumerate(blocks):
        part = pl.ds(row, EDGE_ROWS)
        into = pl.ds(block_rows[chunk][row // EDGE_ROWS], EDGE_ROWS)
        copies = [
            pltpu.make_async_copy(
                pixels_hbm[chunk * groups + group].at[part], pixels[chunk].at[group, part], pixel_sems.at[place, group]
            )
            for group in range(0 if chunk == chunks - 1 else far, groups)
        ]
        pixel_copies.append(copies)
        moved_copies.append(
            pltpu.make_async_copy(moved_hbm[chunk].at[:, part], moved.at[:, into], moved_sems.at[place])
        )
        for copy in copies + moved_copies[-1:]:
            copy.start()

    last_blocks = sizes[-1] // EDGE_ROWS
    for copies in pixel_copies[:last_blocks]:
        for copy in copies:
            copy.wait()
    total = gram_ref[...]
    for first in range(0, sizes[-1], GRAM_ROWS):
        data = stacked([pixels[-1].at[group] for group in range(groups)], first, GRAM_ROWS)
        total = total + dot_nt(data, data)
    gram = jnp.zeros((size, size), F32)
    for i in range(GRAM_ROWS):
        gram = gram + total[i * size : (i + 1) * size, i * size : (i + 1) * size]
    inverse, frob_norm = newton_schulz(gram)
    factor = shrink_ref[0] * jnp.sqrt(all_rows * side_len / frob_norm)
    select = (iota((own, size), 0) == iota((own, size), 1)).astype(F32)
    weights = (dot_nt(select, inverse, HIGHEST) * factor).astype(BF16)
    spread = POLAR_ROWS * own
    repeat = (iota((spread, own), 0) // POLAR_ROWS == iota((spread, own), 1)).astype(BF16)
    weights = dot_nn(repeat, weights).astype(BF16)

    def widened(count, first, channel_of, pixel_row_of):
        columns = iota((size, count), 1)
        chosen = dot_nn(weights, (iota((size, count), 0) == first + channel_of(columns)).astype(BF16))
        columns = iota((spread, count), 1)
        keep = iota((spread, count), 0) % POLAR_ROWS == pixel_row_of(columns)
        return jnp.where(keep, chosen, 0.0).astype(BF16)

    others = size - far * own
    far_weights = widened(POLAR_ROWS * others, far * own, lambda c: c % others, lambda c: c // others)
    if far:
        own_weights = widened(spread, 0, lambda c: c // POLAR_ROWS, lambda c: c % POLAR_ROWS)
        far_weights = jnp.concatenate([own_weights, far_weights], axis=1)

    out_copies = []
    for place, (chunk, row) in enumerate(blocks):
        if place >= last_blocks:
            for copy in pixel_copies[place]:
                copy.wait()
        moved_copies[place].wait()
        for first in range(row, row + EDGE_ROWS, POLAR_ROWS):
            into = block_rows[chunk][row // EDGE_ROWS] + first - row
            rows = moved[:, into : into + POLAR_ROWS]
            data = stacked([pixels[chunk].at[group] for group in range(far, groups)], first, POLAR_ROWS)
            if far:
                data = jnp.concatenate([rows.reshape(spread, side_len).astype(BF16), data], axis=0)
            polar = dot_nn(far_weights, data).reshape(own, POLAR_ROWS, side_len)
            moved[:, into : into + POLAR_ROWS] = rows - polar
        part = pl.ds(block_rows[chunk][row // EDGE_ROWS], EDGE_ROWS)
        copy = pltpu.make_async_copy(moved.at[:, part], out_hbm.at[:, part], out_sems.at[place])
        copy.start()
        out_copies.append(copy)
    for copy in out_copies:
        copy.wait()


def polar_step(shrinkage, gram, moved, gathered, block_rows):
    chunks = len(gathered)
    groups = len(gathered[0])
    chans, _, side_len = moved[0].shape
    blocks = sum(len(rows) for rows in block_rows)
    shape = (chans, blocks * EDGE_ROWS, side_len)
    flat = [piece for pieces in gathered for piece in pieces]
    return pl.pallas_call(
        functools.partial(polar_body, block_rows, groups),
        in_specs=[SMEM, pl.BlockSpec(memory_space=pltpu.VMEM)] + [ANY] * (chunks + len(flat)),
        out_specs=ANY,
        out_shape=jax.ShapeDtypeStruct(shape, F32),
        scratch_shapes=[
            pltpu.VMEM(shape, F32),
            pltpu.SemaphoreType.DMA((blocks, groups)),
            pltpu.SemaphoreType.DMA((blocks,)),
            pltpu.SemaphoreType.DMA((blocks,)),
        ]
        + [pltpu.VMEM((groups,) + pieces[0].shape, BF16) for pieces in gathered],
        compiler_params=kernel_params(63),
        cost_estimate=COST,
        name="polar_step",
    )(shrinkage, gram, *moved, *flat)


def neighbour_rows(model_image, reach):
    ends = lax.axis_size("strip") - 1
    head, tail = lax.optimization_barrier((model_image[:, :reach], model_image[:, model_image.shape[1] - reach :]))
    before = lax.ppermute(tail.astype(BF16), "strip", [(i, i + 1) for i in range(ends)])
    after = lax.ppermute(head.astype(BF16), "strip", [(i + 1, i) for i in range(ends)])
    return before, after


def swap(value, axis, bits):
    count = lax.axis_size(axis)
    return lax.ppermute(value, axis, [(i, i ^ bits) for i in range(count)])


def gather_channels(pixels, after):
    devices = lax.axis_size("chan")
    kept = [pixels] + [swap(pixels, "chan", bits) for bits in range(2, devices, 2)]
    for value in after:
        kept = [pixels] + [gate(piece, value) for piece in kept[1:]]
    if devices == 1:
        return kept
    return kept + [swap(piece, "chan", 1) for piece in kept]


def local(grid, model_image, step_size, highpass, shrinkage):
    chans, own_rows, side_len = model_image.shape
    strips = lax.axis_size("strip")
    size = chans * lax.axis_size("chan")
    levels, taps = highpass.shape
    reach = (taps - 1) * 2 ** (levels - 1)
    blocks, near = chunk_blocks(own_rows, reach)
    chunks = len(blocks)
    strip = lax.axis_index("strip").astype(jnp.int32).reshape(1)

    cosine, sine_table = make_tables(side_len)
    split = np.stack([cosine.reshape(strips, own_rows, side_len), sine_table.reshape(strips, own_rows, side_len)])
    tables = [
        np.concatenate([split[:, :, row : row + EDGE_ROWS] for row in rows], axis=2).reshape(-1, side_len)
        for rows in blocks
    ]

    sides = neighbour_rows(model_image, reach)
    edges = jnp.concatenate(sides, axis=1)

    halves = {}
    moved = {}
    gathered = {}
    pixels = {}
    done = set()
    state = dict(last=strip, gram=jnp.zeros((GRAM_ROWS * size, GRAM_ROWS * size), F32), bases={})

    def first(chunk):
        sent, state["last"] = first_transform(tables[chunk], grid, strips, state["last"])
        if chunk == 1:
            base(False)
            sent = gate(sent, state["last"])
        if chunk == 2:
            gather(0)
            gram(0)
            done.add(0)
            sent = gate(sent, state["last"])
        if chunk == 3:
            base(True)
            sent = gate(sent, state["last"])
        halves[chunk] = lax.all_to_all(sent, "strip", split_axis=0, concat_axis=0, tiled=True)

    def base(with_edges):
        wanted = [chunk for chunk in range(chunks) if near[chunk] == with_edges]
        results = base_step(
            strip,
            strips,
            step_size,
            highpass,
            model_image,
            edges if with_edges else None,
            reach,
            [blocks[chunk] for chunk in wanted],
            state["last"],
        )
        state["bases"].update(zip(wanted, results))
        state["last"] = results[0]

    def second(chunk):
        moved[chunk], pixels[chunk] = second_transform(
            step_size, halves[chunk], cosine, sine_table, state["bases"][chunk], state["last"]
        )
        state["last"] = pixels[chunk]

    def gather(chunk):
        pieces = gather_channels(pixels[chunk], [state["last"]] + (list(sides) if chunk == 0 else []))
        if chans % 16:
            pieces = [jnp.concatenate(pieces, axis=1)]
        gathered[chunk] = pieces

    def gram(chunk):
        state["gram"] = gram_step(gathered[chunk], state["gram"], state["last"])
        state["last"] = state["gram"]

    first(0)
    first(1)
    for chunk in range(chunks):
        second(chunk)
        if chunk + 2 < chunks:
            first(chunk + 2)
        if chunk == 1:
            gather(1)
        if chunk >= 1 and chunk - 1 not in done:
            if chunk - 1 not in gathered:
                gather(chunk - 1)
            gram(chunk - 1)
    if chunks - 1 not in gathered:
        gather(chunks - 1)
    order = range(chunks)
    return polar_step(
        shrinkage, state["gram"], [moved[k] for k in order], [gathered[k] for k in order], blocks
    )


def solution(mesh):
    return jax.shard_map(
        local,
        mesh=mesh,
        in_specs=(
            P(None, "chan", "strip", None),
            P("chan", "strip", None),
            P("chan"),
            P(),
            P("strip"),
        ),
        out_specs=P("chan", "strip", None),
        check_vma=False,
    )
```

```python
import functools

import jax
import jax.numpy as jnp
import ml_dtypes
import numpy as np
from jax import lax
from jax.experimental import pallas as pl
from jax.experimental.pallas import tpu as pltpu
from jax.sharding import PartitionSpec as P

NS_ITERS = 5
EDGE_ROWS = 16
GRAM_ROWS = 4
POLAR_ROWS = 8
HIGHEST = lax.Precision.HIGHEST
F32 = jnp.float32
BF16 = jnp.bfloat16
MIB = 1 << 20

ANY = pl.BlockSpec(memory_space=pl.ANY)
SMEM = pl.BlockSpec(memory_space=pltpu.SMEM)


def kernel_params(mebibytes):
    return pltpu.CompilerParams(vmem_limit_bytes=mebibytes * MIB)


COST = pl.CostEstimate(flops=0, bytes_accessed=1 << 16, transcendentals=0)


def dot_nt(a, b, precision=None):
    return lax.dot_general(
        a, b, (((1,), (1,)), ((), ())), precision=precision, preferred_element_type=F32
    )


def dot_nn(a, b, precision=None):
    return lax.dot_general(
        a, b, (((1,), (0,)), ((), ())), precision=precision, preferred_element_type=F32
    )


def iota(shape, dim):
    return lax.broadcasted_iota(jnp.int32, shape, dim)


def make_tables(side_len):
    indices = np.arange(side_len, dtype=np.int64)
    phases = (np.outer(indices, indices) % side_len).astype(np.float32) * np.float32(
        2.0 * 3.141592653589793 / side_len
    )
    unit_scale = np.float32(float(side_len) ** (-0.5))
    cosine = (np.cos(phases) * unit_scale).astype(ml_dtypes.bfloat16)
    sine_table = (np.sin(phases) * unit_scale).astype(ml_dtypes.bfloat16)
    return cosine, sine_table


def chunk_rows(own_rows):
    quarter = own_rows // 4
    sizes = [quarter, own_rows - 2 * quarter - EDGE_ROWS, quarter, EDGE_ROWS]
    sizes = [size for size in sizes if size > 0]
    return [sum(sizes[:place]) for place in range(len(sizes))], sizes


def gate_body(value_ref, after_ref, out_ref):
    pass


def gate(value, after):
    return pl.pallas_call(
        gate_body,
        in_specs=[ANY, ANY],
        out_specs=ANY,
        out_shape=jax.ShapeDtypeStruct(value.shape, value.dtype),
        input_output_aliases={0: 0},
        compiler_params=kernel_params(63),
        cost_estimate=COST,
        name="gate",
    )(value, after)


def first_body(table_ref, grid_ref, after_ref, out_ref, token_ref):
    token_ref[...] = jnp.zeros(token_ref.shape, F32)
    strips, _, chans, rows, width = out_ref.shape
    side_len = table_ref.shape[-1]
    table = table_ref[...]
    middle = strips * rows
    turned = jnp.concatenate([-table[middle:], table[:middle]], axis=0)
    total = dot_nt(table, grid_ref[0].reshape(chans * width, side_len))
    total = total + dot_nt(turned, grid_ref[1].reshape(chans * width, side_len))
    total = total.astype(BF16)
    for part in range(2):
        for strip in range(strips):
            first = (part * strips + strip) * rows
            for chan in range(chans):
                out_ref[strip, part, chan] = total[first : first + rows, chan * width : (chan + 1) * width]


def first_transform(table, grid, strips, after):
    _, chans, width, side_len = grid.shape
    rows = table.shape[0] // (2 * strips)
    shape = (strips, 2, chans, rows, width)
    if width % 128 or rows % 16:
        middle = strips * rows
        turned = jnp.concatenate([-table[middle:], table[:middle]], axis=0)
        total = jnp.einsum("mv,cuv->mcu", table, grid[0], preferred_element_type=F32)
        total = total + jnp.einsum("mv,cuv->mcu", turned, grid[1], preferred_element_type=F32)
        total = total.astype(BF16).reshape(2, strips, rows, chans, width)
        return total.transpose(1, 0, 3, 2, 4), jnp.zeros((8, 128), F32)
    block = 4 if chans % 4 == 0 else 1
    return pl.pallas_call(
        first_body,
        grid=(chans // block,),
        in_specs=[
            pl.BlockSpec(table.shape, lambda i: (0, 0)),
            pl.BlockSpec((2, block, width, side_len), lambda i: (0, i, 0, 0)),
            ANY,
        ],
        out_specs=[
            pl.BlockSpec((strips, 2, block, rows, width), lambda i: (0, 0, i, 0, 0)),
            pl.BlockSpec((8, 128), lambda i: (0, 0)),
        ],
        out_shape=[jax.ShapeDtypeStruct(shape, BF16), jax.ShapeDtypeStruct((8, 128), F32)],
        compiler_params=kernel_params(63),
        cost_estimate=COST,
        name="first_transform",
    )(table, grid, after)


def band_matrix(taps_of, levels, taps, own_rows, reach, first_row, image_rows):
    half_taps = taps // 2
    shape = (own_rows, own_rows + 2 * reach)
    row = iota(shape, 0)
    column = iota(shape, 1)
    place = jnp.where(
        column < own_rows, column, jnp.where(column < own_rows + reach, column - own_rows - reach, column - reach)
    )
    total = jnp.zeros(shape, F32)
    for level in range(levels):
        dilation = 2**level
        for outer in range(taps):
            detail_row = row - (outer - half_taps) * dilation
            inside = (detail_row + first_row >= 0) & (detail_row + first_row < image_rows)
            for inner in range(taps):
                hit = inside & (place == detail_row + (inner - half_taps) * dilation)
                total = total + jnp.where(hit, taps_of(level, outer) * taps_of(level, inner), 0.0)
    return total


def base_body(levels, taps, starts, strips, strip_ref, step_ref, highpass_ref, model_ref, edge_ref, after_ref, *refs):
    high, low = refs[-2:]
    out_refs = refs[:-2]
    block, own_rows, side_len = model_ref.shape
    reach = edge_ref.shape[1] // 2

    @pl.when(pl.program_id(0) == 0)
    def _():
        band = band_matrix(
            lambda level, tap: highpass_ref[level, tap],
            levels,
            taps,
            own_rows,
            reach,
            strip_ref[0] * own_rows,
            strips * own_rows,
        )
        top = band.astype(BF16)
        high[...] = top
        low[...] = (band - top.astype(F32)).astype(BF16)

    first = pl.program_id(0) * block
    for chan in range(block):
        model = model_ref[chan]
        top = model.astype(BF16)
        rest = (model - top.astype(F32)).astype(BF16)
        edge = edge_ref[chan].astype(F32)
        whole = jnp.concatenate([top.astype(F32), edge], axis=0).astype(BF16)
        gradient = dot_nn(high[...], whole)
        gradient = gradient + dot_nn(low[...], whole)
        gradient = gradient + dot_nn(high[:, :own_rows], rest)
        base = model - step_ref[first + chan] * gradient
        for start, out_ref in zip(starts, out_refs):
            out_ref[chan] = base[start : start + out_ref.shape[1]]


def base_step(strip, strips, step_size, highpass, model_image, edges, starts, sizes, after):
    chans, rows, side_len = model_image.shape
    levels, taps = highpass.shape
    reach = edges.shape[1] // 2
    block = 2 if chans % 2 == 0 else 1
    wide = rows + 2 * reach
    return pl.pallas_call(
        functools.partial(base_body, levels, taps, starts, strips),
        grid=(chans // block,),
        in_specs=[
            SMEM,
            SMEM,
            SMEM,
            pl.BlockSpec((block, rows, side_len), lambda i: (i, 0, 0)),
            pl.BlockSpec((block, 2 * reach, side_len), lambda i: (i, 0, 0)),
            ANY,
        ],
        out_specs=[pl.BlockSpec((block, part, side_len), lambda i: (i, 0, 0)) for part in sizes],
        out_shape=[jax.ShapeDtypeStruct((chans, part, side_len), F32) for part in sizes],
        scratch_shapes=[pltpu.VMEM((rows, wide), BF16), pltpu.VMEM((rows, wide), BF16)],
        compiler_params=kernel_params(63),
        cost_estimate=COST,
        name="base_step",
    )(strip, step_size, highpass, model_image, edges, after)


def second_body(step_ref, half_ref, cosine_ref, sine_ref, base_ref, after_ref, moved_ref, pixels_ref):
    strips, _, chans, rows, width = half_ref.shape
    real = jnp.concatenate([half_ref[s, 0].reshape(chans * rows, width) for s in range(strips)], axis=1)
    imag = jnp.concatenate([half_ref[s, 1].reshape(chans * rows, width) for s in range(strips)], axis=1)
    dirty = dot_nn(real, cosine_ref[...]) - dot_nn(imag, sine_ref[...])
    pieces = []
    for chan in range(chans):
        moved = base_ref[chan] + step_ref[chan] * dirty[chan * rows : (chan + 1) * rows]
        moved_ref[chan] = moved
        pieces.append(moved)
    pixels_ref[...] = jnp.swapaxes(jnp.stack(pieces), 0, 1).astype(BF16)


def second_transform(step_size, half, cosine, sine_table, base, after):
    strips, _, chans, rows, width = half.shape
    side_len = cosine.shape[0]
    if width % 128 or rows % 16 or chans % 16:
        split = (strips, width, side_len)
        dirty = jnp.einsum("scmu,sul->cml", half[:, 0], cosine.reshape(split), preferred_element_type=F32)
        dirty = dirty - jnp.einsum("scmu,sul->cml", half[:, 1], sine_table.reshape(split), preferred_element_type=F32)
        moved = base + step_size[:, None, None] * dirty
        return moved, moved.astype(BF16).transpose(1, 0, 2)
    block = min(256, side_len)
    return pl.pallas_call(
        second_body,
        grid=(side_len // block,),
        in_specs=[
            SMEM,
            pl.BlockSpec(half.shape, lambda i: (0, 0, 0, 0, 0)),
            pl.BlockSpec((side_len, block), lambda i: (0, i)),
            pl.BlockSpec((side_len, block), lambda i: (0, i)),
            pl.BlockSpec((chans, rows, block), lambda i: (0, 0, i)),
            ANY,
        ],
        out_specs=[
            pl.BlockSpec((chans, rows, block), lambda i: (0, 0, i)),
            pl.BlockSpec((rows, chans, block), lambda i: (0, 0, i)),
        ],
        out_shape=[
            jax.ShapeDtypeStruct(base.shape, F32),
            jax.ShapeDtypeStruct((rows, chans, side_len), BF16),
        ],
        compiler_params=kernel_params(63),
        cost_estimate=COST,
        name="second_transform",
    )(step_size, half, cosine, sine_table, base, after)


def stacked(group_refs, first, count):
    return jnp.concatenate([ref[first + i] for i in range(count) for ref in group_refs], axis=0)


def gram_body(groups, before_ref, after_ref, *refs):
    total_ref = refs[groups]

    @pl.when(pl.program_id(0) == 0)
    def _():
        total_ref[...] = before_ref[...]

    total = total_ref[...]
    for first in range(0, refs[0].shape[0], GRAM_ROWS):
        pixels = stacked(refs[:groups], first, GRAM_ROWS)
        total = total + dot_nt(pixels, pixels)
    total_ref[...] = total


def gram_step(pieces, before, after):
    rows, chans, side_len = pieces[0].shape
    block = EDGE_ROWS // 2
    spec = pl.BlockSpec((block, chans, side_len), lambda i: (i, 0, 0))
    return pl.pallas_call(
        functools.partial(gram_body, len(pieces)),
        grid=(rows // block,),
        in_specs=[pl.BlockSpec(before.shape, lambda i: (0, 0)), ANY] + [spec] * len(pieces),
        out_specs=pl.BlockSpec(before.shape, lambda i: (0, 0)),
        out_shape=jax.ShapeDtypeStruct(before.shape, F32),
        compiler_params=kernel_params(63),
        cost_estimate=COST,
        name="gram_step",
    )(before, after, *pieces)


def newton_schulz(gram):
    size = gram.shape[0]
    frob_norm = jnp.sqrt(jnp.sum(gram * gram))
    identity = (iota((size, size), 0) == iota((size, size), 1)).astype(F32)
    current = gram / frob_norm
    middle = 0.5 * (3.0 * identity - current)
    inverse = middle
    for iteration in range(1, NS_ITERS):
        current = dot_nn(current, middle, HIGHEST)
        middle = 0.5 * (3.0 * identity - dot_nn(inverse, current, HIGHEST))
        inverse = dot_nn(middle, inverse, HIGHEST)
    return inverse, frob_norm


def polar_body(starts, sizes, groups, shrink_ref, gram_ref, *refs):
    chunks = len(sizes)
    moved_hbm = refs[:chunks]
    pixels_hbm = refs[chunks : chunks * (groups + 1)]
    out_hbm, moved, pixel_sems, moved_sems, out_sems = refs[chunks * (groups + 1) : chunks * (groups + 1) + 5]
    pixels = refs[chunks * (groups + 1) + 5 :]
    own, all_rows, side_len = moved.shape
    size = pixels[0].shape[2] * groups

    blocks = [
        (chunk, row) for chunk in [chunks - 1] + list(range(chunks - 1)) for row in range(0, sizes[chunk], EDGE_ROWS)
    ]
    far = 1 if groups > 1 else 0
    pixel_copies = []
    moved_copies = []
    for place, (chunk, row) in enumerate(blocks):
        part = pl.ds(row, EDGE_ROWS)
        into = pl.ds(starts[chunk] + row, EDGE_ROWS)
        copies = [
            pltpu.make_async_copy(
                pixels_hbm[chunk * groups + group].at[part], pixels[chunk].at[group, part], pixel_sems.at[place, group]
            )
            for group in range(0 if chunk == chunks - 1 else far, groups)
        ]
        pixel_copies.append(copies)
        moved_copies.append(
            pltpu.make_async_copy(moved_hbm[chunk].at[:, part], moved.at[:, into], moved_sems.at[place])
        )
        for copy in copies + moved_copies[-1:]:
            copy.start()

    last_blocks = sizes[-1] // EDGE_ROWS
    for copies in pixel_copies[:last_blocks]:
        for copy in copies:
            copy.wait()
    total = gram_ref[...]
    for first in range(0, sizes[-1], GRAM_ROWS):
        data = stacked([pixels[-1].at[group] for group in range(groups)], first, GRAM_ROWS)
        total = total + dot_nt(data, data)
    gram = jnp.zeros((size, size), F32)
    for i in range(GRAM_ROWS):
        gram = gram + total[i * size : (i + 1) * size, i * size : (i + 1) * size]
    inverse, frob_norm = newton_schulz(gram)
    factor = shrink_ref[0] * jnp.sqrt(all_rows * side_len / frob_norm)
    select = (iota((own, size), 0) == iota((own, size), 1)).astype(F32)
    weights = (dot_nt(select, inverse, HIGHEST) * factor).astype(BF16)
    spread = POLAR_ROWS * own
    repeat = (iota((spread, own), 0) // POLAR_ROWS == iota((spread, own), 1)).astype(BF16)
    weights = dot_nn(repeat, weights).astype(BF16)

    def widened(count, first, channel_of, pixel_row_of):
        columns = iota((size, count), 1)
        chosen = dot_nn(weights, (iota((size, count), 0) == first + channel_of(columns)).astype(BF16))
        columns = iota((spread, count), 1)
        keep = iota((spread, count), 0) % POLAR_ROWS == pixel_row_of(columns)
        return jnp.where(keep, chosen, 0.0).astype(BF16)

    others = size - far * own
    far_weights = widened(POLAR_ROWS * others, far * own, lambda c: c % others, lambda c: c // others)
    if far:
        own_weights = widened(spread, 0, lambda c: c // POLAR_ROWS, lambda c: c % POLAR_ROWS)
        far_weights = jnp.concatenate([own_weights, far_weights], axis=1)

    out_copies = []
    for place, (chunk, row) in enumerate(blocks):
        if place >= last_blocks:
            for copy in pixel_copies[place]:
                copy.wait()
        moved_copies[place].wait()
        for first in range(row, row + EDGE_ROWS, POLAR_ROWS):
            into = starts[chunk] + first
            rows = moved[:, into : into + POLAR_ROWS]
            data = stacked([pixels[chunk].at[group] for group in range(far, groups)], first, POLAR_ROWS)
            if far:
                data = jnp.concatenate([rows.reshape(spread, side_len).astype(BF16), data], axis=0)
            polar = dot_nn(far_weights, data).reshape(own, POLAR_ROWS, side_len)
            moved[:, into : into + POLAR_ROWS] = rows - polar
        part = pl.ds(starts[chunk] + row, EDGE_ROWS)
        copy = pltpu.make_async_copy(moved.at[:, part], out_hbm.at[:, part], out_sems.at[place])
        copy.start()
        out_copies.append(copy)
    for copy in out_copies:
        copy.wait()


def polar_step(shrinkage, gram, moved, gathered, starts, sizes):
    chunks = len(gathered)
    groups = len(gathered[0])
    chans, _, side_len = moved[0].shape
    shape = (chans, sum(sizes), side_len)
    blocks = sum(sizes) // EDGE_ROWS
    flat = [piece for pieces in gathered for piece in pieces]
    return pl.pallas_call(
        functools.partial(polar_body, starts, sizes, groups),
        in_specs=[SMEM, pl.BlockSpec(memory_space=pltpu.VMEM)] + [ANY] * (chunks + len(flat)),
        out_specs=ANY,
        out_shape=jax.ShapeDtypeStruct(shape, F32),
        scratch_shapes=[
            pltpu.VMEM(shape, F32),
            pltpu.SemaphoreType.DMA((blocks, groups)),
            pltpu.SemaphoreType.DMA((blocks,)),
            pltpu.SemaphoreType.DMA((blocks,)),
        ]
        + [pltpu.VMEM((groups,) + pieces[0].shape, BF16) for pieces in gathered],
        compiler_params=kernel_params(63),
        cost_estimate=COST,
        name="polar_step",
    )(shrinkage, gram, *moved, *flat)


def neighbour_rows(strip, model_image, reach):
    count = lax.axis_size("strip")
    head, tail = model_image[:, :reach], model_image[:, model_image.shape[1] - reach :]
    odd = strip[0] % 2 == 1
    outer, inner = lax.optimization_barrier((jnp.where(odd, tail, head), jnp.where(odd, head, tail)))

    def exchanged(rows, firsts):
        pairs = [(i, i + 1) for i in firsts if i + 1 < count]
        return lax.ppermute(rows.astype(BF16), "strip", pairs + [(j, i) for i, j in pairs])

    return exchanged(outer, range(1, count, 2)), exchanged(inner, range(0, count, 2))


def swap(value, axis, bits):
    count = lax.axis_size(axis)
    return lax.ppermute(value, axis, [(i, i ^ bits) for i in range(count)])


def gather_channels(pixels, after=None):
    devices = lax.axis_size("chan")
    kept = [pixels] + [swap(pixels, "chan", bits) for bits in range(2, devices, 2)]
    if after is not None:
        kept = [pixels] + [gate(piece, after) for piece in kept[1:]]
    if devices == 1:
        return kept
    return kept + [swap(piece, "chan", 1) for piece in kept]


def local(grid, model_image, step_size, highpass, shrinkage):
    chans, own_rows, side_len = model_image.shape
    strips = lax.axis_size("strip")
    size = chans * lax.axis_size("chan")
    starts, sizes = chunk_rows(own_rows)
    chunks = len(sizes)
    strip = lax.axis_index("strip").astype(jnp.int32).reshape(1)

    cosine, sine_table = make_tables(side_len)
    split = np.stack([cosine.reshape(strips, own_rows, side_len), sine_table.reshape(strips, own_rows, side_len)])
    tables = [
        np.ascontiguousarray(split[:, :, start : start + rows]).reshape(2 * strips * rows, side_len)
        for start, rows in zip(starts, sizes)
    ]

    levels, taps = highpass.shape
    reach = (taps - 1) * 2 ** (levels - 1)
    outer, inner = neighbour_rows(strip, model_image, reach)
    odd = strip[0] % 2 == 1
    edges = jnp.concatenate([jnp.where(odd, inner, outer), jnp.where(odd, outer, inner)], axis=1)

    halves = {}
    moved = {}
    gathered = {}
    pixels = {}
    done = set()
    state = dict(last=strip, gram=jnp.zeros((GRAM_ROWS * size, GRAM_ROWS * size), F32), bases=None)

    def first(chunk):
        sent, state["last"] = first_transform(tables[chunk], grid, strips, state["last"])
        if chunk == 0:
            sent = gate(sent, outer)
            state["last"] = gate(state["last"], outer)
        if chunk == 1:
            sent = gate(sent, inner)
        if chunk == 2:
            gather(0)
            gram(0)
            done.add(0)
            sent = gate(sent, state["gram"])
        halves[chunk] = lax.all_to_all(sent, "strip", split_axis=0, concat_axis=0, tiled=True)

    def base():
        state["bases"] = base_step(
            strip, strips, step_size, highpass, model_image, edges, starts, sizes, state["last"]
        )
        state["last"] = state["bases"][0]

    def second(chunk):
        moved[chunk], pixels[chunk] = second_transform(
            step_size, halves[chunk], cosine, sine_table, state["bases"][chunk], state["last"]
        )
        state["last"] = pixels[chunk]

    def gather(chunk):
        pieces = gather_channels(pixels[chunk], state["last"])
        if chans % 16:
            pieces = [jnp.concatenate(pieces, axis=1)]
        gathered[chunk] = pieces

    def gram(chunk):
        state["gram"] = gram_step(gathered[chunk], state["gram"], state["last"])
        state["last"] = state["gram"]

    first(0)
    if chunks > 1:
        first(1)
    base()
    for chunk in range(chunks):
        second(chunk)
        if chunk + 2 < chunks:
            first(chunk + 2)
        if chunk == 1:
            gather(1)
        if chunk >= 1 and chunk - 1 not in done:
            if chunk - 1 not in gathered:
                gather(chunk - 1)
            gram(chunk - 1)
    if chunks - 1 not in gathered:
        gather(chunks - 1)
    order = range(chunks)
    return polar_step(
        shrinkage, state["gram"], [moved[k] for k in order], [gathered[k] for k in order], starts, sizes
    )


def solution(mesh):
    return jax.shard_map(
        local,
        mesh=mesh,
        in_specs=(
            P(None, "chan", "strip", None),
            P("chan", "strip", None),
            P("chan"),
            P(),
            P("strip"),
        ),
        out_specs=P("chan", "strip", None),
        check_vma=False,
    )
```

```python
import functools

import jax
import jax.numpy as jnp
import ml_dtypes
import numpy as np
from jax import lax
from jax.experimental import pallas as pl
from jax.experimental.pallas import tpu as pltpu
from jax.sharding import PartitionSpec as P

NS_ITERS = 5
EDGE_ROWS = 16
GRAM_ROWS = 4
POLAR_ROWS = 8
HIGHEST = lax.Precision.HIGHEST
F32 = jnp.float32
BF16 = jnp.bfloat16
MIB = 1 << 20

ANY = pl.BlockSpec(memory_space=pl.ANY)
SMEM = pl.BlockSpec(memory_space=pltpu.SMEM)


def kernel_params(mebibytes):
    return pltpu.CompilerParams(vmem_limit_bytes=mebibytes * MIB)


COST = pl.CostEstimate(flops=0, bytes_accessed=1 << 16, transcendentals=0)


def dot_nt(a, b, precision=None):
    return lax.dot_general(
        a, b, (((1,), (1,)), ((), ())), precision=precision, preferred_element_type=F32
    )


def dot_nn(a, b, precision=None):
    return lax.dot_general(
        a, b, (((1,), (0,)), ((), ())), precision=precision, preferred_element_type=F32
    )


def iota(shape, dim):
    return lax.broadcasted_iota(jnp.int32, shape, dim)


def make_tables(side_len):
    indices = np.arange(side_len, dtype=np.int64)
    phases = (np.outer(indices, indices) % side_len).astype(np.float32) * np.float32(
        2.0 * 3.141592653589793 / side_len
    )
    unit_scale = np.float32(float(side_len) ** (-0.5))
    cosine = (np.cos(phases) * unit_scale).astype(ml_dtypes.bfloat16)
    sine_table = (np.sin(phases) * unit_scale).astype(ml_dtypes.bfloat16)
    return cosine, sine_table


def chunk_rows(own_rows):
    quarter = own_rows // 4
    sizes = [quarter, own_rows - 2 * quarter - EDGE_ROWS, quarter, EDGE_ROWS]
    sizes = [size for size in sizes if size > 0]
    return [sum(sizes[:place]) for place in range(len(sizes))], sizes


def gate_body(value_ref, after_ref, out_ref):
    pass


def gate(value, after):
    return pl.pallas_call(
        gate_body,
        in_specs=[ANY, ANY],
        out_specs=ANY,
        out_shape=jax.ShapeDtypeStruct(value.shape, value.dtype),
        input_output_aliases={0: 0},
        compiler_params=kernel_params(63),
        cost_estimate=COST,
        name="gate",
    )(value, after)


def first_body(table_ref, grid_ref, after_ref, out_ref, token_ref):
    token_ref[...] = jnp.zeros(token_ref.shape, F32)
    strips, _, chans, rows, width = out_ref.shape
    side_len = table_ref.shape[-1]
    table = table_ref[...]
    middle = strips * rows
    turned = jnp.concatenate([-table[middle:], table[:middle]], axis=0)
    total = dot_nt(table, grid_ref[0].reshape(chans * width, side_len))
    total = total + dot_nt(turned, grid_ref[1].reshape(chans * width, side_len))
    total = total.astype(BF16)
    for part in range(2):
        for strip in range(strips):
            first = (part * strips + strip) * rows
            for chan in range(chans):
                out_ref[strip, part, chan] = total[first : first + rows, chan * width : (chan + 1) * width]


def first_transform(table, grid, strips, after):
    _, chans, width, side_len = grid.shape
    rows = table.shape[0] // (2 * strips)
    shape = (strips, 2, chans, rows, width)
    if width % 128 or rows % 16:
        middle = strips * rows
        turned = jnp.concatenate([-table[middle:], table[:middle]], axis=0)
        total = jnp.einsum("mv,cuv->mcu", table, grid[0], preferred_element_type=F32)
        total = total + jnp.einsum("mv,cuv->mcu", turned, grid[1], preferred_element_type=F32)
        total = total.astype(BF16).reshape(2, strips, rows, chans, width)
        return total.transpose(1, 0, 3, 2, 4), jnp.zeros((8, 128), F32)
    block = 4 if chans % 4 == 0 else 1
    return pl.pallas_call(
        first_body,
        grid=(chans // block,),
        in_specs=[
            pl.BlockSpec(table.shape, lambda i: (0, 0)),
            pl.BlockSpec((2, block, width, side_len), lambda i: (0, i, 0, 0)),
            ANY,
        ],
        out_specs=[
            pl.BlockSpec((strips, 2, block, rows, width), lambda i: (0, 0, i, 0, 0)),
            pl.BlockSpec((8, 128), lambda i: (0, 0)),
        ],
        out_shape=[jax.ShapeDtypeStruct(shape, BF16), jax.ShapeDtypeStruct((8, 128), F32)],
        compiler_params=kernel_params(63),
        cost_estimate=COST,
        name="first_transform",
    )(table, grid, after)


def band_matrix(taps_of, levels, taps, own_rows, reach, first_row, image_rows):
    half_taps = taps // 2
    shape = (own_rows, own_rows + 2 * reach)
    row = iota(shape, 0)
    column = iota(shape, 1)
    place = jnp.where(
        column < own_rows, column, jnp.where(column < own_rows + reach, column - own_rows - reach, column - reach)
    )
    total = jnp.zeros(shape, F32)
    for level in range(levels):
        dilation = 2**level
        for outer in range(taps):
            detail_row = row - (outer - half_taps) * dilation
            inside = (detail_row + first_row >= 0) & (detail_row + first_row < image_rows)
            for inner in range(taps):
                hit = inside & (place == detail_row + (inner - half_taps) * dilation)
                total = total + jnp.where(hit, taps_of(level, outer) * taps_of(level, inner), 0.0)
    return total


def base_body(levels, taps, starts, strips, strip_ref, step_ref, highpass_ref, model_ref, edge_ref, after_ref, *refs):
    high, low = refs[-2:]
    out_refs = refs[:-2]
    block, own_rows, side_len = model_ref.shape
    reach = edge_ref.shape[1] // 2

    @pl.when(pl.program_id(0) == 0)
    def _():
        band = band_matrix(
            lambda level, tap: highpass_ref[level, tap],
            levels,
            taps,
            own_rows,
            reach,
            strip_ref[0] * own_rows,
            strips * own_rows,
        )
        top = band.astype(BF16)
        high[...] = top
        low[...] = (band - top.astype(F32)).astype(BF16)

    first = pl.program_id(0) * block
    for chan in range(block):
        model = model_ref[chan]
        top = model.astype(BF16)
        rest = (model - top.astype(F32)).astype(BF16)
        edge = edge_ref[chan].astype(F32)
        whole = jnp.concatenate([top.astype(F32), edge], axis=0).astype(BF16)
        gradient = dot_nn(high[...], whole)
        gradient = gradient + dot_nn(low[...], whole)
        gradient = gradient + dot_nn(high[:, :own_rows], rest)
        base = model - step_ref[first + chan] * gradient
        for start, out_ref in zip(starts, out_refs):
            out_ref[chan] = base[start : start + out_ref.shape[1]]


def base_step(strip, strips, step_size, highpass, model_image, edges, starts, sizes, after):
    chans, rows, side_len = model_image.shape
    levels, taps = highpass.shape
    reach = edges.shape[1] // 2
    block = 2 if chans % 2 == 0 else 1
    wide = rows + 2 * reach
    return pl.pallas_call(
        functools.partial(base_body, levels, taps, starts, strips),
        grid=(chans // block,),
        in_specs=[
            SMEM,
            SMEM,
            SMEM,
            pl.BlockSpec((block, rows, side_len), lambda i: (i, 0, 0)),
            pl.BlockSpec((block, 2 * reach, side_len), lambda i: (i, 0, 0)),
            ANY,
        ],
        out_specs=[pl.BlockSpec((block, part, side_len), lambda i: (i, 0, 0)) for part in sizes],
        out_shape=[jax.ShapeDtypeStruct((chans, part, side_len), F32) for part in sizes],
        scratch_shapes=[pltpu.VMEM((rows, wide), BF16), pltpu.VMEM((rows, wide), BF16)],
        compiler_params=kernel_params(63),
        cost_estimate=COST,
        name="base_step",
    )(strip, step_size, highpass, model_image, edges, after)


def second_body(step_ref, half_ref, cosine_ref, sine_ref, base_ref, after_ref, moved_ref, pixels_ref):
    strips, _, chans, rows, width = half_ref.shape
    real = jnp.concatenate([half_ref[s, 0].reshape(chans * rows, width) for s in range(strips)], axis=1)
    imag = jnp.concatenate([half_ref[s, 1].reshape(chans * rows, width) for s in range(strips)], axis=1)
    dirty = dot_nn(real, cosine_ref[...]) - dot_nn(imag, sine_ref[...])
    pieces = []
    for chan in range(chans):
        moved = base_ref[chan] + step_ref[chan] * dirty[chan * rows : (chan + 1) * rows]
        moved_ref[chan] = moved
        pieces.append(moved)
    pixels_ref[...] = jnp.swapaxes(jnp.stack(pieces), 0, 1).astype(BF16)


def second_transform(step_size, half, cosine, sine_table, base, after):
    strips, _, chans, rows, width = half.shape
    side_len = cosine.shape[0]
    if width % 128 or rows % 16 or chans % 16:
        split = (strips, width, side_len)
        dirty = jnp.einsum("scmu,sul->cml", half[:, 0], cosine.reshape(split), preferred_element_type=F32)
        dirty = dirty - jnp.einsum("scmu,sul->cml", half[:, 1], sine_table.reshape(split), preferred_element_type=F32)
        moved = base + step_size[:, None, None] * dirty
        return moved, moved.astype(BF16).transpose(1, 0, 2)
    block = min(256, side_len)
    return pl.pallas_call(
        second_body,
        grid=(side_len // block,),
        in_specs=[
            SMEM,
            pl.BlockSpec(half.shape, lambda i: (0, 0, 0, 0, 0)),
            pl.BlockSpec((side_len, block), lambda i: (0, i)),
            pl.BlockSpec((side_len, block), lambda i: (0, i)),
            pl.BlockSpec((chans, rows, block), lambda i: (0, 0, i)),
            ANY,
        ],
        out_specs=[
            pl.BlockSpec((chans, rows, block), lambda i: (0, 0, i)),
            pl.BlockSpec((rows, chans, block), lambda i: (0, 0, i)),
        ],
        out_shape=[
            jax.ShapeDtypeStruct(base.shape, F32),
            jax.ShapeDtypeStruct((rows, chans, side_len), BF16),
        ],
        compiler_params=kernel_params(63),
        cost_estimate=COST,
        name="second_transform",
    )(step_size, half, cosine, sine_table, base, after)


def stacked(group_refs, first, count):
    return jnp.concatenate([ref[first + i] for i in range(count) for ref in group_refs], axis=0)


def gram_body(groups, before_ref, after_ref, *refs):
    total_ref = refs[groups]

    @pl.when(pl.program_id(0) == 0)
    def _():
        total_ref[...] = before_ref[...]

    total = total_ref[...]
    for first in range(0, refs[0].shape[0], GRAM_ROWS):
        pixels = stacked(refs[:groups], first, GRAM_ROWS)
        total = total + dot_nt(pixels, pixels)
    total_ref[...] = total


def gram_step(pieces, before, after):
    rows, chans, side_len = pieces[0].shape
    block = EDGE_ROWS // 2
    spec = pl.BlockSpec((block, chans, side_len), lambda i: (i, 0, 0))
    return pl.pallas_call(
        functools.partial(gram_body, len(pieces)),
        grid=(rows // block,),
        in_specs=[pl.BlockSpec(before.shape, lambda i: (0, 0)), ANY] + [spec] * len(pieces),
        out_specs=pl.BlockSpec(before.shape, lambda i: (0, 0)),
        out_shape=jax.ShapeDtypeStruct(before.shape, F32),
        compiler_params=kernel_params(63),
        cost_estimate=COST,
        name="gram_step",
    )(before, after, *pieces)


def product(a, b):
    a_high, b_high = a.astype(BF16), b.astype(BF16)
    a_low, b_low = (a - a_high.astype(F32)).astype(BF16), (b - b_high.astype(F32)).astype(BF16)
    left = jnp.concatenate([a_high, a_high, a_low], axis=1)
    return dot_nn(left, jnp.concatenate([b_high, b_low, b_high], axis=0))


def newton_schulz(gram):
    size = gram.shape[0]
    frob_norm = jnp.sqrt(jnp.sum(gram * gram))
    identity = (iota((size, size), 0) == iota((size, size), 1)).astype(F32)
    current = gram / frob_norm
    middle = 0.5 * (3.0 * identity - current)
    inverse = middle
    for iteration in range(1, NS_ITERS):
        current = product(current, middle)
        middle = 0.5 * (3.0 * identity - product(inverse, current))
        inverse = product(middle, inverse)
    return inverse, frob_norm


def polar_body(starts, sizes, groups, shrink_ref, gram_ref, *refs):
    chunks = len(sizes)
    moved_hbm = refs[:chunks]
    pixels_hbm = refs[chunks : chunks * (groups + 1)]
    out_hbm, moved, pixel_sems, moved_sems, out_sems = refs[chunks * (groups + 1) : chunks * (groups + 1) + 5]
    pixels = refs[chunks * (groups + 1) + 5 :]
    own, all_rows, side_len = moved.shape
    size = pixels[0].shape[2] * groups

    blocks = [
        (chunk, row) for chunk in [chunks - 1] + list(range(chunks - 1)) for row in range(0, sizes[chunk], EDGE_ROWS)
    ]
    far = 1 if groups > 1 else 0
    pixel_copies = []
    moved_copies = []
    for place, (chunk, row) in enumerate(blocks):
        part = pl.ds(row, EDGE_ROWS)
        into = pl.ds(starts[chunk] + row, EDGE_ROWS)
        copies = [
            pltpu.make_async_copy(
                pixels_hbm[chunk * groups + group].at[part], pixels[chunk].at[group, part], pixel_sems.at[place, group]
            )
            for group in range(0 if chunk == chunks - 1 else far, groups)
        ]
        pixel_copies.append(copies)
        moved_copies.append(
            pltpu.make_async_copy(moved_hbm[chunk].at[:, part], moved.at[:, into], moved_sems.at[place])
        )
        for copy in copies + moved_copies[-1:]:
            copy.start()

    last_blocks = sizes[-1] // EDGE_ROWS
    for copies in pixel_copies[:last_blocks]:
        for copy in copies:
            copy.wait()
    total = gram_ref[...]
    for first in range(0, sizes[-1], GRAM_ROWS):
        data = stacked([pixels[-1].at[group] for group in range(groups)], first, GRAM_ROWS)
        total = total + dot_nt(data, data)
    gram = jnp.zeros((size, size), F32)
    for i in range(GRAM_ROWS):
        gram = gram + total[i * size : (i + 1) * size, i * size : (i + 1) * size]
    inverse, frob_norm = newton_schulz(gram)
    factor = shrink_ref[0] * jnp.sqrt(all_rows * side_len / frob_norm)
    select = (iota((own, size), 0) == iota((own, size), 1)).astype(F32)
    weights = (dot_nt(select, inverse, HIGHEST) * factor).astype(BF16)
    spread = POLAR_ROWS * own
    repeat = (iota((spread, own), 0) // POLAR_ROWS == iota((spread, own), 1)).astype(BF16)
    weights = dot_nn(repeat, weights).astype(BF16)

    def widened(count, first, channel_of, pixel_row_of):
        columns = iota((size, count), 1)
        chosen = dot_nn(weights, (iota((size, count), 0) == first + channel_of(columns)).astype(BF16))
        columns = iota((spread, count), 1)
        keep = iota((spread, count), 0) % POLAR_ROWS == pixel_row_of(columns)
        return jnp.where(keep, chosen, 0.0).astype(BF16)

    others = size - far * own
    far_weights = widened(POLAR_ROWS * others, far * own, lambda c: c % others, lambda c: c // others)
    if far:
        own_weights = widened(spread, 0, lambda c: c // POLAR_ROWS, lambda c: c % POLAR_ROWS)
        far_weights = jnp.concatenate([own_weights, far_weights], axis=1)

    out_copies = []
    for place, (chunk, row) in enumerate(blocks):
        if place >= last_blocks:
            for copy in pixel_copies[place]:
                copy.wait()
        moved_copies[place].wait()
        for first in range(row, row + EDGE_ROWS, POLAR_ROWS):
            into = starts[chunk] + first
            rows = moved[:, into : into + POLAR_ROWS]
            data = stacked([pixels[chunk].at[group] for group in range(far, groups)], first, POLAR_ROWS)
            if far:
                data = jnp.concatenate([rows.reshape(spread, side_len).astype(BF16), data], axis=0)
            polar = dot_nn(far_weights, data).reshape(own, POLAR_ROWS, side_len)
            moved[:, into : into + POLAR_ROWS] = rows - polar
        part = pl.ds(starts[chunk] + row, EDGE_ROWS)
        copy = pltpu.make_async_copy(moved.at[:, part], out_hbm.at[:, part], out_sems.at[place])
        copy.start()
        out_copies.append(copy)
    for copy in out_copies:
        copy.wait()


def polar_step(shrinkage, gram, moved, gathered, starts, sizes):
    chunks = len(gathered)
    groups = len(gathered[0])
    chans, _, side_len = moved[0].shape
    shape = (chans, sum(sizes), side_len)
    blocks = sum(sizes) // EDGE_ROWS
    flat = [piece for pieces in gathered for piece in pieces]
    return pl.pallas_call(
        functools.partial(polar_body, starts, sizes, groups),
        in_specs=[SMEM, pl.BlockSpec(memory_space=pltpu.VMEM)] + [ANY] * (chunks + len(flat)),
        out_specs=ANY,
        out_shape=jax.ShapeDtypeStruct(shape, F32),
        scratch_shapes=[
            pltpu.VMEM(shape, F32),
            pltpu.SemaphoreType.DMA((blocks, groups)),
            pltpu.SemaphoreType.DMA((blocks,)),
            pltpu.SemaphoreType.DMA((blocks,)),
        ]
        + [pltpu.VMEM((groups,) + pieces[0].shape, BF16) for pieces in gathered],
        compiler_params=kernel_params(63),
        cost_estimate=COST,
        name="polar_step",
    )(shrinkage, gram, *moved, *flat)


def neighbour_rows(strip, model_image, reach):
    count = lax.axis_size("strip")
    head, tail = model_image[:, :reach], model_image[:, model_image.shape[1] - reach :]
    odd = strip[0] % 2 == 1
    outer, inner = lax.optimization_barrier((jnp.where(odd, tail, head), jnp.where(odd, head, tail)))

    def exchanged(rows, firsts):
        pairs = [(i, i + 1) for i in firsts if i + 1 < count]
        return lax.ppermute(rows.astype(BF16), "strip", pairs + [(j, i) for i, j in pairs])

    return exchanged(outer, range(1, count, 2)), exchanged(inner, range(0, count, 2))


def swap(value, axis, bits):
    count = lax.axis_size(axis)
    return lax.ppermute(value, axis, [(i, i ^ bits) for i in range(count)])


def gather_channels(pixels, after=None):
    devices = lax.axis_size("chan")
    kept = [pixels] + [swap(pixels, "chan", bits) for bits in range(2, devices, 2)]
    if after is not None:
        kept = [pixels] + [gate(piece, after) for piece in kept[1:]]
    if devices == 1:
        return kept
    return kept + [swap(piece, "chan", 1) for piece in kept]


def local(grid, model_image, step_size, highpass, shrinkage):
    chans, own_rows, side_len = model_image.shape
    strips = lax.axis_size("strip")
    size = chans * lax.axis_size("chan")
    starts, sizes = chunk_rows(own_rows)
    chunks = len(sizes)
    strip = lax.axis_index("strip").astype(jnp.int32).reshape(1)

    cosine, sine_table = make_tables(side_len)
    split = np.stack([cosine.reshape(strips, own_rows, side_len), sine_table.reshape(strips, own_rows, side_len)])
    tables = [
        np.ascontiguousarray(split[:, :, start : start + rows]).reshape(2 * strips * rows, side_len)
        for start, rows in zip(starts, sizes)
    ]

    levels, taps = highpass.shape
    reach = (taps - 1) * 2 ** (levels - 1)
    outer, inner = neighbour_rows(strip, model_image, reach)
    odd = strip[0] % 2 == 1
    edges = jnp.concatenate([jnp.where(odd, inner, outer), jnp.where(odd, outer, inner)], axis=1)

    halves = {}
    moved = {}
    gathered = {}
    pixels = {}
    done = set()
    state = dict(last=strip, gram=jnp.zeros((GRAM_ROWS * size, GRAM_ROWS * size), F32), bases=None)

    def first(chunk):
        sent, state["last"] = first_transform(tables[chunk], grid, strips, state["last"])
        if chunk == 0:
            sent = gate(sent, outer)
            state["last"] = gate(state["last"], outer)
        if chunk == 1:
            sent = gate(sent, inner)
        if chunk == 2:
            gather(0)
            gram(0)
            done.add(0)
            sent = gate(sent, state["gram"])
        halves[chunk] = lax.all_to_all(sent, "strip", split_axis=0, concat_axis=0, tiled=True)

    def base():
        state["bases"] = base_step(
            strip, strips, step_size, highpass, model_image, edges, starts, sizes, state["last"]
        )
        state["last"] = state["bases"][0]

    def second(chunk):
        moved[chunk], pixels[chunk] = second_transform(
            step_size, halves[chunk], cosine, sine_table, state["bases"][chunk], state["last"]
        )
        state["last"] = pixels[chunk]

    def gather(chunk):
        pieces = gather_channels(pixels[chunk], state["last"])
        if chans % 16:
            pieces = [jnp.concatenate(pieces, axis=1)]
        gathered[chunk] = pieces

    def gram(chunk):
        state["gram"] = gram_step(gathered[chunk], state["gram"], state["last"])
        state["last"] = state["gram"]

    first(0)
    if chunks > 1:
        first(1)
    base()
    for chunk in range(chunks):
        second(chunk)
        if chunk + 2 < chunks:
            first(chunk + 2)
        if chunk == 1:
            gather(1)
        if chunk >= 1 and chunk - 1 not in done:
            if chunk - 1 not in gathered:
                gather(chunk - 1)
            gram(chunk - 1)
    if chunks - 1 not in gathered:
        gather(chunks - 1)
    order = range(chunks)
    return polar_step(
        shrinkage, state["gram"], [moved[k] for k in order], [gathered[k] for k in order], starts, sizes
    )


def solution(mesh):
    return jax.shard_map(
        local,
        mesh=mesh,
        in_specs=(
            P(None, "chan", "strip", None),
            P("chan", "strip", None),
            P("chan"),
            P(),
            P("strip"),
        ),
        out_specs=P("chan", "strip", None),
        check_vma=False,
    )
```

```python
import functools

import jax
import jax.numpy as jnp
import ml_dtypes
import numpy as np
from jax import lax
from jax.experimental import pallas as pl
from jax.experimental.pallas import tpu as pltpu
from jax.sharding import PartitionSpec as P

NS_ITERS = 5
EDGE_ROWS = 16
GRAM_ROWS = 4
POLAR_ROWS = 8
HIGHEST = lax.Precision.HIGHEST
F32 = jnp.float32
BF16 = jnp.bfloat16
MIB = 1 << 20

ANY = pl.BlockSpec(memory_space=pl.ANY)
SMEM = pl.BlockSpec(memory_space=pltpu.SMEM)


def kernel_params(mebibytes):
    return pltpu.CompilerParams(vmem_limit_bytes=mebibytes * MIB)


COST = pl.CostEstimate(flops=0, bytes_accessed=1 << 16, transcendentals=0)


def dot_nt(a, b, precision=None):
    return lax.dot_general(
        a, b, (((1,), (1,)), ((), ())), precision=precision, preferred_element_type=F32
    )


def dot_nn(a, b, precision=None):
    return lax.dot_general(
        a, b, (((1,), (0,)), ((), ())), precision=precision, preferred_element_type=F32
    )


def iota(shape, dim):
    return lax.broadcasted_iota(jnp.int32, shape, dim)


def make_tables(side_len):
    indices = np.arange(side_len, dtype=np.int64)
    phases = (np.outer(indices, indices) % side_len).astype(np.float32) * np.float32(
        2.0 * 3.141592653589793 / side_len
    )
    unit_scale = np.float32(float(side_len) ** (-0.5))
    cosine = (np.cos(phases) * unit_scale).astype(ml_dtypes.bfloat16)
    sine_table = (np.sin(phases) * unit_scale).astype(ml_dtypes.bfloat16)
    return cosine, sine_table


def chunk_rows(own_rows):
    quarter = own_rows // 4
    sizes = [own_rows - quarter - EDGE_ROWS, quarter, EDGE_ROWS]
    return [sum(sizes[:place]) for place in range(len(sizes))], sizes


def gate_body(value_ref, after_ref, out_ref):
    pass


def gate(value, after):
    return pl.pallas_call(
        gate_body,
        in_specs=[ANY, ANY],
        out_specs=ANY,
        out_shape=jax.ShapeDtypeStruct(value.shape, value.dtype),
        input_output_aliases={0: 0},
        compiler_params=kernel_params(63),
        cost_estimate=COST,
        name="gate",
    )(value, after)


def first_body(table_ref, grid_ref, after_ref, out_ref, token_ref):
    token_ref[...] = jnp.zeros(token_ref.shape, F32)
    strips, _, chans, rows, width = out_ref.shape
    side_len = table_ref.shape[-1]
    table = table_ref[...]
    middle = strips * rows
    turned = jnp.concatenate([-table[middle:], table[:middle]], axis=0)
    total = dot_nt(table, grid_ref[0].reshape(chans * width, side_len))
    total = total + dot_nt(turned, grid_ref[1].reshape(chans * width, side_len))
    total = total.astype(BF16)
    for part in range(2):
        for strip in range(strips):
            first = (part * strips + strip) * rows
            for chan in range(chans):
                out_ref[strip, part, chan] = total[first : first + rows, chan * width : (chan + 1) * width]


def first_transform(table, grid, strips, after):
    _, chans, width, side_len = grid.shape
    rows = table.shape[0] // (2 * strips)
    shape = (strips, 2, chans, rows, width)
    if width % 128 or rows % 16:
        middle = strips * rows
        turned = jnp.concatenate([-table[middle:], table[:middle]], axis=0)
        total = jnp.einsum("mv,cuv->mcu", table, grid[0], preferred_element_type=F32)
        total = total + jnp.einsum("mv,cuv->mcu", turned, grid[1], preferred_element_type=F32)
        total = total.astype(BF16).reshape(2, strips, rows, chans, width)
        return total.transpose(1, 0, 3, 2, 4), jnp.zeros((8, 128), F32)
    block = 4 if chans % 4 == 0 else 1
    return pl.pallas_call(
        first_body,
        grid=(chans // block,),
        in_specs=[
            pl.BlockSpec(table.shape, lambda i: (0, 0)),
            pl.BlockSpec((2, block, width, side_len), lambda i: (0, i, 0, 0)),
            ANY,
        ],
        out_specs=[
            pl.BlockSpec((strips, 2, block, rows, width), lambda i: (0, 0, i, 0, 0)),
            pl.BlockSpec((8, 128), lambda i: (0, 0)),
        ],
        out_shape=[jax.ShapeDtypeStruct(shape, BF16), jax.ShapeDtypeStruct((8, 128), F32)],
        compiler_params=kernel_params(63),
        cost_estimate=COST,
        name="first_transform",
    )(table, grid, after)


def band_matrix(taps_of, levels, taps, own_rows, reach, first_row, image_rows):
    half_taps = taps // 2
    shape = (own_rows, own_rows + 2 * reach)
    row = iota(shape, 0)
    column = iota(shape, 1)
    place = jnp.where(
        column < own_rows, column, jnp.where(column < own_rows + reach, column - own_rows - reach, column - reach)
    )
    total = jnp.zeros(shape, F32)
    for level in range(levels):
        dilation = 2**level
        for outer in range(taps):
            detail_row = row - (outer - half_taps) * dilation
            inside = (detail_row + first_row >= 0) & (detail_row + first_row < image_rows)
            for inner in range(taps):
                hit = inside & (place == detail_row + (inner - half_taps) * dilation)
                total = total + jnp.where(hit, taps_of(level, outer) * taps_of(level, inner), 0.0)
    return total


def base_body(levels, taps, starts, strips, strip_ref, step_ref, highpass_ref, model_ref, edge_ref, after_ref, *refs):
    high, low = refs[-2:]
    out_refs = refs[:-2]
    block, own_rows, side_len = model_ref.shape
    reach = edge_ref.shape[1] // 2

    @pl.when(pl.program_id(0) == 0)
    def _():
        band = band_matrix(
            lambda level, tap: highpass_ref[level, tap],
            levels,
            taps,
            own_rows,
            reach,
            strip_ref[0] * own_rows,
            strips * own_rows,
        )
        top = band.astype(BF16)
        high[...] = top
        low[...] = (band - top.astype(F32)).astype(BF16)

    first = pl.program_id(0) * block
    for chan in range(block):
        model = model_ref[chan]
        top = model.astype(BF16)
        rest = (model - top.astype(F32)).astype(BF16)
        edge = edge_ref[chan].astype(F32)
        whole = jnp.concatenate([top.astype(F32), edge], axis=0).astype(BF16)
        gradient = dot_nn(high[...], whole)
        gradient = gradient + dot_nn(low[...], whole)
        gradient = gradient + dot_nn(high[:, :own_rows], rest)
        base = model - step_ref[first + chan] * gradient
        for start, out_ref in zip(starts, out_refs):
            out_ref[chan] = base[start : start + out_ref.shape[1]]


def base_step(strip, strips, step_size, highpass, model_image, edges, starts, sizes, after):
    chans, rows, side_len = model_image.shape
    levels, taps = highpass.shape
    reach = edges.shape[1] // 2
    block = 2 if chans % 2 == 0 else 1
    wide = rows + 2 * reach
    return pl.pallas_call(
        functools.partial(base_body, levels, taps, starts, strips),
        grid=(chans // block,),
        in_specs=[
            SMEM,
            SMEM,
            SMEM,
            pl.BlockSpec((block, rows, side_len), lambda i: (i, 0, 0)),
            pl.BlockSpec((block, 2 * reach, side_len), lambda i: (i, 0, 0)),
            ANY,
        ],
        out_specs=[pl.BlockSpec((block, part, side_len), lambda i: (i, 0, 0)) for part in sizes],
        out_shape=[jax.ShapeDtypeStruct((chans, part, side_len), F32) for part in sizes],
        scratch_shapes=[pltpu.VMEM((rows, wide), BF16), pltpu.VMEM((rows, wide), BF16)],
        compiler_params=kernel_params(63),
        cost_estimate=COST,
        name="base_step",
    )(strip, step_size, highpass, model_image, edges, after)


def second_body(step_ref, half_ref, cosine_ref, sine_ref, base_ref, after_ref, moved_ref, pixels_ref):
    strips, _, chans, rows, width = half_ref.shape
    real = jnp.concatenate([half_ref[s, 0].reshape(chans * rows, width) for s in range(strips)], axis=1)
    imag = jnp.concatenate([half_ref[s, 1].reshape(chans * rows, width) for s in range(strips)], axis=1)
    dirty = dot_nn(real, cosine_ref[...]) - dot_nn(imag, sine_ref[...])
    pieces = []
    for chan in range(chans):
        moved = base_ref[chan] + step_ref[chan] * dirty[chan * rows : (chan + 1) * rows]
        moved_ref[chan] = moved
        pieces.append(moved)
    pixels_ref[...] = jnp.swapaxes(jnp.stack(pieces), 0, 1).astype(BF16)


def second_transform(step_size, half, cosine, sine_table, base, after):
    strips, _, chans, rows, width = half.shape
    side_len = cosine.shape[0]
    if width % 128 or rows % 16 or chans % 16:
        split = (strips, width, side_len)
        dirty = jnp.einsum("scmu,sul->cml", half[:, 0], cosine.reshape(split), preferred_element_type=F32)
        dirty = dirty - jnp.einsum("scmu,sul->cml", half[:, 1], sine_table.reshape(split), preferred_element_type=F32)
        moved = base + step_size[:, None, None] * dirty
        return moved, moved.astype(BF16).transpose(1, 0, 2)
    block = min(256, side_len)
    return pl.pallas_call(
        second_body,
        grid=(side_len // block,),
        in_specs=[
            SMEM,
            pl.BlockSpec(half.shape, lambda i: (0, 0, 0, 0, 0)),
            pl.BlockSpec((side_len, block), lambda i: (0, i)),
            pl.BlockSpec((side_len, block), lambda i: (0, i)),
            pl.BlockSpec((chans, rows, block), lambda i: (0, 0, i)),
            ANY,
        ],
        out_specs=[
            pl.BlockSpec((chans, rows, block), lambda i: (0, 0, i)),
            pl.BlockSpec((rows, chans, block), lambda i: (0, 0, i)),
        ],
        out_shape=[
            jax.ShapeDtypeStruct(base.shape, F32),
            jax.ShapeDtypeStruct((rows, chans, side_len), BF16),
        ],
        compiler_params=kernel_params(63),
        cost_estimate=COST,
        name="second_transform",
    )(step_size, half, cosine, sine_table, base, after)


def stacked(group_refs, first, count):
    return jnp.concatenate([ref[first + i] for i in range(count) for ref in group_refs], axis=0)


def gram_body(groups, before_ref, after_ref, *refs):
    total_ref = refs[groups]

    @pl.when(pl.program_id(0) == 0)
    def _():
        total_ref[...] = before_ref[...]

    total = total_ref[...]
    for first in range(0, refs[0].shape[0], GRAM_ROWS):
        pixels = stacked(refs[:groups], first, GRAM_ROWS)
        total = total + dot_nt(pixels, pixels)
    total_ref[...] = total


def gram_step(pieces, before, after):
    rows, chans, side_len = pieces[0].shape
    block = EDGE_ROWS // 2
    spec = pl.BlockSpec((block, chans, side_len), lambda i: (i, 0, 0))
    return pl.pallas_call(
        functools.partial(gram_body, len(pieces)),
        grid=(rows // block,),
        in_specs=[pl.BlockSpec(before.shape, lambda i: (0, 0)), ANY] + [spec] * len(pieces),
        out_specs=pl.BlockSpec(before.shape, lambda i: (0, 0)),
        out_shape=jax.ShapeDtypeStruct(before.shape, F32),
        compiler_params=kernel_params(63),
        cost_estimate=COST,
        name="gram_step",
    )(before, after, *pieces)


def newton_schulz(gram):
    size = gram.shape[0]
    frob_norm = jnp.sqrt(jnp.sum(gram * gram))
    identity = (iota((size, size), 0) == iota((size, size), 1)).astype(F32)
    current = gram / frob_norm
    middle = 0.5 * (3.0 * identity - current)
    inverse = middle
    for iteration in range(1, NS_ITERS):
        current = dot_nn(current, middle, HIGHEST)
        middle = 0.5 * (3.0 * identity - dot_nn(inverse, current, HIGHEST))
        inverse = dot_nn(middle, inverse, HIGHEST)
    return inverse, frob_norm


def polar_body(starts, sizes, groups, shrink_ref, gram_ref, *refs):
    chunks = len(sizes)
    moved_hbm = refs[:chunks]
    pixels_hbm = refs[chunks : chunks * (groups + 1)]
    out_hbm, moved, pixel_sems, moved_sems, out_sems = refs[chunks * (groups + 1) : chunks * (groups + 1) + 5]
    pixels = refs[chunks * (groups + 1) + 5 :]
    own, all_rows, side_len = moved.shape
    size = pixels[0].shape[2] * groups

    blocks = [
        (chunk, row) for chunk in [chunks - 1] + list(range(chunks - 1)) for row in range(0, sizes[chunk], EDGE_ROWS)
    ]
    far = 1 if groups > 1 else 0
    pixel_copies = []
    moved_copies = []
    for place, (chunk, row) in enumerate(blocks):
        part = pl.ds(row, EDGE_ROWS)
        into = pl.ds(starts[chunk] + row, EDGE_ROWS)
        copies = [
            pltpu.make_async_copy(
                pixels_hbm[chunk * groups + group].at[part], pixels[chunk].at[group, part], pixel_sems.at[place, group]
            )
            for group in range(0 if chunk == chunks - 1 else far, groups)
        ]
        pixel_copies.append(copies)
        moved_copies.append(
            pltpu.make_async_copy(moved_hbm[chunk].at[:, part], moved.at[:, into], moved_sems.at[place])
        )
        for copy in copies + moved_copies[-1:]:
            copy.start()

    last_blocks = sizes[-1] // EDGE_ROWS
    for copies in pixel_copies[:last_blocks]:
        for copy in copies:
            copy.wait()
    total = gram_ref[...]
    for first in range(0, sizes[-1], GRAM_ROWS):
        data = stacked([pixels[-1].at[group] for group in range(groups)], first, GRAM_ROWS)
        total = total + dot_nt(data, data)
    gram = jnp.zeros((size, size), F32)
    for i in range(GRAM_ROWS):
        gram = gram + total[i * size : (i + 1) * size, i * size : (i + 1) * size]
    inverse, frob_norm = newton_schulz(gram)
    factor = shrink_ref[0] * jnp.sqrt(all_rows * side_len / frob_norm)
    select = (iota((own, size), 0) == iota((own, size), 1)).astype(F32)
    weights = (dot_nt(select, inverse, HIGHEST) * factor).astype(BF16)
    spread = POLAR_ROWS * own
    repeat = (iota((spread, own), 0) // POLAR_ROWS == iota((spread, own), 1)).astype(BF16)
    weights = dot_nn(repeat, weights).astype(BF16)

    def widened(count, first, channel_of, pixel_row_of):
        columns = iota((size, count), 1)
        chosen = dot_nn(weights, (iota((size, count), 0) == first + channel_of(columns)).astype(BF16))
        columns = iota((spread, count), 1)
        keep = iota((spread, count), 0) % POLAR_ROWS == pixel_row_of(columns)
        return jnp.where(keep, chosen, 0.0).astype(BF16)

    others = size - far * own
    far_weights = widened(POLAR_ROWS * others, far * own, lambda c: c % others, lambda c: c // others)
    if far:
        own_weights = widened(spread, 0, lambda c: c // POLAR_ROWS, lambda c: c % POLAR_ROWS)
        far_weights = jnp.concatenate([own_weights, far_weights], axis=1)

    out_copies = []
    for place, (chunk, row) in enumerate(blocks):
        if place >= last_blocks:
            for copy in pixel_copies[place]:
                copy.wait()
        moved_copies[place].wait()
        for first in range(row, row + EDGE_ROWS, POLAR_ROWS):
            into = starts[chunk] + first
            rows = moved[:, into : into + POLAR_ROWS]
            data = stacked([pixels[chunk].at[group] for group in range(far, groups)], first, POLAR_ROWS)
            if far:
                data = jnp.concatenate([rows.reshape(spread, side_len).astype(BF16), data], axis=0)
            polar = dot_nn(far_weights, data).reshape(own, POLAR_ROWS, side_len)
            moved[:, into : into + POLAR_ROWS] = rows - polar
        part = pl.ds(starts[chunk] + row, EDGE_ROWS)
        copy = pltpu.make_async_copy(moved.at[:, part], out_hbm.at[:, part], out_sems.at[place])
        copy.start()
        out_copies.append(copy)
    for copy in out_copies:
        copy.wait()


def polar_step(shrinkage, gram, moved, gathered, starts, sizes):
    chunks = len(gathered)
    groups = len(gathered[0])
    chans, _, side_len = moved[0].shape
    shape = (chans, sum(sizes), side_len)
    blocks = sum(sizes) // EDGE_ROWS
    flat = [piece for pieces in gathered for piece in pieces]
    return pl.pallas_call(
        functools.partial(polar_body, starts, sizes, groups),
        in_specs=[SMEM, pl.BlockSpec(memory_space=pltpu.VMEM)] + [ANY] * (chunks + len(flat)),
        out_specs=ANY,
        out_shape=jax.ShapeDtypeStruct(shape, F32),
        scratch_shapes=[
            pltpu.VMEM(shape, F32),
            pltpu.SemaphoreType.DMA((blocks, groups)),
            pltpu.SemaphoreType.DMA((blocks,)),
            pltpu.SemaphoreType.DMA((blocks,)),
        ]
        + [pltpu.VMEM((groups,) + pieces[0].shape, BF16) for pieces in gathered],
        compiler_params=kernel_params(63),
        cost_estimate=COST,
        name="polar_step",
    )(shrinkage, gram, *moved, *flat)


def neighbour_rows(strip, model_image, reach):
    count = lax.axis_size("strip")
    head, tail = model_image[:, :reach], model_image[:, model_image.shape[1] - reach :]
    odd = strip[0] % 2 == 1
    outer, inner = lax.optimization_barrier((jnp.where(odd, tail, head), jnp.where(odd, head, tail)))

    def exchanged(rows, firsts):
        pairs = [(i, i + 1) for i in firsts if i + 1 < count]
        return lax.ppermute(rows.astype(BF16), "strip", pairs + [(j, i) for i, j in pairs])

    return exchanged(outer, range(1, count, 2)), exchanged(inner, range(0, count, 2))


def swap(value, axis, bits):
    count = lax.axis_size(axis)
    return lax.ppermute(value, axis, [(i, i ^ bits) for i in range(count)])


def gather_channels(pixels, after=None):
    devices = lax.axis_size("chan")
    kept = [pixels] + [swap(pixels, "chan", bits) for bits in range(2, devices, 2)]
    if after is not None:
        kept = [pixels] + [gate(piece, after) for piece in kept[1:]]
    if devices == 1:
        return kept
    return kept + [swap(piece, "chan", 1) for piece in kept]


def local(grid, model_image, step_size, highpass, shrinkage):
    chans, own_rows, side_len = model_image.shape
    strips = lax.axis_size("strip")
    size = chans * lax.axis_size("chan")
    starts, sizes = chunk_rows(own_rows)
    chunks = len(sizes)
    strip = lax.axis_index("strip").astype(jnp.int32).reshape(1)

    cosine, sine_table = make_tables(side_len)
    split = np.stack([cosine.reshape(strips, own_rows, side_len), sine_table.reshape(strips, own_rows, side_len)])
    tables = [
        np.ascontiguousarray(split[:, :, start : start + rows]).reshape(2 * strips * rows, side_len)
        for start, rows in zip(starts, sizes)
    ]

    levels, taps = highpass.shape
    reach = (taps - 1) * 2 ** (levels - 1)
    outer, inner = neighbour_rows(strip, model_image, reach)
    odd = strip[0] % 2 == 1
    edges = jnp.concatenate([jnp.where(odd, inner, outer), jnp.where(odd, outer, inner)], axis=1)

    halves = {}
    moved = {}
    gathered = {}
    pixels = {}
    state = dict(last=strip, gram=jnp.zeros((GRAM_ROWS * size, GRAM_ROWS * size), F32), bases=None)

    def first(chunk):
        sent, state["last"] = first_transform(tables[chunk], grid, strips, state["last"])
        if chunk == 0:
            sent = gate(sent, outer)
            state["last"] = gate(state["last"], outer)
        if chunk == 1:
            sent = gate(sent, inner)
            base()
            sent = gate(sent, state["last"])
        halves[chunk] = lax.all_to_all(sent, "strip", split_axis=0, concat_axis=0, tiled=True)

    def base():
        state["bases"] = base_step(
            strip, strips, step_size, highpass, model_image, edges, starts, sizes, state["last"]
        )
        state["last"] = state["bases"][0]

    def second(chunk):
        moved[chunk], pixels[chunk] = second_transform(
            step_size, halves[chunk], cosine, sine_table, state["bases"][chunk], state["last"]
        )
        state["last"] = pixels[chunk]

    def gather(chunk):
        pieces = gather_channels(pixels[chunk], state["last"])
        if chans % 16:
            pieces = [jnp.concatenate(pieces, axis=1)]
        gathered[chunk] = pieces

    def gram(chunk):
        state["gram"] = gram_step(gathered[chunk], state["gram"], state["last"])
        state["last"] = state["gram"]

    first(0)
    first(1)
    first(2)
    second(0)
    second(1)
    gather(0)
    second(2)
    gather(1)
    gram(0)
    gram(1)
    gather(2)
    order = range(chunks)
    return polar_step(
        shrinkage, state["gram"], [moved[k] for k in order], [gathered[k] for k in order], starts, sizes
    )


def solution(mesh):
    return jax.shard_map(
        local,
        mesh=mesh,
        in_specs=(
            P(None, "chan", "strip", None),
            P("chan", "strip", None),
            P("chan"),
            P(),
            P("strip"),
        ),
        out_specs=P("chan", "strip", None),
        check_vma=False,
    )
```

```python
import functools

import jax
import jax.numpy as jnp
import ml_dtypes
import numpy as np
from jax import lax
from jax.experimental import pallas as pl
from jax.experimental.pallas import tpu as pltpu
from jax.sharding import PartitionSpec as P

NS_ITERS = 5
EDGE_ROWS = 16
GRAM_ROWS = 4
POLAR_ROWS = 8
HIGHEST = lax.Precision.HIGHEST
F32 = jnp.float32
BF16 = jnp.bfloat16
MIB = 1 << 20

ANY = pl.BlockSpec(memory_space=pl.ANY)
SMEM = pl.BlockSpec(memory_space=pltpu.SMEM)


def kernel_params(mebibytes):
    return pltpu.CompilerParams(vmem_limit_bytes=mebibytes * MIB)


COST = pl.CostEstimate(flops=0, bytes_accessed=1 << 16, transcendentals=0)


def dot_nt(a, b, precision=None):
    return lax.dot_general(
        a, b, (((1,), (1,)), ((), ())), precision=precision, preferred_element_type=F32
    )


def dot_nn(a, b, precision=None):
    return lax.dot_general(
        a, b, (((1,), (0,)), ((), ())), precision=precision, preferred_element_type=F32
    )


def iota(shape, dim):
    return lax.broadcasted_iota(jnp.int32, shape, dim)


def make_tables(side_len):
    indices = np.arange(side_len, dtype=np.int64)
    phases = (np.outer(indices, indices) % side_len).astype(np.float32) * np.float32(
        2.0 * 3.141592653589793 / side_len
    )
    unit_scale = np.float32(float(side_len) ** (-0.5))
    cosine = (np.cos(phases) * unit_scale).astype(ml_dtypes.bfloat16)
    sine_table = (np.sin(phases) * unit_scale).astype(ml_dtypes.bfloat16)
    return cosine, sine_table


def chunk_rows(own_rows):
    quarter = own_rows // 4
    sizes = [quarter, own_rows - 2 * quarter - EDGE_ROWS, quarter, EDGE_ROWS]
    sizes = [size for size in sizes if size > 0]
    return [sum(sizes[:place]) for place in range(len(sizes))], sizes


def gate_body(value_ref, after_ref, out_ref):
    pass


def gate(value, after):
    return pl.pallas_call(
        gate_body,
        in_specs=[ANY, ANY],
        out_specs=ANY,
        out_shape=jax.ShapeDtypeStruct(value.shape, value.dtype),
        input_output_aliases={0: 0},
        compiler_params=kernel_params(63),
        cost_estimate=COST,
        name="gate",
    )(value, after)


def first_body(table_ref, grid_ref, after_ref, out_ref, token_ref):
    token_ref[...] = jnp.zeros(token_ref.shape, F32)
    strips, _, chans, rows, width = out_ref.shape
    side_len = table_ref.shape[-1]
    table = table_ref[...]
    middle = strips * rows
    turned = jnp.concatenate([-table[middle:], table[:middle]], axis=0)
    total = dot_nt(table, grid_ref[0].reshape(chans * width, side_len))
    total = total + dot_nt(turned, grid_ref[1].reshape(chans * width, side_len))
    total = total.astype(BF16)
    for part in range(2):
        for strip in range(strips):
            first = (part * strips + strip) * rows
            for chan in range(chans):
                out_ref[strip, part, chan] = total[first : first + rows, chan * width : (chan + 1) * width]


def first_transform(table, grid, strips, after):
    _, chans, width, side_len = grid.shape
    rows = table.shape[0] // (2 * strips)
    shape = (strips, 2, chans, rows, width)
    if width % 128 or rows % 16:
        middle = strips * rows
        turned = jnp.concatenate([-table[middle:], table[:middle]], axis=0)
        total = jnp.einsum("mv,cuv->mcu", table, grid[0], preferred_element_type=F32)
        total = total + jnp.einsum("mv,cuv->mcu", turned, grid[1], preferred_element_type=F32)
        total = total.astype(BF16).reshape(2, strips, rows, chans, width)
        return total.transpose(1, 0, 3, 2, 4), jnp.zeros((8, 128), F32)
    block = 4 if chans % 4 == 0 else 1
    return pl.pallas_call(
        first_body,
        grid=(chans // block,),
        in_specs=[
            pl.BlockSpec(table.shape, lambda i: (0, 0)),
            pl.BlockSpec((2, block, width, side_len), lambda i: (0, i, 0, 0)),
            ANY,
        ],
        out_specs=[
            pl.BlockSpec((strips, 2, block, rows, width), lambda i: (0, 0, i, 0, 0)),
            pl.BlockSpec((8, 128), lambda i: (0, 0)),
        ],
        out_shape=[jax.ShapeDtypeStruct(shape, BF16), jax.ShapeDtypeStruct((8, 128), F32)],
        compiler_params=kernel_params(63),
        cost_estimate=COST,
        name="first_transform",
    )(table, grid, after)


def band_matrix(taps_of, levels, taps, own_rows, reach, first_row, image_rows):
    half_taps = taps // 2
    shape = (own_rows, own_rows + 2 * reach)
    row = iota(shape, 0)
    column = iota(shape, 1)
    place = jnp.where(
        column < own_rows, column, jnp.where(column < own_rows + reach, column - own_rows - reach, column - reach)
    )
    total = jnp.zeros(shape, F32)
    for level in range(levels):
        dilation = 2**level
        for outer in range(taps):
            detail_row = row - (outer - half_taps) * dilation
            inside = (detail_row + first_row >= 0) & (detail_row + first_row < image_rows)
            for inner in range(taps):
                hit = inside & (place == detail_row + (inner - half_taps) * dilation)
                total = total + jnp.where(hit, taps_of(level, outer) * taps_of(level, inner), 0.0)
    return total


def base_body(levels, taps, starts, strips, strip_ref, step_ref, highpass_ref, model_ref, edge_ref, after_ref, *refs):
    high, low = refs[-2:]
    out_refs = refs[:-2]
    block, own_rows, side_len = model_ref.shape
    reach = edge_ref.shape[1] // 2

    @pl.when(pl.program_id(0) == 0)
    def _():
        band = band_matrix(
            lambda level, tap: highpass_ref[level, tap],
            levels,
            taps,
            own_rows,
            reach,
            strip_ref[0] * own_rows,
            strips * own_rows,
        )
        top = band.astype(BF16)
        high[...] = top
        low[...] = (band - top.astype(F32)).astype(BF16)

    first = pl.program_id(0) * block
    for chan in range(block):
        model = model_ref[chan]
        top = model.astype(BF16)
        rest = (model - top.astype(F32)).astype(BF16)
        edge = edge_ref[chan].astype(F32)
        whole = jnp.concatenate([top.astype(F32), edge], axis=0).astype(BF16)
        gradient = dot_nn(high[...], whole)
        gradient = gradient + dot_nn(low[...], whole)
        gradient = gradient + dot_nn(high[:, :own_rows], rest)
        base = model - step_ref[first + chan] * gradient
        for start, out_ref in zip(starts, out_refs):
            out_ref[chan] = base[start : start + out_ref.shape[1]]


def base_step(strip, strips, step_size, highpass, model_image, edges, starts, sizes, after):
    chans, rows, side_len = model_image.shape
    levels, taps = highpass.shape
    reach = edges.shape[1] // 2
    block = 2 if chans % 2 == 0 else 1
    wide = rows + 2 * reach
    return pl.pallas_call(
        functools.partial(base_body, levels, taps, starts, strips),
        grid=(chans // block,),
        in_specs=[
            SMEM,
            SMEM,
            SMEM,
            pl.BlockSpec((block, rows, side_len), lambda i: (i, 0, 0)),
            pl.BlockSpec((block, 2 * reach, side_len), lambda i: (i, 0, 0)),
            ANY,
        ],
        out_specs=[pl.BlockSpec((block, part, side_len), lambda i: (i, 0, 0)) for part in sizes],
        out_shape=[jax.ShapeDtypeStruct((chans, part, side_len), F32) for part in sizes],
        scratch_shapes=[pltpu.VMEM((rows, wide), BF16), pltpu.VMEM((rows, wide), BF16)],
        compiler_params=kernel_params(63),
        cost_estimate=COST,
        name="base_step",
    )(strip, step_size, highpass, model_image, edges, after)


def second_body(step_ref, half_ref, cosine_ref, sine_ref, base_ref, after_ref, moved_ref, pixels_ref):
    strips, _, chans, rows, width = half_ref.shape
    real = jnp.concatenate([half_ref[s, 0].reshape(chans * rows, width) for s in range(strips)], axis=1)
    imag = jnp.concatenate([half_ref[s, 1].reshape(chans * rows, width) for s in range(strips)], axis=1)
    dirty = dot_nn(real, cosine_ref[...]) - dot_nn(imag, sine_ref[...])
    pieces = []
    for chan in range(chans):
        moved = base_ref[chan] + step_ref[chan] * dirty[chan * rows : (chan + 1) * rows]
        moved_ref[chan] = moved
        pieces.append(moved)
    pixels_ref[...] = jnp.swapaxes(jnp.stack(pieces), 0, 1).astype(BF16)


def second_transform(step_size, half, cosine, sine_table, base, after):
    strips, _, chans, rows, width = half.shape
    side_len = cosine.shape[0]
    if width % 128 or rows % 16 or chans % 16:
        split = (strips, width, side_len)
        dirty = jnp.einsum("scmu,sul->cml", half[:, 0], cosine.reshape(split), preferred_element_type=F32)
        dirty = dirty - jnp.einsum("scmu,sul->cml", half[:, 1], sine_table.reshape(split), preferred_element_type=F32)
        moved = base + step_size[:, None, None] * dirty
        return moved, moved.astype(BF16).transpose(1, 0, 2)
    block = min(512, side_len)
    return pl.pallas_call(
        second_body,
        grid=(side_len // block,),
        in_specs=[
            SMEM,
            pl.BlockSpec(half.shape, lambda i: (0, 0, 0, 0, 0)),
            pl.BlockSpec((side_len, block), lambda i: (0, i)),
            pl.BlockSpec((side_len, block), lambda i: (0, i)),
            pl.BlockSpec((chans, rows, block), lambda i: (0, 0, i)),
            ANY,
        ],
        out_specs=[
            pl.BlockSpec((chans, rows, block), lambda i: (0, 0, i)),
            pl.BlockSpec((rows, chans, block), lambda i: (0, 0, i)),
        ],
        out_shape=[
            jax.ShapeDtypeStruct(base.shape, F32),
            jax.ShapeDtypeStruct((rows, chans, side_len), BF16),
        ],
        compiler_params=kernel_params(63),
        cost_estimate=COST,
        name="second_transform",
    )(step_size, half, cosine, sine_table, base, after)


def stacked(group_refs, first, count):
    return jnp.concatenate([ref[first + i] for i in range(count) for ref in group_refs], axis=0)


def gram_body(groups, before_ref, after_ref, *refs):
    total_ref = refs[groups]

    @pl.when(pl.program_id(0) == 0)
    def _():
        total_ref[...] = before_ref[...]

    total = total_ref[...]
    for first in range(0, refs[0].shape[0], GRAM_ROWS):
        pixels = stacked(refs[:groups], first, GRAM_ROWS)
        total = total + dot_nt(pixels, pixels)
    total_ref[...] = total


def gram_step(pieces, before, after):
    rows, chans, side_len = pieces[0].shape
    block = EDGE_ROWS // 2
    spec = pl.BlockSpec((block, chans, side_len), lambda i: (i, 0, 0))
    return pl.pallas_call(
        functools.partial(gram_body, len(pieces)),
        grid=(rows // block,),
        in_specs=[pl.BlockSpec(before.shape, lambda i: (0, 0)), ANY] + [spec] * len(pieces),
        out_specs=pl.BlockSpec(before.shape, lambda i: (0, 0)),
        out_shape=jax.ShapeDtypeStruct(before.shape, F32),
        compiler_params=kernel_params(63),
        cost_estimate=COST,
        name="gram_step",
    )(before, after, *pieces)


def newton_schulz(gram):
    size = gram.shape[0]
    frob_norm = jnp.sqrt(jnp.sum(gram * gram))
    identity = (iota((size, size), 0) == iota((size, size), 1)).astype(F32)
    current = gram / frob_norm
    middle = 0.5 * (3.0 * identity - current)
    inverse = middle
    for iteration in range(1, NS_ITERS):
        current = dot_nn(current, middle, HIGHEST)
        middle = 0.5 * (3.0 * identity - dot_nn(inverse, current, HIGHEST))
        inverse = dot_nn(middle, inverse, HIGHEST)
    return inverse, frob_norm


def polar_body(starts, sizes, groups, shrink_ref, gram_ref, *refs):
    chunks = len(sizes)
    moved_hbm = refs[:chunks]
    pixels_hbm = refs[chunks : chunks * (groups + 1)]
    out_hbm, moved, pixel_sems, moved_sems, out_sems = refs[chunks * (groups + 1) : chunks * (groups + 1) + 5]
    pixels = refs[chunks * (groups + 1) + 5 :]
    own, all_rows, side_len = moved.shape
    size = pixels[0].shape[2] * groups

    blocks = [
        (chunk, row) for chunk in [chunks - 1] + list(range(chunks - 1)) for row in range(0, sizes[chunk], EDGE_ROWS)
    ]
    far = 1 if groups > 1 else 0
    pixel_copies = []
    moved_copies = []
    for place, (chunk, row) in enumerate(blocks):
        part = pl.ds(row, EDGE_ROWS)
        into = pl.ds(starts[chunk] + row, EDGE_ROWS)
        copies = [
            pltpu.make_async_copy(
                pixels_hbm[chunk * groups + group].at[part], pixels[chunk].at[group, part], pixel_sems.at[place, group]
            )
            for group in range(0 if chunk == chunks - 1 else far, groups)
        ]
        pixel_copies.append(copies)
        moved_copies.append(
            pltpu.make_async_copy(moved_hbm[chunk].at[:, part], moved.at[:, into], moved_sems.at[place])
        )
        for copy in copies + moved_copies[-1:]:
            copy.start()

    last_blocks = sizes[-1] // EDGE_ROWS
    for copies in pixel_copies[:last_blocks]:
        for copy in copies:
            copy.wait()
    total = gram_ref[...]
    for first in range(0, sizes[-1], GRAM_ROWS):
        data = stacked([pixels[-1].at[group] for group in range(groups)], first, GRAM_ROWS)
        total = total + dot_nt(data, data)
    gram = jnp.zeros((size, size), F32)
    for i in range(GRAM_ROWS):
        gram = gram + total[i * size : (i + 1) * size, i * size : (i + 1) * size]
    inverse, frob_norm = newton_schulz(gram)
    factor = shrink_ref[0] * jnp.sqrt(all_rows * side_len / frob_norm)
    select = (iota((own, size), 0) == iota((own, size), 1)).astype(F32)
    weights = (dot_nt(select, inverse, HIGHEST) * factor).astype(BF16)
    spread = POLAR_ROWS * own
    repeat = (iota((spread, own), 0) // POLAR_ROWS == iota((spread, own), 1)).astype(BF16)
    weights = dot_nn(repeat, weights).astype(BF16)

    def widened(count, first, channel_of, pixel_row_of):
        columns = iota((size, count), 1)
        chosen = dot_nn(weights, (iota((size, count), 0) == first + channel_of(columns)).astype(BF16))
        columns = iota((spread, count), 1)
        keep = iota((spread, count), 0) % POLAR_ROWS == pixel_row_of(columns)
        return jnp.where(keep, chosen, 0.0).astype(BF16)

    others = size - far * own
    far_weights = widened(POLAR_ROWS * others, far * own, lambda c: c % others, lambda c: c // others)
    if far:
        own_weights = widened(spread, 0, lambda c: c // POLAR_ROWS, lambda c: c % POLAR_ROWS)
        far_weights = jnp.concatenate([own_weights, far_weights], axis=1)

    out_copies = []
    for place, (chunk, row) in enumerate(blocks):
        if place >= last_blocks:
            for copy in pixel_copies[place]:
                copy.wait()
        moved_copies[place].wait()
        for first in range(row, row + EDGE_ROWS, POLAR_ROWS):
            into = starts[chunk] + first
            rows = moved[:, into : into + POLAR_ROWS]
            data = stacked([pixels[chunk].at[group] for group in range(far, groups)], first, POLAR_ROWS)
            if far:
                data = jnp.concatenate([rows.reshape(spread, side_len).astype(BF16), data], axis=0)
            polar = dot_nn(far_weights, data).reshape(own, POLAR_ROWS, side_len)
            moved[:, into : into + POLAR_ROWS] = rows - polar
        part = pl.ds(starts[chunk] + row, EDGE_ROWS)
        copy = pltpu.make_async_copy(moved.at[:, part], out_hbm.at[:, part], out_sems.at[place])
        copy.start()
        out_copies.append(copy)
    for copy in out_copies:
        copy.wait()


def polar_step(shrinkage, gram, moved, gathered, starts, sizes):
    chunks = len(gathered)
    groups = len(gathered[0])
    chans, _, side_len = moved[0].shape
    shape = (chans, sum(sizes), side_len)
    blocks = sum(sizes) // EDGE_ROWS
    flat = [piece for pieces in gathered for piece in pieces]
    return pl.pallas_call(
        functools.partial(polar_body, starts, sizes, groups),
        in_specs=[SMEM, pl.BlockSpec(memory_space=pltpu.VMEM)] + [ANY] * (chunks + len(flat)),
        out_specs=ANY,
        out_shape=jax.ShapeDtypeStruct(shape, F32),
        scratch_shapes=[
            pltpu.VMEM(shape, F32),
            pltpu.SemaphoreType.DMA((blocks, groups)),
            pltpu.SemaphoreType.DMA((blocks,)),
            pltpu.SemaphoreType.DMA((blocks,)),
        ]
        + [pltpu.VMEM((groups,) + pieces[0].shape, BF16) for pieces in gathered],
        compiler_params=kernel_params(63),
        cost_estimate=COST,
        name="polar_step",
    )(shrinkage, gram, *moved, *flat)


def neighbour_rows(strip, model_image, reach):
    count = lax.axis_size("strip")
    head, tail = model_image[:, :reach], model_image[:, model_image.shape[1] - reach :]
    odd = strip[0] % 2 == 1
    outer, inner = lax.optimization_barrier((jnp.where(odd, tail, head), jnp.where(odd, head, tail)))

    def exchanged(rows, firsts):
        pairs = [(i, i + 1) for i in firsts if i + 1 < count]
        return lax.ppermute(rows.astype(BF16), "strip", pairs + [(j, i) for i, j in pairs])

    return exchanged(outer, range(1, count, 2)), exchanged(inner, range(0, count, 2))


def swap(value, axis, bits):
    count = lax.axis_size(axis)
    return lax.ppermute(value, axis, [(i, i ^ bits) for i in range(count)])


def gather_channels(pixels, after=None):
    devices = lax.axis_size("chan")
    kept = [pixels] + [swap(pixels, "chan", bits) for bits in range(2, devices, 2)]
    if after is not None:
        kept = [pixels] + [gate(piece, after) for piece in kept[1:]]
    if devices == 1:
        return kept
    return kept + [swap(piece, "chan", 1) for piece in kept]


def local(grid, model_image, step_size, highpass, shrinkage):
    chans, own_rows, side_len = model_image.shape
    strips = lax.axis_size("strip")
    size = chans * lax.axis_size("chan")
    starts, sizes = chunk_rows(own_rows)
    chunks = len(sizes)
    strip = lax.axis_index("strip").astype(jnp.int32).reshape(1)

    cosine, sine_table = make_tables(side_len)
    split = np.stack([cosine.reshape(strips, own_rows, side_len), sine_table.reshape(strips, own_rows, side_len)])
    tables = [
        np.ascontiguousarray(split[:, :, start : start + rows]).reshape(2 * strips * rows, side_len)
        for start, rows in zip(starts, sizes)
    ]

    levels, taps = highpass.shape
    reach = (taps - 1) * 2 ** (levels - 1)
    outer, inner = neighbour_rows(strip, model_image, reach)
    odd = strip[0] % 2 == 1
    edges = jnp.concatenate([jnp.where(odd, inner, outer), jnp.where(odd, outer, inner)], axis=1)

    halves = {}
    moved = {}
    gathered = {}
    pixels = {}
    done = set()
    state = dict(last=strip, gram=jnp.zeros((GRAM_ROWS * size, GRAM_ROWS * size), F32), bases=None)

    def first(chunk):
        sent, state["last"] = first_transform(tables[chunk], grid, strips, state["last"])
        if chunk == 0:
            sent = gate(sent, outer)
            state["last"] = gate(state["last"], outer)
        if chunk == 1:
            sent = gate(sent, inner)
        if chunk == 2:
            gather(0)
            gram(0)
            done.add(0)
            sent = gate(sent, state["gram"])
        halves[chunk] = lax.all_to_all(sent, "strip", split_axis=0, concat_axis=0, tiled=True)

    def base():
        state["bases"] = base_step(
            strip, strips, step_size, highpass, model_image, edges, starts, sizes, state["last"]
        )
        state["last"] = state["bases"][0]

    def second(chunk):
        moved[chunk], pixels[chunk] = second_transform(
            step_size, halves[chunk], cosine, sine_table, state["bases"][chunk], state["last"]
        )
        state["last"] = pixels[chunk]

    def gather(chunk):
        pieces = gather_channels(pixels[chunk], state["last"])
        if chans % 16:
            pieces = [jnp.concatenate(pieces, axis=1)]
        gathered[chunk] = pieces

    def gram(chunk):
        state["gram"] = gram_step(gathered[chunk], state["gram"], state["last"])
        state["last"] = state["gram"]

    first(0)
    if chunks > 1:
        first(1)
    base()
    for chunk in range(chunks):
        second(chunk)
        if chunk + 2 < chunks:
            first(chunk + 2)
        if chunk == 1:
            gather(1)
        if chunk >= 1 and chunk - 1 not in done:
            if chunk - 1 not in gathered:
                gather(chunk - 1)
            gram(chunk - 1)
    if chunks - 1 not in gathered:
        gather(chunks - 1)
    order = range(chunks)
    return polar_step(
        shrinkage, state["gram"], [moved[k] for k in order], [gathered[k] for k in order], starts, sizes
    )


def solution(mesh):
    return jax.shard_map(
        local,
        mesh=mesh,
        in_specs=(
            P(None, "chan", "strip", None),
            P("chan", "strip", None),
            P("chan"),
            P(),
            P("strip"),
        ),
        out_specs=P("chan", "strip", None),
        check_vma=False,
    )
```

```python
import functools

import jax
import jax.numpy as jnp
import ml_dtypes
import numpy as np
from jax import lax
from jax.experimental import pallas as pl
from jax.experimental.pallas import tpu as pltpu
from jax.sharding import PartitionSpec as P

NS_ITERS = 5
EDGE_ROWS = 16
GRAM_ROWS = 4
POLAR_ROWS = 8
HIGHEST = lax.Precision.HIGHEST
F32 = jnp.float32
BF16 = jnp.bfloat16
MIB = 1 << 20

ANY = pl.BlockSpec(memory_space=pl.ANY)
SMEM = pl.BlockSpec(memory_space=pltpu.SMEM)


def kernel_params(mebibytes):
    return pltpu.CompilerParams(vmem_limit_bytes=mebibytes * MIB)


COST = pl.CostEstimate(flops=0, bytes_accessed=1 << 16, transcendentals=0)


def dot_nt(a, b, precision=None):
    return lax.dot_general(
        a, b, (((1,), (1,)), ((), ())), precision=precision, preferred_element_type=F32
    )


def dot_nn(a, b, precision=None):
    return lax.dot_general(
        a, b, (((1,), (0,)), ((), ())), precision=precision, preferred_element_type=F32
    )


def iota(shape, dim):
    return lax.broadcasted_iota(jnp.int32, shape, dim)


def make_tables(side_len):
    indices = np.arange(side_len, dtype=np.int64)
    phases = (np.outer(indices, indices) % side_len).astype(np.float32) * np.float32(
        2.0 * 3.141592653589793 / side_len
    )
    unit_scale = np.float32(float(side_len) ** (-0.5))
    cosine = (np.cos(phases) * unit_scale).astype(ml_dtypes.bfloat16)
    sine_table = (np.sin(phases) * unit_scale).astype(ml_dtypes.bfloat16)
    return cosine, sine_table


def chunk_rows(own_rows):
    large = own_rows // 2 - EDGE_ROWS
    sizes = [large, large, EDGE_ROWS, EDGE_ROWS]
    sizes = [size for size in sizes if size > 0]
    return [sum(sizes[:place]) for place in range(len(sizes))], sizes


def gate_body(value_ref, after_ref, out_ref):
    pass


def gate(value, after):
    return pl.pallas_call(
        gate_body,
        in_specs=[ANY, ANY],
        out_specs=ANY,
        out_shape=jax.ShapeDtypeStruct(value.shape, value.dtype),
        input_output_aliases={0: 0},
        compiler_params=kernel_params(63),
        cost_estimate=COST,
        name="gate",
    )(value, after)


def first_body(table_ref, grid_ref, after_ref, out_ref, token_ref):
    token_ref[...] = jnp.zeros(token_ref.shape, F32)
    strips, _, chans, rows, width = out_ref.shape
    side_len = table_ref.shape[-1]
    table = table_ref[...]
    middle = strips * rows
    turned = jnp.concatenate([-table[middle:], table[:middle]], axis=0)
    total = dot_nt(table, grid_ref[0].reshape(chans * width, side_len))
    total = total + dot_nt(turned, grid_ref[1].reshape(chans * width, side_len))
    total = total.astype(BF16)
    for part in range(2):
        for strip in range(strips):
            first = (part * strips + strip) * rows
            for chan in range(chans):
                out_ref[strip, part, chan] = total[first : first + rows, chan * width : (chan + 1) * width]


def first_transform(table, grid, strips, after):
    _, chans, width, side_len = grid.shape
    rows = table.shape[0] // (2 * strips)
    shape = (strips, 2, chans, rows, width)
    if width % 128 or rows % 16:
        middle = strips * rows
        turned = jnp.concatenate([-table[middle:], table[:middle]], axis=0)
        total = jnp.einsum("mv,cuv->mcu", table, grid[0], preferred_element_type=F32)
        total = total + jnp.einsum("mv,cuv->mcu", turned, grid[1], preferred_element_type=F32)
        total = total.astype(BF16).reshape(2, strips, rows, chans, width)
        return total.transpose(1, 0, 3, 2, 4), jnp.zeros((8, 128), F32)
    block = 4 if chans % 4 == 0 else 1
    return pl.pallas_call(
        first_body,
        grid=(chans // block,),
        in_specs=[
            pl.BlockSpec(table.shape, lambda i: (0, 0)),
            pl.BlockSpec((2, block, width, side_len), lambda i: (0, i, 0, 0)),
            ANY,
        ],
        out_specs=[
            pl.BlockSpec((strips, 2, block, rows, width), lambda i: (0, 0, i, 0, 0)),
            pl.BlockSpec((8, 128), lambda i: (0, 0)),
        ],
        out_shape=[jax.ShapeDtypeStruct(shape, BF16), jax.ShapeDtypeStruct((8, 128), F32)],
        compiler_params=kernel_params(63),
        cost_estimate=COST,
        name="first_transform",
    )(table, grid, after)


def band_matrix(taps_of, levels, taps, own_rows, reach, first_row, image_rows):
    half_taps = taps // 2
    shape = (own_rows, own_rows + 2 * reach)
    row = iota(shape, 0)
    column = iota(shape, 1)
    place = jnp.where(
        column < own_rows, column, jnp.where(column < own_rows + reach, column - own_rows - reach, column - reach)
    )
    total = jnp.zeros(shape, F32)
    for level in range(levels):
        dilation = 2**level
        for outer in range(taps):
            detail_row = row - (outer - half_taps) * dilation
            inside = (detail_row + first_row >= 0) & (detail_row + first_row < image_rows)
            for inner in range(taps):
                hit = inside & (place == detail_row + (inner - half_taps) * dilation)
                total = total + jnp.where(hit, taps_of(level, outer) * taps_of(level, inner), 0.0)
    return total


def base_body(levels, taps, starts, strips, strip_ref, step_ref, highpass_ref, model_ref, edge_ref, after_ref, *refs):
    high, low = refs[-2:]
    out_refs = refs[:-2]
    block, own_rows, side_len = model_ref.shape
    reach = edge_ref.shape[1] // 2

    @pl.when(pl.program_id(0) == 0)
    def _():
        band = band_matrix(
            lambda level, tap: highpass_ref[level, tap],
            levels,
            taps,
            own_rows,
            reach,
            strip_ref[0] * own_rows,
            strips * own_rows,
        )
        top = band.astype(BF16)
        high[...] = top
        low[...] = (band - top.astype(F32)).astype(BF16)

    first = pl.program_id(0) * block
    for chan in range(block):
        model = model_ref[chan]
        top = model.astype(BF16)
        rest = (model - top.astype(F32)).astype(BF16)
        edge = edge_ref[chan].astype(F32)
        whole = jnp.concatenate([top.astype(F32), edge], axis=0).astype(BF16)
        gradient = dot_nn(high[...], whole)
        gradient = gradient + dot_nn(low[...], whole)
        gradient = gradient + dot_nn(high[:, :own_rows], rest)
        base = model - step_ref[first + chan] * gradient
        for start, out_ref in zip(starts, out_refs):
            out_ref[chan] = base[start : start + out_ref.shape[1]]


def base_step(strip, strips, step_size, highpass, model_image, edges, starts, sizes, after):
    chans, rows, side_len = model_image.shape
    levels, taps = highpass.shape
    reach = edges.shape[1] // 2
    block = 2 if chans % 2 == 0 else 1
    wide = rows + 2 * reach
    return pl.pallas_call(
        functools.partial(base_body, levels, taps, starts, strips),
        grid=(chans // block,),
        in_specs=[
            SMEM,
            SMEM,
            SMEM,
            pl.BlockSpec((block, rows, side_len), lambda i: (i, 0, 0)),
            pl.BlockSpec((block, 2 * reach, side_len), lambda i: (i, 0, 0)),
            ANY,
        ],
        out_specs=[pl.BlockSpec((block, part, side_len), lambda i: (i, 0, 0)) for part in sizes],
        out_shape=[jax.ShapeDtypeStruct((chans, part, side_len), F32) for part in sizes],
        scratch_shapes=[pltpu.VMEM((rows, wide), BF16), pltpu.VMEM((rows, wide), BF16)],
        compiler_params=kernel_params(63),
        cost_estimate=COST,
        name="base_step",
    )(strip, step_size, highpass, model_image, edges, after)


def second_body(step_ref, half_ref, cosine_ref, sine_ref, base_ref, after_ref, moved_ref, pixels_ref):
    strips, _, chans, rows, width = half_ref.shape
    real = jnp.concatenate([half_ref[s, 0].reshape(chans * rows, width) for s in range(strips)], axis=1)
    imag = jnp.concatenate([half_ref[s, 1].reshape(chans * rows, width) for s in range(strips)], axis=1)
    dirty = dot_nn(real, cosine_ref[...]) - dot_nn(imag, sine_ref[...])
    pieces = []
    for chan in range(chans):
        moved = base_ref[chan] + step_ref[chan] * dirty[chan * rows : (chan + 1) * rows]
        moved_ref[chan] = moved
        pieces.append(moved)
    pixels_ref[...] = jnp.swapaxes(jnp.stack(pieces), 0, 1).astype(BF16)


def second_transform(step_size, half, cosine, sine_table, base, after):
    strips, _, chans, rows, width = half.shape
    side_len = cosine.shape[0]
    if width % 128 or rows % 16 or chans % 16:
        split = (strips, width, side_len)
        dirty = jnp.einsum("scmu,sul->cml", half[:, 0], cosine.reshape(split), preferred_element_type=F32)
        dirty = dirty - jnp.einsum("scmu,sul->cml", half[:, 1], sine_table.reshape(split), preferred_element_type=F32)
        moved = base + step_size[:, None, None] * dirty
        return moved, moved.astype(BF16).transpose(1, 0, 2)
    block = min(512, side_len)
    return pl.pallas_call(
        second_body,
        grid=(side_len // block,),
        in_specs=[
            SMEM,
            pl.BlockSpec(half.shape, lambda i: (0, 0, 0, 0, 0)),
            pl.BlockSpec((side_len, block), lambda i: (0, i)),
            pl.BlockSpec((side_len, block), lambda i: (0, i)),
            pl.BlockSpec((chans, rows, block), lambda i: (0, 0, i)),
            ANY,
        ],
        out_specs=[
            pl.BlockSpec((chans, rows, block), lambda i: (0, 0, i)),
            pl.BlockSpec((rows, chans, block), lambda i: (0, 0, i)),
        ],
        out_shape=[
            jax.ShapeDtypeStruct(base.shape, F32),
            jax.ShapeDtypeStruct((rows, chans, side_len), BF16),
        ],
        compiler_params=kernel_params(63),
        cost_estimate=COST,
        name="second_transform",
    )(step_size, half, cosine, sine_table, base, after)


def stacked(group_refs, first, count):
    return jnp.concatenate([ref[first + i] for i in range(count) for ref in group_refs], axis=0)


def gram_body(groups, before_ref, after_ref, *refs):
    total_ref = refs[groups]

    @pl.when(pl.program_id(0) == 0)
    def _():
        total_ref[...] = before_ref[...]

    total = total_ref[...]
    for first in range(0, refs[0].shape[0], GRAM_ROWS):
        pixels = stacked(refs[:groups], first, GRAM_ROWS)
        total = total + dot_nt(pixels, pixels)
    total_ref[...] = total


def gram_step(pieces, before, after):
    rows, chans, side_len = pieces[0].shape
    block = EDGE_ROWS // 2
    spec = pl.BlockSpec((block, chans, side_len), lambda i: (i, 0, 0))
    return pl.pallas_call(
        functools.partial(gram_body, len(pieces)),
        grid=(rows // block,),
        in_specs=[pl.BlockSpec(before.shape, lambda i: (0, 0)), ANY] + [spec] * len(pieces),
        out_specs=pl.BlockSpec(before.shape, lambda i: (0, 0)),
        out_shape=jax.ShapeDtypeStruct(before.shape, F32),
        compiler_params=kernel_params(63),
        cost_estimate=COST,
        name="gram_step",
    )(before, after, *pieces)


def newton_schulz(gram):
    size = gram.shape[0]
    frob_norm = jnp.sqrt(jnp.sum(gram * gram))
    identity = (iota((size, size), 0) == iota((size, size), 1)).astype(F32)
    current = gram / frob_norm
    middle = 0.5 * (3.0 * identity - current)
    inverse = middle
    for iteration in range(1, NS_ITERS):
        current = dot_nn(current, middle, HIGHEST)
        middle = 0.5 * (3.0 * identity - dot_nn(inverse, current, HIGHEST))
        inverse = dot_nn(middle, inverse, HIGHEST)
    return inverse, frob_norm


def polar_body(starts, sizes, groups, shrink_ref, gram_ref, *refs):
    chunks = len(sizes)
    moved_hbm = refs[:chunks]
    pixels_hbm = refs[chunks : chunks * (groups + 1)]
    out_hbm, moved, pixel_sems, moved_sems, out_sems = refs[chunks * (groups + 1) : chunks * (groups + 1) + 5]
    pixels = refs[chunks * (groups + 1) + 5 :]
    own, all_rows, side_len = moved.shape
    size = pixels[0].shape[2] * groups

    blocks = [
        (chunk, row) for chunk in [chunks - 1] + list(range(chunks - 1)) for row in range(0, sizes[chunk], EDGE_ROWS)
    ]
    far = 1 if groups > 1 else 0
    pixel_copies = []
    moved_copies = []
    for place, (chunk, row) in enumerate(blocks):
        part = pl.ds(row, EDGE_ROWS)
        into = pl.ds(starts[chunk] + row, EDGE_ROWS)
        copies = [
            pltpu.make_async_copy(
                pixels_hbm[chunk * groups + group].at[part], pixels[chunk].at[group, part], pixel_sems.at[place, group]
            )
            for group in range(0 if chunk == chunks - 1 else far, groups)
        ]
        pixel_copies.append(copies)
        moved_copies.append(
            pltpu.make_async_copy(moved_hbm[chunk].at[:, part], moved.at[:, into], moved_sems.at[place])
        )
        for copy in copies + moved_copies[-1:]:
            copy.start()

    last_blocks = sizes[-1] // EDGE_ROWS
    for copies in pixel_copies[:last_blocks]:
        for copy in copies:
            copy.wait()
    total = gram_ref[...]
    for first in range(0, sizes[-1], GRAM_ROWS):
        data = stacked([pixels[-1].at[group] for group in range(groups)], first, GRAM_ROWS)
        total = total + dot_nt(data, data)
    gram = jnp.zeros((size, size), F32)
    for i in range(GRAM_ROWS):
        gram = gram + total[i * size : (i + 1) * size, i * size : (i + 1) * size]
    inverse, frob_norm = newton_schulz(gram)
    factor = shrink_ref[0] * jnp.sqrt(all_rows * side_len / frob_norm)
    select = (iota((own, size), 0) == iota((own, size), 1)).astype(F32)
    weights = (dot_nt(select, inverse, HIGHEST) * factor).astype(BF16)
    spread = POLAR_ROWS * own
    repeat = (iota((spread, own), 0) // POLAR_ROWS == iota((spread, own), 1)).astype(BF16)
    weights = dot_nn(repeat, weights).astype(BF16)

    def widened(count, first, channel_of, pixel_row_of):
        columns = iota((size, count), 1)
        chosen = dot_nn(weights, (iota((size, count), 0) == first + channel_of(columns)).astype(BF16))
        columns = iota((spread, count), 1)
        keep = iota((spread, count), 0) % POLAR_ROWS == pixel_row_of(columns)
        return jnp.where(keep, chosen, 0.0).astype(BF16)

    others = size - far * own
    far_weights = widened(POLAR_ROWS * others, far * own, lambda c: c % others, lambda c: c // others)
    if far:
        own_weights = widened(spread, 0, lambda c: c // POLAR_ROWS, lambda c: c % POLAR_ROWS)
        far_weights = jnp.concatenate([own_weights, far_weights], axis=1)

    out_copies = []
    for place, (chunk, row) in enumerate(blocks):
        if place >= last_blocks:
            for copy in pixel_copies[place]:
                copy.wait()
        moved_copies[place].wait()
        for first in range(row, row + EDGE_ROWS, POLAR_ROWS):
            into = starts[chunk] + first
            rows = moved[:, into : into + POLAR_ROWS]
            data = stacked([pixels[chunk].at[group] for group in range(far, groups)], first, POLAR_ROWS)
            if far:
                data = jnp.concatenate([rows.reshape(spread, side_len).astype(BF16), data], axis=0)
            polar = dot_nn(far_weights, data).reshape(own, POLAR_ROWS, side_len)
            moved[:, into : into + POLAR_ROWS] = rows - polar
        part = pl.ds(starts[chunk] + row, EDGE_ROWS)
        copy = pltpu.make_async_copy(moved.at[:, part], out_hbm.at[:, part], out_sems.at[place])
        copy.start()
        out_copies.append(copy)
    for copy in out_copies:
        copy.wait()


def polar_step(shrinkage, gram, moved, gathered, starts, sizes):
    chunks = len(gathered)
    groups = len(gathered[0])
    chans, _, side_len = moved[0].shape
    shape = (chans, sum(sizes), side_len)
    blocks = sum(sizes) // EDGE_ROWS
    flat = [piece for pieces in gathered for piece in pieces]
    return pl.pallas_call(
        functools.partial(polar_body, starts, sizes, groups),
        in_specs=[SMEM, pl.BlockSpec(memory_space=pltpu.VMEM)] + [ANY] * (chunks + len(flat)),
        out_specs=ANY,
        out_shape=jax.ShapeDtypeStruct(shape, F32),
        scratch_shapes=[
            pltpu.VMEM(shape, F32),
            pltpu.SemaphoreType.DMA((blocks, groups)),
            pltpu.SemaphoreType.DMA((blocks,)),
            pltpu.SemaphoreType.DMA((blocks,)),
        ]
        + [pltpu.VMEM((groups,) + pieces[0].shape, BF16) for pieces in gathered],
        compiler_params=kernel_params(63),
        cost_estimate=COST,
        name="polar_step",
    )(shrinkage, gram, *moved, *flat)


def neighbour_rows(strip, model_image, reach):
    count = lax.axis_size("strip")
    head, tail = model_image[:, :reach], model_image[:, model_image.shape[1] - reach :]
    odd = strip[0] % 2 == 1
    outer, inner = lax.optimization_barrier((jnp.where(odd, tail, head), jnp.where(odd, head, tail)))

    def exchanged(rows, firsts):
        pairs = [(i, i + 1) for i in firsts if i + 1 < count]
        return lax.ppermute(rows.astype(BF16), "strip", pairs + [(j, i) for i, j in pairs])

    return exchanged(outer, range(1, count, 2)), exchanged(inner, range(0, count, 2))


def swap(value, axis, bits):
    count = lax.axis_size(axis)
    return lax.ppermute(value, axis, [(i, i ^ bits) for i in range(count)])


def gather_channels(pixels, after=None):
    devices = lax.axis_size("chan")
    kept = [pixels] + [swap(pixels, "chan", bits) for bits in range(2, devices, 2)]
    if after is not None:
        kept = [pixels] + [gate(piece, after) for piece in kept[1:]]
    if devices == 1:
        return kept
    return kept + [swap(piece, "chan", 1) for piece in kept]


def local(grid, model_image, step_size, highpass, shrinkage):
    chans, own_rows, side_len = model_image.shape
    strips = lax.axis_size("strip")
    size = chans * lax.axis_size("chan")
    starts, sizes = chunk_rows(own_rows)
    chunks = len(sizes)
    strip = lax.axis_index("strip").astype(jnp.int32).reshape(1)

    cosine, sine_table = make_tables(side_len)
    split = np.stack([cosine.reshape(strips, own_rows, side_len), sine_table.reshape(strips, own_rows, side_len)])
    tables = [
        np.ascontiguousarray(split[:, :, start : start + rows]).reshape(2 * strips * rows, side_len)
        for start, rows in zip(starts, sizes)
    ]

    levels, taps = highpass.shape
    reach = (taps - 1) * 2 ** (levels - 1)
    outer, inner = neighbour_rows(strip, model_image, reach)
    odd = strip[0] % 2 == 1
    edges = jnp.concatenate([jnp.where(odd, inner, outer), jnp.where(odd, outer, inner)], axis=1)

    halves = {}
    moved = {}
    gathered = {}
    pixels = {}
    done = set()
    state = dict(last=strip, gram=jnp.zeros((GRAM_ROWS * size, GRAM_ROWS * size), F32), bases=None)

    def first(chunk):
        sent, state["last"] = first_transform(tables[chunk], grid, strips, state["last"])
        if chunk == 0:
            sent = gate(sent, outer)
            state["last"] = gate(state["last"], outer)
        if chunk == 1:
            sent = gate(sent, inner)
        if chunk == 2:
            gather(0)
            gram(0)
            done.add(0)
            sent = gate(sent, state["gram"])
        halves[chunk] = lax.all_to_all(sent, "strip", split_axis=0, concat_axis=0, tiled=True)

    def base():
        state["bases"] = base_step(
            strip, strips, step_size, highpass, model_image, edges, starts, sizes, state["last"]
        )
        state["last"] = state["bases"][0]

    def second(chunk):
        moved[chunk], pixels[chunk] = second_transform(
            step_size, halves[chunk], cosine, sine_table, state["bases"][chunk], state["last"]
        )
        state["last"] = pixels[chunk]

    def gather(chunk):
        pieces = gather_channels(pixels[chunk], state["last"])
        if chans % 16:
            pieces = [jnp.concatenate(pieces, axis=1)]
        gathered[chunk] = pieces

    def gram(chunk):
        state["gram"] = gram_step(gathered[chunk], state["gram"], state["last"])
        state["last"] = state["gram"]

    first(0)
    if chunks > 1:
        first(1)
    base()
    for chunk in range(chunks):
        second(chunk)
        if chunk + 2 < chunks:
            first(chunk + 2)
        if chunk == 1:
            gather(1)
        if chunk >= 1 and chunk - 1 not in done:
            if chunk - 1 not in gathered:
                gather(chunk - 1)
            gram(chunk - 1)
    if chunks - 1 not in gathered:
        gather(chunks - 1)
    order = range(chunks)
    return polar_step(
        shrinkage, state["gram"], [moved[k] for k in order], [gathered[k] for k in order], starts, sizes
    )


def solution(mesh):
    return jax.shard_map(
        local,
        mesh=mesh,
        in_specs=(
            P(None, "chan", "strip", None),
            P("chan", "strip", None),
            P("chan"),
            P(),
            P("strip"),
        ),
        out_specs=P("chan", "strip", None),
        check_vma=False,
    )
```
